128 devices in a mesh: seq: 16 (over y_hi, x, core), fsdp: 8 (over z, y_lo).
Axes of the slice: x: 4, y: 4 (y_hi: 2, y_lo: 2; y = y_hi * 2 + y_lo), z: 4, core: 2. Of those that a mesh axis runs over, the one named last changes fastest.
Arguments:
- input_token_index: int32 [2, 8, 1024], P(None, None, 'seq'), may hold values from 0 to 31999
- target_token_index: int32 [2, 8, 512], P(None, None, 'seq'), may hold values from 0 to 31999
- loss_position_index: int32 [2, 8, 512], replicated, may hold values from 0 to 63, as said below
- document_slot_index: int32 [2, 8, 1024], replicated, may hold values from 0 to 2, as said below
- row_used_length: int32 [2, 8], replicated, may hold values from 512 to 1024, as said below
- head_group_offsets: int32 [4], replicated, may hold values from 0 to 128, as said below
- embedding: float32 [32000, 2048], P('fsdp', 'seq'), may hold values from -6 to 6
- embedding_first_moment: float32 [32000, 2048], P('fsdp', 'seq'), may hold values from -2.3841858e-06 to 2.3841858e-06
- embedding_second_moment: float32 [32000, 2048], P('fsdp', 'seq'), may hold values from 2.9802322e-14 to 1.1920929e-13
- frozen_output_table: bfloat16 [32000, 2048], P('fsdp', 'seq')
- frozen_query_key_value_weight: bfloat16 [2048, 2560], P(('seq', 'fsdp')), may hold values from -0.125 to 0.125
- frozen_attention_output_weight: bfloat16 [2048, 2048], P(('seq', 'fsdp')), may hold values from -0.25 to 0.25
- frozen_gate_up_weight: bfloat16 [2048, 11264], P(('seq', 'fsdp')), may hold values from -0.125 to 0.125
- frozen_down_weight: bfloat16 [5632, 2048], P(('seq', 'fsdp')), may hold values from -0.078125 to 0.078125
- norm_gain_vectors: float32 [3, 2048], P(None, ('seq', 'fsdp')), as said below
- norm_gain_first_moment: float32 [3, 2048], P(None, ('seq', 'fsdp')), may hold values from -1.9073486e-05 to 1.9073486e-05
- norm_gain_second_moment: float32 [3, 2048], P(None, ('seq', 'fsdp')), may hold values from 1.9073486e-12 to 7.6293945e-12
- adapter_down_factors: float32 [32, 2048], P(None, ('seq', 'fsdp')), may hold values from -0.125 to 0.125
- adapter_up_factors: float32 [8, 4608], P(None, ('seq', 'fsdp')), may hold values from -1.5 to 1.5
- rank_side_statistics: float32 [8, 8, 8], replicated, as said below
- down_width_statistics: float32 [4, 2048], P(None, ('seq', 'fsdp')), may hold values from 2.3841857e-11 to 3.8146972e-10
- up_width_statistics: float32 [4608], P(('seq', 'fsdp')), may hold values from 2.3841858e-13 to 9.536743e-13
Outputs:
- document_loss_sum: float32 [], replicated
- document_total: float32 [], replicated
- global_gradient_norm: float32 [], replicated
- clipped_embedding_gradient: float32 [32000, 2048], P('fsdp', 'seq')
- updated_embedding_second_moment: float32 [32000, 2048], P('fsdp', 'seq')
- updated_embedding_table: float32 [32000, 2048], P('fsdp', 'seq')
- updated_gain_first_moment: float32 [3, 2048], P(None, ('seq', 'fsdp'))
- updated_gain_second_moment: float32 [3, 2048], P(None, ('seq', 'fsdp'))
- updated_norm_gains: float32 [3, 2048], P(None, ('seq', 'fsdp'))
- lora_a_grad: float32 [32, 2048], P(None, ('seq', 'fsdp'))
- lora_b_grad: float32 [8, 4608], P(None, ('seq', 'fsdp'))
- updated_rank_statistics: float32 [8, 8, 8], replicated
- updated_down_width_statistics: float32 [4, 2048], P(None, ('seq', 'fsdp'))
- updated_up_width_statistics: float32 [4608], P(('seq', 'fsdp'))
- updated_down_factors: float32 [32, 2048], P(None, ('seq', 'fsdp'))
- updated_up_factors: float32 [8, 4608], P(None, ('seq', 'fsdp'))
The draws below stay inside these ranges and needn't reach their ends.
Inputs may be any that keep to these rules, and one draw needn't show every extreme that they name: `loss_position_index`: each block of 32 entries holds distinct increasing offsets. `document_slot_index`: ids never fall along a row; slots at or beyond the row's length have id 2. `row_used_length`: for every row index, one of the micro-batches uses all 1024 slots. `head_group_offsets`: half of the key-value heads have a nonzero offset, one of them exactly 128; the others 0. `norm_gain_vectors`: positive. `rank_side_statistics`: diagonal with positive diagonal.
All inputs are finite; a program needn't handle non-finite values.
Results may differ from the reference program's by a relative error of at most 0.02.
Values may be sent and summed in bfloat16 or wider, within the bound.
A program may use at most 384 MiB of HBM per device.

```python
import math
import jax
import jax.numpy as jnp
import numpy as np
from jax import lax

MODEL_WIDTH = 2048
HEADS = 32
KV_HEADS = 4
HEAD_DIM = 64
FF = 5632
VOCAB = 32000
ADAPTER_RANK = 8
MICRO = 2
STEP = 5
SEQ_LEN = 1024
BATCH_ROWS = 8
TOK_DEV = 64
LOSS_DEV = 32
LOSS_LEN = 512
GROUP = 256
ADAPTER_COLUMNS = 4608


def row_layout(key):
    full_key, length_key, cut_key = jax.random.split(key, 3)
    full_micro = jax.random.randint(full_key, (BATCH_ROWS,), 0, MICRO)
    short_len = jax.random.randint(length_key, (MICRO, BATCH_ROWS), SEQ_LEN // 2, SEQ_LEN)
    is_full = jnp.arange(MICRO)[:, None] == full_micro[None, :]
    lengths = jnp.where(is_full, SEQ_LEN, short_len)
    offsets = jax.random.randint(cut_key, (MICRO, BATCH_ROWS), 0, 1 << 20)
    cut_at = GROUP // 2 + offsets % (lengths - GROUP + 1)
    places = jnp.arange(SEQ_LEN)[None, None, :]
    segments = (places >= cut_at[..., None]).astype(jnp.int32) + (places >= lengths[..., None]).astype(jnp.int32)
    segments = jnp.where(is_full[..., None], 0, segments)
    return (lengths.astype(jnp.int32), segments.astype(jnp.int32))


def draw_row_used_length(key, part):
    return row_layout(key)[0]


def draw_document_slot_index(key, part):
    return row_layout(key)[1]


def draw_loss_position_index(key, part):
    key = jax.random.fold_in(key, 5)
    blocks_n = LOSS_LEN // LOSS_DEV
    scores = jax.random.randint(key, (MICRO, BATCH_ROWS, blocks_n, TOK_DEV), 0, 1 << 14) * TOK_DEV + jnp.arange(TOK_DEV)
    picked = lax.top_k(scores, LOSS_DEV)[1]
    return jnp.sort(picked, axis=-1).reshape(MICRO, BATCH_ROWS, LOSS_LEN).astype(jnp.int32)


def draw_head_group_offsets(key, part):
    key = jax.random.fold_in(key, 7)
    order_key, value_key = jax.random.split(key)
    order = jax.random.permutation(order_key, KV_HEADS)
    free_vals = jax.random.randint(value_key, (KV_HEADS,), 1, GROUP // 2)
    free_vals = jnp.where(free_vals % TOK_DEV == 0, free_vals - 1, free_vals)
    offsets = jnp.where(order == 0, GROUP // 2, jnp.where(order < KV_HEADS // 2, free_vals, 0))
    return offsets.astype(jnp.int32)


def draw_norm_gain_vectors(key, part):
    key = jax.random.fold_in(key, 9)
    ramp_pos = jnp.arange(MODEL_WIDTH).astype(jnp.float32) / MODEL_WIDTH
    noise = jax.random.uniform(key, (3, MODEL_WIDTH), jnp.float32, 0.8, 1.2)
    ramp = 0.6 + 1.2 * ramp_pos
    return ramp[None, :] * noise


def draw_frozen_output_table(key, part):
    key = jax.random.fold_in(key, 11)
    row_pos = jnp.arange(VOCAB).astype(jnp.float32) / VOCAB
    base = jax.random.normal(key, (VOCAB, MODEL_WIDTH), jnp.float32)
    spread = 1.0 + 2.0 * row_pos
    return (base * spread[:, None] * MODEL_WIDTH ** (-0.5)).astype(jnp.bfloat16)


def draw_rank_side_statistics(key, part):
    key = jax.random.fold_in(key, 13)
    wide = 200.0 * MODEL_WIDTH
    widths = jnp.array([MODEL_WIDTH, MODEL_WIDTH, MODEL_WIDTH, MODEL_WIDTH, wide, wide, wide, wide], jnp.float32)
    base = 1e-06 / (MICRO * BATCH_ROWS * SEQ_LEN * MODEL_WIDTH)
    diag_vals = jnp.exp(jax.random.uniform(key, (8, ADAPTER_RANK), jnp.float32, 0.0, 1.3863)) * widths[:, None] * base
    return diag_vals[:, :, None] * jnp.eye(ADAPTER_RANK, dtype=jnp.float32)[None]


def set_ends(values, stream_key, low, high):
    dims = values.shape
    spot = [jax.random.randint(jax.random.fold_in(stream_key, axis), (), 0, dims[axis]) for axis in range(len(dims))]
    values = values.at[tuple(spot)].set(low)
    longest = dims.index(max(dims))
    spot[longest] = (spot[longest] + 1) % dims[longest]
    return values.at[tuple(spot)].set(high)


def block_levels(key, shape, cuts, smallest, largest):
    level = 1.0
    for axis_at, shards_of in cuts:
        steps = jax.random.uniform(jax.random.fold_in(jax.random.fold_in(key, 6), axis_at), (shards_of,), jnp.float32, smallest / len(cuts), largest / len(cuts))
        level = level * jnp.repeat(jnp.exp(steps), shape[axis_at] // shards_of).reshape((-1,) + (1,) * (len(shape) - 1 - axis_at))
    return level


def rank_table(amount, lean):
    loads = [(1 << 20) // math.isqrt(grade ** lean) + 1 for grade in range(1, amount + 1)]
    scale = 1 + sum(loads) // (1 << 30)
    return np.cumsum(np.array([max(1, weight // scale) for weight in loads]))


def skewed_ids(stream_key, dims, count, skew):
    listing = rank_table(count, skew)
    pick = jax.random.randint(jax.random.fold_in(stream_key, 1), dims, 0, int(listing[count - 1]))
    rank = jnp.searchsorted(jnp.asarray(listing, jnp.int32), pick, side="right")
    return jax.random.permutation(jax.random.fold_in(stream_key, 2), count)[rank].astype(jnp.int32)


def centred(own_key, shape, scale, bound, cuts=(), held_as=jnp.bfloat16):
    values = jax.random.normal(own_key, shape, jnp.float32) * scale
    if len(cuts) > 0:
        values = block_levels(own_key, shape, cuts, -0.22, 0.18) * values
    return jnp.clip(values, min=-bound, max=bound).astype(held_as)


def setup_inputs(seed: int = 0) -> dict:
    keys = jax.random.split(jax.random.key(seed), 23)
    input_token_index = set_ends(skewed_ids(keys[0], (MICRO, BATCH_ROWS, SEQ_LEN), VOCAB, 2), jax.random.fold_in(keys[0], 3), 0, VOCAB - 1).astype(jnp.int32)
    target_token_index = set_ends(skewed_ids(keys[1], (MICRO, BATCH_ROWS, LOSS_LEN), VOCAB, 2), jax.random.fold_in(keys[1], 3), 0, VOCAB - 1).astype(jnp.int32)
    loss_position_index = draw_loss_position_index(jax.random.fold_in(keys[22], 71), 0)
    document_slot_index = draw_document_slot_index(jax.random.fold_in(keys[22], 71), 0)
    row_used_length = draw_row_used_length(jax.random.fold_in(keys[22], 71), 0)
    head_group_offsets = draw_head_group_offsets(jax.random.fold_in(keys[22], 71), 0)
    embedding = centred(keys[6], (VOCAB, MODEL_WIDTH), 1.0, 6.0, ((0, 8), (1, 16)), jnp.float32)
    embedding_first_moment = centred(keys[7], (VOCAB, MODEL_WIDTH), (0.001 / (MICRO * BATCH_ROWS * SEQ_LEN * MODEL_WIDTH) ** 0.5), 2.384185791015625e-06, ((0, 8), (1, 16)), jnp.float32)
    embedding_second_moment = jnp.clip(jnp.exp(math.log(1.1920928924980673e-13) - 1.3862944 * jax.random.uniform(keys[8], (VOCAB, MODEL_WIDTH), jnp.float32) ** block_levels(keys[8], (VOCAB, MODEL_WIDTH), ((0, 8), (1, 16)), -0.2, 0.2)), 2.980232231245168e-14, 1.1920928924980673e-13)
    frozen_output_table = draw_frozen_output_table(jax.random.fold_in(keys[22], 71), 0)
    frozen_query_key_value_weight = centred(keys[10], (MODEL_WIDTH, MODEL_WIDTH + 2 * KV_HEADS * HEAD_DIM), MODEL_WIDTH ** -0.5, 0.125, ((0, 128),))
    frozen_attention_output_weight = centred(keys[11], (MODEL_WIDTH, MODEL_WIDTH), (MODEL_WIDTH // 4) ** -0.5, 0.25, ((0, 128),))
    frozen_gate_up_weight = centred(keys[12], (MODEL_WIDTH, 2 * FF), MODEL_WIDTH ** -0.5, 0.125, ((0, 128),))
    frozen_down_weight = centred(keys[13], (FF, MODEL_WIDTH), FF ** -0.5, 0.078125, ((0, 128),))
    norm_gain_vectors = draw_norm_gain_vectors(jax.random.fold_in(keys[22], 71), 0)
    norm_gain_first_moment = centred(keys[15], (3, MODEL_WIDTH), (0.008 / (MICRO * BATCH_ROWS * SEQ_LEN * MODEL_WIDTH) ** 0.5), 1.9073486328125e-05, ((1, 128),), jnp.float32)
    norm_gain_second_moment = jnp.clip(jnp.exp(math.log(7.62939451198763e-12) - 1.3862944 * jax.random.uniform(keys[16], (3, MODEL_WIDTH), jnp.float32) ** block_levels(keys[16], (3, MODEL_WIDTH), ((1, 128),), -0.2, 0.2)), 1.9073486279969076e-12, 7.62939451198763e-12)
    adapter_down_factors = centred(keys[17], (4 * ADAPTER_RANK, MODEL_WIDTH), MODEL_WIDTH ** -0.5, 0.125, ((1, 128),), jnp.float32)
    adapter_up_factors = centred(keys[18], (ADAPTER_RANK, ADAPTER_COLUMNS), 0.1, 1.5, ((1, 128),), jnp.float32)
    rank_side_statistics = draw_rank_side_statistics(jax.random.fold_in(keys[22], 71), 0)
    down_width_statistics = jnp.clip(jnp.exp(math.log(3.8146971692576415e-10) - 2.7725887 * jax.random.uniform(keys[20], (4, MODEL_WIDTH), jnp.float32) ** block_levels(keys[20], (4, MODEL_WIDTH), ((1, 128),), -0.2, 0.2)), 2.384185730786026e-11, 3.8146971692576415e-10)
    up_width_statistics = jnp.clip(jnp.exp(math.log(9.536743139984538e-13) - 1.3862944 * jax.random.uniform(keys[21], (ADAPTER_COLUMNS,), jnp.float32) ** block_levels(keys[21], (ADAPTER_COLUMNS,), ((0, 128),), -0.2, 0.2)), 2.3841857849961345e-13, 9.536743139984538e-13)
    return dict(input_token_index=input_token_index, target_token_index=target_token_index, loss_position_index=loss_position_index, document_slot_index=document_slot_index, row_used_length=row_used_length, head_group_offsets=head_group_offsets, embedding=embedding, embedding_first_moment=embedding_first_moment, embedding_second_moment=embedding_second_moment, frozen_output_table=frozen_output_table, frozen_query_key_value_weight=frozen_query_key_value_weight, frozen_attention_output_weight=frozen_attention_output_weight, frozen_gate_up_weight=frozen_gate_up_weight, frozen_down_weight=frozen_down_weight, norm_gain_vectors=norm_gain_vectors, norm_gain_first_moment=norm_gain_first_moment, norm_gain_second_moment=norm_gain_second_moment, adapter_down_factors=adapter_down_factors, adapter_up_factors=adapter_up_factors, rank_side_statistics=rank_side_statistics, down_width_statistics=down_width_statistics, up_width_statistics=up_width_statistics)


@jax.custom_vjp
def low(v):
    return lax.optimization_barrier(v.astype(jnp.bfloat16)).astype(jnp.float32)

@jax.custom_vjp
def low_back(v):
    return v

def low_keep(v):
    return (low(v), None)

def low_pass(kept, grad):
    return (grad,)

def back_keep(v):
    return (v, None)

def back_low(kept, grad):
    return (low(grad),)
low.defvjp(low_keep, low_pass)
low_back.defvjp(back_keep, back_low)
NORM_EPS = 1e-05
ADAPTER_SCALE = 2.0
ROPE_BASE = 10000.0
CLIP_MAX = 0.001
FIRST_DECAY = 0.5
SECOND_DECAY = 0.5
RATE_EMBED = 0.3
RATE_GAIN = 0.1
LEARN_RATE_DOWN = 0.1
LEARN_RATE_UP = 0.5
WEIGHT_DECAY = 0.01
ADAM_EPS = 1e-12
HIGHEST = lax.Precision.HIGHEST

def matrix_product(left_op, right_op):
    return jnp.dot(left_op, right_op, precision=HIGHEST)

def rms_norm(values, gain):
    return values * lax.rsqrt(lax.optimization_barrier(jnp.mean(values * values, axis=-1, keepdims=True)) + NORM_EPS) * gain

def rotate(values, places):
    half_dim = values.shape[-1] // 2
    freqs = ROPE_BASE ** (-2.0 * jnp.arange(half_dim).astype(jnp.float32) / values.shape[-1])
    angles = places[:, None] * freqs[None, :]
    cosine = jnp.cos(angles)[:, None, :]
    sine_of = jnp.sin(angles)[:, None, :]
    first_half = values[..., :half_dim]
    second_half = values[..., half_dim:]
    return jnp.concatenate([first_half * cosine - second_half * sine_of, second_half * cosine + first_half * sine_of], -1)

def rounding_twice(values):
    return low(low_back(values))

def attention(queries, key_rows, value_rows, segments, shifts):
    length = queries.shape[0]
    places = jnp.arange(length)
    grouped = queries.reshape(length, KV_HEADS, HEADS // KV_HEADS, HEAD_DIM)
    scores = low_back(jnp.einsum('ihgd,jhd->hgij', grouped, key_rows, precision=HIGHEST)) * 0.125
    group_ids = (places[None, :] + shifts[:, None]) // GROUP
    allowed = (places[:, None] >= places[None, :])[None] & (group_ids[:, :, None] == group_ids[:, None, :]) & (segments[:, None] == segments[None, :])[None]
    scores = jnp.where(allowed[:, None], scores, -1e+30)
    probs = low(jax.nn.softmax(scores, axis=-1))
    mixed = jnp.einsum('hgij,jhd->ihgd', probs, value_rows, precision=HIGHEST)
    return mixed.reshape(length, HEADS * HEAD_DIM)

def row_forward(x_start, segments, shifts, frozen, down_factor_reduced, up_factor_reduced, gain_vals):
    frozen_query_key_value_weight, frozen_attention_output_weight, frozen_gate_up_weight, frozen_down_weight = frozen
    length = x_start.shape[0]
    places = jnp.arange(length).astype(jnp.float32)
    key_value_width = KV_HEADS * HEAD_DIM
    normalized_rows = low(rms_norm(x_start, gain_vals[0]))
    adapter_input = rounding_twice(matrix_product(normalized_rows, down_factor_reduced[:3 * ADAPTER_RANK].T))
    adapter_output = jnp.concatenate([matrix_product(adapter_input[:, :ADAPTER_RANK], up_factor_reduced[:, :MODEL_WIDTH]), matrix_product(adapter_input[:, ADAPTER_RANK:2 * ADAPTER_RANK], up_factor_reduced[:, MODEL_WIDTH:MODEL_WIDTH + key_value_width]), matrix_product(adapter_input[:, 2 * ADAPTER_RANK:], up_factor_reduced[:, MODEL_WIDTH + key_value_width:MODEL_WIDTH + 2 * key_value_width])], 1)
    packed_rows = low_back(matrix_product(normalized_rows, frozen_query_key_value_weight) + ADAPTER_SCALE * adapter_output)
    queries = low(rotate(packed_rows[:, :MODEL_WIDTH].reshape(length, HEADS, HEAD_DIM), places))
    key_rows = low(rotate(packed_rows[:, MODEL_WIDTH:MODEL_WIDTH + key_value_width].reshape(length, KV_HEADS, HEAD_DIM), places))
    value_rows = low(packed_rows[:, MODEL_WIDTH + key_value_width:].reshape(length, KV_HEADS, HEAD_DIM))
    attention_output = rounding_twice(attention(queries, key_rows, value_rows, segments, shifts))
    adapter_middle = rounding_twice(matrix_product(attention_output, down_factor_reduced[3 * ADAPTER_RANK:].T))
    adapter_branch = low_back(matrix_product(attention_output, frozen_attention_output_weight) + ADAPTER_SCALE * matrix_product(adapter_middle, up_factor_reduced[:, MODEL_WIDTH + 2 * key_value_width:]))
    x_mid = x_start + adapter_branch
    normed_two = low(rms_norm(x_mid, gain_vals[1]))
    gate_up = low_back(matrix_product(normed_two, frozen_gate_up_weight))
    hidden = low(jax.nn.silu(gate_up[:, :FF]) * gate_up[:, FF:])
    x_end = x_mid + low_back(matrix_product(hidden, frozen_down_weight))
    return low(rms_norm(x_end, gain_vals[2]))

def adam_update(weight_vals, first_old, second_old, gradient, rate):
    first_new = FIRST_DECAY * first_old + (1.0 - FIRST_DECAY) * gradient
    second_new = SECOND_DECAY * second_old + (1.0 - SECOND_DECAY) * gradient * gradient
    first_hat = first_new / (1.0 - FIRST_DECAY ** STEP)
    second_hat = second_new / (1.0 - SECOND_DECAY ** STEP)
    step_vals = first_hat / (jnp.sqrt(second_hat) + ADAM_EPS) + WEIGHT_DECAY * weight_vals
    return (first_new, second_new, weight_vals - rate * step_vals)

def factor_onehot(columns, model_width_value, key_value_width):
    factor_id = (columns >= model_width_value).astype(jnp.int32) + (columns >= model_width_value + key_value_width).astype(jnp.int32) + (columns >= model_width_value + 2 * key_value_width).astype(jnp.int32)
    return (factor_id[None, :] == jnp.arange(4)[:, None]).astype(jnp.float32)

def shampoo_parts(down_factor_gradient, up_factor_gradient, onehot):
    left_three = down_factor_gradient.reshape(4, up_factor_gradient.shape[0], -1)
    stats_left = jnp.einsum('krd,ksd->krs', left_three, left_three, precision=HIGHEST)
    stats_right = jnp.einsum('rc,sc,kc->krs', up_factor_gradient, up_factor_gradient, onehot, precision=HIGHEST)
    return jnp.concatenate([stats_left, stats_right], 0)

def inverse_root(stats):
    unit_mat = jnp.eye(stats.shape[-1], dtype=stats.dtype)[None]
    norm_of = jnp.sqrt(lax.optimization_barrier(jnp.sum(stats * stats, axis=(1, 2), keepdims=True)))
    matrix = stats / norm_of
    root_mat = unit_mat * lax.rsqrt(jnp.sqrt(norm_of))
    for iteration in range(10):
        factor = (5.0 * unit_mat - matrix) * 0.25
        root_mat = jnp.einsum('kab,kbc->kac', root_mat, factor, precision=HIGHEST)
        square = jnp.einsum('kab,kbc->kac', factor, factor, precision=HIGHEST)
        fourth = jnp.einsum('kab,kbc->kac', square, square, precision=HIGHEST)
        matrix = jnp.einsum('kab,kbc->kac', fourth, matrix, precision=HIGHEST)
    return root_mat

def shampoo_apply(stats_new, width_left, width_right, down_factor_gradient, up_factor_gradient, onehot):
    roots = inverse_root(stats_new)
    left_three = down_factor_gradient.reshape(4, up_factor_gradient.shape[0], -1)
    down_factor_step = jnp.einsum('krs,ksd->krd', roots[:4], left_three, precision=HIGHEST) * lax.rsqrt(jnp.sqrt(width_left))[:, None, :]
    up_factor_step = jnp.einsum('krs,sc,kc->rc', roots[4:], up_factor_gradient, onehot, precision=HIGHEST) * lax.rsqrt(jnp.sqrt(width_right))[None, :]
    return (down_factor_step.reshape(down_factor_gradient.shape), up_factor_step)

def reference(input_token_index, target_token_index, loss_position_index, document_slot_index, row_used_length, head_group_offsets, embedding, embedding_first_moment, embedding_second_moment, frozen_output_table, frozen_query_key_value_weight, frozen_attention_output_weight, frozen_gate_up_weight, frozen_down_weight, norm_gain_vectors, norm_gain_first_moment, norm_gain_second_moment, adapter_down_factors, adapter_up_factors, rank_side_statistics, down_width_statistics, up_width_statistics):
    blocks = jnp.arange(LOSS_LEN) // LOSS_DEV
    spot_rows = (blocks * TOK_DEV + loss_position_index).astype(jnp.int32)
    counted = spot_rows < row_used_length[..., None]
    seg_at = jnp.take_along_axis(document_slot_index, spot_rows, axis=2)
    member = seg_at[..., None] == jnp.arange(3)
    counts = lax.optimization_barrier(jnp.sum((counted[..., None] & member).astype(jnp.int32), axis=2))
    document_total = jnp.sum((counts > 0).astype(jnp.float32))
    per_doc = lax.optimization_barrier(jnp.sum(jnp.where(member, counts[:, :, None, :], 0), axis=-1))
    doc_weight = jnp.where(counted, 1.0 / jnp.maximum(per_doc, 1).astype(jnp.float32), 0.0)
    frozen = tuple((weight_mat.astype(jnp.float32) for weight_mat in (frozen_query_key_value_weight, frozen_attention_output_weight, frozen_gate_up_weight, frozen_down_weight)))
    head_f32 = frozen_output_table.astype(jnp.float32)

    def training_objective(table_master, gain_vals, left_master, right_master):
        table_low = low(table_master)
        down_factor_reduced = low(left_master)
        up_factor_reduced = low(right_master)
        starts = table_low[input_token_index.reshape(-1, SEQ_LEN)]

        def per_row(running, row_items):
            x_start, segments, positions, targets, weights = row_items
            final_norm = row_forward(x_start, segments, head_group_offsets, frozen, down_factor_reduced, up_factor_reduced, gain_vals)
            logits = low_back(matrix_product(final_norm[positions], head_f32.T))
            picked = jnp.take_along_axis(logits, targets[:, None], axis=1)[:, 0]
            row_loss = jax.nn.logsumexp(logits, axis=-1) - picked
            return (running + jnp.sum(row_loss * weights), None)
        running, unused = lax.scan(jax.checkpoint(per_row), jnp.zeros((), jnp.float32), (starts, document_slot_index.reshape(-1, SEQ_LEN), spot_rows.reshape(-1, LOSS_LEN), target_token_index.reshape(-1, LOSS_LEN), doc_weight.reshape(-1, LOSS_LEN)))
        return running
    document_loss_sum, backward_function = jax.vjp(training_objective, embedding, norm_gain_vectors, adapter_down_factors, adapter_up_factors)
    grad_embed, grad_gain, down_factor_gradient, up_factor_gradient = backward_function(1.0 / document_total)
    squares = jnp.sum(grad_embed * grad_embed) + jnp.sum(grad_gain * grad_gain) + jnp.sum(down_factor_gradient * down_factor_gradient) + jnp.sum(up_factor_gradient * up_factor_gradient)
    global_gradient_norm = jnp.sqrt(squares)
    clip_factor = CLIP_MAX / jnp.maximum(global_gradient_norm, CLIP_MAX)
    grad_embed = grad_embed * clip_factor
    grad_gain = grad_gain * clip_factor
    down_factor_gradient = down_factor_gradient * clip_factor
    up_factor_gradient = up_factor_gradient * clip_factor
    unused_first, updated_embedding_second_moment, updated_embedding_table = adam_update(embedding, embedding_first_moment, embedding_second_moment, grad_embed, RATE_EMBED)
    updated_gain_first_moment, updated_gain_second_moment, updated_norm_gains = adam_update(norm_gain_vectors, norm_gain_first_moment, norm_gain_second_moment, grad_gain, RATE_GAIN)
    onehot = factor_onehot(jnp.arange(ADAPTER_COLUMNS), MODEL_WIDTH, KV_HEADS * HEAD_DIM)
    updated_rank_statistics = SECOND_DECAY * rank_side_statistics + (1.0 - SECOND_DECAY) * shampoo_parts(down_factor_gradient, up_factor_gradient, onehot)
    updated_down_width_statistics = SECOND_DECAY * down_width_statistics + (1.0 - SECOND_DECAY) * lax.optimization_barrier(jnp.sum(down_factor_gradient.reshape(4, ADAPTER_RANK, MODEL_WIDTH) ** 2, axis=1))
    updated_up_width_statistics = SECOND_DECAY * up_width_statistics + (1.0 - SECOND_DECAY) * lax.optimization_barrier(jnp.sum(up_factor_gradient * up_factor_gradient, axis=0))
    down_factor_step, up_factor_step = shampoo_apply(updated_rank_statistics, updated_down_width_statistics, updated_up_width_statistics, down_factor_gradient, up_factor_gradient, onehot)
    updated_down_factors = adapter_down_factors - LEARN_RATE_DOWN * down_factor_step
    updated_up_factors = adapter_up_factors - LEARN_RATE_UP * up_factor_step
    return (document_loss_sum, document_total, global_gradient_norm, grad_embed, updated_embedding_second_moment, updated_embedding_table, updated_gain_first_moment, updated_gain_second_moment, updated_norm_gains, down_factor_gradient, up_factor_gradient, updated_rank_statistics, updated_down_width_statistics, updated_up_width_statistics, updated_down_factors, updated_up_factors)
```

```python
import functools

import jax
import jax.numpy as jnp
from jax import lax
from jax.experimental import pallas as pl
from jax.experimental.pallas import tpu as pltpu
from jax.sharding import Mesh
from jax.sharding import PartitionSpec as P

STEP = 5
GROUP = 256
SEQ = ("seq_0", "seq_1", "seq_2")
FSDP = ("fsdp_0", "fsdp_1")
SEQ_FSDP = SEQ + FSDP
SEQ_N = 16
FSDP_N = 8
TOK = 64
PAD_FF = 6144
NORM_EPS = 1e-05
ADAPTER_SCALE = 2.0
ROPE_BASE = 10000.0
CLIP_MAX = 0.001
FIRST_DECAY = 0.5
SECOND_DECAY = 0.5
RATE_EMBED = 0.3
RATE_GAIN = 0.1
LEARN_RATE_DOWN = 0.1
LEARN_RATE_UP = 0.5
WEIGHT_DECAY = 0.01
ADAM_EPS = 1e-12
HIGHEST = lax.Precision.HIGHEST
MESH_ID = pl.DeviceIdType.MESH
ANY = pl.BlockSpec(memory_space=pl.ANY)
VMEM = pl.BlockSpec(memory_space=pltpu.VMEM)
SMEM = pl.BlockSpec(memory_space=pltpu.SMEM)
DMA = pltpu.SemaphoreType.DMA
VMEM_LIMIT = 56 * 1024 * 1024


def seq_me():
    return lax.axis_index("seq_0") * 8 + lax.axis_index("seq_1") * 2 + lax.axis_index("seq_2")


def fsdp_me():
    return lax.axis_index("fsdp_0") * 2 + lax.axis_index("fsdp_1")


def seq_at(i):
    return {"seq_0": i // 8, "seq_1": (i // 2) % 4, "seq_2": i % 2}


def fsdp_at(i):
    return {"fsdp_0": i // 2, "fsdp_1": i % 2}


RINGS = {"seq": (SEQ_N, seq_me, seq_at), "fsdp": (FSDP_N, fsdp_me, fsdp_at)}


def greet(kind, offsets):
    count, where, at = RINGS[kind]
    me = where()
    barrier = pltpu.get_barrier_semaphore()
    for k in offsets:
        pl.semaphore_signal(
            barrier, inc=1, device_id=at((me + count - k) % count), device_id_type=MESH_ID
        )
    pl.semaphore_wait(barrier, len(offsets))
    return me


def send_each(kind, me, offsets, src_of, dst_of, send_sem, recv_sem):
    count, _, at = RINGS[kind]
    copies = []
    for n, k in enumerate(offsets):
        peer = (me + k) % count
        copy = pltpu.make_async_remote_copy(
            src_ref=src_of(k, peer),
            dst_ref=dst_of(k, peer),
            send_sem=send_sem.at[n],
            recv_sem=recv_sem.at[n],
            device_id=at(peer),
            device_id_type=MESH_ID,
        )
        copy.start()
        copies.append(copy)
    return copies


def remote_call(body, out_shape, in_specs, out_specs, scratch, collective_id, name):
    return pl.pallas_call(
        body,
        out_shape=out_shape,
        in_specs=in_specs,
        out_specs=out_specs,
        scratch_shapes=scratch,
        compiler_params=pltpu.CompilerParams(
            collective_id=collective_id, has_side_effects=True, vmem_limit_bytes=VMEM_LIMIT
        ),
        name=name,
    )


def sems(n):
    return [DMA((n,)), DMA((n,))]


ALL16 = range(1, SEQ_N)
ALL8 = range(1, FSDP_N)


def gather_fsdp(blocks, collective_id, name):
    count = len(blocks)

    def body(*refs):
        ins, outs = refs[:count], refs[count : 2 * count]
        ssem, rsem, lsem = refs[2 * count :]
        me = greet("fsdp", ALL8)
        copies = []
        for n in range(count):
            copies += send_each(
                "fsdp", me, ALL8, lambda k, p: ins[n], lambda k, p: outs[n].at[me],
                ssem.at[pl.ds(7 * n, 7)], rsem.at[pl.ds(7 * n, 7)],
            )
            own = pltpu.make_async_copy(ins[n], outs[n].at[me], lsem.at[n])
            own.start()
            copies.append(own)
        for copy in copies:
            copy.wait()

    return remote_call(
        body,
        [jax.ShapeDtypeStruct((FSDP_N, *b.shape), b.dtype) for b in blocks],
        [ANY] * count,
        [ANY] * count,
        sems(7 * count) + [DMA((count,))],
        collective_id,
        name,
    )(*blocks)


def sum_over(kind, block, collective_id, name, scatter):
    count = RINGS[kind][0]
    offsets = ALL16 if kind == "seq" else ALL8
    part = block.shape[1:] if scatter else block.shape

    def body(src, out, held, ssem, rsem):
        me = greet(kind, offsets)
        copies = send_each(
            kind, me, offsets,
            (lambda k, p: src.at[p]) if scatter else (lambda k, p: src),
            lambda k, p: held.at[k - 1], ssem, rsem,
        )
        total = (src[me] if scatter else src[...]).astype(jnp.float32)
        for n, copy in enumerate(copies):
            copy.wait_recv()
            total = total + held[n].astype(jnp.float32)
        out[...] = total
        for copy in copies:
            copy.wait_send()

    return remote_call(
        body,
        jax.ShapeDtypeStruct(part, jnp.float32),
        [VMEM],
        VMEM,
        [pltpu.VMEM((count - 1, *part), block.dtype)] + sems(count - 1),
        collective_id,
        name,
    )(block)


def sum_rows(block, collective_id, name):
    _, rows, width = block.shape

    def body(src, out, held, ssem, rsem):
        me = greet("fsdp", ALL8)
        copies = send_each(
            "fsdp", me, ALL8, lambda k, p: src.at[p], lambda k, p: held.at[k - 1], ssem, rsem
        )
        out[...] = src[me].astype(jnp.float32)
        for n, copy in enumerate(copies):
            copy.wait_recv()
            out[...] += held[n].astype(jnp.float32)
        for copy in copies:
            copy.wait_send()

    return remote_call(
        body,
        jax.ShapeDtypeStruct((rows, width), jnp.float32),
        [VMEM],
        VMEM,
        [pltpu.VMEM((7, rows, width), block.dtype)] + sems(7),
        collective_id,
        name,
    )(block)


def columns_to_rows(block, collective_id, name):
    _, rows, width = block.shape

    def body(src, out, ssem, rsem, lsem):
        me = greet("seq", ALL16)
        spot = pl.ds(pl.multiple_of(me * width, width), width)
        copies = send_each(
            "seq", me, ALL16, lambda k, p: src.at[p], lambda k, p: out.at[:, spot], ssem, rsem
        )
        own = pltpu.make_async_copy(src.at[me], out.at[:, spot], lsem)
        own.start()
        for copy in copies:
            copy.wait()
        own.wait()

    return remote_call(
        body,
        jax.ShapeDtypeStruct((rows, SEQ_N * width), block.dtype),
        [ANY],
        ANY,
        sems(15) + [DMA],
        collective_id,
        name,
    )(block)


def rows_to_columns(block, summed, collective_id, name):
    rows = block.shape[0]
    width = block.shape[1] // SEQ_N
    part = summed.shape[1:]

    def body(src, part_src, out, total_out, held, ssem, rsem, psem, qsem, lsem):
        me = greet("seq", ALL16)

        def cols(p):
            return pl.ds(pl.multiple_of(p * width, width), width)

        copies = send_each(
            "seq", me, ALL16, lambda k, p: src.at[:, cols(p)], lambda k, p: out.at[me], ssem, rsem
        )
        parts = send_each(
            "seq", me, ALL16, lambda k, p: part_src.at[p], lambda k, p: held.at[k - 1], psem, qsem
        )
        own = pltpu.make_async_copy(src.at[:, cols(me)], out.at[me], lsem)
        own.start()
        total = part_src[me]
        for n, copy in enumerate(parts):
            copy.wait_recv()
            total = total + held[n]
        total_out[...] = total
        for copy in copies:
            copy.wait()
        for copy in parts:
            copy.wait_send()
        own.wait()

    return remote_call(
        body,
        [
            jax.ShapeDtypeStruct((SEQ_N, rows, width), block.dtype),
            jax.ShapeDtypeStruct(part, jnp.float32),
        ],
        [ANY, VMEM],
        [ANY, VMEM],
        [pltpu.VMEM((15, *part), jnp.float32)] + sems(15) + sems(15) + [DMA],
        collective_id,
        name,
    )(block, summed)


def gather_and_sum(block, summed, collective_id, name):
    def body(src, part_src, out, total_out, held, ssem, rsem, psem, qsem, lsem):
        me = greet("fsdp", ALL8)
        parts = send_each(
            "fsdp", me, ALL8, lambda k, p: part_src, lambda k, p: held.at[k - 1], psem, qsem
        )
        copies = send_each(
            "fsdp", me, ALL8, lambda k, p: src, lambda k, p: out.at[me], ssem, rsem
        )
        own = pltpu.make_async_copy(src, out.at[me], lsem)
        own.start()
        total = part_src[...]
        for n, copy in enumerate(parts):
            copy.wait_recv()
            total = total + held[n]
        total_out[...] = total
        for copy in copies:
            copy.wait()
        for copy in parts:
            copy.wait_send()
        own.wait()

    return remote_call(
        body,
        [
            jax.ShapeDtypeStruct((FSDP_N, *block.shape), block.dtype),
            jax.ShapeDtypeStruct(summed.shape, jnp.float32),
        ],
        [ANY, VMEM],
        [ANY, VMEM],
        [pltpu.VMEM((7, *summed.shape), jnp.float32)] + sems(7) + sems(7) + [DMA],
        collective_id,
        name,
    )(block, summed)


class Piece:
    def __init__(self, block, order, whole, halves):
        self.block, self.order, self.whole, self.halves = block, order, whole, halves


def gather_weights(qkvo, gate_up, down, small, head, table, ids):
    out_shape = [
        jax.ShapeDtypeStruct((2, 4, 2, 4, 2, *qkvo.shape), qkvo.dtype),
        jax.ShapeDtypeStruct((2, 4, 2, 4, 2, *gate_up.shape), gate_up.dtype),
        jax.ShapeDtypeStruct((2, 4, 2, 4, 2, *down.shape), down.dtype),
        jax.ShapeDtypeStruct((2, 4, 2, 4, 2, *small.shape), small.dtype),
        jax.ShapeDtypeStruct((head.shape[0], SEQ_N * head.shape[1]), head.dtype),
        jax.ShapeDtypeStruct((4, 2, *table.shape), table.dtype),
        jax.ShapeDtypeStruct((SEQ_N, *ids.shape), ids.dtype),
    ]
    sem_count = 400

    def body(*refs):
        ins, outs, sem = refs[:7], refs[7:14], refs[14]
        yh, x, c, z, yl = (lax.axis_index(a) for a in SEQ_FSDP)
        y = 2 * yh + yl
        where = {"x": x, "y": y, "z": z}
        seq = seq_me()
        used = [0]

        def fresh():
            used[0] += 1
            return sem.at[used[0] - 1]

        def beside(axis, step):
            at = (where[axis] + step + 4) % 4
            if axis == "x":
                return {"seq_1": at}
            if axis == "z":
                return {"fsdp_0": at}
            return {"seq_0": at // 2, "fsdp_1": at % 2}

        other = {"seq_2": 1 - c}

        barrier = pltpu.get_barrier_semaphore()
        greeted = [beside("y", 1), beside("y", -1), beside("z", 1), beside("z", -1)]
        greeted += [seq_at((seq + k) % SEQ_N) for k in ALL16]
        for device in greeted:
            pl.semaphore_signal(barrier, inc=1, device_id=device, device_id_type=MESH_ID)

        late = []

        def remote(src, dst, ssem, rsem, device):
            pltpu.make_async_remote_copy(
                src_ref=src, dst_ref=dst, send_sem=ssem, recv_sem=rsem,
                device_id=device, device_id_type=MESH_ID,
            ).start()

        def arrived(ref, rsem):
            pltpu.make_async_copy(ref, ref, rsem).wait()

        def weight_stream(ref, order, whole, halves):
            def block(done, axis, at, tail, core=c):
                place = {"yh": yh, "x": x, "z": z, "yl": yl}
                for a, value in [(a, slice(None)) for a in done] + [(axis, at)]:
                    if a == "y":
                        if isinstance(value, slice):
                            place["yh"] = place["yl"] = value
                        else:
                            place["yh"], place["yl"] = value // 2, value % 2
                    elif a is not None:
                        place[a] = value
                return ref.at[(place["yh"], place["x"], core, place["z"], place["yl"]) + tail]

            send = [fresh() for _ in order]
            across_s, across_r = fresh(), fresh()
            late.append((send[0], ref.at[(0, 0, 0, pl.ds(0, 3), 0) + whole]))
            late.append((send[1], ref.at[(0, pl.ds(0, 2), 0, pl.ds(0, 3), slice(None)) + whole]))
            late.append(
                (send[2], ref.at[(slice(None), slice(None), 0, pl.ds(0, 3), slice(None)) + whole])
            )
            late.append((across_s, ref.at[(slice(None), slice(None), c, slice(None), slice(None)) + whole]))
            late.append((across_r, ref.at[(slice(None), slice(None), 1 - c, slice(None), slice(None)) + whole]))

            def across(view):
                remote(view, view, across_s, across_r, other)

            across(block([], None, None, whole))
            for n, axis in enumerate(order):
                done = order[:n]
                at = where[axis]
                before, after, far = (at + 3) % 4, (at + 1) % 4, (at + 2) % 4
                from_before, from_after = fresh(), fresh()
                own = block(done, axis, at, whole)
                remote(own, own, send[n], from_before, beside(axis, 1))
                remote(own, own, send[n], from_after, beside(axis, -1))
                yield
                got = block(done, axis, before, whole)
                arrived(got, from_before)
                far_first = fresh()
                half = block(done, axis, before, halves[0])
                remote(half, half, send[n], far_first, beside(axis, 1))
                across(got)
                got = block(done, axis, after, whole)
                arrived(got, from_after)
                if len(halves) > 1:
                    far_second = fresh()
                    half = block(done, axis, after, halves[1])
                    remote(half, half, send[n], far_second, beside(axis, -1))
                across(got)
                yield
                arrived(block(done, axis, far, halves[0]), far_first)
                if len(halves) > 1:
                    arrived(block(done, axis, far, halves[1]), far_second)
                across(block(done, axis, far, whole))

        def table_stream(ref):
            send_y, send_z, recv_y = fresh(), fresh(), fresh()
            late.append((send_y, ref.at[0, 0]))
            late.append((send_z, ref.at[pl.ds(0, 3)]))
            own = ref.at[z, yl]
            remote(own, own, send_y, recv_y, {"fsdp_1": 1 - yl})
            yield
            arrived(ref.at[z, 1 - yl], recv_y)
            half_rows = ref.shape[2] // 2
            first, second = pl.ds(0, half_rows), pl.ds(half_rows, half_rows)
            before, after, far = (z + 3) % 4, (z + 1) % 4, (z + 2) % 4
            from_before, from_after, far_first, far_second = (fresh() for _ in range(4))
            remote(ref.at[z], ref.at[z], send_z, from_before, beside("z", 1))
            remote(ref.at[z], ref.at[z], send_z, from_after, beside("z", -1))
            yield
            arrived(ref.at[before], from_before)
            half = ref.at[before, :, first]
            remote(half, half, send_z, far_first, beside("z", 1))
            arrived(ref.at[after], from_after)
            half = ref.at[after, :, second]
            remote(half, half, send_z, far_second, beside("z", -1))
            yield
            arrived(ref.at[far, :, first], far_first)
            arrived(ref.at[far, :, second], far_second)

        def head_stream(ref):
            width = head.shape[1]
            rows = ref.shape[0]

            def cols(h, at, take=slice(None)):
                start = pl.multiple_of(((h * 4 + at) * 2 + c) * width, width)
                return ref.at[take, pl.ds(start, width)]

            send_y, send_x, recv_y, across_s, across_r = (fresh() for _ in range(5))
            late.append((send_y, ref.at[:, pl.ds(0, width)]))
            late.append((send_x, ref.at[:, pl.ds(0, 6 * width)]))
            late.append((across_s, ref.at[:, pl.ds(0, 8 * width)]))
            late.append((across_r, ref.at[:, pl.ds(0, 8 * width)]))

            def across(view):
                remote(view, view, across_s, across_r, other)

            own = cols(yh, x)
            remote(own, own, send_y, recv_y, {"seq_0": 1 - yh})
            across(own)
            yield
            got = cols(1 - yh, x)
            arrived(got, recv_y)
            across(got)
            first, second = pl.ds(0, rows // 2), pl.ds(rows // 2, rows // 2)
            before, after, far = (x + 3) % 4, (x + 1) % 4, (x + 2) % 4
            marks = [[fresh() for _ in range(4)] for _ in range(2)]
            for h in range(2):
                own = cols(h, x)
                remote(own, own, send_x, marks[h][0], beside("x", 1))
                remote(own, own, send_x, marks[h][1], beside("x", -1))
            yield
            for h in range(2):
                got = cols(h, before)
                arrived(got, marks[h][0])
                half = cols(h, before, first)
                remote(half, half, send_x, marks[h][2], beside("x", 1))
                across(got)
                got = cols(h, after)
                arrived(got, marks[h][1])
                half = cols(h, after, second)
                remote(half, half, send_x, marks[h][3], beside("x", -1))
                across(got)
            yield
            for h in range(2):
                arrived(cols(h, far, first), marks[h][2])
                arrived(cols(h, far, second), marks[h][3])
                across(cols(h, far))

        def ids_stream(src, ref):
            send, recv = fresh(), fresh()
            for k in ALL16:
                remote(src, ref.at[seq], send, recv, seq_at((seq + k) % SEQ_N))
            late.append((send, ref.at[pl.ds(0, 15)]))
            late.append((recv, ref.at[pl.ds(0, 15)]))
            return
            yield

        own_views = [
            outs[0].at[yh, x, c, z, yl],
            outs[1].at[yh, x, c, z, yl],
            outs[2].at[yh, x, c, z, yl],
            outs[3].at[yh, x, c, z, yl],
            outs[4].at[:, pl.ds(pl.multiple_of(seq * head.shape[1], head.shape[1]), head.shape[1])],
            outs[5].at[z, yl],
            outs[6].at[seq],
        ]
        local = []
        for src, dst in zip(ins, own_views):
            copy = pltpu.make_async_copy(src, dst, fresh())
            copy.start()
            local.append(copy)
        for copy in local:
            copy.wait()
        pl.semaphore_wait(barrier, len(greeted))

        turns = (("x", "y", "z"), ("y", "z", "x"), ("z", "x", "y"))

        def column_streams(ref, start, width):
            third = width // 3
            for n, order in enumerate(turns):
                at = start + n * third
                yield weight_stream(
                    ref, order,
                    (slice(None), pl.ds(at, third)),
                    [(slice(None), pl.ds(at + k * third // 2, third // 2)) for k in range(2)],
                )

        def down_streams(ref):
            width = ref.shape[-1]
            for n, order in enumerate(turns):
                yield weight_stream(
                    ref, order,
                    (n, slice(None), slice(None)),
                    [(n, slice(None), pl.ds(k * width // 2, width // 2)) for k in range(2)],
                )

        small_all = (slice(None), slice(None))
        wide = gate_up.shape[1]
        starts = [
            [ids_stream(ins[6], outs[6]), table_stream(outs[5])]
            + list(column_streams(outs[0], 0, qkvo.shape[1]))
            + [weight_stream(outs[3], turns[0], small_all, [small_all])],
            [head_stream(outs[4])] + list(column_streams(outs[1], 0, wide // 2)),
            list(column_streams(outs[1], wide // 2, wide // 2)),
            list(down_streams(outs[2])),
        ]
        active = []
        while starts or active:
            if starts:
                active += starts.pop(0)
            still = []
            for stream in active:
                try:
                    next(stream)
                    still.append(stream)
                except StopIteration:
                    pass
            active = still
        for mark, view in late:
            arrived(view, mark)
        assert used[0] <= sem_count, used[0]

    return remote_call(
        body, out_shape, [ANY] * 7, [ANY] * 7, [DMA((sem_count,))], 1, "gather_weights"
    )(qkvo, gate_up, down, small, head, table, ids)


def look_up(table, ids):
    vocab, width = table.shape

    def body(ids_ref, table_ref, out_ref, wide, rows):
        wide[...] = table_ref[...].astype(jnp.float32)
        for s in range(SEQ_N):

            def step(t, carry):
                rows[pl.ds(t, 1), :] = wide[pl.ds(ids_ref[s, t], 1), :]
                return carry

            lax.fori_loop(0, 128, step, 0, unroll=16)
            out_ref[s] = rows[...].astype(jnp.bfloat16)

    return pl.pallas_call(
        body,
        out_shape=jax.ShapeDtypeStruct((SEQ_N, 128, width), jnp.bfloat16),
        in_specs=[SMEM, VMEM],
        out_specs=VMEM,
        scratch_shapes=[
            pltpu.VMEM((vocab, width), jnp.float32),
            pltpu.VMEM((128, width), jnp.float32),
        ],
        compiler_params=pltpu.CompilerParams(vmem_limit_bytes=VMEM_LIMIT),
        name="look_up",
    )(ids, table)


def add_rows(gradient, local_ids, vocab):
    count, width = gradient.shape
    tile = 512
    padded = -(-vocab // 512) * 512

    def body(ids_ref, grad_ref, out_ref):
        @pl.when(pl.program_id(0) == 0)
        def _():
            out_ref[...] = jnp.zeros_like(out_ref)

        ids = ids_ref[...]
        grad = grad_ref[...]

        def step(n, carry):
            start = pl.multiple_of(n * 512, 512)
            row = lax.broadcasted_iota(jnp.int32, (512, tile), 0) + start
            hot = (row == ids).astype(jnp.float32).astype(jnp.bfloat16)
            out_ref[pl.ds(start, 512), :] += jnp.dot(
                hot, grad, preferred_element_type=jnp.float32
            )
            return carry

        lax.fori_loop(0, padded // 512, step, 0)

    return pl.pallas_call(
        body,
        out_shape=jax.ShapeDtypeStruct((padded, width), jnp.float32),
        grid=(count // tile,),
        in_specs=[
            pl.BlockSpec((1, tile), lambda i: (0, i)),
            pl.BlockSpec((tile, width), lambda i: (i, 0)),
        ],
        out_specs=pl.BlockSpec((padded, width), lambda i: (0, 0)),
        compiler_params=pltpu.CompilerParams(vmem_limit_bytes=VMEM_LIMIT),
        name="add_rows",
    )(local_ids.reshape(1, count), gradient)


def turn(values, cosine, sine):
    width = values.shape[-1]
    lane = lax.broadcasted_iota(jnp.int32, values.shape, values.ndim - 1)
    swapped = jnp.where(
        lane % 64 < 32,
        pltpu.roll(values, width - 32, values.ndim - 1),
        pltpu.roll(values, 32, values.ndim - 1),
    )
    return values * cosine + swapped * sine


def key_value_window(key_value, cosine, sine, collective_id):
    def body(kv_ref, cos_ref, sin_ref, out, held, ssem, rsem, lsem):
        me = greet("seq", range(1, 5))
        for m in range(2):
            rows = kv_ref[pl.ds(m * TOK, TOK), :]
            held[m, :, 0:256] = turn(rows[:, 0:256], cos_ref[:, 0:256], sin_ref[:, 0:256]).astype(
                jnp.bfloat16
            )
            held[m, :, 256:512] = rows[:, 256:512].astype(jnp.bfloat16)
        copies = send_each(
            "seq", me, range(1, 5), lambda k, p: held,
            lambda k, p: out.at[:, pl.ds((4 - k) * TOK, TOK), :], ssem, rsem,
        )
        own = pltpu.make_async_copy(held, out.at[:, pl.ds(4 * TOK, TOK), :], lsem)
        own.start()
        for copy in copies:
            copy.wait()
        own.wait()

    return remote_call(
        body,
        jax.ShapeDtypeStruct((2, 5 * TOK, 512), jnp.bfloat16),
        [VMEM] * 3,
        VMEM,
        [pltpu.VMEM((2, TOK, 512), jnp.bfloat16)] + sems(4) + [DMA],
        collective_id,
        "key_value_window",
    )(key_value, cosine, sine)


def key_value_back(far, own, cosine, sine, collective_id):
    def body(far_ref, own_ref, cos_ref, sin_ref, out, held, ssem, rsem):
        me = greet("seq", range(12, 16))
        copies = send_each(
            "seq", me, range(12, 16),
            lambda k, p: far_ref.at[:, pl.ds((k - 12) * TOK, TOK), :],
            lambda k, p: held.at[k - 12], ssem, rsem,
        )
        for copy in copies:
            copy.wait_recv()
        for m in range(2):
            total = own_ref[m]
            for n in range(3, -1, -1):
                total = total + held[n, m].astype(jnp.float32)
            keys = turn(total[:, 0:256], cos_ref[:, 0:256], -sin_ref[:, 0:256])
            out[pl.ds(m * TOK, TOK), 0:256] = keys.astype(jnp.bfloat16)
            out[pl.ds(m * TOK, TOK), 256:512] = total[:, 256:512].astype(jnp.bfloat16)
        for copy in copies:
            copy.wait_send()

    return remote_call(
        body,
        jax.ShapeDtypeStruct((2 * TOK, 512), jnp.bfloat16),
        [VMEM] * 4,
        VMEM,
        [pltpu.VMEM((4, 2, TOK, 512), jnp.bfloat16)] + sems(4),
        collective_id,
        "key_value_back",
    )(far, own, cosine, sine)


def spread_heads(block):
    return jnp.concatenate([block[:, 64 * g : 64 * g + 64] for g in range(8)], axis=0)


def join_heads(block):
    return jnp.concatenate([block[64 * g : 64 * g + 64, :] for g in range(8)], axis=1)


def window_mask(start_ref, query_seg, key_seg, shift):
    start = start_ref[0]
    query = start + lax.broadcasted_iota(jnp.int32, (TOK, 5 * TOK), 0)
    key = start - 4 * TOK + lax.broadcasted_iota(jnp.int32, (TOK, 5 * TOK), 1)
    allowed = (
        (key <= query)
        & (key >= 0)
        & (query_seg == key_seg)
        & (((query + shift) >> 8) == ((key + shift) >> 8))
    )
    return jnp.concatenate([allowed.astype(jnp.float32)] * 8, axis=0) > 0.5


def nt(left, right):
    return lax.dot_general(
        left, right, (((1,), (1,)), ((), ())), preferred_element_type=jnp.float32
    )


def tn(left, right):
    return lax.dot_general(
        left, right, (((0,), (0,)), ((), ())), preferred_element_type=jnp.float32
    )


def probabilities(queries, keys, mask):
    scores = jnp.where(mask, nt(queries, keys) * 0.125, -1e30)
    top = jnp.max(scores, axis=-1, keepdims=True)
    raised = jnp.where(mask, jnp.exp(scores - top), 0.0)
    return raised / jnp.sum(raised, axis=-1, keepdims=True)


def attend(queries, window, cosine, sine, query_seg, key_seg, start, shifts):
    def body(start_ref, shift_ref, q_ref, kv_ref, cos_ref, sin_ref, qs_ref, ks_ref, q_out, a_out):
        for h in range(4):
            cols = slice(512 * h, 512 * h + 512)
            turned = turn(q_ref[:, cols], cos_ref[...], sin_ref[...]).astype(jnp.bfloat16)
            q_out[:, cols] = turned
            mask = window_mask(start_ref, qs_ref[0], ks_ref[0], shift_ref[h])
            probs = probabilities(spread_heads(turned), kv_ref[0, :, 64 * h : 64 * h + 64], mask)
            values = kv_ref[0, :, 256 + 64 * h : 256 + 64 * h + 64]
            mixed = jnp.dot(probs.astype(jnp.bfloat16), values, preferred_element_type=jnp.float32)
            a_out[:, cols] = join_heads(mixed).astype(jnp.bfloat16)

    wide = pl.BlockSpec((TOK, 2048), lambda m: (m, 0))
    return pl.pallas_call(
        body,
        out_shape=[jax.ShapeDtypeStruct((2 * TOK, 2048), jnp.bfloat16)] * 2,
        grid=(2,),
        in_specs=[
            SMEM,
            SMEM,
            wide,
            pl.BlockSpec((1, 5 * TOK, 512), lambda m: (m, 0, 0)),
            pl.BlockSpec((TOK, 512), lambda m: (0, 0)),
            pl.BlockSpec((TOK, 512), lambda m: (0, 0)),
            pl.BlockSpec((1, TOK, 1), lambda m: (m, 0, 0)),
            pl.BlockSpec((1, 1, 5 * TOK), lambda m: (m, 0, 0)),
        ],
        out_specs=[wide, wide],
        compiler_params=pltpu.CompilerParams(vmem_limit_bytes=VMEM_LIMIT),
        name="attend",
    )(start, shifts, queries, window, cosine, sine, query_seg, key_seg)


def attend_back(queries, window, upstream, cosine, sine, query_seg, key_seg, start, shifts):
    def body(
        start_ref, shift_ref, q_ref, kv_ref, g_ref, cos_ref, sin_ref, qs_ref, ks_ref,
        dq_out, far_out, own_out,
    ):
        for h in range(4):
            cols = slice(512 * h, 512 * h + 512)
            mask = window_mask(start_ref, qs_ref[0], ks_ref[0], shift_ref[h])
            spread = spread_heads(q_ref[:, cols])
            keys = kv_ref[0, :, 64 * h : 64 * h + 64]
            values = kv_ref[0, :, 256 + 64 * h : 256 + 64 * h + 64]
            probs = probabilities(spread, keys, mask)
            grads = spread_heads(g_ref[:, cols])
            d_probs = nt(grads, values)
            d_values = tn(probs.astype(jnp.bfloat16), grads)
            inner = jnp.sum(probs * d_probs, axis=-1, keepdims=True)
            d_scores = (0.125 * probs * (d_probs - inner)).astype(jnp.bfloat16)
            d_queries = join_heads(jnp.dot(d_scores, keys, preferred_element_type=jnp.float32))
            dq_out[:, cols] = turn(d_queries, cos_ref[...], -sin_ref[...]).astype(jnp.bfloat16)
            d_keys = tn(d_scores, spread)
            for at, part in ((64 * h, d_keys), (256 + 64 * h, d_values)):
                far_out[0, :, at : at + 64] = part[0 : 4 * TOK].astype(jnp.bfloat16)
                own_out[0, :, at : at + 64] = part[4 * TOK :]

    wide = pl.BlockSpec((TOK, 2048), lambda m: (m, 0))
    return pl.pallas_call(
        body,
        out_shape=[
            jax.ShapeDtypeStruct((2 * TOK, 2048), jnp.bfloat16),
            jax.ShapeDtypeStruct((2, 4 * TOK, 512), jnp.bfloat16),
            jax.ShapeDtypeStruct((2, TOK, 512), jnp.float32),
        ],
        grid=(2,),
        in_specs=[
            SMEM,
            SMEM,
            wide,
            pl.BlockSpec((1, 5 * TOK, 512), lambda m: (m, 0, 0)),
            wide,
            pl.BlockSpec((TOK, 512), lambda m: (0, 0)),
            pl.BlockSpec((TOK, 512), lambda m: (0, 0)),
            pl.BlockSpec((1, TOK, 1), lambda m: (m, 0, 0)),
            pl.BlockSpec((1, 1, 5 * TOK), lambda m: (m, 0, 0)),
        ],
        out_specs=[
            wide,
            pl.BlockSpec((1, 4 * TOK, 512), lambda m: (m, 0, 0)),
            pl.BlockSpec((1, TOK, 512), lambda m: (m, 0, 0)),
        ],
        compiler_params=pltpu.CompilerParams(vmem_limit_bytes=VMEM_LIMIT),
        name="attend_back",
    )(start, shifts, queries, window, upstream, cosine, sine, query_seg, key_seg)


def dot(left, right):
    return jnp.dot(left, right, preferred_element_type=jnp.float32)


def dot_exact(left, right):
    return jnp.dot(left, right, precision=HIGHEST)


def norm_scale(values):
    return lax.rsqrt(jnp.mean(values * values, axis=-1, keepdims=True) + NORM_EPS)


def norm_back(values, gain, upstream):
    scale_of = norm_scale(values)
    scaled = gain * upstream
    inward = scale_of * scaled - values * scale_of**3 * jnp.mean(
        scaled * values, axis=-1, keepdims=True
    )
    return (inward, jnp.sum(upstream * values * scale_of, axis=0))


def adam_update(weight_vals, first_old, second_old, gradient, rate):
    first_new = FIRST_DECAY * first_old + (1.0 - FIRST_DECAY) * gradient
    second_new = SECOND_DECAY * second_old + (1.0 - SECOND_DECAY) * gradient * gradient
    first_hat = first_new / (1.0 - FIRST_DECAY**STEP)
    second_hat = second_new / (1.0 - SECOND_DECAY**STEP)
    step_vals = first_hat / (jnp.sqrt(second_hat) + ADAM_EPS) + WEIGHT_DECAY * weight_vals
    return (first_new, second_new, weight_vals - rate * step_vals)


def factor_onehot(columns):
    factor_id = (
        (columns >= 2048).astype(jnp.int32)
        + (columns >= 2048 + 256).astype(jnp.int32)
        + (columns >= 2048 + 512).astype(jnp.int32)
    )
    return (factor_id[None, :] == jnp.arange(4)[:, None]).astype(jnp.float32)


def shampoo_parts(down_factor_gradient, up_factor_gradient, onehot):
    left_three = down_factor_gradient.reshape(4, up_factor_gradient.shape[0], -1)
    stats_left = jnp.einsum("krd,ksd->krs", left_three, left_three, precision=HIGHEST)
    stats_right = jnp.einsum(
        "rc,sc,kc->krs", up_factor_gradient, up_factor_gradient, onehot, precision=HIGHEST
    )
    return jnp.concatenate([stats_left, stats_right], 0)


def inverse_root(stats):
    unit_mat = jnp.eye(stats.shape[-1], dtype=stats.dtype)[None]
    norm_of = jnp.sqrt(jnp.sum(stats * stats, axis=(1, 2), keepdims=True))
    matrix = stats / norm_of
    root_mat = unit_mat * lax.rsqrt(jnp.sqrt(norm_of))
    for iteration in range(10):
        factor = (5.0 * unit_mat - matrix) * 0.25
        root_mat = jnp.einsum("kab,kbc->kac", root_mat, factor, precision=HIGHEST)
        square = jnp.einsum("kab,kbc->kac", factor, factor, precision=HIGHEST)
        fourth = jnp.einsum("kab,kbc->kac", square, square, precision=HIGHEST)
        matrix = jnp.einsum("kab,kbc->kac", fourth, matrix, precision=HIGHEST)
    return root_mat


def shampoo_apply(
    stats_new, width_left, width_right, down_factor_gradient, up_factor_gradient, onehot
):
    roots = inverse_root(stats_new)
    left_three = down_factor_gradient.reshape(4, up_factor_gradient.shape[0], -1)
    down_factor_step = (
        jnp.einsum("krs,ksd->krd", roots[:4], left_three, precision=HIGHEST)
        * lax.rsqrt(jnp.sqrt(width_left))[:, None, :]
    )
    up_factor_step = (
        jnp.einsum("krs,sc,kc->rc", roots[4:], up_factor_gradient, onehot, precision=HIGHEST)
        * lax.rsqrt(jnp.sqrt(width_right))[None, :]
    )
    return (down_factor_step.reshape(down_factor_gradient.shape), up_factor_step)


def per_device(
    input_token_index,
    target_token_index,
    loss_position_index,
    document_slot_index,
    row_used_length,
    head_group_offsets,
    embedding,
    embedding_first_moment,
    embedding_second_moment,
    frozen_output_table,
    frozen_query_key_value_weight,
    frozen_attention_output_weight,
    frozen_gate_up_weight,
    frozen_down_weight,
    norm_gain_vectors,
    norm_gain_first_moment,
    norm_gain_second_moment,
    adapter_down_factors,
    adapter_up_factors,
    rank_side_statistics,
    down_width_statistics,
    up_width_statistics,
):
    fsdp_here = lax.axis_index(FSDP)
    seq_here = lax.axis_index(SEQ)
    vocab_dev = embedding.shape[0]

    qkvo_own = jnp.concatenate([frozen_query_key_value_weight, frozen_attention_output_weight], 1)
    gate_up_own = jnp.pad(
        frozen_gate_up_weight.reshape(16, 256, 44), ((0, 0), (0, 0), (0, 4))
    ).reshape(16, 2 * PAD_FF)
    down_own = jnp.pad(frozen_down_weight, ((0, 4), (0, 0))).reshape(3, 16, 2048)
    small_own = jnp.pad(
        jnp.concatenate(
            [
                adapter_down_factors.reshape(-1),
                norm_gain_vectors.reshape(-1),
                adapter_up_factors.reshape(-1),
            ]
        ),
        (0, 1024 - 848),
    ).reshape(8, 128)
    ids_own = jnp.pad(input_token_index.reshape(16, TOK), ((0, 0), (0, 64)))
    qkvo, gate_up_w, down_w, small, head, table, ids = gather_weights(
        qkvo_own,
        gate_up_own,
        down_own,
        small_own,
        frozen_output_table,
        embedding.astype(jnp.bfloat16),
        ids_own,
    )
    qkvo = qkvo.reshape(2048, 4608)
    w_qkv, w_out = qkvo[:, :2560], qkvo[:, 2560:]
    gate_up_w = gate_up_w.reshape(2048, 2 * PAD_FF)
    down_w = down_w.reshape(PAD_FF, 2048)
    small = small.reshape(128, 1024)
    down_full = small[:, :512].reshape(128, 32, 16).transpose(1, 0, 2).reshape(32, 2048)
    gain = small[:, 512:560].reshape(128, 3, 16).transpose(1, 0, 2).reshape(3, 2048)
    up_full = small[:, 560:848].reshape(128, 8, 36).transpose(1, 0, 2).reshape(8, 4608)
    a_low = down_full.astype(jnp.bfloat16)
    b_low = up_full.astype(jnp.bfloat16)
    a_in, a_out = a_low[:24], a_low[24:]
    factor_of = (jnp.arange(2560) >= 2048).astype(jnp.int32) + (jnp.arange(2560) >= 2304)
    b_in = jnp.where(
        (jnp.arange(24) // 8)[:, None] == factor_of[None, :],
        jnp.concatenate([b_low[:, :2560]] * 3, 0),
        jnp.zeros((), jnp.bfloat16),
    )
    b_out = b_low[:, 2560:]

    places = loss_position_index.reshape(2, 8, SEQ_N, 32)
    spots = jnp.arange(SEQ_N)[:, None] * TOK + places
    counted = spots < row_used_length[..., None, None]
    seg_blocks = document_slot_index.reshape(2, 8, SEQ_N, 1, TOK)
    seg_at = jnp.sum(
        jnp.where(places[..., None] == jnp.arange(TOK), seg_blocks, 0), axis=-1
    )
    member = counted[..., None] & (seg_at[..., None] == jnp.arange(3))
    counts = jnp.sum(member.astype(jnp.int32), axis=(2, 3))
    document_total = jnp.sum((counts > 0).astype(jnp.float32))
    own_places = lax.dynamic_index_in_dim(places, seq_here, 2, keepdims=False)
    own_counted = lax.dynamic_index_in_dim(counted, seq_here, 2, keepdims=False)
    own_seg = lax.dynamic_index_in_dim(seg_at, seq_here, 2, keepdims=False)
    per_doc = jnp.sum(
        jnp.where(own_seg[..., None] == jnp.arange(3), counts[:, :, None, :], 0), axis=-1
    )
    own_weight = jnp.where(own_counted, 1.0 / jnp.maximum(per_doc, 1).astype(jnp.float32), 0.0)
    weight_flat = own_weight.transpose(1, 0, 2).reshape(-1)
    row_places = lax.dynamic_index_in_dim(own_places, fsdp_here, 1, keepdims=False)
    chosen_at = (row_places + jnp.arange(2)[:, None] * TOK).reshape(64)
    pick = (chosen_at[:, None] == jnp.arange(128)[None, :]).astype(jnp.float32)

    ids = ids[:, :, :TOK].reshape(SEQ_N, 2, 8, TOK)
    row_ids = lax.dynamic_index_in_dim(ids, fsdp_here, 2, keepdims=False).reshape(SEQ_N, 128)
    x_start = columns_to_rows(
        look_up(table.reshape(8 * vocab_dev, 128), row_ids), 2, "rows_of_tokens"
    ).astype(jnp.float32)

    half = 32
    freqs = ROPE_BASE ** (-2.0 * jnp.arange(half).astype(jnp.float32) / 64)
    angles = (seq_here * TOK + jnp.arange(TOK)).astype(jnp.float32)[:, None] * freqs[None, :]
    cosine = jnp.tile(jnp.cos(angles), (1, 16))
    sine = jnp.sin(angles)
    sine = jnp.tile(jnp.concatenate([-sine, sine], 1), (1, 8))
    own_docs = lax.dynamic_index_in_dim(document_slot_index, fsdp_here, 1, keepdims=False)
    padded = jnp.concatenate([jnp.full((2, 4 * TOK), -1, jnp.int32), own_docs], 1)
    key_seg = lax.dynamic_slice_in_dim(padded, seq_here * TOK, 5 * TOK, 1)[:, None, :]
    query_seg = key_seg[:, 0, 4 * TOK :][:, :, None]
    start = (seq_here * TOK).reshape(1)
    normed_one = (x_start * norm_scale(x_start) * gain[0]).astype(jnp.bfloat16)
    adapter_in = nt(normed_one, a_in).astype(jnp.bfloat16)
    packed = dot(normed_one, w_qkv) + ADAPTER_SCALE * dot(adapter_in, b_in)
    window = key_value_window(packed[:, 2048:], cosine, sine, 3)
    queries, attended = attend(
        packed, window, cosine, sine, query_seg, key_seg, start, head_group_offsets
    )
    adapter_mid = nt(attended, a_out).astype(jnp.bfloat16)
    x_mid = x_start + dot(attended, w_out) + ADAPTER_SCALE * dot(adapter_mid, b_out)

    normed_two = (x_mid * norm_scale(x_mid) * gain[1]).astype(jnp.bfloat16)
    gate_up = dot(normed_two, gate_up_w)
    gate, up = gate_up[:, :PAD_FF], gate_up[:, PAD_FF:]
    hidden = (jax.nn.silu(gate) * up).astype(jnp.bfloat16)
    x_end = x_mid + dot(hidden, down_w)
    normed_end = (x_end * norm_scale(x_end) * gain[2]).astype(jnp.bfloat16)

    chosen = dot(pick.astype(jnp.bfloat16), normed_end).astype(jnp.bfloat16)
    (rows,) = gather_fsdp([chosen], 4, "chosen_rows")
    rows = rows.reshape(512, 2048)
    logits = nt(rows, head)
    local_target = target_token_index.transpose(1, 0, 2).reshape(-1) - fsdp_here * vocab_dev
    is_target = jnp.arange(vocab_dev)[None, :] == local_target[:, None]
    top_local = jnp.max(logits, axis=1)
    exp_local = jnp.sum(jnp.exp(logits - top_local[:, None]), axis=1)
    target_local = jnp.sum(jnp.where(is_target, logits, 0.0), axis=1)
    (stats,) = gather_fsdp(
        [jnp.pad(jnp.stack([top_local, exp_local]), ((0, 6), (0, 0)))], 5, "softmax_parts"
    )
    top_all = jnp.max(stats[:, 0], axis=0)
    exp_all = jnp.sum(stats[:, 1] * jnp.exp(stats[:, 0] - top_all[None, :]), axis=0)
    log_norm = top_all + jnp.log(exp_all)
    peer_of = jnp.arange(512) // 64
    loss_part = jnp.sum(jnp.where(peer_of == fsdp_here, log_norm * weight_flat, 0.0)) - jnp.sum(
        weight_flat * target_local
    )
    d_logits = (
        (weight_flat / document_total)[:, None]
        * (jnp.exp(logits - log_norm[:, None]) - is_target.astype(jnp.float32))
    ).astype(jnp.bfloat16)
    d_chosen = sum_rows(
        dot(d_logits, head).astype(jnp.bfloat16).reshape(8, 64, 2048), 6, "row_gradients"
    )

    upstream = lax.dot_general(pick, d_chosen, (((0,), (0,)), ((), ())), precision=HIGHEST)
    d_end, gain_end = norm_back(x_end, gain[2], upstream)
    d_hidden = nt(d_end.astype(jnp.bfloat16), down_w)
    sigmoid_of = jax.nn.sigmoid(gate)
    d_gate = d_hidden * up * sigmoid_of * (1.0 + gate * (1.0 - sigmoid_of))
    d_up = d_hidden * gate * sigmoid_of
    d_gate_up = jnp.concatenate([d_gate.astype(jnp.bfloat16), d_up.astype(jnp.bfloat16)], 1)
    back_two, gain_mid = norm_back(x_mid, gain[1], nt(d_gate_up, gate_up_w))
    d_mid = d_end + back_two

    d_branch = d_mid.astype(jnp.bfloat16)
    d_adapter_mid = (ADAPTER_SCALE * nt(d_branch, b_out)).astype(jnp.bfloat16)
    d_attended = (nt(d_branch, w_out) + dot(d_adapter_mid, a_out)).astype(jnp.bfloat16)
    up_gradient_out = ADAPTER_SCALE * tn(adapter_mid, d_branch)
    down_gradient_out = tn(d_adapter_mid, attended)
    d_queries, d_far, d_own = attend_back(
        queries, window, d_attended, cosine, sine, query_seg, key_seg, start, head_group_offsets
    )
    d_key_value = key_value_back(d_far, d_own, cosine, sine, 7)
    d_packed = jnp.concatenate([d_queries, d_key_value], 1)
    d_adapter_in = (ADAPTER_SCALE * nt(d_packed, b_in)).astype(jnp.bfloat16)
    up_gradient_in = ADAPTER_SCALE * jnp.concatenate(
        [
            tn(adapter_in[:, 0:8], d_packed[:, :2048]),
            tn(adapter_in[:, 8:16], d_packed[:, 2048:2304]),
            tn(adapter_in[:, 16:24], d_packed[:, 2304:]),
        ],
        1,
    )
    down_gradient_in = tn(d_adapter_in, normed_one)
    back_one, gain_start = norm_back(
        x_start, gain[0], nt(d_packed, w_qkv) + dot(d_adapter_in, a_in)
    )
    d_start = (d_mid + back_one).astype(jnp.bfloat16)

    left = jnp.concatenate(
        [
            down_gradient_in,
            down_gradient_out,
            jnp.stack([gain_start, gain_mid, gain_end]),
            jnp.zeros((5, 2048), jnp.float32),
        ],
        0,
    )
    left = left.reshape(40, 16, 128).transpose(1, 0, 2)
    right = jnp.concatenate([up_gradient_in, up_gradient_out], 1).reshape(8, 16, 288)
    right = jnp.pad(right, ((0, 0), (0, 0), (0, 96))).transpose(1, 0, 2).reshape(16, 24, 128)
    d_columns, small_sum = rows_to_columns(
        d_start, jnp.concatenate([left, right], 1), 8, "token_gradients"
    )
    d_tokens, small_sum = gather_and_sum(d_columns, small_sum, 9, "token_gradients_all")
    all_ids = ids.transpose(2, 0, 1, 3).reshape(-1) - fsdp_here * vocab_dev
    grad_embed = add_rows(d_tokens.reshape(-1, 128), all_ids, vocab_dev)[:vocab_dev]
    left_sum = small_sum[:40]
    right_sum = small_sum[40:].reshape(8, 384)[:, :288]
    group_onehot = factor_onehot(seq_here * 288 + jnp.arange(288))
    stats_part = shampoo_parts(left_sum[:32], right_sum, group_onehot)
    first = (fsdp_here == 0).astype(jnp.float32)
    squares = jnp.sum(grad_embed * grad_embed) + first * (
        jnp.sum(left_sum[:35] * left_sum[:35]) + jnp.sum(right_sum * right_sum)
    )
    totals = jnp.concatenate(
        [
            (first * stats_part).reshape(-1),
            squares.reshape(1),
            loss_part.reshape(1),
            jnp.zeros((510,), jnp.float32),
        ]
    ).reshape(8, 128)
    totals = sum_over("seq", totals, 10, "totals_seq", False)
    totals = sum_over("fsdp", totals, 11, "totals_fsdp", False)
    stats_all = totals[:4].reshape(8, 8, 8)
    document_loss_sum = totals[4, 1]
    global_gradient_norm = jnp.sqrt(totals[4, 0])
    clip_factor = CLIP_MAX / jnp.maximum(global_gradient_norm, CLIP_MAX)

    own_left = lax.dynamic_slice_in_dim(left_sum, fsdp_here * 16, 16, 1)
    down_factor_gradient = own_left[:32] * clip_factor
    grad_gain = own_left[32:35] * clip_factor
    up_factor_gradient = (
        lax.dynamic_slice_in_dim(right_sum, fsdp_here * 36, 36, 1) * clip_factor
    )
    grad_embed = grad_embed * clip_factor
    unused_first, updated_embedding_second_moment, updated_embedding_table = adam_update(
        embedding, embedding_first_moment, embedding_second_moment, grad_embed, RATE_EMBED
    )
    updated_gain_first_moment, updated_gain_second_moment, updated_norm_gains = adam_update(
        norm_gain_vectors, norm_gain_first_moment, norm_gain_second_moment, grad_gain, RATE_GAIN
    )
    updated_rank_statistics = (
        SECOND_DECAY * rank_side_statistics
        + (1.0 - SECOND_DECAY) * (clip_factor * clip_factor) * stats_all
    )
    updated_down_width_statistics = SECOND_DECAY * down_width_statistics + (
        1.0 - SECOND_DECAY
    ) * jnp.sum(down_factor_gradient.reshape(4, 8, -1) ** 2, axis=1)
    updated_up_width_statistics = SECOND_DECAY * up_width_statistics + (
        1.0 - SECOND_DECAY
    ) * jnp.sum(up_factor_gradient * up_factor_gradient, axis=0)
    onehot = factor_onehot((seq_here * 8 + fsdp_here) * 36 + jnp.arange(36))
    down_factor_step, up_factor_step = shampoo_apply(
        updated_rank_statistics,
        updated_down_width_statistics,
        updated_up_width_statistics,
        down_factor_gradient,
        up_factor_gradient,
        onehot,
    )
    updated_down_factors = adapter_down_factors - LEARN_RATE_DOWN * down_factor_step
    updated_up_factors = adapter_up_factors - LEARN_RATE_UP * up_factor_step
    return (
        document_loss_sum,
        document_total,
        global_gradient_norm,
        grad_embed,
        updated_embedding_second_moment,
        updated_embedding_table,
        updated_gain_first_moment,
        updated_gain_second_moment,
        updated_norm_gains,
        down_factor_gradient,
        up_factor_gradient,
        updated_rank_statistics,
        updated_down_width_statistics,
        updated_up_width_statistics,
        updated_down_factors,
        updated_up_factors,
    )


def solution(mesh):
    torus = Mesh(
        mesh.devices.reshape(2, 4, 2, 4, 2), SEQ_FSDP
    )
    return jax.shard_map(
        per_device,
        mesh=torus,
        in_specs=(
            P(None, None, SEQ),
            P(None, None, SEQ),
            P(),
            P(),
            P(),
            P(),
            P(FSDP, SEQ),
            P(FSDP, SEQ),
            P(FSDP, SEQ),
            P(FSDP, SEQ),
            P(SEQ_FSDP, None),
            P(SEQ_FSDP, None),
            P(SEQ_FSDP, None),
            P(SEQ_FSDP, None),
            P(None, SEQ_FSDP),
            P(None, SEQ_FSDP),
            P(None, SEQ_FSDP),
            P(None, SEQ_FSDP),
            P(None, SEQ_FSDP),
            P(),
            P(None, SEQ_FSDP),
            P(SEQ_FSDP),
        ),
        out_specs=(
            P(),
            P(),
            P(),
            P(FSDP, SEQ),
            P(FSDP, SEQ),
            P(FSDP, SEQ),
            P(None, SEQ_FSDP),
            P(None, SEQ_FSDP),
            P(None, SEQ_FSDP),
            P(None, SEQ_FSDP),
            P(None, SEQ_FSDP),
            P(),
            P(None, SEQ_FSDP),
            P(SEQ_FSDP),
            P(None, SEQ_FSDP),
            P(None, SEQ_FSDP),
        ),
        check_vma=False,
    )
```

```python
import functools

import jax
import jax.numpy as jnp
from jax import lax
from jax.experimental import pallas as pl
from jax.experimental.pallas import tpu as pltpu
from jax.sharding import Mesh
from jax.sharding import PartitionSpec as P

STEP = 5
GROUP = 256
SEQ = ("seq_0", "seq_1", "seq_2")
FSDP = ("fsdp_0", "fsdp_1")
SEQ_FSDP = SEQ + FSDP
SEQ_N = 16
FSDP_N = 8
TOK = 64
PAD_FF = 6144
NORM_EPS = 1e-05
ADAPTER_SCALE = 2.0
ROPE_BASE = 10000.0
CLIP_MAX = 0.001
FIRST_DECAY = 0.5
SECOND_DECAY = 0.5
RATE_EMBED = 0.3
RATE_GAIN = 0.1
LEARN_RATE_DOWN = 0.1
LEARN_RATE_UP = 0.5
WEIGHT_DECAY = 0.01
ADAM_EPS = 1e-12
HIGHEST = lax.Precision.HIGHEST
MESH_ID = pl.DeviceIdType.MESH
ANY = pl.BlockSpec(memory_space=pl.ANY)
VMEM = pl.BlockSpec(memory_space=pltpu.VMEM)
SMEM = pl.BlockSpec(memory_space=pltpu.SMEM)
DMA = pltpu.SemaphoreType.DMA
VMEM_LIMIT = 56 * 1024 * 1024


def seq_me():
    return lax.axis_index("seq_0") * 8 + lax.axis_index("seq_1") * 2 + lax.axis_index("seq_2")


def fsdp_me():
    return lax.axis_index("fsdp_0") * 2 + lax.axis_index("fsdp_1")


def seq_at(i):
    return {"seq_0": i // 8, "seq_1": (i // 2) % 4, "seq_2": i % 2}


def fsdp_at(i):
    return {"fsdp_0": i // 2, "fsdp_1": i % 2}


RINGS = {"seq": (SEQ_N, seq_me, seq_at), "fsdp": (FSDP_N, fsdp_me, fsdp_at)}


def greet(kind, offsets):
    count, where, at = RINGS[kind]
    me = where()
    barrier = pltpu.get_barrier_semaphore()
    for k in offsets:
        pl.semaphore_signal(
            barrier, inc=1, device_id=at((me + count - k) % count), device_id_type=MESH_ID
        )
    pl.semaphore_wait(barrier, len(offsets))
    return me


def send_each(kind, me, offsets, src_of, dst_of, send_sem, recv_sem):
    count, _, at = RINGS[kind]
    copies = []
    for n, k in enumerate(offsets):
        peer = (me + k) % count
        copy = pltpu.make_async_remote_copy(
            src_ref=src_of(k, peer),
            dst_ref=dst_of(k, peer),
            send_sem=send_sem.at[n],
            recv_sem=recv_sem.at[n],
            device_id=at(peer),
            device_id_type=MESH_ID,
        )
        copy.start()
        copies.append(copy)
    return copies


def remote_call(body, out_shape, in_specs, out_specs, scratch, collective_id, name):
    return pl.pallas_call(
        body,
        out_shape=out_shape,
        in_specs=in_specs,
        out_specs=out_specs,
        scratch_shapes=scratch,
        compiler_params=pltpu.CompilerParams(
            collective_id=collective_id, has_side_effects=True, vmem_limit_bytes=VMEM_LIMIT
        ),
        name=name,
    )


def sems(n):
    return [DMA((n,)), DMA((n,))]


ALL16 = range(1, SEQ_N)
ALL8 = range(1, FSDP_N)


def gather_fsdp(blocks, collective_id, name):
    count = len(blocks)

    def body(*refs):
        ins, outs = refs[:count], refs[count : 2 * count]
        ssem, rsem, lsem = refs[2 * count :]
        me = greet("fsdp", ALL8)
        copies = []
        for n in range(count):
            copies += send_each(
                "fsdp", me, ALL8, lambda k, p: ins[n], lambda k, p: outs[n].at[me],
                ssem.at[pl.ds(7 * n, 7)], rsem.at[pl.ds(7 * n, 7)],
            )
            own = pltpu.make_async_copy(ins[n], outs[n].at[me], lsem.at[n])
            own.start()
            copies.append(own)
        for copy in copies:
            copy.wait()

    return remote_call(
        body,
        [jax.ShapeDtypeStruct((FSDP_N, *b.shape), b.dtype) for b in blocks],
        [ANY] * count,
        [ANY] * count,
        sems(7 * count) + [DMA((count,))],
        collective_id,
        name,
    )(*blocks)


def sum_over(kind, block, collective_id, name, scatter):
    count = RINGS[kind][0]
    offsets = ALL16 if kind == "seq" else ALL8
    part = block.shape[1:] if scatter else block.shape

    def body(src, out, held, ssem, rsem):
        me = greet(kind, offsets)
        copies = send_each(
            kind, me, offsets,
            (lambda k, p: src.at[p]) if scatter else (lambda k, p: src),
            lambda k, p: held.at[k - 1], ssem, rsem,
        )
        total = (src[me] if scatter else src[...]).astype(jnp.float32)
        for n, copy in enumerate(copies):
            copy.wait_recv()
            total = total + held[n].astype(jnp.float32)
        out[...] = total
        for copy in copies:
            copy.wait_send()

    return remote_call(
        body,
        jax.ShapeDtypeStruct(part, jnp.float32),
        [VMEM],
        VMEM,
        [pltpu.VMEM((count - 1, *part), block.dtype)] + sems(count - 1),
        collective_id,
        name,
    )(block)


def sum_rows(block, collective_id, name):
    _, rows, width = block.shape

    def body(src, out, held, ssem, rsem):
        me = greet("fsdp", ALL8)
        copies = send_each(
            "fsdp", me, ALL8, lambda k, p: src.at[p], lambda k, p: held.at[k - 1], ssem, rsem
        )
        out[...] = src[me].astype(jnp.float32)
        for n, copy in enumerate(copies):
            copy.wait_recv()
            out[...] += held[n].astype(jnp.float32)
        for copy in copies:
            copy.wait_send()

    return remote_call(
        body,
        jax.ShapeDtypeStruct((rows, width), jnp.float32),
        [VMEM],
        VMEM,
        [pltpu.VMEM((7, rows, width), block.dtype)] + sems(7),
        collective_id,
        name,
    )(block)


def columns_to_rows(block, collective_id, name):
    _, rows, width = block.shape

    def body(src, out, ssem, rsem, lsem):
        me = greet("seq", ALL16)
        spot = pl.ds(pl.multiple_of(me * width, width), width)
        copies = send_each(
            "seq", me, ALL16, lambda k, p: src.at[p], lambda k, p: out.at[:, spot], ssem, rsem
        )
        own = pltpu.make_async_copy(src.at[me], out.at[:, spot], lsem)
        own.start()
        for copy in copies:
            copy.wait()
        own.wait()

    return remote_call(
        body,
        jax.ShapeDtypeStruct((rows, SEQ_N * width), block.dtype),
        [ANY],
        ANY,
        sems(15) + [DMA],
        collective_id,
        name,
    )(block)


def rows_to_columns(block, summed, collective_id, name):
    rows = block.shape[0]
    width = block.shape[1] // SEQ_N
    part = summed.shape[1:]

    def body(src, part_src, out, total_out, held, ssem, rsem, psem, qsem, lsem):
        me = greet("seq", ALL16)

        def cols(p):
            return pl.ds(pl.multiple_of(p * width, width), width)

        copies = send_each(
            "seq", me, ALL16, lambda k, p: src.at[:, cols(p)], lambda k, p: out.at[me], ssem, rsem
        )
        parts = send_each(
            "seq", me, ALL16, lambda k, p: part_src.at[p], lambda k, p: held.at[k - 1], psem, qsem
        )
        own = pltpu.make_async_copy(src.at[:, cols(me)], out.at[me], lsem)
        own.start()
        total = part_src[me]
        for n, copy in enumerate(parts):
            copy.wait_recv()
            total = total + held[n]
        total_out[...] = total
        for copy in copies:
            copy.wait()
        for copy in parts:
            copy.wait_send()
        own.wait()

    return remote_call(
        body,
        [
            jax.ShapeDtypeStruct((SEQ_N, rows, width), block.dtype),
            jax.ShapeDtypeStruct(part, jnp.float32),
        ],
        [ANY, VMEM],
        [ANY, VMEM],
        [pltpu.VMEM((15, *part), jnp.float32)] + sems(15) + sems(15) + [DMA],
        collective_id,
        name,
    )(block, summed)


def gather_and_sum(block, summed, collective_id, name):
    def body(src, part_src, out, total_out, held, ssem, rsem, psem, qsem, lsem):
        me = greet("fsdp", ALL8)
        parts = send_each(
            "fsdp", me, ALL8, lambda k, p: part_src, lambda k, p: held.at[k - 1], psem, qsem
        )
        copies = send_each(
            "fsdp", me, ALL8, lambda k, p: src, lambda k, p: out.at[me], ssem, rsem
        )
        own = pltpu.make_async_copy(src, out.at[me], lsem)
        own.start()
        total = part_src[...]
        for n, copy in enumerate(parts):
            copy.wait_recv()
            total = total + held[n]
        total_out[...] = total
        for copy in copies:
            copy.wait()
        for copy in parts:
            copy.wait_send()
        own.wait()

    return remote_call(
        body,
        [
            jax.ShapeDtypeStruct((FSDP_N, *block.shape), block.dtype),
            jax.ShapeDtypeStruct(summed.shape, jnp.float32),
        ],
        [ANY, VMEM],
        [ANY, VMEM],
        [pltpu.VMEM((7, *summed.shape), jnp.float32)] + sems(7) + sems(7) + [DMA],
        collective_id,
        name,
    )(block, summed)


ORDER = (
    "s", "q0", "q1", "q2", "t", "g0", "g1", "d0", "d1", "s", "s", "q0",
    "q0", "q1", "q1", "s", "q0", "q1", "s", "s", "s", "q2", "q2", "q0",
    "q0", "q2", "d0", "d1", "s", "s", "q0", "g0", "g1", "q1", "q1", "s",
    "q2", "q2", "d1", "d1", "d0", "d0", "q1", "q2", "t", "d1", "d0", "g1",
    "g1", "g0", "g0", "q0", "q0", "g1", "g0", "q0", "q2", "q2", "q1", "q1",
    "d0", "d0", "d1", "d1", "t", "t", "q2", "d0", "q1", "d1", "t", "g0",
    "g0", "g1", "g1", "g0", "g1",
)


def gather_weights(qkvo, gate_up, down, small, table, ids):
    quarter = gate_up.shape[1] // 4
    out_shape = [
        jax.ShapeDtypeStruct((2, 4, 2, 4, 2, *qkvo.shape), qkvo.dtype),
        jax.ShapeDtypeStruct((2, 4, 2, 4, 2, gate_up.shape[0], quarter), gate_up.dtype),
        jax.ShapeDtypeStruct((2, 4, 2, 2, *down.shape), down.dtype),
        jax.ShapeDtypeStruct((2, 4, 2, 4, 2, *small.shape), small.dtype),
        jax.ShapeDtypeStruct((4, 2, *table.shape), table.dtype),
        jax.ShapeDtypeStruct((SEQ_N, *ids.shape), ids.dtype),
    ]
    sem_count = 300
    every = slice(None)

    def body(*refs):
        ins, outs, sem = refs[:6], refs[6:12], refs[12]
        yh, x, c, z, yl = (lax.axis_index(a) for a in SEQ_FSDP)
        y = 2 * yh + yl
        where = {"x": x, "y": y, "z": z}
        seq = seq_me()
        used = [0]

        def fresh():
            used[0] += 1
            return sem.at[used[0] - 1]

        def beside(axis, step):
            at = (where[axis] + step + 4) % 4
            if axis == "x":
                return {"seq_1": at}
            if axis == "z":
                return {"fsdp_0": at}
            return {"seq_0": at // 2, "fsdp_1": at % 2}

        other = {"seq_2": 1 - c}
        column = [
            (dz, dc, {"fsdp_0": (z + dz) % 4, "seq_2": (c + dc) % 2})
            for dz in range(4)
            for dc in range(2)
            if dz or dc
        ]

        barrier = pltpu.get_barrier_semaphore()
        greeted = [beside("y", 1), beside("y", -1)]
        greeted += [device for dz, dc, device in column if dz]
        greeted += [seq_at((seq + k) % SEQ_N) for k in ALL16]
        for device in greeted:
            pl.semaphore_signal(barrier, inc=1, device_id=device, device_id_type=MESH_ID)

        late = []

        def remote(src, dst, ssem, rsem, device):
            pltpu.make_async_remote_copy(
                src_ref=src, dst_ref=dst, send_sem=ssem, recv_sem=rsem,
                device_id=device, device_id_type=MESH_ID,
            ).start()

        def arrived(ref, rsem):
            pltpu.make_async_copy(ref, ref, rsem).wait()

        def rings(block, order, sizes, halves, across):
            for n, axis in enumerate(order):
                done = order[:n]
                at = where[axis]
                before, after, far = (at + 3) % 4, (at + 1) % 4, (at + 2) % 4
                send, from_before, from_after, far_first = (fresh() for _ in range(4))
                late.append((send, sizes[n]))
                own = block(done, axis, at, None)
                remote(own, own, send, from_before, beside(axis, 1))
                remote(own, own, send, from_after, beside(axis, -1))
                yield
                got = block(done, axis, before, None)
                arrived(got, from_before)
                half = block(done, axis, before, 0)
                remote(half, half, send, far_first, beside(axis, 1))
                across(got)
                yield
                got = block(done, axis, after, None)
                arrived(got, from_after)
                if halves:
                    far_second = fresh()
                    half = block(done, axis, after, 1)
                    remote(half, half, send, far_second, beside(axis, -1))
                across(got)
                yield
                arrived(block(done, axis, far, 0), far_first)
                if halves:
                    arrived(block(done, axis, far, 1), far_second)
                across(block(done, axis, far, None))

        def place(done, axis, at):
            spot = {"yh": yh, "x": x, "z": z, "yl": yl}
            for a in done:
                if a == "y":
                    spot["yh"] = spot["yl"] = every
                else:
                    spot[a] = every
            if axis == "y":
                spot["yh"], spot["yl"] = at // 2, at % 2
            elif axis is not None:
                spot[axis] = at
            return spot

        def all_stream(ref, order, tails, halves=True):
            def block(done, axis, at, half):
                spot = place(done, axis, at)
                tail = tails[0 if half is None else half + 1]
                return ref.at[(spot["yh"], spot["x"], c, spot["z"], spot["yl"]) + tail]

            across_s, across_r = fresh(), fresh()
            late.append((across_s, ref.at[(every, every, c, every, every) + tails[0]]))
            late.append((across_r, ref.at[(every, every, 1 - c, every, every) + tails[0]]))

            def across(view):
                remote(view, view, across_s, across_r, other)

            three = pl.ds(0, 3)
            sizes = [
                ref.at[(0, 0, 0, three, 0) + tails[0]],
                ref.at[(0, pl.ds(0, 2), 0, three, every) + tails[0]],
                ref.at[(every, every, 0, three, every) + tails[0]],
            ]
            across(block([], None, None, None))
            yield from rings(block, order, sizes, halves, across)

        def nothing(view):
            return None

        def gate_up_stream(src, ref, order, start, width):
            tails = [
                (every, pl.ds(start, width)),
                (every, pl.ds(start, width // 2)),
                (every, pl.ds(start + width // 2, width // 2)),
            ]

            def block(done, axis, at, half):
                spot = place(done, axis, at)
                tail = tails[0 if half is None else half + 1]
                return ref.at[(spot["yh"], spot["x"], every, every, spot["yl"]) + tail]

            marks = []
            for dz, dc, device in column:
                send, recv = fresh(), fresh()
                first = pl.multiple_of(
                    (2 * (device["fsdp_0"] % 2) + device["seq_2"]) * quarter + start, 128
                )
                here = ref.at[(yh, x, c, z, yl) + tails[0]]
                remote(src.at[:, pl.ds(first, width)], here, send, recv, device)
                late.append((send, here))
                marks.append((ref.at[(yh, x, (c + dc) % 2, (z + 4 - dz) % 4, yl) + tails[0]], recv))
            yield
            for view, recv in marks:
                arrived(view, recv)
            three = pl.ds(0, 3)
            sizes = [
                ref.at[(0, three, every, every, 0) + tails[0]],
                ref.at[(every, three, every, every, every) + tails[0]],
            ]
            yield from rings(block, order, sizes, True, nothing)

        def down_stream(ref, order, start, width):
            tails = [
                (every, pl.ds(start, width)),
                (every, pl.ds(start, width // 2)),
                (every, pl.ds(start + width // 2, width // 2)),
            ]
            zh = z // 2

            def block(done, axis, at, half):
                spot = place(done, axis, at)
                tail = tails[0 if half is None else half + 1]
                return ref.at[(spot["yh"], spot["x"], every, spot["yl"]) + tail]

            send, recv = fresh(), fresh()
            here = ref.at[(yh, x, zh, yl) + tails[0]]
            remote(here, here, send, recv, {"fsdp_0": (z + 2) % 4})
            late.append((send, here))
            yield
            arrived(ref.at[(yh, x, 1 - zh, yl) + tails[0]], recv)
            three = pl.ds(0, 3)
            sizes = [
                ref.at[(0, three, every, 0) + tails[0]],
                ref.at[(every, three, every, every) + tails[0]],
            ]
            yield from rings(block, order, sizes, True, nothing)

        def table_stream(ref):
            send_y, recv_y = fresh(), fresh()
            late.append((send_y, ref.at[0, 0]))
            own = ref.at[z, yl]
            remote(own, own, send_y, recv_y, {"fsdp_1": 1 - yl})
            yield
            arrived(ref.at[z, 1 - yl], recv_y)
            half_rows = ref.shape[2] // 2
            part = (every, pl.ds(0, half_rows), pl.ds(half_rows, half_rows))

            def block(done, axis, at, half):
                return ref.at[at, :, part[0 if half is None else half + 1]]

            yield from rings(block, ("z",), [ref.at[pl.ds(0, 3)]], True, nothing)

        own_views = [
            (ins[0], outs[0].at[yh, x, c, z, yl]),
            (
                ins[1].at[:, pl.ds(pl.multiple_of((2 * (z % 2) + c) * quarter, 128), quarter)],
                outs[1].at[yh, x, c, z, yl],
            ),
            (ins[2], outs[2].at[yh, x, z // 2, yl]),
            (ins[3], outs[3].at[yh, x, c, z, yl]),
            (ins[4], outs[4].at[z, yl]),
            (ins[5], outs[5].at[seq]),
        ]
        local = []
        for src, dst in own_views:
            copy = pltpu.make_async_copy(src, dst, fresh())
            copy.start()
            local.append(copy)
        for copy in local:
            copy.wait()
        pl.semaphore_wait(barrier, len(greeted))

        send, recv = fresh(), fresh()
        for k in ALL16:
            remote(ins[5], outs[5].at[seq], send, recv, seq_at((seq + k) % SEQ_N))
        late.append((send, outs[5].at[pl.ds(0, 15)]))
        late.append((recv, outs[5].at[pl.ds(0, 15)]))

        third = qkvo.shape[1] // 3
        half = quarter // 2
        wide = down.shape[1] // 2
        streams = {
            "s": all_stream(outs[3], "xyz", [(every, every)] * 2, False),
            "t": table_stream(outs[4]),
            "g0": gate_up_stream(ins[1], outs[1], "xy", 0, half),
            "g1": gate_up_stream(ins[1], outs[1], "yx", half, half),
            "d0": down_stream(outs[2], "xy", 0, wide),
            "d1": down_stream(outs[2], "yx", wide, wide),
        }
        for n, order in enumerate(("xyz", "yzx", "zxy")):
            streams["q%d" % n] = all_stream(
                outs[0], order,
                [
                    (every, pl.ds(n * third, third)),
                    (every, pl.ds(n * third, third // 2)),
                    (every, pl.ds(n * third + third // 2, third // 2)),
                ],
            )
        for name in ORDER:
            next(streams[name], None)
        for name in sorted(streams):
            assert next(streams[name], "end") == "end", name
        for mark, view in late:
            arrived(view, mark)
        assert used[0] <= sem_count, used[0]

    return remote_call(
        body, out_shape, [ANY] * 6, [ANY] * 6, [DMA((sem_count,))], 1, "gather_weights"
    )(qkvo, gate_up, down, small, table, ids)


def feed_forward(rows, gate_up_w, down_w, saved, collective_id, name):
    forward = saved is None
    count, width = rows.shape
    quarter = gate_up_w.shape[1]
    units = quarter // 2
    chunk = count // 2
    tile = 512

    def body(*refs):
        if forward:
            (src, gu_hbm, dn_hbm, out, gu_out, held, gu, dn, saved_v, mid, part, give, got, sem) = refs
        else:
            (src, gu_hbm, dn_hbm, gu_in, out, held, gu, dn, saved_v, mid, part, give, got, sem) = refs
        c, z = lax.axis_index("seq_2"), lax.axis_index("fsdp_0")
        sibling = {"seq_2": 1 - c}
        partner = {"fsdp_0": z + 1 - 2 * (z % 2)}
        used = [0]

        def fresh():
            used[0] += 1
            return sem.at[used[0] - 1]

        loads = [pltpu.make_async_copy(gu_hbm, gu, fresh()), pltpu.make_async_copy(dn_hbm, dn, fresh())]
        if not forward:
            loads.append(pltpu.make_async_copy(gu_in, saved_v, fresh()))
            loads = [loads[1], loads[2], loads[0]]
        for load in loads:
            load.start()

        barrier = pltpu.get_barrier_semaphore()
        for device in (sibling, partner):
            pl.semaphore_signal(barrier, inc=1, device_id=device, device_id_type=MESH_ID)
        pl.semaphore_wait(barrier, 2)

        started = []

        def remote(src_ref, dst_ref, device):
            copy = pltpu.make_async_remote_copy(
                src_ref=src_ref, dst_ref=dst_ref, send_sem=fresh(), recv_sem=fresh(),
                device_id=device, device_id_type=MESH_ID,
            )
            copy.start()
            started.append(copy)
            return copy

        def lines(block, k=None):
            if k is None:
                return pl.ds(block * count, count)
            return pl.ds(block * count + k * chunk, chunk)

        along = [
            remote(src.at[pl.ds(k * chunk, chunk)], held.at[lines(2, k)], partner) for k in range(2)
        ]
        beside = remote(src, held.at[lines(1)], sibling)
        held[lines(0), :] = src[...]

        def first_product(pair):
            mine = pl.ds(pair * 2 * count, 2 * count)

            def step(n, carry):
                at = pl.multiple_of(n * tile, tile)
                low, high = pl.ds(at, tile), pl.ds(pl.multiple_of(at + units, tile), tile)
                block = held[mine, :]
                if forward:
                    gate = jnp.dot(block, gu[:, low], preferred_element_type=jnp.float32)
                    up = jnp.dot(block, gu[:, high], preferred_element_type=jnp.float32)
                    saved_v[mine, low] = gate
                    saved_v[mine, high] = up
                    mid[:, low] = (gate * jax.nn.sigmoid(gate) * up).astype(jnp.bfloat16)
                else:
                    d_hidden = nt(block, dn[low, :])
                    gate, up = saved_v[mine, low], saved_v[mine, high]
                    sigmoid_of = jax.nn.sigmoid(gate)
                    mid[:, low] = (
                        d_hidden * up * sigmoid_of * (1.0 + gate * (1.0 - sigmoid_of))
                    ).astype(jnp.bfloat16)
                    mid[:, high] = (d_hidden * gate * sigmoid_of).astype(jnp.bfloat16)
                return carry

            lax.fori_loop(0, units // tile, step, 0)

        def second_product(pair):
            def step(n, carry):
                at = pl.ds(pl.multiple_of(n * tile, tile), tile)
                if forward:
                    part[pair, :, at] = jnp.dot(
                        mid[...], dn[:, at], preferred_element_type=jnp.float32
                    )
                else:
                    part[pair, :, at] = nt(mid[...], gu[at, :])
                return carry

            lax.fori_loop(0, width // tile, step, 0)

        loads[0].wait()
        if not forward:
            loads[1].wait()
        beside.wait_recv()
        first_product(0)
        along[0].wait_recv()
        passed = [remote(held.at[lines(2, 0)], held.at[lines(3, 0)], sibling)]
        loads[-1].wait()
        second_product(0)
        along[1].wait_recv()
        passed.append(remote(held.at[lines(2, 1)], held.at[lines(3, 1)], sibling))
        give[0] = part[0, count:, :].astype(jnp.bfloat16)
        home = remote(give.at[0], got.at[0], sibling)
        if forward:
            stores = [
                pltpu.make_async_copy(
                    saved_v.at[pl.ds(0, 2 * count)], gu_out.at[pl.ds(0, 2 * count)], fresh()
                )
            ]
            stores[0].start()
        for copy in passed:
            copy.wait_recv()
        first_product(1)
        if forward:
            stores.append(
                pltpu.make_async_copy(
                    saved_v.at[pl.ds(2 * count, 2 * count)], gu_out.at[pl.ds(2 * count, 2 * count)], fresh()
                )
            )
            stores[1].start()
        second_product(1)
        give[1] = part[1, count:, :].astype(jnp.bfloat16)
        over = remote(give.at[1], got.at[1], sibling)
        over.wait_recv()
        back = []
        for k in range(2):
            some = pl.ds(k * chunk, chunk)
            give[2, some, :] = (part[1, some, :] + got[1, some, :].astype(jnp.float32)).astype(
                jnp.bfloat16
            )
            back.append(remote(give.at[2, some], got.at[2, some], partner))
        home.wait_recv()
        out[...] = part[0, 0:count, :] + got[0].astype(jnp.float32)
        for k in range(2):
            some = pl.ds(k * chunk, chunk)
            back[k].wait_recv()
            out[some, :] += got[2, some, :].astype(jnp.float32)
        for copy in started:
            copy.wait_send()
        if forward:
            for copy in stores:
                copy.wait()

    scratch = [
        pltpu.VMEM((4 * count, width), jnp.bfloat16),
        pltpu.VMEM(gate_up_w.shape, jnp.bfloat16),
        pltpu.VMEM(down_w.shape, jnp.bfloat16),
        pltpu.VMEM((4 * count, quarter), jnp.float32),
        pltpu.VMEM((2 * count, units if forward else quarter), jnp.bfloat16),
        pltpu.VMEM((2, 2 * count, width), jnp.float32),
        pltpu.VMEM((3, count, width), jnp.bfloat16),
        pltpu.VMEM((3, count, width), jnp.bfloat16),
        DMA((24,)),
    ]
    total = jax.ShapeDtypeStruct((count, width), jnp.float32)
    if forward:
        products = jax.ShapeDtypeStruct((4 * count, quarter), jnp.float32)
        return remote_call(
            body, [total, products], [VMEM, ANY, ANY], [VMEM, ANY], scratch, collective_id, name
        )(rows, gate_up_w, down_w)
    return remote_call(
        body, total, [VMEM, ANY, ANY, ANY], VMEM, scratch, collective_id, name
    )(rows, gate_up_w, down_w, saved)


def look_up(table, ids):
    vocab, width = table.shape

    def body(ids_ref, table_ref, out_ref, wide, rows):
        wide[...] = table_ref[...].astype(jnp.float32)
        for s in range(SEQ_N):

            def step(t, carry):
                rows[pl.ds(t, 1), :] = wide[pl.ds(ids_ref[s, t], 1), :]
                return carry

            lax.fori_loop(0, 128, step, 0, unroll=16)
            out_ref[s] = rows[...].astype(jnp.bfloat16)

    return pl.pallas_call(
        body,
        out_shape=jax.ShapeDtypeStruct((SEQ_N, 128, width), jnp.bfloat16),
        in_specs=[SMEM, VMEM],
        out_specs=VMEM,
        scratch_shapes=[
            pltpu.VMEM((vocab, width), jnp.float32),
            pltpu.VMEM((128, width), jnp.float32),
        ],
        compiler_params=pltpu.CompilerParams(vmem_limit_bytes=VMEM_LIMIT),
        name="look_up",
    )(ids, table)


def add_rows(gradient, local_ids, vocab):
    count, width = gradient.shape
    tile, low_n = 1024, 1024

    def body(ids_ref, grad_ref, out_ref, total, spread):
        @pl.when(pl.program_id(0) == 0)
        def _():
            total[...] = jnp.zeros_like(total)

        ids = ids_ref[...]
        high, low = ids >> 10, ids & 1023
        part = lax.broadcasted_iota(jnp.int32, (8, tile), 0)
        which = jnp.transpose((part == high).astype(jnp.float32))
        grad = grad_ref[...]
        for h in range(4):
            spread[:, h * width : (h + 1) * width] = jnp.where(
                which[:, h : h + 1] > 0.5, grad.astype(jnp.float32), 0.0
            ).astype(jnp.bfloat16)

        def step(n, carry):
            start = pl.multiple_of(n * 256, 256)
            row = lax.broadcasted_iota(jnp.int32, (256, tile), 0) + start
            hot = (row == low).astype(jnp.float32).astype(jnp.bfloat16)
            total[pl.ds(start, 256), :] += jnp.dot(
                hot, spread[...], preferred_element_type=jnp.float32
            )
            return carry

        lax.fori_loop(0, low_n // 256, step, 0)

        @pl.when(pl.program_id(0) == count // tile - 1)
        def _():
            for h in range(4):
                rows = min(low_n, vocab - h * low_n)
                out_ref[h * low_n : h * low_n + rows, :] = total[0:rows, h * width : (h + 1) * width]

    return pl.pallas_call(
        body,
        out_shape=jax.ShapeDtypeStruct((vocab, width), jnp.float32),
        grid=(count // tile,),
        in_specs=[
            pl.BlockSpec((1, tile), lambda i: (0, i)),
            pl.BlockSpec((tile, width), lambda i: (i, 0)),
        ],
        out_specs=pl.BlockSpec((vocab, width), lambda i: (0, 0)),
        scratch_shapes=[
            pltpu.VMEM((low_n, 4 * width), jnp.float32),
            pltpu.VMEM((tile, 4 * width), jnp.bfloat16),
        ],
        compiler_params=pltpu.CompilerParams(vmem_limit_bytes=VMEM_LIMIT),
        name="add_rows",
    )(local_ids.reshape(1, count), gradient)


def turn(values, cosine, sine):
    width = values.shape[-1]
    lane = lax.broadcasted_iota(jnp.int32, values.shape, values.ndim - 1)
    swapped = jnp.where(
        lane % 64 < 32,
        pltpu.roll(values, width - 32, values.ndim - 1),
        pltpu.roll(values, 32, values.ndim - 1),
    )
    return values * cosine + swapped * sine


def key_value_window(key_value, cosine, sine, collective_id):
    def body(kv_ref, cos_ref, sin_ref, out, held, ssem, rsem, lsem):
        me = greet("seq", range(1, 5))
        for m in range(2):
            rows = kv_ref[pl.ds(m * TOK, TOK), :]
            held[m, :, 0:256] = turn(rows[:, 0:256], cos_ref[:, 0:256], sin_ref[:, 0:256]).astype(
                jnp.bfloat16
            )
            held[m, :, 256:512] = rows[:, 256:512].astype(jnp.bfloat16)
        copies = send_each(
            "seq", me, range(1, 5), lambda k, p: held,
            lambda k, p: out.at[:, pl.ds((4 - k) * TOK, TOK), :], ssem, rsem,
        )
        own = pltpu.make_async_copy(held, out.at[:, pl.ds(4 * TOK, TOK), :], lsem)
        own.start()
        for copy in copies:
            copy.wait()
        own.wait()

    return remote_call(
        body,
        jax.ShapeDtypeStruct((2, 5 * TOK, 512), jnp.bfloat16),
        [VMEM] * 3,
        VMEM,
        [pltpu.VMEM((2, TOK, 512), jnp.bfloat16)] + sems(4) + [DMA],
        collective_id,
        "key_value_window",
    )(key_value, cosine, sine)


def key_value_back(far, own, cosine, sine, collective_id):
    def body(far_ref, own_ref, cos_ref, sin_ref, out, held, ssem, rsem):
        me = greet("seq", range(12, 16))
        copies = send_each(
            "seq", me, range(12, 16),
            lambda k, p: far_ref.at[:, pl.ds((k - 12) * TOK, TOK), :],
            lambda k, p: held.at[k - 12], ssem, rsem,
        )
        for copy in copies:
            copy.wait_recv()
        for m in range(2):
            total = own_ref[m]
            for n in range(3, -1, -1):
                total = total + held[n, m].astype(jnp.float32)
            keys = turn(total[:, 0:256], cos_ref[:, 0:256], -sin_ref[:, 0:256])
            out[pl.ds(m * TOK, TOK), 0:256] = keys.astype(jnp.bfloat16)
            out[pl.ds(m * TOK, TOK), 256:512] = total[:, 256:512].astype(jnp.bfloat16)
        for copy in copies:
            copy.wait_send()

    return remote_call(
        body,
        jax.ShapeDtypeStruct((2 * TOK, 512), jnp.bfloat16),
        [VMEM] * 4,
        VMEM,
        [pltpu.VMEM((4, 2, TOK, 512), jnp.bfloat16)] + sems(4),
        collective_id,
        "key_value_back",
    )(far, own, cosine, sine)


def spread_heads(block):
    return jnp.concatenate([block[:, 64 * g : 64 * g + 64] for g in range(8)], axis=0)


def join_heads(block):
    return jnp.concatenate([block[64 * g : 64 * g + 64, :] for g in range(8)], axis=1)


def window_mask(start_ref, query_seg, key_seg, shift):
    start = start_ref[0]
    query = start + lax.broadcasted_iota(jnp.int32, (TOK, 5 * TOK), 0)
    key = start - 4 * TOK + lax.broadcasted_iota(jnp.int32, (TOK, 5 * TOK), 1)
    allowed = (
        (key <= query)
        & (key >= 0)
        & (query_seg == key_seg)
        & (((query + shift) >> 8) == ((key + shift) >> 8))
    )
    return jnp.concatenate([allowed.astype(jnp.float32)] * 8, axis=0) > 0.5


def nt(left, right):
    return lax.dot_general(
        left, right, (((1,), (1,)), ((), ())), preferred_element_type=jnp.float32
    )


def tn(left, right):
    return lax.dot_general(
        left, right, (((0,), (0,)), ((), ())), preferred_element_type=jnp.float32
    )


def probabilities(queries, keys, mask):
    scores = jnp.where(mask, nt(queries, keys) * 0.125, -1e30)
    top = jnp.max(scores, axis=-1, keepdims=True)
    raised = jnp.where(mask, jnp.exp(scores - top), 0.0)
    return raised / jnp.sum(raised, axis=-1, keepdims=True)


def attend(queries, window, cosine, sine, query_seg, key_seg, start, shifts):
    def body(start_ref, shift_ref, q_ref, kv_ref, cos_ref, sin_ref, qs_ref, ks_ref, q_out, a_out):
        for h in range(4):
            cols = slice(512 * h, 512 * h + 512)
            turned = turn(q_ref[:, cols], cos_ref[...], sin_ref[...]).astype(jnp.bfloat16)
            q_out[:, cols] = turned
            mask = window_mask(start_ref, qs_ref[0], ks_ref[0], shift_ref[h])
            probs = probabilities(spread_heads(turned), kv_ref[0, :, 64 * h : 64 * h + 64], mask)
            values = kv_ref[0, :, 256 + 64 * h : 256 + 64 * h + 64]
            mixed = jnp.dot(probs.astype(jnp.bfloat16), values, preferred_element_type=jnp.float32)
            a_out[:, cols] = join_heads(mixed).astype(jnp.bfloat16)

    wide = pl.BlockSpec((TOK, 2048), lambda m: (m, 0))
    return pl.pallas_call(
        body,
        out_shape=[jax.ShapeDtypeStruct((2 * TOK, 2048), jnp.bfloat16)] * 2,
        grid=(2,),
        in_specs=[
            SMEM,
            SMEM,
            wide,
            pl.BlockSpec((1, 5 * TOK, 512), lambda m: (m, 0, 0)),
            pl.BlockSpec((TOK, 512), lambda m: (0, 0)),
            pl.BlockSpec((TOK, 512), lambda m: (0, 0)),
            pl.BlockSpec((1, TOK, 1), lambda m: (m, 0, 0)),
            pl.BlockSpec((1, 1, 5 * TOK), lambda m: (m, 0, 0)),
        ],
        out_specs=[wide, wide],
        compiler_params=pltpu.CompilerParams(vmem_limit_bytes=VMEM_LIMIT),
        name="attend",
    )(start, shifts, queries, window, cosine, sine, query_seg, key_seg)


def attend_back(queries, window, upstream, cosine, sine, query_seg, key_seg, start, shifts):
    def body(
        start_ref, shift_ref, q_ref, kv_ref, g_ref, cos_ref, sin_ref, qs_ref, ks_ref,
        dq_out, far_out, own_out,
    ):
        for h in range(4):
            cols = slice(512 * h, 512 * h + 512)
            mask = window_mask(start_ref, qs_ref[0], ks_ref[0], shift_ref[h])
            spread = spread_heads(q_ref[:, cols])
            keys = kv_ref[0, :, 64 * h : 64 * h + 64]
            values = kv_ref[0, :, 256 + 64 * h : 256 + 64 * h + 64]
            probs = probabilities(spread, keys, mask)
            grads = spread_heads(g_ref[:, cols])
            d_probs = nt(grads, values)
            d_values = tn(probs.astype(jnp.bfloat16), grads)
            inner = jnp.sum(probs * d_probs, axis=-1, keepdims=True)
            d_scores = (0.125 * probs * (d_probs - inner)).astype(jnp.bfloat16)
            d_queries = join_heads(jnp.dot(d_scores, keys, preferred_element_type=jnp.float32))
            dq_out[:, cols] = turn(d_queries, cos_ref[...], -sin_ref[...]).astype(jnp.bfloat16)
            d_keys = tn(d_scores, spread)
            for at, part in ((64 * h, d_keys), (256 + 64 * h, d_values)):
                far_out[0, :, at : at + 64] = part[0 : 4 * TOK].astype(jnp.bfloat16)
                own_out[0, :, at : at + 64] = part[4 * TOK :]

    wide = pl.BlockSpec((TOK, 2048), lambda m: (m, 0))
    return pl.pallas_call(
        body,
        out_shape=[
            jax.ShapeDtypeStruct((2 * TOK, 2048), jnp.bfloat16),
            jax.ShapeDtypeStruct((2, 4 * TOK, 512), jnp.bfloat16),
            jax.ShapeDtypeStruct((2, TOK, 512), jnp.float32),
        ],
        grid=(2,),
        in_specs=[
            SMEM,
            SMEM,
            wide,
            pl.BlockSpec((1, 5 * TOK, 512), lambda m: (m, 0, 0)),
            wide,
            pl.BlockSpec((TOK, 512), lambda m: (0, 0)),
            pl.BlockSpec((TOK, 512), lambda m: (0, 0)),
            pl.BlockSpec((1, TOK, 1), lambda m: (m, 0, 0)),
            pl.BlockSpec((1, 1, 5 * TOK), lambda m: (m, 0, 0)),
        ],
        out_specs=[
            wide,
            pl.BlockSpec((1, 4 * TOK, 512), lambda m: (m, 0, 0)),
            pl.BlockSpec((1, TOK, 512), lambda m: (m, 0, 0)),
        ],
        compiler_params=pltpu.CompilerParams(vmem_limit_bytes=VMEM_LIMIT),
        name="attend_back",
    )(start, shifts, queries, window, upstream, cosine, sine, query_seg, key_seg)


def dot(left, right):
    return jnp.dot(left, right, preferred_element_type=jnp.float32)


def dot_exact(left, right):
    return jnp.dot(left, right, precision=HIGHEST)


def norm_scale(values):
    return lax.rsqrt(jnp.mean(values * values, axis=-1, keepdims=True) + NORM_EPS)


def norm_back(values, gain, upstream):
    scale_of = norm_scale(values)
    scaled = gain * upstream
    inward = scale_of * scaled - values * scale_of**3 * jnp.mean(
        scaled * values, axis=-1, keepdims=True
    )
    return (inward, jnp.sum(upstream * values * scale_of, axis=0))


def adam_update(weight_vals, first_old, second_old, gradient, rate):
    first_new = FIRST_DECAY * first_old + (1.0 - FIRST_DECAY) * gradient
    second_new = SECOND_DECAY * second_old + (1.0 - SECOND_DECAY) * gradient * gradient
    first_hat = first_new / (1.0 - FIRST_DECAY**STEP)
    second_hat = second_new / (1.0 - SECOND_DECAY**STEP)
    step_vals = first_hat / (jnp.sqrt(second_hat) + ADAM_EPS) + WEIGHT_DECAY * weight_vals
    return (first_new, second_new, weight_vals - rate * step_vals)


def factor_onehot(columns):
    factor_id = (
        (columns >= 2048).astype(jnp.int32)
        + (columns >= 2048 + 256).astype(jnp.int32)
        + (columns >= 2048 + 512).astype(jnp.int32)
    )
    return (factor_id[None, :] == jnp.arange(4)[:, None]).astype(jnp.float32)


def shampoo_parts(down_factor_gradient, up_factor_gradient, onehot):
    left_three = down_factor_gradient.reshape(4, up_factor_gradient.shape[0], -1)
    stats_left = jnp.einsum("krd,ksd->krs", left_three, left_three, precision=HIGHEST)
    stats_right = jnp.einsum(
        "rc,sc,kc->krs", up_factor_gradient, up_factor_gradient, onehot, precision=HIGHEST
    )
    return jnp.concatenate([stats_left, stats_right], 0)


def inverse_root(stats):
    unit_mat = jnp.eye(stats.shape[-1], dtype=stats.dtype)[None]
    norm_of = jnp.sqrt(jnp.sum(stats * stats, axis=(1, 2), keepdims=True))
    matrix = stats / norm_of
    root_mat = unit_mat * lax.rsqrt(jnp.sqrt(norm_of))
    for iteration in range(10):
        factor = (5.0 * unit_mat - matrix) * 0.25
        root_mat = jnp.einsum("kab,kbc->kac", root_mat, factor, precision=HIGHEST)
        square = jnp.einsum("kab,kbc->kac", factor, factor, precision=HIGHEST)
        fourth = jnp.einsum("kab,kbc->kac", square, square, precision=HIGHEST)
        matrix = jnp.einsum("kab,kbc->kac", fourth, matrix, precision=HIGHEST)
    return root_mat


def shampoo_apply(
    stats_new, width_left, width_right, down_factor_gradient, up_factor_gradient, onehot
):
    roots = inverse_root(stats_new)
    left_three = down_factor_gradient.reshape(4, up_factor_gradient.shape[0], -1)
    down_factor_step = (
        jnp.einsum("krs,ksd->krd", roots[:4], left_three, precision=HIGHEST)
        * lax.rsqrt(jnp.sqrt(width_left))[:, None, :]
    )
    up_factor_step = (
        jnp.einsum("krs,sc,kc->rc", roots[4:], up_factor_gradient, onehot, precision=HIGHEST)
        * lax.rsqrt(jnp.sqrt(width_right))[None, :]
    )
    return (down_factor_step.reshape(down_factor_gradient.shape), up_factor_step)


def per_device(
    input_token_index,
    target_token_index,
    loss_position_index,
    document_slot_index,
    row_used_length,
    head_group_offsets,
    embedding,
    embedding_first_moment,
    embedding_second_moment,
    frozen_output_table,
    frozen_query_key_value_weight,
    frozen_attention_output_weight,
    frozen_gate_up_weight,
    frozen_down_weight,
    norm_gain_vectors,
    norm_gain_first_moment,
    norm_gain_second_moment,
    adapter_down_factors,
    adapter_up_factors,
    rank_side_statistics,
    down_width_statistics,
    up_width_statistics,
):
    fsdp_here = lax.axis_index(FSDP)
    seq_here = lax.axis_index(SEQ)
    vocab_dev = embedding.shape[0]

    qkvo_own = jnp.concatenate([frozen_query_key_value_weight, frozen_attention_output_weight], 1)
    gate_up_own = frozen_gate_up_weight.reshape(16, 2, 8, 2, 2, 2, 2, 44).transpose(
        0, 5, 3, 1, 2, 4, 6, 7
    )
    gate_up_own = jnp.pad(gate_up_own, [(0, 0)] * 7 + [(0, 4)]).reshape(16, 2 * PAD_FF)
    down_own = jnp.pad(frozen_down_weight, ((0, 4), (0, 0)))
    small_own = jnp.pad(
        jnp.concatenate(
            [
                adapter_down_factors.reshape(-1),
                norm_gain_vectors.reshape(-1),
                adapter_up_factors.reshape(-1),
            ]
        ),
        (0, 1024 - 848),
    ).reshape(8, 128)
    ids_own = jnp.pad(input_token_index.reshape(16, TOK), ((0, 0), (0, 64)))
    qkvo, gate_up_w, down_w, small, table, ids = gather_weights(
        qkvo_own,
        gate_up_own,
        down_own,
        small_own,
        embedding.astype(jnp.bfloat16),
        ids_own,
    )
    qkvo = qkvo.reshape(2048, 4608)
    w_qkv, w_out = qkvo[:, :2560], qkvo[:, 2560:]
    gate_up_w = gate_up_w.reshape(2048, PAD_FF // 2)
    down_w = down_w.reshape(PAD_FF // 4, 2048)
    head_own, ids = lax.optimization_barrier((frozen_output_table, ids))
    head = lax.all_gather(head_own, SEQ, axis=1, tiled=True)
    small = small.reshape(128, 1024)
    down_full = small[:, :512].reshape(128, 32, 16).transpose(1, 0, 2).reshape(32, 2048)
    gain = small[:, 512:560].reshape(128, 3, 16).transpose(1, 0, 2).reshape(3, 2048)
    up_full = small[:, 560:848].reshape(128, 8, 36).transpose(1, 0, 2).reshape(8, 4608)
    a_low = down_full.astype(jnp.bfloat16)
    b_low = up_full.astype(jnp.bfloat16)
    a_in, a_out = a_low[:24], a_low[24:]
    factor_of = (jnp.arange(2560) >= 2048).astype(jnp.int32) + (jnp.arange(2560) >= 2304)
    b_in = jnp.where(
        (jnp.arange(24) // 8)[:, None] == factor_of[None, :],
        jnp.concatenate([b_low[:, :2560]] * 3, 0),
        jnp.zeros((), jnp.bfloat16),
    )
    b_out = b_low[:, 2560:]

    places = loss_position_index.reshape(2, 8, SEQ_N, 32)
    spots = jnp.arange(SEQ_N)[:, None] * TOK + places
    counted = spots < row_used_length[..., None, None]
    seg_blocks = document_slot_index.reshape(2, 8, SEQ_N, 1, TOK)
    seg_at = jnp.sum(
        jnp.where(places[..., None] == jnp.arange(TOK), seg_blocks, 0), axis=-1
    )
    member = counted[..., None] & (seg_at[..., None] == jnp.arange(3))
    counts = jnp.sum(member.astype(jnp.int32), axis=(2, 3))
    document_total = jnp.sum((counts > 0).astype(jnp.float32))
    own_places = lax.dynamic_index_in_dim(places, seq_here, 2, keepdims=False)
    own_counted = lax.dynamic_index_in_dim(counted, seq_here, 2, keepdims=False)
    own_seg = lax.dynamic_index_in_dim(seg_at, seq_here, 2, keepdims=False)
    per_doc = jnp.sum(
        jnp.where(own_seg[..., None] == jnp.arange(3), counts[:, :, None, :], 0), axis=-1
    )
    own_weight = jnp.where(own_counted, 1.0 / jnp.maximum(per_doc, 1).astype(jnp.float32), 0.0)
    weight_flat = own_weight.transpose(1, 0, 2).reshape(-1)
    row_places = lax.dynamic_index_in_dim(own_places, fsdp_here, 1, keepdims=False)
    chosen_at = (row_places + jnp.arange(2)[:, None] * TOK).reshape(64)
    pick = (chosen_at[:, None] == jnp.arange(128)[None, :]).astype(jnp.float32)

    ids = ids[:, :, :TOK].reshape(SEQ_N, 2, 8, TOK)
    row_ids = lax.dynamic_index_in_dim(ids, fsdp_here, 2, keepdims=False).reshape(SEQ_N, 128)
    x_start = columns_to_rows(
        look_up(table.reshape(8 * vocab_dev, 128), row_ids), 2, "rows_of_tokens"
    ).astype(jnp.float32)

    half = 32
    freqs = ROPE_BASE ** (-2.0 * jnp.arange(half).astype(jnp.float32) / 64)
    angles = (seq_here * TOK + jnp.arange(TOK)).astype(jnp.float32)[:, None] * freqs[None, :]
    cosine = jnp.tile(jnp.cos(angles), (1, 16))
    sine = jnp.sin(angles)
    sine = jnp.tile(jnp.concatenate([-sine, sine], 1), (1, 8))
    own_docs = lax.dynamic_index_in_dim(document_slot_index, fsdp_here, 1, keepdims=False)
    padded = jnp.concatenate([jnp.full((2, 4 * TOK), -1, jnp.int32), own_docs], 1)
    key_seg = lax.dynamic_slice_in_dim(padded, seq_here * TOK, 5 * TOK, 1)[:, None, :]
    query_seg = key_seg[:, 0, 4 * TOK :][:, :, None]
    start = (seq_here * TOK).reshape(1)
    normed_one = (x_start * norm_scale(x_start) * gain[0]).astype(jnp.bfloat16)
    adapter_in = nt(normed_one, a_in).astype(jnp.bfloat16)
    packed = dot(normed_one, w_qkv) + ADAPTER_SCALE * dot(adapter_in, b_in)
    window = key_value_window(packed[:, 2048:], cosine, sine, 3)
    queries, attended = attend(
        packed, window, cosine, sine, query_seg, key_seg, start, head_group_offsets
    )
    adapter_mid = nt(attended, a_out).astype(jnp.bfloat16)
    x_mid = x_start + dot(attended, w_out) + ADAPTER_SCALE * dot(adapter_mid, b_out)

    normed_two = (x_mid * norm_scale(x_mid) * gain[1]).astype(jnp.bfloat16)
    hidden_sum, gate_up = feed_forward(normed_two, gate_up_w, down_w, None, 12, "feed_forward")
    x_end = x_mid + hidden_sum
    normed_end = (x_end * norm_scale(x_end) * gain[2]).astype(jnp.bfloat16)

    chosen = dot(pick.astype(jnp.bfloat16), normed_end).astype(jnp.bfloat16)
    (rows,) = gather_fsdp([chosen], 4, "chosen_rows")
    rows = rows.reshape(512, 2048)
    logits = nt(rows, head)
    local_target = target_token_index.transpose(1, 0, 2).reshape(-1) - fsdp_here * vocab_dev
    is_target = jnp.arange(vocab_dev)[None, :] == local_target[:, None]
    top_local = jnp.max(logits, axis=1)
    exp_local = jnp.sum(jnp.exp(logits - top_local[:, None]), axis=1)
    target_local = jnp.sum(jnp.where(is_target, logits, 0.0), axis=1)
    (stats,) = gather_fsdp(
        [jnp.pad(jnp.stack([top_local, exp_local]), ((0, 6), (0, 0)))], 5, "softmax_parts"
    )
    top_all = jnp.max(stats[:, 0], axis=0)
    exp_all = jnp.sum(stats[:, 1] * jnp.exp(stats[:, 0] - top_all[None, :]), axis=0)
    log_norm = top_all + jnp.log(exp_all)
    peer_of = jnp.arange(512) // 64
    loss_part = jnp.sum(jnp.where(peer_of == fsdp_here, log_norm * weight_flat, 0.0)) - jnp.sum(
        weight_flat * target_local
    )
    d_logits = (
        (weight_flat / document_total)[:, None]
        * (jnp.exp(logits - log_norm[:, None]) - is_target.astype(jnp.float32))
    ).astype(jnp.bfloat16)
    d_chosen = sum_rows(
        dot(d_logits, head).astype(jnp.bfloat16).reshape(8, 64, 2048), 6, "row_gradients"
    )

    upstream = lax.dot_general(pick, d_chosen, (((0,), (0,)), ((), ())), precision=HIGHEST)
    d_end, gain_end = norm_back(x_end, gain[2], upstream)
    d_normed = feed_forward(
        d_end.astype(jnp.bfloat16), gate_up_w, down_w, gate_up, 13, "feed_forward_back"
    )
    back_two, gain_mid = norm_back(x_mid, gain[1], d_normed)
    d_mid = d_end + back_two

    d_branch = d_mid.astype(jnp.bfloat16)
    d_adapter_mid = (ADAPTER_SCALE * nt(d_branch, b_out)).astype(jnp.bfloat16)
    d_attended = (nt(d_branch, w_out) + dot(d_adapter_mid, a_out)).astype(jnp.bfloat16)
    up_gradient_out = ADAPTER_SCALE * tn(adapter_mid, d_branch)
    down_gradient_out = tn(d_adapter_mid, attended)
    d_queries, d_far, d_own = attend_back(
        queries, window, d_attended, cosine, sine, query_seg, key_seg, start, head_group_offsets
    )
    d_key_value = key_value_back(d_far, d_own, cosine, sine, 7)
    d_packed = jnp.concatenate([d_queries, d_key_value], 1)
    d_adapter_in = (ADAPTER_SCALE * nt(d_packed, b_in)).astype(jnp.bfloat16)
    up_gradient_in = ADAPTER_SCALE * jnp.concatenate(
        [
            tn(adapter_in[:, 0:8], d_packed[:, :2048]),
            tn(adapter_in[:, 8:16], d_packed[:, 2048:2304]),
            tn(adapter_in[:, 16:24], d_packed[:, 2304:]),
        ],
        1,
    )
    down_gradient_in = tn(d_adapter_in, normed_one)
    back_one, gain_start = norm_back(
        x_start, gain[0], nt(d_packed, w_qkv) + dot(d_adapter_in, a_in)
    )
    d_start = (d_mid + back_one).astype(jnp.bfloat16)

    left = jnp.concatenate(
        [
            down_gradient_in,
            down_gradient_out,
            jnp.stack([gain_start, gain_mid, gain_end]),
            jnp.zeros((5, 2048), jnp.float32),
        ],
        0,
    )
    left = left.reshape(40, 16, 128).transpose(1, 0, 2)
    right = jnp.concatenate([up_gradient_in, up_gradient_out], 1).reshape(8, 16, 288)
    right = jnp.pad(right, ((0, 0), (0, 0), (0, 96))).transpose(1, 0, 2).reshape(16, 24, 128)
    d_columns, small_sum = rows_to_columns(
        d_start, jnp.concatenate([left, right], 1), 8, "token_gradients"
    )
    d_tokens, small_sum = gather_and_sum(d_columns, small_sum, 9, "token_gradients_all")
    all_ids = ids.transpose(2, 0, 1, 3).reshape(-1) - fsdp_here * vocab_dev
    grad_embed = add_rows(d_tokens.reshape(-1, 128), all_ids, vocab_dev)[:vocab_dev]
    left_sum = small_sum[:40]
    right_sum = small_sum[40:].reshape(8, 384)[:, :288]
    group_onehot = factor_onehot(seq_here * 288 + jnp.arange(288))
    stats_part = shampoo_parts(left_sum[:32], right_sum, group_onehot)
    first = (fsdp_here == 0).astype(jnp.float32)
    squares = jnp.sum(grad_embed * grad_embed) + first * (
        jnp.sum(left_sum[:35] * left_sum[:35]) + jnp.sum(right_sum * right_sum)
    )
    totals = jnp.concatenate(
        [
            (first * stats_part).reshape(-1),
            squares.reshape(1),
            loss_part.reshape(1),
            jnp.zeros((510,), jnp.float32),
        ]
    ).reshape(8, 128)
    totals = sum_over("seq", totals, 10, "totals_seq", False)
    totals = sum_over("fsdp", totals, 11, "totals_fsdp", False)
    stats_all = totals[:4].reshape(8, 8, 8)
    document_loss_sum = totals[4, 1]
    global_gradient_norm = jnp.sqrt(totals[4, 0])
    clip_factor = CLIP_MAX / jnp.maximum(global_gradient_norm, CLIP_MAX)

    own_left = lax.dynamic_slice_in_dim(left_sum, fsdp_here * 16, 16, 1)
    down_factor_gradient = own_left[:32] * clip_factor
    grad_gain = own_left[32:35] * clip_factor
    up_factor_gradient = (
        lax.dynamic_slice_in_dim(right_sum, fsdp_here * 36, 36, 1) * clip_factor
    )
    grad_embed = grad_embed * clip_factor
    unused_first, updated_embedding_second_moment, updated_embedding_table = adam_update(
        embedding, embedding_first_moment, embedding_second_moment, grad_embed, RATE_EMBED
    )
    updated_gain_first_moment, updated_gain_second_moment, updated_norm_gains = adam_update(
        norm_gain_vectors, norm_gain_first_moment, norm_gain_second_moment, grad_gain, RATE_GAIN
    )
    updated_rank_statistics = (
        SECOND_DECAY * rank_side_statistics
        + (1.0 - SECOND_DECAY) * (clip_factor * clip_factor) * stats_all
    )
    updated_down_width_statistics = SECOND_DECAY * down_width_statistics + (
        1.0 - SECOND_DECAY
    ) * jnp.sum(down_factor_gradient.reshape(4, 8, -1) ** 2, axis=1)
    updated_up_width_statistics = SECOND_DECAY * up_width_statistics + (
        1.0 - SECOND_DECAY
    ) * jnp.sum(up_factor_gradient * up_factor_gradient, axis=0)
    onehot = factor_onehot((seq_here * 8 + fsdp_here) * 36 + jnp.arange(36))
    down_factor_step, up_factor_step = shampoo_apply(
        updated_rank_statistics,
        updated_down_width_statistics,
        updated_up_width_statistics,
        down_factor_gradient,
        up_factor_gradient,
        onehot,
    )
    updated_down_factors = adapter_down_factors - LEARN_RATE_DOWN * down_factor_step
    updated_up_factors = adapter_up_factors - LEARN_RATE_UP * up_factor_step
    return (
        document_loss_sum,
        document_total,
        global_gradient_norm,
        grad_embed,
        updated_embedding_second_moment,
        updated_embedding_table,
        updated_gain_first_moment,
        updated_gain_second_moment,
        updated_norm_gains,
        down_factor_gradient,
        up_factor_gradient,
        updated_rank_statistics,
        updated_down_width_statistics,
        updated_up_width_statistics,
        updated_down_factors,
        updated_up_factors,
    )


def solution(mesh):
    torus = Mesh(
        mesh.devices.reshape(2, 4, 2, 4, 2), SEQ_FSDP
    )
    return jax.shard_map(
        per_device,
        mesh=torus,
        in_specs=(
            P(None, None, SEQ),
            P(None, None, SEQ),
            P(),
            P(),
            P(),
            P(),
            P(FSDP, SEQ),
            P(FSDP, SEQ),
            P(FSDP, SEQ),
            P(FSDP, SEQ),
            P(SEQ_FSDP, None),
            P(SEQ_FSDP, None),
            P(SEQ_FSDP, None),
            P(SEQ_FSDP, None),
            P(None, SEQ_FSDP),
            P(None, SEQ_FSDP),
            P(None, SEQ_FSDP),
            P(None, SEQ_FSDP),
            P(None, SEQ_FSDP),
            P(),
            P(None, SEQ_FSDP),
            P(SEQ_FSDP),
        ),
        out_specs=(
            P(),
            P(),
            P(),
            P(FSDP, SEQ),
            P(FSDP, SEQ),
            P(FSDP, SEQ),
            P(None, SEQ_FSDP),
            P(None, SEQ_FSDP),
            P(None, SEQ_FSDP),
            P(None, SEQ_FSDP),
            P(None, SEQ_FSDP),
            P(),
            P(None, SEQ_FSDP),
            P(SEQ_FSDP),
            P(None, SEQ_FSDP),
            P(None, SEQ_FSDP),
        ),
        check_vma=False,
    )
```

```python
import functools

import jax
import jax.numpy as jnp
from jax import lax
from jax.experimental import pallas as pl
from jax.experimental.pallas import tpu as pltpu
from jax.sharding import Mesh
from jax.sharding import PartitionSpec as P

STEP = 5
GROUP = 256
SEQ = ("seq_0", "seq_1", "seq_2")
FSDP = ("fsdp_0", "fsdp_1", "fsdp_2")
SEQ_FSDP = SEQ + FSDP
SEQ_N = 16
FSDP_N = 8
TOK = 64
PAD_FF = 6144
NORM_EPS = 1e-05
ADAPTER_SCALE = 2.0
ROPE_BASE = 10000.0
CLIP_MAX = 0.001
FIRST_DECAY = 0.5
SECOND_DECAY = 0.5
RATE_EMBED = 0.3
RATE_GAIN = 0.1
LEARN_RATE_DOWN = 0.1
LEARN_RATE_UP = 0.5
WEIGHT_DECAY = 0.01
ADAM_EPS = 1e-12
HIGHEST = lax.Precision.HIGHEST
MESH_ID = pl.DeviceIdType.MESH
ANY = pl.BlockSpec(memory_space=pl.ANY)
VMEM = pl.BlockSpec(memory_space=pltpu.VMEM)
SMEM = pl.BlockSpec(memory_space=pltpu.SMEM)
DMA = pltpu.SemaphoreType.DMA
VMEM_LIMIT = 56 * 1024 * 1024


def seq_me():
    return lax.axis_index("seq_0") * 8 + lax.axis_index("seq_1") * 2 + lax.axis_index("seq_2")


def z_me():
    return lax.axis_index("fsdp_0") * 2 + lax.axis_index("fsdp_1")


def z_at(i):
    return {"fsdp_0": i // 2, "fsdp_1": i % 2}


def fsdp_me():
    return z_me() * 2 + lax.axis_index("fsdp_2")


def seq_at(i):
    return {"seq_0": i // 8, "seq_1": (i // 2) % 4, "seq_2": i % 2}


def fsdp_at(i):
    return {**z_at(i // 2), "fsdp_2": i % 2}


RINGS = {"seq": (SEQ_N, seq_me, seq_at), "fsdp": (FSDP_N, fsdp_me, fsdp_at)}


def greet(kind, offsets):
    count, where, at = RINGS[kind]
    me = where()
    barrier = pltpu.get_barrier_semaphore()
    for k in offsets:
        pl.semaphore_signal(
            barrier, inc=1, device_id=at((me + count - k) % count), device_id_type=MESH_ID
        )
    pl.semaphore_wait(barrier, len(offsets))
    return me


def send_each(kind, me, offsets, src_of, dst_of, send_sem, recv_sem):
    count, _, at = RINGS[kind]
    copies = []
    for n, k in enumerate(offsets):
        peer = (me + k) % count
        copy = pltpu.make_async_remote_copy(
            src_ref=src_of(k, peer),
            dst_ref=dst_of(k, peer),
            send_sem=send_sem.at[n],
            recv_sem=recv_sem.at[n],
            device_id=at(peer),
            device_id_type=MESH_ID,
        )
        copy.start()
        copies.append(copy)
    return copies


def remote_call(body, out_shape, in_specs, out_specs, scratch, collective_id, name):
    return pl.pallas_call(
        body,
        out_shape=out_shape,
        in_specs=in_specs,
        out_specs=out_specs,
        scratch_shapes=scratch,
        compiler_params=pltpu.CompilerParams(
            collective_id=collective_id, has_side_effects=True, vmem_limit_bytes=VMEM_LIMIT
        ),
        name=name,
    )


def sems(n):
    return [DMA((n,)), DMA((n,))]


ALL16 = range(1, SEQ_N)
ALL8 = range(1, FSDP_N)


def sum_over(kind, block, collective_id, name, scatter):
    count = RINGS[kind][0]
    offsets = ALL16 if kind == "seq" else ALL8
    part = block.shape[1:] if scatter else block.shape

    def body(src, out, held, ssem, rsem):
        me = greet(kind, offsets)
        copies = send_each(
            kind, me, offsets,
            (lambda k, p: src.at[p]) if scatter else (lambda k, p: src),
            lambda k, p: held.at[k - 1], ssem, rsem,
        )
        total = (src[me] if scatter else src[...]).astype(jnp.float32)
        for n, copy in enumerate(copies):
            copy.wait_recv()
            total = total + held[n].astype(jnp.float32)
        out[...] = total
        for copy in copies:
            copy.wait_send()

    return remote_call(
        body,
        jax.ShapeDtypeStruct(part, jnp.float32),
        [VMEM],
        VMEM,
        [pltpu.VMEM((count - 1, *part), block.dtype)] + sems(count - 1),
        collective_id,
        name,
    )(block)


ORDER = (
    "s", "t", "q0", "q1", "q2", "s", "s", "q0", "q0", "s", "q1", "q2",
    "q1", "q2", "s", "s", "q0", "s", "q1", "q2", "s", "s", "q2", "q2",
    "q1", "q1", "q2", "q0", "q0", "s", "q1", "t", "q0", "q2", "q2", "t",
    "t", "t", "t", "q2", "q1", "q1", "q0", "q0", "t", "q1", "t", "q0",
)


class Post:
    def __init__(self, sem, count):
        self.sem, self.count, self.used, self.sent, self.late = sem, count, 0, [], []

    def fresh(self):
        self.used += 1
        assert self.used <= self.count, self.used
        return self.sem.at[self.used - 1]

    def start(self, src, dst, ssem, rsem, device):
        copy = pltpu.make_async_remote_copy(
            src_ref=src, dst_ref=dst, send_sem=ssem, recv_sem=rsem,
            device_id=device, device_id_type=MESH_ID,
        )
        copy.start()
        return copy

    def send(self, src, dst, device):
        copy = self.start(src, dst, self.fresh(), self.fresh(), device)
        self.sent.append(copy)
        return copy

    def finish(self):
        for copy in self.sent:
            copy.wait_send()
        for mark, view in self.late:
            pltpu.make_async_copy(view, view, mark).wait()


def greet_devices(devices):
    barrier = pltpu.get_barrier_semaphore()
    for device in devices:
        pl.semaphore_signal(barrier, inc=1, device_id=device, device_id_type=MESH_ID)
    pl.semaphore_wait(barrier, len(devices))


def fsdp_peers():
    me = fsdp_me()
    return [fsdp_at((me + k) % FSDP_N) for k in ALL8]


def seq_peers():
    me = seq_me()
    return [seq_at((me + k) % SEQ_N) for k in ALL16]


def relay(post, out, first, second, first_a, first_b):
    z, yl = z_me(), lax.axis_index("fsdp_2")
    partner, up, down = {"fsdp_2": 1 - yl}, z_at((z + 1) % 4), z_at((z + 3) % 4)
    before, after, far = (z + 3) % 4, (z + 1) % 4, (z + 2) % 4

    def at(zz, y, part=()):
        return out.at[(zz * 2 + y,) + part]

    def send(zz, y, part, device):
        view = at(zz, y, part)
        return post.send(view, view, device)

    to_partner = send(z, yl, (), partner)
    ring_up = send(z, yl, (), up)
    ring_down = send(z, yl, (), down)
    yield
    to_partner.wait_recv()
    other_up = send(z, 1 - yl, first, up)
    other_down = send(z, 1 - yl, first, down)
    yield
    ring_up.wait_recv()
    far_up = send(before, yl, first, up)
    across = [send(before, yl, second, partner)]
    yield
    ring_down.wait_recv()
    far_down = send(after, yl, second, down)
    across.append(send(after, yl, second, partner))
    yield
    other_up.wait_recv()
    last_up = send(before, 1 - yl, first_a, up)
    yield
    other_down.wait_recv()
    last_down = send(after, 1 - yl, first_b, down)
    yield
    far_up.wait_recv()
    far_down.wait_recv()
    across.append(send(far, yl, second, partner))
    yield
    last_up.wait_recv()
    last_down.wait_recv()
    for copy in across:
        copy.wait_recv()


def spread_gate_up(gate_up, collective_id):
    rows = gate_up.shape[0]
    quarter = gate_up.shape[1] // 4

    def body(src, out, sem, lsem):
        post = Post(sem, 14)
        z, c = z_me(), lax.axis_index("seq_2")
        column = [((z + dz) % 4, (c + dc) % 2) for dz in range(4) for dc in range(2) if dz or dc]
        greet_devices([{**z_at(zz), "seq_2": cc} for zz, cc in column])

        def part(zz, cc):
            first = pl.multiple_of((2 * (zz % 2) + cc) * quarter, 128)
            return src.at[:, pl.ds(first, quarter)]

        for zz, cc in column:
            post.send(part(zz, cc), out.at[c, z], {**z_at(zz), "seq_2": cc})
        own = pltpu.make_async_copy(part(z, c), out.at[c, z], lsem)
        own.start()
        for copy in post.sent:
            copy.wait_recv()
        post.finish()
        own.wait()

    return remote_call(
        body,
        jax.ShapeDtypeStruct((2, 4, rows, quarter), gate_up.dtype),
        [ANY], ANY, [DMA((14,)), DMA], collective_id, "spread_gate_up",
    )(gate_up)


def gather_weights(qkvo, small, table, ids):
    out_shape = [
        jax.ShapeDtypeStruct((2, 4, 2, 4, 2, *qkvo.shape), qkvo.dtype),
        jax.ShapeDtypeStruct((2, 4, 2, 4, 2, *small.shape), small.dtype),
        jax.ShapeDtypeStruct((FSDP_N, *table.shape), table.dtype),
        jax.ShapeDtypeStruct((SEQ_N, *ids.shape), ids.dtype),
    ]
    sem_count = 160
    every = slice(None)

    def body(*refs):
        ins, outs, sem = refs[:4], refs[4:8], refs[8]
        post = Post(sem, sem_count)
        yh, x, c, z, yl = (
            lax.axis_index("seq_0"), lax.axis_index("seq_1"), lax.axis_index("seq_2"), z_me(),
            lax.axis_index("fsdp_2"),
        )
        where = {"x": x, "y": 2 * yh + yl, "z": z}
        seq = seq_me()

        def beside(axis, step):
            at = (where[axis] + step + 4) % 4
            if axis == "x":
                return {"seq_1": at}
            if axis == "z":
                return z_at(at)
            return {"seq_0": at // 2, "fsdp_2": at % 2}

        other = {"seq_2": 1 - c}

        def arrived(ref, rsem):
            pltpu.make_async_copy(ref, ref, rsem).wait()

        def rings(block, order, sizes, halves, across):
            for n, axis in enumerate(order):
                done = order[:n]
                at = where[axis]
                before, after, far = (at + 3) % 4, (at + 1) % 4, (at + 2) % 4
                send, from_before, from_after, far_first = (post.fresh() for _ in range(4))
                post.late.append((send, sizes[axis, n]))
                own = block(done, axis, at, None)
                post.start(own, own, send, from_before, beside(axis, 1))
                post.start(own, own, send, from_after, beside(axis, -1))
                yield
                got = block(done, axis, before, None)
                arrived(got, from_before)
                half = block(done, axis, before, 0)
                post.start(half, half, send, far_first, beside(axis, 1))
                across(got)
                yield
                got = block(done, axis, after, None)
                arrived(got, from_after)
                if halves:
                    far_second = post.fresh()
                    half = block(done, axis, after, 1)
                    post.start(half, half, send, far_second, beside(axis, -1))
                across(got)
                yield
                arrived(block(done, axis, far, 0), far_first)
                if halves:
                    arrived(block(done, axis, far, 1), far_second)
                across(block(done, axis, far, None))

        def all_stream(ref, order, tails, halves=True):
            def block(done, axis, at, half):
                spot = {"yh": yh, "x": x, "z": z, "yl": yl}
                for a in done:
                    if a == "y":
                        spot["yh"] = spot["yl"] = every
                    else:
                        spot[a] = every
                if axis == "y":
                    spot["yh"], spot["yl"] = at // 2, at % 2
                elif axis is not None:
                    spot[axis] = at
                tail = tails[0 if half is None else half + 1]
                return ref.at[(spot["yh"], spot["x"], c, spot["z"], spot["yl"]) + tail]

            across_s, across_r = post.fresh(), post.fresh()
            post.late.append((across_s, ref.at[(every, every, c, every, every) + tails[0]]))
            post.late.append((across_r, ref.at[(every, every, 1 - c, every, every) + tails[0]]))

            def across(view):
                post.start(view, view, across_s, across_r, other)

            three = pl.ds(0, 3)
            sizes = {}
            for axis in "xyz":
                sizes[axis, 0] = ref.at[(0, 0, 0, three, 0) + tails[0]]
                sizes[axis, 1] = ref.at[(0, pl.ds(0, 2), 0, three, every) + tails[0]]
                sizes[axis, 2] = ref.at[(every, every, 0, three, every) + tails[0]]
            across(block([], None, None, None))
            yield from rings(block, order, sizes, halves, across)

        own_views = [
            (ins[0], outs[0].at[yh, x, c, z, yl]),
            (ins[1], outs[1].at[yh, x, c, z, yl]),
            (ins[2], outs[2].at[z * 2 + yl]),
            (ins[3], outs[3].at[seq]),
        ]
        local = []
        for src, dst in own_views:
            copy = pltpu.make_async_copy(src, dst, post.fresh())
            copy.start()
            local.append(copy)
        greet_devices(
            [beside(axis, step) for axis in "yz" for step in (1, -1)] + seq_peers()
        )
        for copy in local:
            copy.wait()

        send, recv = post.fresh(), post.fresh()
        for device in seq_peers():
            post.start(ins[3], outs[3].at[seq], send, recv, device)
        post.late.append((send, outs[3].at[pl.ds(0, 15)]))
        post.late.append((recv, outs[3].at[pl.ds(0, 15)]))

        third = qkvo.shape[1] // 3
        streams = {
            "s": all_stream(outs[1], "xyz", [(every, every)] * 2, False),
            "t": relay(
                post, outs[2], (pl.ds(0, 2000),), (pl.ds(2000, 2000),), (pl.ds(0, 1008),),
                (pl.ds(1008, 992),),
            ),
        }
        for n, order in enumerate(("yzx", "zyx", "zxy")):
            streams["q%d" % n] = all_stream(
                outs[0], order,
                [
                    (every, pl.ds(n * third, third)),
                    (every, pl.ds(n * third, third // 2)),
                    (every, pl.ds(n * third + third // 2, third // 2)),
                ],
            )
        for name in ORDER:
            next(streams[name], None)
        for name in sorted(streams):
            assert next(streams[name], "end") == "end", name
        post.finish()

    return remote_call(
        body, out_shape, [ANY] * 4, [ANY] * 4, [DMA((sem_count,))], 1, "gather_weights"
    )(qkvo, small, table, ids)


def rows_of_tokens(table, ids, collective_id):
    vocab, width = table.shape

    def body(ids_ref, table_ref, out, wide, rows, block, sem, lsem):
        post = Post(sem, 30)
        me = seq_me()
        wide[...] = table_ref[...].astype(jnp.float32)
        spot = pl.ds(pl.multiple_of(me * width, width), width)
        greet_devices(seq_peers())

        def fetch(s):
            def step(t, carry):
                rows[pl.ds(t, 1), :] = wide[pl.ds(ids_ref[s, t], 1), :]
                return carry

            lax.fori_loop(0, 128, step, 0, unroll=16)

        for k in list(ALL16) + [0]:
            peer = (me + k) % SEQ_N
            fetch(peer)
            block[k] = rows[...].astype(jnp.bfloat16)
            if k:
                post.send(block.at[k], out.at[:, spot], seq_at(peer))
        own = pltpu.make_async_copy(block.at[0], out.at[:, spot], lsem)
        own.start()
        for copy in post.sent:
            copy.wait_recv()
        post.finish()
        own.wait()

    return remote_call(
        body,
        jax.ShapeDtypeStruct((128, SEQ_N * width), jnp.bfloat16),
        [SMEM, VMEM],
        VMEM,
        [
            pltpu.VMEM((vocab, width), jnp.float32),
            pltpu.VMEM((128, width), jnp.float32),
            pltpu.VMEM((SEQ_N, 128, width), jnp.bfloat16),
            DMA((30,)),
            DMA,
        ],
        collective_id,
        "rows_of_tokens",
    )(ids, table)


def head_step(chosen, head, target, weight, scaled, collective_id):
    vocab, width = head.shape
    padded = -(-vocab // 512) * 512
    tiles = padded // 512

    def body(
        chosen_ref, head_hbm, target_ref, weight_ref, scaled_ref, out, loss, hd, held, raised, d_logits,
        prod, got, stat, stats, sem, lsem,
    ):
        post = Post(sem, 60)
        me = fsdp_me()
        load = pltpu.make_async_copy(head_hbm, hd.at[pl.ds(0, vocab)], lsem)
        load.start()
        held[me] = chosen_ref[...]
        greet_devices(fsdp_peers())
        for _ in relay(
            post, held, (pl.ds(0, 32),), (pl.ds(32, 32),), (pl.ds(0, 16),), (pl.ds(16, 16),)
        ):
            pass
        hd[vocab:, :] = jnp.zeros((padded - vocab, width), jnp.bfloat16)
        load.wait()
        rows = held[...].reshape(512, width)
        target_at = target_ref[...]

        def logits(n, carry):
            top, picked = carry
            at = pl.multiple_of(n * 512, 512)
            tile = nt(held[...].reshape(512, width), hd[pl.ds(at, 512), :])
            column = lax.broadcasted_iota(jnp.int32, (512, 512), 1) + at
            tile = jnp.where(column < vocab, tile, -1e30)
            raised[:, pl.ds(at, 512)] = tile
            top = jnp.maximum(top, jnp.max(tile, axis=1, keepdims=True))
            hit = jnp.where(column == target_at, tile, 0.0)
            return top, picked + jnp.sum(hit, axis=1, keepdims=True)

        top, picked = lax.fori_loop(
            0, tiles, logits, (jnp.full((512, 1), -1e30, jnp.float32), jnp.zeros((512, 1), jnp.float32))
        )

        def exponents(n, total):
            at = pl.ds(pl.multiple_of(n * 512, 512), 512)
            tile = jnp.exp(raised[:, at] - top)
            raised[:, at] = tile
            return total + jnp.sum(tile, axis=1, keepdims=True)

        total = lax.fori_loop(0, tiles, exponents, jnp.zeros((512, 1), jnp.float32))
        lane = lax.broadcasted_iota(jnp.int32, (512, 128), 1)
        both = jnp.where(lane == 0, top, jnp.where(lane == 1, total, 0.0))
        stat[...] = jnp.transpose(both)[0:8, :]
        copies = [
            post.send(stat, stats.at[k - 1], fsdp_at((me + k) % FSDP_N)) for k in ALL8
        ]
        for copy in copies:
            copy.wait_recv()
        top_all = stat[0:1, :]
        for n in range(7):
            top_all = jnp.maximum(top_all, stats[n, 0:1, :])
        sum_all = stat[1:2, :] * jnp.exp(stat[0:1, :] - top_all)
        for n in range(7):
            sum_all = sum_all + stats[n, 1:2, :] * jnp.exp(stats[n, 0:1, :] - top_all)
        log_row = top_all + jnp.log(sum_all)
        log_norm = jnp.transpose(jnp.broadcast_to(log_row, (128, 512)))[:, 0:1]
        weights = weight_ref[...]
        mine = lax.broadcasted_iota(jnp.int32, (512, 1), 0) // 64 == me
        value = jnp.sum(jnp.where(mine, log_norm * weights, 0.0) - weights * picked, axis=0, keepdims=True)
        loss[...] = jnp.broadcast_to(value, (8, 128))
        scale = scaled_ref[...]
        factor = scale * jnp.exp(top - log_norm)

        def slopes(n, carry):
            at = pl.multiple_of(n * 512, 512)
            column = lax.broadcasted_iota(jnp.int32, (512, 512), 1) + at
            hit = jnp.where(column == target_at, scale, 0.0)
            d_logits[:, pl.ds(at, 512)] = (factor * raised[:, pl.ds(at, 512)] - hit).astype(jnp.bfloat16)
            return carry

        lax.fori_loop(0, tiles, slopes, 0)
        half, inner = lax.axis_index("fsdp_0"), me % 4
        sums = []
        for n, part in enumerate((1 - half, half)):
            start = pl.multiple_of(part * 256, 256)

            def product(t, carry):
                at = pl.ds(pl.multiple_of(t * 512, 512), 512)
                tile = jnp.dot(
                    d_logits[pl.ds(start, 256), :], hd[:, at], preferred_element_type=jnp.float32
                )
                prod[pl.ds(part * 4, 4), :, at] = tile.astype(jnp.bfloat16).reshape(4, 64, 512)
                return carry

            lax.fori_loop(0, width // 512, product, 0)
            for j in range(n, 4):
                peer = part * 4 + (inner + j) % 4
                sums.append(post.send(prod.at[peer], got.at[4 * n + j - n], fsdp_at(peer)))
        out[...] = prod[me].astype(jnp.float32)
        for n, copy in enumerate(sums):
            copy.wait_recv()
            out[...] += got[n].astype(jnp.float32)
        post.finish()

    return remote_call(
        body,
        [
            jax.ShapeDtypeStruct((64, width), jnp.float32),
            jax.ShapeDtypeStruct((8, 128), jnp.float32),
        ],
        [VMEM, ANY, VMEM, VMEM, VMEM],
        [VMEM, VMEM],
        [
            pltpu.VMEM((padded, width), jnp.bfloat16),
            pltpu.VMEM((8, 64, width), jnp.bfloat16),
            pltpu.VMEM((512, padded), jnp.float32),
            pltpu.VMEM((512, padded), jnp.bfloat16),
            pltpu.VMEM((8, 64, width), jnp.bfloat16),
            pltpu.VMEM((7, 64, width), jnp.bfloat16),
            pltpu.VMEM((8, 512), jnp.float32),
            pltpu.VMEM((7, 8, 512), jnp.float32),
            DMA((60,)),
            DMA,
        ],
        collective_id,
        "head_step",
    )(chosen, head, target, weight, scaled)


def token_gradients(d_start, small, ids, vocab, collective_id):
    width = 128
    low_n, tile = 1024, 1024
    rows = small.shape[1]

    def body(src, small_ref, ids_ref, out, small_out, held, parts, mid, parts_b, total, spread, sem, lsem):
        post = Post(sem, 120)
        f, s = fsdp_me(), seq_me()
        z, yl = z_me(), lax.axis_index("fsdp_2")
        greet_devices(seq_peers() + fsdp_peers())

        def cols(p):
            return pl.ds(pl.multiple_of(p * width, width), width)

        moves, sums = [], []
        for k in ALL16:
            peer = (s + k) % SEQ_N
            sums.append(post.send(small_ref.at[peer], parts.at[k - 1], seq_at(peer)))
            moves.append(post.send(src.at[:, cols(peer)], held.at[f, s], seq_at(peer)))
        own = pltpu.make_async_copy(src.at[:, cols(s)], held.at[f, s], lsem)
        own.start()
        total[...] = jnp.zeros_like(total)
        amount = small_ref[s]
        for n, copy in enumerate(sums):
            copy.wait_recv()
            amount = amount + parts[n]
        mid[...] = amount
        shares = [post.send(mid, parts_b.at[k - 1], fsdp_at((f + k) % FSDP_N)) for k in ALL8]
        for copy in moves:
            copy.wait_recv()
        own.wait()

        def add(block):
            def one(t, carry):
                ids_row = ids_ref[pl.ds(block * 2 + t, 1), :]
                high, low = ids_row >> 10, ids_row & 1023
                part = lax.broadcasted_iota(jnp.int32, (8, tile), 0)
                which = jnp.transpose((part == high).astype(jnp.float32))
                grad = held[block, pl.ds(t * 8, 8)].reshape(tile, width).astype(jnp.float32)
                for h in range(4):
                    spread[:, h * width : (h + 1) * width] = jnp.where(
                        which[:, h : h + 1] > 0.5, grad, 0.0
                    ).astype(jnp.bfloat16)

                def step(n, inner):
                    start = pl.multiple_of(n * 256, 256)
                    row = lax.broadcasted_iota(jnp.int32, (256, tile), 0) + start
                    hot = (row == low).astype(jnp.float32).astype(jnp.bfloat16)
                    total[pl.ds(start, 256), :] += jnp.dot(
                        hot, spread[...], preferred_element_type=jnp.float32
                    )
                    return inner

                lax.fori_loop(0, low_n // 256, step, 0)
                return carry

            lax.fori_loop(0, 2, one, 0)

        every = slice(None)
        steps = relay(
            post, held, (pl.ds(0, 8),), (pl.ds(8, 8),), (pl.ds(0, 4),), (pl.ds(4, 4),)
        )
        before, after, far = (z + 3) % 4, (z + 1) % 4, (z + 2) % 4
        next(steps)
        add(f)
        next(steps)
        next(steps)
        next(steps)
        add(z * 2 + 1 - yl)
        next(steps)
        next(steps)
        add(before * 2 + yl)
        next(steps)
        add(after * 2 + yl)
        add(far * 2 + yl)
        assert next(steps, "end") == "end"
        for zz in (before, after, far):
            add(zz * 2 + 1 - yl)
        for n, copy in enumerate(shares):
            copy.wait_recv()
            mid_part = parts_b[n]
            amount = amount + mid_part
        small_out[...] = amount
        for h in range(4):
            count = min(low_n, vocab - h * low_n)
            out[h * low_n : h * low_n + count, :] = total[0:count, h * width : (h + 1) * width]
        post.finish()

    return remote_call(
        body,
        [
            jax.ShapeDtypeStruct((vocab, width), jnp.float32),
            jax.ShapeDtypeStruct((rows, width), jnp.float32),
        ],
        [VMEM, VMEM, VMEM],
        [VMEM, VMEM],
        [
            pltpu.VMEM((FSDP_N, SEQ_N, 128, width), jnp.bfloat16),
            pltpu.VMEM((15, rows, width), jnp.float32),
            pltpu.VMEM((rows, width), jnp.float32),
            pltpu.VMEM((7, rows, width), jnp.float32),
            pltpu.VMEM((low_n, 4 * width), jnp.float32),
            pltpu.VMEM((tile, 4 * width), jnp.bfloat16),
            DMA((120,)),
            DMA,
        ],
        collective_id,
        "token_gradients",
    )(d_start, small, ids)


def feed_forward(rows, gate_up_w, down_w, saved, collective_id, name):
    forward = saved is None
    count, width = rows.shape
    quarter = gate_up_w.shape[-1]
    units = quarter // 2
    chunk = count // 2
    tile = 512

    def body(*refs):
        if forward:
            (src, gu_hbm, dn_hbm, out, gu_out, held, gu_blocks, dn, saved_v, mid, part, give, got, sem) = refs
        else:
            (src, gu_hbm, dn_hbm, gu_in, out, held, gu_blocks, dn, saved_v, mid, part, give, got, sem) = refs
        c = lax.axis_index("seq_2")
        sibling = {"seq_2": 1 - c}
        partner = {"fsdp_1": 1 - lax.axis_index("fsdp_1")}
        used = [0]

        def fresh():
            used[0] += 1
            return sem.at[used[0] - 1]

        gu = gu_blocks.reshape(width, quarter)
        load_gu = [
            pltpu.make_async_copy(gu_hbm.at[:, k], gu_blocks.at[:, :, k], fresh()) for k in range(2)
        ]
        load_dn = [pltpu.make_async_copy(dn_hbm, dn, fresh())]
        loads = [load_gu, load_dn]
        if not forward:
            load_dn.append(pltpu.make_async_copy(gu_in, saved_v, fresh()))
            loads = [load_dn, load_gu]
        for load in loads[0] + loads[1]:
            load.start()

        barrier = pltpu.get_barrier_semaphore()
        for device in (sibling, partner):
            pl.semaphore_signal(barrier, inc=1, device_id=device, device_id_type=MESH_ID)
        pl.semaphore_wait(barrier, 2)

        started = []

        def remote(src_ref, dst_ref, device):
            copy = pltpu.make_async_remote_copy(
                src_ref=src_ref, dst_ref=dst_ref, send_sem=fresh(), recv_sem=fresh(),
                device_id=device, device_id_type=MESH_ID,
            )
            copy.start()
            started.append(copy)
            return copy

        def lines(block, k=None):
            if k is None:
                return pl.ds(block * count, count)
            return pl.ds(block * count + k * chunk, chunk)

        along = [
            remote(src.at[pl.ds(k * chunk, chunk)], held.at[lines(2, k)], partner) for k in range(2)
        ]
        beside = remote(src, held.at[lines(1)], sibling)
        held[lines(0), :] = src[...]

        def first_product(pair):
            mine = pl.ds(pair * 2 * count, 2 * count)

            def step(n, carry):
                at = pl.multiple_of(n * tile, tile)
                low, high = pl.ds(at, tile), pl.ds(pl.multiple_of(at + units, tile), tile)
                block = held[mine, :]
                if forward:
                    gate = jnp.dot(block, gu[:, low], preferred_element_type=jnp.float32)
                    up = jnp.dot(block, gu[:, high], preferred_element_type=jnp.float32)
                    saved_v[mine, low] = gate
                    saved_v[mine, high] = up
                    mid[:, low] = (gate * jax.nn.sigmoid(gate) * up).astype(jnp.bfloat16)
                else:
                    d_hidden = nt(block, dn[low, :])
                    gate, up = saved_v[mine, low], saved_v[mine, high]
                    sigmoid_of = jax.nn.sigmoid(gate)
                    mid[:, low] = (
                        d_hidden * up * sigmoid_of * (1.0 + gate * (1.0 - sigmoid_of))
                    ).astype(jnp.bfloat16)
                    mid[:, high] = (d_hidden * gate * sigmoid_of).astype(jnp.bfloat16)
                return carry

            lax.fori_loop(0, units // tile, step, 0)

        def second_product(pair):
            def step(n, carry):
                at = pl.ds(pl.multiple_of(n * tile, tile), tile)
                if forward:
                    part[pair, :, at] = jnp.dot(
                        mid[...], dn[:, at], preferred_element_type=jnp.float32
                    )
                else:
                    part[pair, :, at] = nt(mid[...], gu[at, :])
                return carry

            lax.fori_loop(0, width // tile, step, 0)

        for load in loads[0]:
            load.wait()
        beside.wait_recv()
        first_product(0)
        along[0].wait_recv()
        passed = [remote(held.at[lines(2, 0)], held.at[lines(3, 0)], sibling)]
        for load in loads[1]:
            load.wait()
        second_product(0)
        along[1].wait_recv()
        passed.append(remote(held.at[lines(2, 1)], held.at[lines(3, 1)], sibling))
        give[0] = part[0, count:, :].astype(jnp.bfloat16)
        home = remote(give.at[0], got.at[0], sibling)
        if forward:
            stores = [
                pltpu.make_async_copy(
                    saved_v.at[pl.ds(0, 2 * count)], gu_out.at[pl.ds(0, 2 * count)], fresh()
                )
            ]
            stores[0].start()
        for copy in passed:
            copy.wait_recv()
        first_product(1)
        if forward:
            stores.append(
                pltpu.make_async_copy(
                    saved_v.at[pl.ds(2 * count, 2 * count)], gu_out.at[pl.ds(2 * count, 2 * count)], fresh()
                )
            )
            stores[1].start()
        second_product(1)
        give[1] = part[1, count:, :].astype(jnp.bfloat16)
        over = remote(give.at[1], got.at[1], sibling)
        over.wait_recv()
        back = []
        for k in range(2):
            some = pl.ds(k * chunk, chunk)
            give[2, some, :] = (part[1, some, :] + got[1, some, :].astype(jnp.float32)).astype(
                jnp.bfloat16
            )
            back.append(remote(give.at[2, some], got.at[2, some], partner))
        home.wait_recv()
        out[...] = part[0, 0:count, :] + got[0].astype(jnp.float32)
        for k in range(2):
            some = pl.ds(k * chunk, chunk)
            back[k].wait_recv()
            out[some, :] += got[2, some, :].astype(jnp.float32)
        for copy in started:
            copy.wait_send()
        if forward:
            for copy in stores:
                copy.wait()

    scratch = [
        pltpu.VMEM((4 * count, width), jnp.bfloat16),
        pltpu.VMEM((8, 8, 2, 16, quarter), jnp.bfloat16),
        pltpu.VMEM(down_w.shape, jnp.bfloat16),
        pltpu.VMEM((4 * count, quarter), jnp.float32),
        pltpu.VMEM((2 * count, units if forward else quarter), jnp.bfloat16),
        pltpu.VMEM((2, 2 * count, width), jnp.float32),
        pltpu.VMEM((3, count, width), jnp.bfloat16),
        pltpu.VMEM((3, count, width), jnp.bfloat16),
        DMA((24,)),
    ]
    total = jax.ShapeDtypeStruct((count, width), jnp.float32)
    if forward:
        products = jax.ShapeDtypeStruct((4 * count, quarter), jnp.float32)
        return remote_call(
            body, [total, products], [VMEM, ANY, ANY], [VMEM, ANY], scratch, collective_id, name
        )(rows, gate_up_w, down_w)
    return remote_call(
        body, total, [VMEM, ANY, ANY, ANY], VMEM, scratch, collective_id, name
    )(rows, gate_up_w, down_w, saved)


def turn(values, cosine, sine):
    width = values.shape[-1]
    lane = lax.broadcasted_iota(jnp.int32, values.shape, values.ndim - 1)
    swapped = jnp.where(
        lane % 64 < 32,
        pltpu.roll(values, width - 32, values.ndim - 1),
        pltpu.roll(values, 32, values.ndim - 1),
    )
    return values * cosine + swapped * sine


def key_value_window(key_value, cosine, sine, collective_id):
    def body(kv_ref, cos_ref, sin_ref, out, held, ssem, rsem, lsem):
        me = greet("seq", range(1, 5))
        for m in range(2):
            rows = kv_ref[pl.ds(m * TOK, TOK), :]
            held[m, :, 0:256] = turn(rows[:, 0:256], cos_ref[:, 0:256], sin_ref[:, 0:256]).astype(
                jnp.bfloat16
            )
            held[m, :, 256:512] = rows[:, 256:512].astype(jnp.bfloat16)
        copies = send_each(
            "seq", me, range(1, 5), lambda k, p: held,
            lambda k, p: out.at[:, pl.ds((4 - k) * TOK, TOK), :], ssem, rsem,
        )
        own = pltpu.make_async_copy(held, out.at[:, pl.ds(4 * TOK, TOK), :], lsem)
        own.start()
        for copy in copies:
            copy.wait()
        own.wait()

    return remote_call(
        body,
        jax.ShapeDtypeStruct((2, 5 * TOK, 512), jnp.bfloat16),
        [VMEM] * 3,
        VMEM,
        [pltpu.VMEM((2, TOK, 512), jnp.bfloat16)] + sems(4) + [DMA],
        collective_id,
        "key_value_window",
    )(key_value, cosine, sine)


def key_value_back(far, own, cosine, sine, collective_id):
    def body(far_ref, own_ref, cos_ref, sin_ref, out, held, ssem, rsem):
        me = greet("seq", range(12, 16))
        copies = send_each(
            "seq", me, range(12, 16),
            lambda k, p: far_ref.at[:, pl.ds((k - 12) * TOK, TOK), :],
            lambda k, p: held.at[k - 12], ssem, rsem,
        )
        for copy in copies:
            copy.wait_recv()
        for m in range(2):
            total = own_ref[m]
            for n in range(3, -1, -1):
                total = total + held[n, m].astype(jnp.float32)
            keys = turn(total[:, 0:256], cos_ref[:, 0:256], -sin_ref[:, 0:256])
            out[pl.ds(m * TOK, TOK), 0:256] = keys.astype(jnp.bfloat16)
            out[pl.ds(m * TOK, TOK), 256:512] = total[:, 256:512].astype(jnp.bfloat16)
        for copy in copies:
            copy.wait_send()

    return remote_call(
        body,
        jax.ShapeDtypeStruct((2 * TOK, 512), jnp.bfloat16),
        [VMEM] * 4,
        VMEM,
        [pltpu.VMEM((4, 2, TOK, 512), jnp.bfloat16)] + sems(4),
        collective_id,
        "key_value_back",
    )(far, own, cosine, sine)


def spread_heads(block):
    return jnp.concatenate([block[:, 64 * g : 64 * g + 64] for g in range(8)], axis=0)


def join_heads(block):
    return jnp.concatenate([block[64 * g : 64 * g + 64, :] for g in range(8)], axis=1)


def window_mask(start_ref, query_seg, key_seg, shift):
    start = start_ref[0]
    query = start + lax.broadcasted_iota(jnp.int32, (TOK, 5 * TOK), 0)
    key = start - 4 * TOK + lax.broadcasted_iota(jnp.int32, (TOK, 5 * TOK), 1)
    allowed = (
        (key <= query)
        & (key >= 0)
        & (query_seg == key_seg)
        & (((query + shift) >> 8) == ((key + shift) >> 8))
    )
    return jnp.concatenate([allowed.astype(jnp.float32)] * 8, axis=0) > 0.5


def nt(left, right):
    return lax.dot_general(
        left, right, (((1,), (1,)), ((), ())), preferred_element_type=jnp.float32
    )


def tn(left, right):
    return lax.dot_general(
        left, right, (((0,), (0,)), ((), ())), preferred_element_type=jnp.float32
    )


def probabilities(queries, keys, mask):
    scores = jnp.where(mask, nt(queries, keys) * 0.125, -1e30)
    top = jnp.max(scores, axis=-1, keepdims=True)
    raised = jnp.where(mask, jnp.exp(scores - top), 0.0)
    return raised / jnp.sum(raised, axis=-1, keepdims=True)


def attend(queries, window, cosine, sine, query_seg, key_seg, start, shifts):
    def body(start_ref, shift_ref, q_ref, kv_ref, cos_ref, sin_ref, qs_ref, ks_ref, q_out, a_out):
        for h in range(4):
            cols = slice(512 * h, 512 * h + 512)
            turned = turn(q_ref[:, cols], cos_ref[...], sin_ref[...]).astype(jnp.bfloat16)
            q_out[:, cols] = turned
            mask = window_mask(start_ref, qs_ref[0], ks_ref[0], shift_ref[h])
            probs = probabilities(spread_heads(turned), kv_ref[0, :, 64 * h : 64 * h + 64], mask)
            values = kv_ref[0, :, 256 + 64 * h : 256 + 64 * h + 64]
            mixed = jnp.dot(probs.astype(jnp.bfloat16), values, preferred_element_type=jnp.float32)
            a_out[:, cols] = join_heads(mixed).astype(jnp.bfloat16)

    wide = pl.BlockSpec((TOK, 2048), lambda m: (m, 0))
    return pl.pallas_call(
        body,
        out_shape=[jax.ShapeDtypeStruct((2 * TOK, 2048), jnp.bfloat16)] * 2,
        grid=(2,),
        in_specs=[
            SMEM,
            SMEM,
            wide,
            pl.BlockSpec((1, 5 * TOK, 512), lambda m: (m, 0, 0)),
            pl.BlockSpec((TOK, 512), lambda m: (0, 0)),
            pl.BlockSpec((TOK, 512), lambda m: (0, 0)),
            pl.BlockSpec((1, TOK, 1), lambda m: (m, 0, 0)),
            pl.BlockSpec((1, 1, 5 * TOK), lambda m: (m, 0, 0)),
        ],
        out_specs=[wide, wide],
        compiler_params=pltpu.CompilerParams(vmem_limit_bytes=VMEM_LIMIT),
        name="attend",
    )(start, shifts, queries, window, cosine, sine, query_seg, key_seg)


def attend_back(queries, window, upstream, cosine, sine, query_seg, key_seg, start, shifts):
    def body(
        start_ref, shift_ref, q_ref, kv_ref, g_ref, cos_ref, sin_ref, qs_ref, ks_ref,
        dq_out, far_out, own_out,
    ):
        for h in range(4):
            cols = slice(512 * h, 512 * h + 512)
            mask = window_mask(start_ref, qs_ref[0], ks_ref[0], shift_ref[h])
            spread = spread_heads(q_ref[:, cols])
            keys = kv_ref[0, :, 64 * h : 64 * h + 64]
            values = kv_ref[0, :, 256 + 64 * h : 256 + 64 * h + 64]
            probs = probabilities(spread, keys, mask)
            grads = spread_heads(g_ref[:, cols])
            d_probs = nt(grads, values)
            d_values = tn(probs.astype(jnp.bfloat16), grads)
            inner = jnp.sum(probs * d_probs, axis=-1, keepdims=True)
            d_scores = (0.125 * probs * (d_probs - inner)).astype(jnp.bfloat16)
            d_queries = join_heads(jnp.dot(d_scores, keys, preferred_element_type=jnp.float32))
            dq_out[:, cols] = turn(d_queries, cos_ref[...], -sin_ref[...]).astype(jnp.bfloat16)
            d_keys = tn(d_scores, spread)
            for at, part in ((64 * h, d_keys), (256 + 64 * h, d_values)):
                far_out[0, :, at : at + 64] = part[0 : 4 * TOK].astype(jnp.bfloat16)
                own_out[0, :, at : at + 64] = part[4 * TOK :]

    wide = pl.BlockSpec((TOK, 2048), lambda m: (m, 0))
    return pl.pallas_call(
        body,
        out_shape=[
            jax.ShapeDtypeStruct((2 * TOK, 2048), jnp.bfloat16),
            jax.ShapeDtypeStruct((2, 4 * TOK, 512), jnp.bfloat16),
            jax.ShapeDtypeStruct((2, TOK, 512), jnp.float32),
        ],
        grid=(2,),
        in_specs=[
            SMEM,
            SMEM,
            wide,
            pl.BlockSpec((1, 5 * TOK, 512), lambda m: (m, 0, 0)),
            wide,
            pl.BlockSpec((TOK, 512), lambda m: (0, 0)),
            pl.BlockSpec((TOK, 512), lambda m: (0, 0)),
            pl.BlockSpec((1, TOK, 1), lambda m: (m, 0, 0)),
            pl.BlockSpec((1, 1, 5 * TOK), lambda m: (m, 0, 0)),
        ],
        out_specs=[
            wide,
            pl.BlockSpec((1, 4 * TOK, 512), lambda m: (m, 0, 0)),
            pl.BlockSpec((1, TOK, 512), lambda m: (m, 0, 0)),
        ],
        compiler_params=pltpu.CompilerParams(vmem_limit_bytes=VMEM_LIMIT),
        name="attend_back",
    )(start, shifts, queries, window, upstream, cosine, sine, query_seg, key_seg)


def dot(left, right):
    return jnp.dot(left, right, preferred_element_type=jnp.float32)


def dot_exact(left, right):
    return jnp.dot(left, right, precision=HIGHEST)


def norm_scale(values):
    return lax.rsqrt(jnp.mean(values * values, axis=-1, keepdims=True) + NORM_EPS)


def norm_back(values, gain, upstream):
    scale_of = norm_scale(values)
    scaled = gain * upstream
    inward = scale_of * scaled - values * scale_of**3 * jnp.mean(
        scaled * values, axis=-1, keepdims=True
    )
    return (inward, jnp.sum(upstream * values * scale_of, axis=0))


def adam_update(weight_vals, first_old, second_old, gradient, rate):
    first_new = FIRST_DECAY * first_old + (1.0 - FIRST_DECAY) * gradient
    second_new = SECOND_DECAY * second_old + (1.0 - SECOND_DECAY) * gradient * gradient
    first_hat = first_new / (1.0 - FIRST_DECAY**STEP)
    second_hat = second_new / (1.0 - SECOND_DECAY**STEP)
    step_vals = first_hat / (jnp.sqrt(second_hat) + ADAM_EPS) + WEIGHT_DECAY * weight_vals
    return (first_new, second_new, weight_vals - rate * step_vals)


def factor_onehot(columns):
    factor_id = (
        (columns >= 2048).astype(jnp.int32)
        + (columns >= 2048 + 256).astype(jnp.int32)
        + (columns >= 2048 + 512).astype(jnp.int32)
    )
    return (factor_id[None, :] == jnp.arange(4)[:, None]).astype(jnp.float32)


def shampoo_parts(down_factor_gradient, up_factor_gradient, onehot):
    left_three = down_factor_gradient.reshape(4, up_factor_gradient.shape[0], -1)
    stats_left = jnp.einsum("krd,ksd->krs", left_three, left_three, precision=HIGHEST)
    stats_right = jnp.einsum(
        "rc,sc,kc->krs", up_factor_gradient, up_factor_gradient, onehot, precision=HIGHEST
    )
    return jnp.concatenate([stats_left, stats_right], 0)


def inverse_root(stats):
    unit_mat = jnp.eye(stats.shape[-1], dtype=stats.dtype)[None]
    norm_of = jnp.sqrt(jnp.sum(stats * stats, axis=(1, 2), keepdims=True))
    matrix = stats / norm_of
    root_mat = unit_mat * lax.rsqrt(jnp.sqrt(norm_of))
    for iteration in range(10):
        factor = (5.0 * unit_mat - matrix) * 0.25
        root_mat = jnp.einsum("kab,kbc->kac", root_mat, factor, precision=HIGHEST)
        square = jnp.einsum("kab,kbc->kac", factor, factor, precision=HIGHEST)
        fourth = jnp.einsum("kab,kbc->kac", square, square, precision=HIGHEST)
        matrix = jnp.einsum("kab,kbc->kac", fourth, matrix, precision=HIGHEST)
    return root_mat


def shampoo_apply(
    stats_new, width_left, width_right, down_factor_gradient, up_factor_gradient, onehot
):
    roots = inverse_root(stats_new)
    left_three = down_factor_gradient.reshape(4, up_factor_gradient.shape[0], -1)
    down_factor_step = (
        jnp.einsum("krs,ksd->krd", roots[:4], left_three, precision=HIGHEST)
        * lax.rsqrt(jnp.sqrt(width_left))[:, None, :]
    )
    up_factor_step = (
        jnp.einsum("krs,sc,kc->rc", roots[4:], up_factor_gradient, onehot, precision=HIGHEST)
        * lax.rsqrt(jnp.sqrt(width_right))[None, :]
    )
    return (down_factor_step.reshape(down_factor_gradient.shape), up_factor_step)


def per_device(
    input_token_index,
    target_token_index,
    loss_position_index,
    document_slot_index,
    row_used_length,
    head_group_offsets,
    embedding,
    embedding_first_moment,
    embedding_second_moment,
    frozen_output_table,
    frozen_query_key_value_weight,
    frozen_attention_output_weight,
    frozen_gate_up_weight,
    frozen_down_weight,
    norm_gain_vectors,
    norm_gain_first_moment,
    norm_gain_second_moment,
    adapter_down_factors,
    adapter_up_factors,
    rank_side_statistics,
    down_width_statistics,
    up_width_statistics,
):
    fsdp_here = lax.axis_index(FSDP)
    seq_here = lax.axis_index(SEQ)
    vocab_dev = embedding.shape[0]

    qkvo_own = jnp.concatenate([frozen_query_key_value_weight, frozen_attention_output_weight], 1)
    gate_up_own = frozen_gate_up_weight.reshape(16, 2, 8, 2, 2, 2, 2, 44).transpose(
        0, 5, 3, 1, 2, 4, 6, 7
    )
    gate_up_own = jnp.pad(gate_up_own, [(0, 0)] * 7 + [(0, 4)]).reshape(16, 2 * PAD_FF)
    down_own = jnp.pad(frozen_down_weight, ((0, 4), (0, 0)))
    small_own = jnp.pad(
        jnp.concatenate(
            [
                adapter_down_factors.reshape(-1),
                norm_gain_vectors.reshape(-1),
                adapter_up_factors.reshape(-1),
            ]
        ),
        (0, 1024 - 848),
    ).reshape(8, 128)
    ids_own = jnp.pad(input_token_index.reshape(16, TOK), ((0, 0), (0, 64)))
    gate_up_w = lax.all_gather(
        spread_gate_up(gate_up_own, 14).reshape(128, PAD_FF // 2),
        ("seq_0", "seq_1", "fsdp_2"),
        axis=0,
        tiled=True,
    ).reshape(8, 2, 8, 16, PAD_FF // 2)
    down_w = lax.all_gather(
        down_own, ("seq_0", "seq_1", "fsdp_0", "fsdp_2"), axis=0, tiled=True
    )
    qkvo, small, table, ids = gather_weights(
        qkvo_own,
        small_own,
        embedding.astype(jnp.bfloat16),
        ids_own,
    )
    qkvo = qkvo.reshape(2048, 4608)
    w_qkv, w_out = qkvo[:, :2560], qkvo[:, 2560:]
    head_own, ids = lax.optimization_barrier((frozen_output_table, ids))
    head = lax.all_gather(head_own, SEQ, axis=1, tiled=True)
    small = small.reshape(128, 1024)
    down_full = small[:, :512].reshape(128, 32, 16).transpose(1, 0, 2).reshape(32, 2048)
    gain = small[:, 512:560].reshape(128, 3, 16).transpose(1, 0, 2).reshape(3, 2048)
    up_full = small[:, 560:848].reshape(128, 8, 36).transpose(1, 0, 2).reshape(8, 4608)
    a_low = down_full.astype(jnp.bfloat16)
    b_low = up_full.astype(jnp.bfloat16)
    a_in, a_out = a_low[:24], a_low[24:]
    factor_of = (jnp.arange(2560) >= 2048).astype(jnp.int32) + (jnp.arange(2560) >= 2304)
    b_in = jnp.where(
        (jnp.arange(24) // 8)[:, None] == factor_of[None, :],
        jnp.concatenate([b_low[:, :2560]] * 3, 0),
        jnp.zeros((), jnp.bfloat16),
    )
    b_out = b_low[:, 2560:]

    places = loss_position_index.reshape(2, 8, SEQ_N, 32)
    spots = jnp.arange(SEQ_N)[:, None] * TOK + places
    counted = spots < row_used_length[..., None, None]
    below = jnp.sum(
        (document_slot_index[..., None] < jnp.arange(1, 3)).astype(jnp.int32), axis=2
    )
    seg_at = jnp.sum(
        (spots[..., None] >= below[:, :, None, None, :]).astype(jnp.int32), axis=-1
    )
    member = counted[..., None] & (seg_at[..., None] == jnp.arange(3))
    counts = jnp.sum(member.astype(jnp.int32), axis=(2, 3))
    document_total = jnp.sum((counts > 0).astype(jnp.float32))
    own_places = lax.dynamic_index_in_dim(places, seq_here, 2, keepdims=False)
    own_counted = lax.dynamic_index_in_dim(counted, seq_here, 2, keepdims=False)
    own_seg = lax.dynamic_index_in_dim(seg_at, seq_here, 2, keepdims=False)
    per_doc = jnp.sum(
        jnp.where(own_seg[..., None] == jnp.arange(3), counts[:, :, None, :], 0), axis=-1
    )
    own_weight = jnp.where(own_counted, 1.0 / jnp.maximum(per_doc, 1).astype(jnp.float32), 0.0)
    weight_flat = own_weight.transpose(1, 0, 2).reshape(-1)
    row_places = lax.dynamic_index_in_dim(own_places, fsdp_here, 1, keepdims=False)
    chosen_at = (row_places + jnp.arange(2)[:, None] * TOK).reshape(64)
    pick = (chosen_at[:, None] == jnp.arange(128)[None, :]).astype(jnp.float32)

    ids = ids[:, :, :TOK].reshape(SEQ_N, 2, 8, TOK)
    row_ids = lax.dynamic_index_in_dim(ids, fsdp_here, 2, keepdims=False).reshape(SEQ_N, 128)
    x_start = rows_of_tokens(table.reshape(8 * vocab_dev, 128), row_ids, 2).astype(jnp.float32)

    half = 32
    freqs = ROPE_BASE ** (-2.0 * jnp.arange(half).astype(jnp.float32) / 64)
    angles = (seq_here * TOK + jnp.arange(TOK)).astype(jnp.float32)[:, None] * freqs[None, :]
    cosine = jnp.tile(jnp.cos(angles), (1, 16))
    sine = jnp.sin(angles)
    sine = jnp.tile(jnp.concatenate([-sine, sine], 1), (1, 8))
    own_docs = lax.dynamic_index_in_dim(document_slot_index, fsdp_here, 1, keepdims=False)
    padded = jnp.concatenate([jnp.full((2, 4 * TOK), -1, jnp.int32), own_docs], 1)
    key_seg = lax.dynamic_slice_in_dim(padded, seq_here * TOK, 5 * TOK, 1)[:, None, :]
    query_seg = key_seg[:, 0, 4 * TOK :][:, :, None]
    start = (seq_here * TOK).reshape(1)
    normed_one = (x_start * norm_scale(x_start) * gain[0]).astype(jnp.bfloat16)
    adapter_in = nt(normed_one, a_in).astype(jnp.bfloat16)
    packed = dot(normed_one, w_qkv) + ADAPTER_SCALE * dot(adapter_in, b_in)
    window = key_value_window(packed[:, 2048:], cosine, sine, 3)
    queries, attended = attend(
        packed, window, cosine, sine, query_seg, key_seg, start, head_group_offsets
    )
    adapter_mid = nt(attended, a_out).astype(jnp.bfloat16)
    x_mid = x_start + dot(attended, w_out) + ADAPTER_SCALE * dot(adapter_mid, b_out)

    normed_two = (x_mid * norm_scale(x_mid) * gain[1]).astype(jnp.bfloat16)
    hidden_sum, gate_up = feed_forward(normed_two, gate_up_w, down_w, None, 12, "feed_forward")
    x_end = x_mid + hidden_sum
    normed_end = (x_end * norm_scale(x_end) * gain[2]).astype(jnp.bfloat16)

    chosen = dot(pick.astype(jnp.bfloat16), normed_end).astype(jnp.bfloat16)
    local_target = target_token_index.transpose(1, 0, 2).reshape(512, 1) - fsdp_here * vocab_dev
    local_target = jnp.where(local_target < vocab_dev, local_target, -1)
    weight_column = weight_flat.reshape(512, 1)
    d_chosen, loss_tile = head_step(
        chosen, head, local_target, weight_column, weight_column / document_total, 4
    )
    loss_part = loss_tile[0, 0]

    upstream = lax.dot_general(pick, d_chosen, (((0,), (0,)), ((), ())), precision=HIGHEST)
    d_end, gain_end = norm_back(x_end, gain[2], upstream)
    d_normed = feed_forward(
        d_end.astype(jnp.bfloat16), gate_up_w, down_w, gate_up, 13, "feed_forward_back"
    )
    back_two, gain_mid = norm_back(x_mid, gain[1], d_normed)
    d_mid = d_end + back_two

    d_branch = d_mid.astype(jnp.bfloat16)
    d_adapter_mid = (ADAPTER_SCALE * nt(d_branch, b_out)).astype(jnp.bfloat16)
    d_attended = (nt(d_branch, w_out) + dot(d_adapter_mid, a_out)).astype(jnp.bfloat16)
    up_gradient_out = ADAPTER_SCALE * tn(adapter_mid, d_branch)
    down_gradient_out = tn(d_adapter_mid, attended)
    d_queries, d_far, d_own = attend_back(
        queries, window, d_attended, cosine, sine, query_seg, key_seg, start, head_group_offsets
    )
    d_key_value = key_value_back(d_far, d_own, cosine, sine, 7)
    d_packed = jnp.concatenate([d_queries, d_key_value], 1)
    d_adapter_in = (ADAPTER_SCALE * nt(d_packed, b_in)).astype(jnp.bfloat16)
    up_gradient_in = ADAPTER_SCALE * jnp.concatenate(
        [
            tn(adapter_in[:, 0:8], d_packed[:, :2048]),
            tn(adapter_in[:, 8:16], d_packed[:, 2048:2304]),
            tn(adapter_in[:, 16:24], d_packed[:, 2304:]),
        ],
        1,
    )
    down_gradient_in = tn(d_adapter_in, normed_one)
    back_one, gain_start = norm_back(
        x_start, gain[0], nt(d_packed, w_qkv) + dot(d_adapter_in, a_in)
    )
    d_start = (d_mid + back_one).astype(jnp.bfloat16)

    left = jnp.concatenate(
        [
            down_gradient_in,
            down_gradient_out,
            jnp.stack([gain_start, gain_mid, gain_end]),
            jnp.zeros((5, 2048), jnp.float32),
        ],
        0,
    )
    left = left.reshape(40, 16, 128).transpose(1, 0, 2)
    right = jnp.concatenate([up_gradient_in, up_gradient_out], 1).reshape(8, 16, 288)
    right = jnp.pad(right, ((0, 0), (0, 0), (0, 96))).transpose(1, 0, 2).reshape(16, 24, 128)
    all_ids = ids.transpose(2, 0, 1, 3).reshape(16, 1024) - fsdp_here * vocab_dev
    grad_embed, small_sum = token_gradients(
        d_start, jnp.concatenate([left, right], 1), all_ids, vocab_dev, 8
    )
    left_sum = small_sum[:40]
    right_sum = small_sum[40:].reshape(8, 384)[:, :288]
    group_onehot = factor_onehot(seq_here * 288 + jnp.arange(288))
    stats_part = shampoo_parts(left_sum[:32], right_sum, group_onehot)
    first = (fsdp_here == 0).astype(jnp.float32)
    squares = jnp.sum(grad_embed * grad_embed) + first * (
        jnp.sum(left_sum[:35] * left_sum[:35]) + jnp.sum(right_sum * right_sum)
    )
    totals = jnp.concatenate(
        [
            (first * stats_part).reshape(-1),
            squares.reshape(1),
            loss_part.reshape(1),
            jnp.zeros((510,), jnp.float32),
        ]
    ).reshape(8, 128)
    totals = sum_over("seq", totals, 10, "totals_seq", False)
    totals = sum_over("fsdp", totals, 11, "totals_fsdp", False)
    stats_all = totals[:4].reshape(8, 8, 8)
    document_loss_sum = totals[4, 1]
    global_gradient_norm = jnp.sqrt(totals[4, 0])
    clip_factor = CLIP_MAX / jnp.maximum(global_gradient_norm, CLIP_MAX)

    own_left = lax.dynamic_slice_in_dim(left_sum, fsdp_here * 16, 16, 1)
    down_factor_gradient = own_left[:32] * clip_factor
    grad_gain = own_left[32:35] * clip_factor
    up_factor_gradient = (
        lax.dynamic_slice_in_dim(right_sum, fsdp_here * 36, 36, 1) * clip_factor
    )
    grad_embed = grad_embed * clip_factor
    unused_first, updated_embedding_second_moment, updated_embedding_table = adam_update(
        embedding, embedding_first_moment, embedding_second_moment, grad_embed, RATE_EMBED
    )
    updated_gain_first_moment, updated_gain_second_moment, updated_norm_gains = adam_update(
        norm_gain_vectors, norm_gain_first_moment, norm_gain_second_moment, grad_gain, RATE_GAIN
    )
    updated_rank_statistics = (
        SECOND_DECAY * rank_side_statistics
        + (1.0 - SECOND_DECAY) * (clip_factor * clip_factor) * stats_all
    )
    updated_down_width_statistics = SECOND_DECAY * down_width_statistics + (
        1.0 - SECOND_DECAY
    ) * jnp.sum(down_factor_gradient.reshape(4, 8, -1) ** 2, axis=1)
    updated_up_width_statistics = SECOND_DECAY * up_width_statistics + (
        1.0 - SECOND_DECAY
    ) * jnp.sum(up_factor_gradient * up_factor_gradient, axis=0)
    onehot = factor_onehot((seq_here * 8 + fsdp_here) * 36 + jnp.arange(36))
    down_factor_step, up_factor_step = shampoo_apply(
        updated_rank_statistics,
        updated_down_width_statistics,
        updated_up_width_statistics,
        down_factor_gradient,
        up_factor_gradient,
        onehot,
    )
    updated_down_factors = adapter_down_factors - LEARN_RATE_DOWN * down_factor_step
    updated_up_factors = adapter_up_factors - LEARN_RATE_UP * up_factor_step
    return (
        document_loss_sum,
        document_total,
        global_gradient_norm,
        grad_embed,
        updated_embedding_second_moment,
        updated_embedding_table,
        updated_gain_first_moment,
        updated_gain_second_moment,
        updated_norm_gains,
        down_factor_gradient,
        up_factor_gradient,
        updated_rank_statistics,
        updated_down_width_statistics,
        updated_up_width_statistics,
        updated_down_factors,
        updated_up_factors,
    )


def solution(mesh):
    torus = Mesh(
        mesh.devices.reshape(2, 4, 2, 2, 2, 2), SEQ_FSDP
    )
    return jax.shard_map(
        per_device,
        mesh=torus,
        in_specs=(
            P(None, None, SEQ),
            P(None, None, SEQ),
            P(),
            P(),
            P(),
            P(),
            P(FSDP, SEQ),
            P(FSDP, SEQ),
            P(FSDP, SEQ),
            P(FSDP, SEQ),
            P(SEQ_FSDP, None),
            P(SEQ_FSDP, None),
            P(SEQ_FSDP, None),
            P(SEQ_FSDP, None),
            P(None, SEQ_FSDP),
            P(None, SEQ_FSDP),
            P(None, SEQ_FSDP),
            P(None, SEQ_FSDP),
            P(None, SEQ_FSDP),
            P(),
            P(None, SEQ_FSDP),
            P(SEQ_FSDP),
        ),
        out_specs=(
            P(),
            P(),
            P(),
            P(FSDP, SEQ),
            P(FSDP, SEQ),
            P(FSDP, SEQ),
            P(None, SEQ_FSDP),
            P(None, SEQ_FSDP),
            P(None, SEQ_FSDP),
            P(None, SEQ_FSDP),
            P(None, SEQ_FSDP),
            P(),
            P(None, SEQ_FSDP),
            P(SEQ_FSDP),
            P(None, SEQ_FSDP),
            P(None, SEQ_FSDP),
        ),
        check_vma=False,
    )
```

```python
import functools

import jax
import jax.numpy as jnp
from jax import lax
from jax.experimental import pallas as pl
from jax.experimental.pallas import tpu as pltpu
from jax.sharding import Mesh
from jax.sharding import PartitionSpec as P

STEP = 5
GROUP = 256
SEQ = ("seq_0", "seq_1", "seq_2")
FSDP = ("fsdp_0", "fsdp_1", "fsdp_2")
SEQ_FSDP = SEQ + FSDP
SEQ_N = 16
FSDP_N = 8
TOK = 64
PAD_FF = 6144
NORM_EPS = 1e-05
ADAPTER_SCALE = 2.0
ROPE_BASE = 10000.0
CLIP_MAX = 0.001
FIRST_DECAY = 0.5
SECOND_DECAY = 0.5
RATE_EMBED = 0.3
RATE_GAIN = 0.1
LEARN_RATE_DOWN = 0.1
LEARN_RATE_UP = 0.5
WEIGHT_DECAY = 0.01
ADAM_EPS = 1e-12
HIGHEST = lax.Precision.HIGHEST
MESH_ID = pl.DeviceIdType.MESH
ANY = pl.BlockSpec(memory_space=pl.ANY)
VMEM = pl.BlockSpec(memory_space=pltpu.VMEM)
SMEM = pl.BlockSpec(memory_space=pltpu.SMEM)
DMA = pltpu.SemaphoreType.DMA
VMEM_LIMIT = 56 * 1024 * 1024


def seq_me():
    return lax.axis_index("seq_0") * 8 + lax.axis_index("seq_1") * 2 + lax.axis_index("seq_2")


def z_me():
    return lax.axis_index("fsdp_0") * 2 + lax.axis_index("fsdp_1")


def z_at(i):
    return {"fsdp_0": i // 2, "fsdp_1": i % 2}


def fsdp_me():
    return z_me() * 2 + lax.axis_index("fsdp_2")


def seq_at(i):
    return {"seq_0": i // 8, "seq_1": (i // 2) % 4, "seq_2": i % 2}


def fsdp_at(i):
    return {**z_at(i // 2), "fsdp_2": i % 2}


RINGS = {"seq": (SEQ_N, seq_me, seq_at), "fsdp": (FSDP_N, fsdp_me, fsdp_at)}


def greet(kind, offsets):
    count, where, at = RINGS[kind]
    me = where()
    barrier = pltpu.get_barrier_semaphore()
    for k in offsets:
        pl.semaphore_signal(
            barrier, inc=1, device_id=at((me + count - k) % count), device_id_type=MESH_ID
        )
    pl.semaphore_wait(barrier, len(offsets))
    return me


def send_each(kind, me, offsets, src_of, dst_of, send_sem, recv_sem):
    count, _, at = RINGS[kind]
    copies = []
    for n, k in enumerate(offsets):
        peer = (me + k) % count
        copy = pltpu.make_async_remote_copy(
            src_ref=src_of(k, peer),
            dst_ref=dst_of(k, peer),
            send_sem=send_sem.at[n],
            recv_sem=recv_sem.at[n],
            device_id=at(peer),
            device_id_type=MESH_ID,
        )
        copy.start()
        copies.append(copy)
    return copies


def remote_call(body, out_shape, in_specs, out_specs, scratch, collective_id, name):
    return pl.pallas_call(
        body,
        out_shape=out_shape,
        in_specs=in_specs,
        out_specs=out_specs,
        scratch_shapes=scratch,
        compiler_params=pltpu.CompilerParams(
            collective_id=collective_id, has_side_effects=True, vmem_limit_bytes=VMEM_LIMIT
        ),
        name=name,
    )


def sems(n):
    return [DMA((n,)), DMA((n,))]


ALL16 = range(1, SEQ_N)
ALL8 = range(1, FSDP_N)


def sum_over(kind, block, collective_id, name, scatter):
    count = RINGS[kind][0]
    offsets = ALL16 if kind == "seq" else ALL8
    part = block.shape[1:] if scatter else block.shape

    def body(src, out, held, ssem, rsem):
        me = greet(kind, offsets)
        copies = send_each(
            kind, me, offsets,
            (lambda k, p: src.at[p]) if scatter else (lambda k, p: src),
            lambda k, p: held.at[k - 1], ssem, rsem,
        )
        total = (src[me] if scatter else src[...]).astype(jnp.float32)
        for n, copy in enumerate(copies):
            copy.wait_recv()
            total = total + held[n].astype(jnp.float32)
        out[...] = total
        for copy in copies:
            copy.wait_send()

    return remote_call(
        body,
        jax.ShapeDtypeStruct(part, jnp.float32),
        [VMEM],
        VMEM,
        [pltpu.VMEM((count - 1, *part), block.dtype)] + sems(count - 1),
        collective_id,
        name,
    )(block)


ORDER = (
    "s", "g0", "g1", "d0", "d1", "q0", "q1", "q2", "t", "s", "s", "q1",
    "q1", "q0", "q0", "s", "q1", "q0", "s", "s", "s", "q2", "q2", "q0",
    "q0", "q2", "q0", "d0", "d1", "t", "s", "s", "g0", "g1", "s", "q2",
    "q2", "q1", "q1", "d1", "d1", "d0", "d0", "q1", "q2", "d1", "d0", "q0",
    "q0", "g1", "g1", "g0", "g0", "q0", "g1", "g0", "q1", "q1", "t", "d1",
    "d1", "q2", "q2", "d0", "d0", "q1", "d1", "q2", "d0", "g1", "g1", "t",
    "t", "g0", "g0", "g1", "g0", "t",
)


class Post:
    def __init__(self, sem, count):
        self.sem, self.count, self.used, self.sent, self.late = sem, count, 0, [], []

    def fresh(self):
        self.used += 1
        assert self.used <= self.count, self.used
        return self.sem.at[self.used - 1]

    def start(self, src, dst, ssem, rsem, device):
        copy = pltpu.make_async_remote_copy(
            src_ref=src, dst_ref=dst, send_sem=ssem, recv_sem=rsem,
            device_id=device, device_id_type=MESH_ID,
        )
        copy.start()
        return copy

    def send(self, src, dst, device):
        copy = self.start(src, dst, self.fresh(), self.fresh(), device)
        self.sent.append(copy)
        return copy

    def finish(self):
        for copy in self.sent:
            copy.wait_send()
        for mark, view in self.late:
            pltpu.make_async_copy(view, view, mark).wait()


def greet_devices(devices):
    barrier = pltpu.get_barrier_semaphore()
    for device in devices:
        pl.semaphore_signal(barrier, inc=1, device_id=device, device_id_type=MESH_ID)
    pl.semaphore_wait(barrier, len(devices))


def fsdp_peers():
    me = fsdp_me()
    return [fsdp_at((me + k) % FSDP_N) for k in ALL8]


def seq_peers():
    me = seq_me()
    return [seq_at((me + k) % SEQ_N) for k in ALL16]


def relay(post, out, first, second, first_a, first_b):
    z, yl = z_me(), lax.axis_index("fsdp_2")
    partner, up, down = {"fsdp_2": 1 - yl}, z_at((z + 1) % 4), z_at((z + 3) % 4)
    before, after, far = (z + 3) % 4, (z + 1) % 4, (z + 2) % 4

    def at(zz, y, part=()):
        return out.at[(zz * 2 + y,) + part]

    def send(zz, y, part, device):
        view = at(zz, y, part)
        return post.send(view, view, device)

    to_partner = send(z, yl, (), partner)
    ring_up = send(z, yl, (), up)
    ring_down = send(z, yl, (), down)
    yield
    to_partner.wait_recv()
    other_up = send(z, 1 - yl, first, up)
    other_down = send(z, 1 - yl, first, down)
    yield
    ring_up.wait_recv()
    far_up = send(before, yl, first, up)
    across = [send(before, yl, second, partner)]
    yield
    ring_down.wait_recv()
    far_down = send(after, yl, second, down)
    across.append(send(after, yl, second, partner))
    yield
    other_up.wait_recv()
    last_up = send(before, 1 - yl, first_a, up)
    yield
    other_down.wait_recv()
    last_down = send(after, 1 - yl, first_b, down)
    yield
    far_up.wait_recv()
    far_down.wait_recv()
    across.append(send(far, yl, second, partner))
    yield
    last_up.wait_recv()
    last_down.wait_recv()
    for copy in across:
        copy.wait_recv()


def gather_weights(qkvo, small, table, ids, gate_up, down):
    quarter = gate_up.shape[1] // 4
    out_shape = [
        jax.ShapeDtypeStruct((2, 4, 2, 4, 2, *qkvo.shape), qkvo.dtype),
        jax.ShapeDtypeStruct((2, 4, 2, 4, 2, *small.shape), small.dtype),
        jax.ShapeDtypeStruct((FSDP_N, *table.shape), table.dtype),
        jax.ShapeDtypeStruct((SEQ_N, *ids.shape), ids.dtype),
        jax.ShapeDtypeStruct((2, 4, 2, 4, 2, gate_up.shape[0], quarter), gate_up.dtype),
        jax.ShapeDtypeStruct((2, 4, 2, 2, *down.shape), down.dtype),
    ]
    sem_count = 300
    every = slice(None)

    def body(*refs):
        ins, outs, sem = refs[:6], refs[6:12], refs[12]
        post = Post(sem, sem_count)
        yh, x, c, z, yl = (
            lax.axis_index("seq_0"), lax.axis_index("seq_1"), lax.axis_index("seq_2"), z_me(),
            lax.axis_index("fsdp_2"),
        )
        where = {"x": x, "y": 2 * yh + yl, "z": z}
        seq = seq_me()

        def beside(axis, step):
            at = (where[axis] + step + 4) % 4
            if axis == "x":
                return {"seq_1": at}
            if axis == "z":
                return z_at(at)
            return {"seq_0": at // 2, "fsdp_2": at % 2}

        other = {"seq_2": 1 - c}
        column = [
            ((z + dz) % 4, (c + dc) % 2, dz, dc) for dz in range(4) for dc in range(2) if dz or dc
        ]

        def arrived(ref, rsem):
            pltpu.make_async_copy(ref, ref, rsem).wait()

        def rings(block, order, sizes, halves, across):
            for n, axis in enumerate(order):
                done = order[:n]
                at = where[axis]
                before, after, far = (at + 3) % 4, (at + 1) % 4, (at + 2) % 4
                send, from_before, from_after, far_first = (post.fresh() for _ in range(4))
                post.late.append((send, sizes[axis, n]))
                own = block(done, axis, at, None)
                post.start(own, own, send, from_before, beside(axis, 1))
                post.start(own, own, send, from_after, beside(axis, -1))
                yield
                got = block(done, axis, before, None)
                arrived(got, from_before)
                half = block(done, axis, before, 0)
                post.start(half, half, send, far_first, beside(axis, 1))
                across(got)
                yield
                got = block(done, axis, after, None)
                arrived(got, from_after)
                if halves:
                    far_second = post.fresh()
                    half = block(done, axis, after, 1)
                    post.start(half, half, send, far_second, beside(axis, -1))
                across(got)
                yield
                arrived(block(done, axis, far, 0), far_first)
                if halves:
                    arrived(block(done, axis, far, 1), far_second)
                across(block(done, axis, far, None))

        def place(done, axis, at):
            spot = {"yh": yh, "x": x, "z": z, "yl": yl}
            for a in done:
                if a == "y":
                    spot["yh"] = spot["yl"] = every
                else:
                    spot[a] = every
            if axis == "y":
                spot["yh"], spot["yl"] = at // 2, at % 2
            elif axis is not None:
                spot[axis] = at
            return spot

        def all_stream(ref, order, tails, halves=True):
            def block(done, axis, at, half):
                spot = place(done, axis, at)
                tail = tails[0 if half is None else half + 1]
                return ref.at[(spot["yh"], spot["x"], c, spot["z"], spot["yl"]) + tail]

            across_s, across_r = post.fresh(), post.fresh()
            post.late.append((across_s, ref.at[(every, every, c, every, every) + tails[0]]))
            post.late.append((across_r, ref.at[(every, every, 1 - c, every, every) + tails[0]]))

            def across(view):
                post.start(view, view, across_s, across_r, other)

            three = pl.ds(0, 3)
            sizes = {}
            for axis in "xyz":
                sizes[axis, 0] = ref.at[(0, 0, 0, three, 0) + tails[0]]
                sizes[axis, 1] = ref.at[(0, pl.ds(0, 2), 0, three, every) + tails[0]]
                sizes[axis, 2] = ref.at[(every, every, 0, three, every) + tails[0]]
            across(block([], None, None, None))
            yield from rings(block, order, sizes, halves, across)

        def nothing(view):
            return None

        def gate_up_stream(src, ref, order, start, width):
            tails = [
                (every, pl.ds(start, width)),
                (every, pl.ds(start, width // 2)),
                (every, pl.ds(start + width // 2, width // 2)),
            ]

            def block(done, axis, at, half):
                spot = place(done, axis, at)
                tail = tails[0 if half is None else half + 1]
                return ref.at[(spot["yh"], spot["x"], every, every, spot["yl"]) + tail]

            marks = []
            for zz, cc, dz, dc in column:
                send, recv = post.fresh(), post.fresh()
                first = pl.multiple_of(
                    (2 * (zz % 2) + cc) * quarter + start, 128
                )
                here = ref.at[(yh, x, c, z, yl) + tails[0]]
                post.start(src.at[:, pl.ds(first, width)], here, send, recv, {**z_at(zz), "seq_2": cc})
                post.late.append((send, here))
                marks.append((ref.at[(yh, x, (c + dc) % 2, (z + 4 - dz) % 4, yl) + tails[0]], recv))
            yield
            for view, recv in marks:
                arrived(view, recv)
            three = pl.ds(0, 3)
            sizes = {}
            for axis in "xy":
                sizes[axis, 0] = ref.at[(0, three, every, every, 0) + tails[0]]
                sizes[axis, 1] = ref.at[(every, three, every, every, every) + tails[0]]
            yield from rings(block, order, sizes, True, nothing)

        def down_stream(ref, order, start, width):
            tails = [
                (every, pl.ds(start, width)),
                (every, pl.ds(start, width // 2)),
                (every, pl.ds(start + width // 2, width // 2)),
            ]
            zh = z // 2

            def block(done, axis, at, half):
                spot = place(done, axis, at)
                tail = tails[0 if half is None else half + 1]
                return ref.at[(spot["yh"], spot["x"], every, spot["yl"]) + tail]

            send, recv = post.fresh(), post.fresh()
            here = ref.at[(yh, x, zh, yl) + tails[0]]
            post.start(here, here, send, recv, z_at((z + 2) % 4))
            post.late.append((send, here))
            yield
            arrived(ref.at[(yh, x, 1 - zh, yl) + tails[0]], recv)
            three = pl.ds(0, 3)
            sizes = {}
            for axis in "xy":
                sizes[axis, 0] = ref.at[(0, three, every, 0) + tails[0]]
                sizes[axis, 1] = ref.at[(every, three, every, every) + tails[0]]
            yield from rings(block, order, sizes, True, nothing)

        def table_stream(ref):
            send_y, recv_y = post.fresh(), post.fresh()
            post.late.append((send_y, ref.at[0]))
            own = ref.at[2 * z + yl]
            post.start(own, own, send_y, recv_y, {"fsdp_2": 1 - yl})
            yield
            arrived(ref.at[2 * z + 1 - yl], recv_y)
            half_rows = ref.shape[1] // 2
            part = (every, pl.ds(0, half_rows), pl.ds(half_rows, half_rows))

            def block(done, axis, at, half):
                return ref.at[pl.ds(2 * at, 2), part[0 if half is None else half + 1]]

            yield from rings(block, ("z",), {("z", 0): ref.at[pl.ds(0, 6)]}, True, nothing)

        own_views = [
            (ins[0], outs[0].at[yh, x, c, z, yl]),
            (ins[1], outs[1].at[yh, x, c, z, yl]),
            (ins[2], outs[2].at[z * 2 + yl]),
            (ins[3], outs[3].at[seq]),
            (
                ins[4].at[:, pl.ds(pl.multiple_of((2 * (z % 2) + c) * quarter, 128), quarter)],
                outs[4].at[yh, x, c, z, yl],
            ),
            (ins[5], outs[5].at[yh, x, z // 2, yl]),
        ]
        local = []
        for src, dst in own_views:
            copy = pltpu.make_async_copy(src, dst, post.fresh())
            copy.start()
            local.append(copy)
        greet_devices(
            [beside("y", 1), beside("y", -1)]
            + [{**z_at(zz), "seq_2": cc} for zz, cc, dz, dc in column if dz]
            + seq_peers()
        )
        for copy in local:
            copy.wait()

        send, recv = post.fresh(), post.fresh()
        for device in seq_peers():
            post.start(ins[3], outs[3].at[seq], send, recv, device)
        post.late.append((send, outs[3].at[pl.ds(0, 15)]))
        post.late.append((recv, outs[3].at[pl.ds(0, 15)]))

        third = qkvo.shape[1] // 3
        streams = {
            "s": all_stream(outs[1], "xyz", [(every, every)] * 2, False),
            "t": table_stream(outs[2]),
        }
        half, wide = quarter // 2, down.shape[1] // 2
        streams["g0"] = gate_up_stream(ins[4], outs[4], "xy", 0, half)
        streams["g1"] = gate_up_stream(ins[4], outs[4], "yx", half, half)
        streams["d0"] = down_stream(outs[5], "xy", 0, wide)
        streams["d1"] = down_stream(outs[5], "yx", wide, wide)
        for n, order in enumerate(('xyz', 'yzx', 'zxy')):
            streams["q%d" % n] = all_stream(
                outs[0], order,
                [
                    (every, pl.ds(n * third, third)),
                    (every, pl.ds(n * third, third // 2)),
                    (every, pl.ds(n * third + third // 2, third // 2)),
                ],
            )
        for name in ORDER:
            next(streams[name], None)
        for name in sorted(streams):
            assert next(streams[name], "end") == "end", name
        post.finish()

    return remote_call(
        body, out_shape, [ANY] * 6, [ANY] * 6, [DMA((sem_count,))], 1, "gather_weights"
    )(qkvo, small, table, ids, gate_up, down)


def rows_of_tokens(table, ids, collective_id):
    vocab, width = table.shape

    def body(ids_ref, table_ref, out, wide, rows, block, sem, lsem):
        post = Post(sem, 30)
        me = seq_me()
        wide[...] = table_ref[...].astype(jnp.float32)
        spot = pl.ds(pl.multiple_of(me * width, width), width)
        greet_devices(seq_peers())

        def fetch(s):
            def step(t, carry):
                rows[pl.ds(t, 1), :] = wide[pl.ds(ids_ref[s, t], 1), :]
                return carry

            lax.fori_loop(0, 128, step, 0, unroll=16)

        for k in list(ALL16) + [0]:
            peer = (me + k) % SEQ_N
            fetch(peer)
            block[k] = rows[...].astype(jnp.bfloat16)
            if k:
                post.send(block.at[k], out.at[:, spot], seq_at(peer))
        own = pltpu.make_async_copy(block.at[0], out.at[:, spot], lsem)
        own.start()
        for copy in post.sent:
            copy.wait_recv()
        post.finish()
        own.wait()

    return remote_call(
        body,
        jax.ShapeDtypeStruct((128, SEQ_N * width), jnp.bfloat16),
        [SMEM, VMEM],
        VMEM,
        [
            pltpu.VMEM((vocab, width), jnp.float32),
            pltpu.VMEM((128, width), jnp.float32),
            pltpu.VMEM((SEQ_N, 128, width), jnp.bfloat16),
            DMA((30,)),
            DMA,
        ],
        collective_id,
        "rows_of_tokens",
    )(ids, table)


def head_step(chosen, head, target, weight, scaled, collective_id):
    vocab, width = head.shape
    padded = -(-vocab // 512) * 512
    tiles = padded // 512

    def body(
        chosen_ref, head_hbm, target_ref, weight_ref, scaled_ref, out, loss, hd, held, raised, d_logits,
        prod, got, stat, stats, sem, lsem,
    ):
        post = Post(sem, 60)
        me = fsdp_me()
        load = pltpu.make_async_copy(head_hbm, hd.at[pl.ds(0, vocab)], lsem)
        load.start()
        held[me] = chosen_ref[...]
        greet_devices(fsdp_peers())
        for _ in relay(
            post, held, (pl.ds(0, 32),), (pl.ds(32, 32),), (pl.ds(0, 16),), (pl.ds(16, 16),)
        ):
            pass
        hd[vocab:, :] = jnp.zeros((padded - vocab, width), jnp.bfloat16)
        load.wait()
        rows = held[...].reshape(512, width)
        target_at = target_ref[...]

        def logits(n, carry):
            top, picked = carry
            at = pl.multiple_of(n * 512, 512)
            tile = nt(held[...].reshape(512, width), hd[pl.ds(at, 512), :])
            column = lax.broadcasted_iota(jnp.int32, (512, 512), 1) + at
            tile = jnp.where(column < vocab, tile, -1e30)
            raised[:, pl.ds(at, 512)] = tile
            top = jnp.maximum(top, jnp.max(tile, axis=1, keepdims=True))
            hit = jnp.where(column == target_at, tile, 0.0)
            return top, picked + jnp.sum(hit, axis=1, keepdims=True)

        top, picked = lax.fori_loop(
            0, tiles, logits, (jnp.full((512, 1), -1e30, jnp.float32), jnp.zeros((512, 1), jnp.float32))
        )

        def exponents(n, total):
            at = pl.ds(pl.multiple_of(n * 512, 512), 512)
            tile = jnp.exp(raised[:, at] - top)
            raised[:, at] = tile
            return total + jnp.sum(tile, axis=1, keepdims=True)

        total = lax.fori_loop(0, tiles, exponents, jnp.zeros((512, 1), jnp.float32))
        lane = lax.broadcasted_iota(jnp.int32, (512, 128), 1)
        both = jnp.where(lane == 0, top, jnp.where(lane == 1, total, 0.0))
        stat[...] = jnp.transpose(both)[0:8, :]
        copies = [
            post.send(stat, stats.at[k - 1], fsdp_at((me + k) % FSDP_N)) for k in ALL8
        ]
        for copy in copies:
            copy.wait_recv()
        top_all = stat[0:1, :]
        for n in range(7):
            top_all = jnp.maximum(top_all, stats[n, 0:1, :])
        sum_all = stat[1:2, :] * jnp.exp(stat[0:1, :] - top_all)
        for n in range(7):
            sum_all = sum_all + stats[n, 1:2, :] * jnp.exp(stats[n, 0:1, :] - top_all)
        log_row = top_all + jnp.log(sum_all)
        log_norm = jnp.transpose(jnp.broadcast_to(log_row, (128, 512)))[:, 0:1]
        weights = weight_ref[...]
        mine = lax.broadcasted_iota(jnp.int32, (512, 1), 0) // 64 == me
        value = jnp.sum(jnp.where(mine, log_norm * weights, 0.0) - weights * picked, axis=0, keepdims=True)
        loss[...] = jnp.broadcast_to(value, (8, 128))
        scale = scaled_ref[...]
        factor = scale * jnp.exp(top - log_norm)

        def slopes(n, carry):
            at = pl.multiple_of(n * 512, 512)
            column = lax.broadcasted_iota(jnp.int32, (512, 512), 1) + at
            hit = jnp.where(column == target_at, scale, 0.0)
            d_logits[:, pl.ds(at, 512)] = (factor * raised[:, pl.ds(at, 512)] - hit).astype(jnp.bfloat16)
            return carry

        lax.fori_loop(0, tiles, slopes, 0)
        half, inner = lax.axis_index("fsdp_0"), me % 4
        sums = []
        for n, part in enumerate((1 - half, half)):
            start = pl.multiple_of(part * 256, 256)

            def product(t, carry):
                at = pl.ds(pl.multiple_of(t * 512, 512), 512)
                tile = jnp.dot(
                    d_logits[pl.ds(start, 256), :], hd[:, at], preferred_element_type=jnp.float32
                )
                prod[pl.ds(part * 4, 4), :, at] = tile.astype(jnp.bfloat16).reshape(4, 64, 512)
                return carry

            lax.fori_loop(0, width // 512, product, 0)
            for j in range(n, 4):
                peer = part * 4 + (inner + j) % 4
                sums.append(post.send(prod.at[peer], got.at[4 * n + j - n], fsdp_at(peer)))
        out[...] = prod[me].astype(jnp.float32)
        for n, copy in enumerate(sums):
            copy.wait_recv()
            out[...] += got[n].astype(jnp.float32)
        post.finish()

    return remote_call(
        body,
        [
            jax.ShapeDtypeStruct((64, width), jnp.float32),
            jax.ShapeDtypeStruct((8, 128), jnp.float32),
        ],
        [VMEM, ANY, VMEM, VMEM, VMEM],
        [VMEM, VMEM],
        [
            pltpu.VMEM((padded, width), jnp.bfloat16),
            pltpu.VMEM((8, 64, width), jnp.bfloat16),
            pltpu.VMEM((512, padded), jnp.float32),
            pltpu.VMEM((512, padded), jnp.bfloat16),
            pltpu.VMEM((8, 64, width), jnp.bfloat16),
            pltpu.VMEM((7, 64, width), jnp.bfloat16),
            pltpu.VMEM((8, 512), jnp.float32),
            pltpu.VMEM((7, 8, 512), jnp.float32),
            DMA((60,)),
            DMA,
        ],
        collective_id,
        "head_step",
    )(chosen, head, target, weight, scaled)


def token_gradients(d_start, small, ids, vocab, collective_id):
    width = 128
    low_n, tile = 1024, 1024
    rows = small.shape[1]

    def body(src, small_ref, ids_ref, out, small_out, held, parts, mid, parts_b, total, spread, sem, lsem):
        post = Post(sem, 120)
        f, s = fsdp_me(), seq_me()
        z, yl = z_me(), lax.axis_index("fsdp_2")
        greet_devices(seq_peers() + fsdp_peers())

        def cols(p):
            return pl.ds(pl.multiple_of(p * width, width), width)

        moves, sums = [], []
        for k in ALL16:
            peer = (s + k) % SEQ_N
            sums.append(post.send(small_ref.at[peer], parts.at[k - 1], seq_at(peer)))
            moves.append(post.send(src.at[:, cols(peer)], held.at[f, s], seq_at(peer)))
        own = pltpu.make_async_copy(src.at[:, cols(s)], held.at[f, s], lsem)
        own.start()
        total[...] = jnp.zeros_like(total)
        amount = small_ref[s]
        for n, copy in enumerate(sums):
            copy.wait_recv()
            amount = amount + parts[n]
        mid[...] = amount
        shares = [post.send(mid, parts_b.at[k - 1], fsdp_at((f + k) % FSDP_N)) for k in ALL8]
        for copy in moves:
            copy.wait_recv()
        own.wait()

        def add(block):
            def one(t, carry):
                ids_row = ids_ref[pl.ds(block * 2 + t, 1), :]
                high, low = ids_row >> 10, ids_row & 1023
                part = lax.broadcasted_iota(jnp.int32, (8, tile), 0)
                which = jnp.transpose((part == high).astype(jnp.float32))
                grad = held[block, pl.ds(t * 8, 8)].reshape(tile, width).astype(jnp.float32)
                for h in range(4):
                    spread[:, h * width : (h + 1) * width] = jnp.where(
                        which[:, h : h + 1] > 0.5, grad, 0.0
                    ).astype(jnp.bfloat16)

                def step(n, inner):
                    start = pl.multiple_of(n * 256, 256)
                    row = lax.broadcasted_iota(jnp.int32, (256, tile), 0) + start
                    hot = (row == low).astype(jnp.float32).astype(jnp.bfloat16)
                    total[pl.ds(start, 256), :] += jnp.dot(
                        hot, spread[...], preferred_element_type=jnp.float32
                    )
                    return inner

                lax.fori_loop(0, low_n // 256, step, 0)
                return carry

            lax.fori_loop(0, 2, one, 0)

        every = slice(None)
        steps = relay(
            post, held, (pl.ds(0, 8),), (pl.ds(8, 8),), (pl.ds(0, 4),), (pl.ds(4, 4),)
        )
        before, after, far = (z + 3) % 4, (z + 1) % 4, (z + 2) % 4
        next(steps)
        add(f)
        next(steps)
        next(steps)
        next(steps)
        add(z * 2 + 1 - yl)
        next(steps)
        next(steps)
        add(before * 2 + yl)
        next(steps)
        add(after * 2 + yl)
        add(far * 2 + yl)
        assert next(steps, "end") == "end"
        for zz in (before, after, far):
            add(zz * 2 + 1 - yl)
        for n, copy in enumerate(shares):
            copy.wait_recv()
            mid_part = parts_b[n]
            amount = amount + mid_part
        small_out[...] = amount
        for h in range(4):
            count = min(low_n, vocab - h * low_n)
            out[h * low_n : h * low_n + count, :] = total[0:count, h * width : (h + 1) * width]
        post.finish()

    return remote_call(
        body,
        [
            jax.ShapeDtypeStruct((vocab, width), jnp.float32),
            jax.ShapeDtypeStruct((rows, width), jnp.float32),
        ],
        [VMEM, VMEM, VMEM],
        [VMEM, VMEM],
        [
            pltpu.VMEM((FSDP_N, SEQ_N, 128, width), jnp.bfloat16),
            pltpu.VMEM((15, rows, width), jnp.float32),
            pltpu.VMEM((rows, width), jnp.float32),
            pltpu.VMEM((7, rows, width), jnp.float32),
            pltpu.VMEM((low_n, 4 * width), jnp.float32),
            pltpu.VMEM((tile, 4 * width), jnp.bfloat16),
            DMA((120,)),
            DMA,
        ],
        collective_id,
        "token_gradients",
    )(d_start, small, ids)


def feed_forward(rows, gate_up_w, down_w, saved, collective_id, name):
    forward = saved is None
    count, width = rows.shape
    quarter = gate_up_w.shape[-1]
    units = quarter // 2
    chunk = count // 2
    tile = 512

    def body(*refs):
        if forward:
            (src, gu_hbm, dn_hbm, out, gu_out, held, gu, dn, saved_v, mid, part, give, got, sem) = refs
        else:
            (src, gu_hbm, dn_hbm, gu_in, out, held, gu, dn, saved_v, mid, part, give, got, sem) = refs
        c = lax.axis_index("seq_2")
        sibling = {"seq_2": 1 - c}
        partner = {"fsdp_1": 1 - lax.axis_index("fsdp_1")}
        used = [0]

        def fresh():
            used[0] += 1
            return sem.at[used[0] - 1]

        load_gu = [pltpu.make_async_copy(gu_hbm, gu, fresh())]
        load_dn = [pltpu.make_async_copy(dn_hbm, dn, fresh())]
        loads = [load_gu, load_dn]
        if not forward:
            load_dn.append(pltpu.make_async_copy(gu_in, saved_v, fresh()))
            loads = [load_dn, load_gu]
        for load in loads[0] + loads[1]:
            load.start()

        barrier = pltpu.get_barrier_semaphore()
        for device in (sibling, partner):
            pl.semaphore_signal(barrier, inc=1, device_id=device, device_id_type=MESH_ID)
        pl.semaphore_wait(barrier, 2)

        started = []

        def remote(src_ref, dst_ref, device):
            copy = pltpu.make_async_remote_copy(
                src_ref=src_ref, dst_ref=dst_ref, send_sem=fresh(), recv_sem=fresh(),
                device_id=device, device_id_type=MESH_ID,
            )
            copy.start()
            started.append(copy)
            return copy

        def lines(block, k=None):
            if k is None:
                return pl.ds(block * count, count)
            return pl.ds(block * count + k * chunk, chunk)

        along = [
            remote(src.at[pl.ds(k * chunk, chunk)], held.at[lines(2, k)], partner) for k in range(2)
        ]
        beside = remote(src, held.at[lines(1)], sibling)
        held[lines(0), :] = src[...]

        def first_product(pair):
            mine = pl.ds(pair * 2 * count, 2 * count)

            def step(n, carry):
                at = pl.multiple_of(n * tile, tile)
                low, high = pl.ds(at, tile), pl.ds(pl.multiple_of(at + units, tile), tile)
                block = held[mine, :]
                if forward:
                    gate = jnp.dot(block, gu[:, low], preferred_element_type=jnp.float32)
                    up = jnp.dot(block, gu[:, high], preferred_element_type=jnp.float32)
                    saved_v[mine, low] = gate
                    saved_v[mine, high] = up
                    mid[:, low] = (gate * jax.nn.sigmoid(gate) * up).astype(jnp.bfloat16)
                else:
                    d_hidden = nt(block, dn[low, :])
                    gate, up = saved_v[mine, low], saved_v[mine, high]
                    sigmoid_of = jax.nn.sigmoid(gate)
                    mid[:, low] = (
                        d_hidden * up * sigmoid_of * (1.0 + gate * (1.0 - sigmoid_of))
                    ).astype(jnp.bfloat16)
                    mid[:, high] = (d_hidden * gate * sigmoid_of).astype(jnp.bfloat16)
                return carry

            lax.fori_loop(0, units // tile, step, 0)

        def second_product(pair):
            def step(n, carry):
                at = pl.ds(pl.multiple_of(n * tile, tile), tile)
                if forward:
                    part[pair, :, at] = jnp.dot(
                        mid[...], dn[:, at], preferred_element_type=jnp.float32
                    )
                else:
                    part[pair, :, at] = nt(mid[...], gu[at, :])
                return carry

            lax.fori_loop(0, width // tile, step, 0)

        for load in loads[0]:
            load.wait()
        beside.wait_recv()
        first_product(0)
        along[0].wait_recv()
        passed = [remote(held.at[lines(2, 0)], held.at[lines(3, 0)], sibling)]
        for load in loads[1]:
            load.wait()
        second_product(0)
        along[1].wait_recv()
        passed.append(remote(held.at[lines(2, 1)], held.at[lines(3, 1)], sibling))
        give[0] = part[0, count:, :].astype(jnp.bfloat16)
        home = remote(give.at[0], got.at[0], sibling)
        if forward:
            stores = [
                pltpu.make_async_copy(
                    saved_v.at[pl.ds(0, 2 * count)], gu_out.at[pl.ds(0, 2 * count)], fresh()
                )
            ]
            stores[0].start()
        for copy in passed:
            copy.wait_recv()
        first_product(1)
        if forward:
            stores.append(
                pltpu.make_async_copy(
                    saved_v.at[pl.ds(2 * count, 2 * count)], gu_out.at[pl.ds(2 * count, 2 * count)], fresh()
                )
            )
            stores[1].start()
        second_product(1)
        give[1] = part[1, count:, :].astype(jnp.bfloat16)
        over = remote(give.at[1], got.at[1], sibling)
        over.wait_recv()
        back = []
        for k in range(2):
            some = pl.ds(k * chunk, chunk)
            give[2, some, :] = (part[1, some, :] + got[1, some, :].astype(jnp.float32)).astype(
                jnp.bfloat16
            )
            back.append(remote(give.at[2, some], got.at[2, some], partner))
        home.wait_recv()
        out[...] = part[0, 0:count, :] + got[0].astype(jnp.float32)
        for k in range(2):
            some = pl.ds(k * chunk, chunk)
            back[k].wait_recv()
            out[some, :] += got[2, some, :].astype(jnp.float32)
        for copy in started:
            copy.wait_send()
        if forward:
            for copy in stores:
                copy.wait()

    scratch = [
        pltpu.VMEM((4 * count, width), jnp.bfloat16),
        pltpu.VMEM(gate_up_w.shape, jnp.bfloat16),
        pltpu.VMEM(down_w.shape, jnp.bfloat16),
        pltpu.VMEM((4 * count, quarter), jnp.float32),
        pltpu.VMEM((2 * count, units if forward else quarter), jnp.bfloat16),
        pltpu.VMEM((2, 2 * count, width), jnp.float32),
        pltpu.VMEM((3, count, width), jnp.bfloat16),
        pltpu.VMEM((3, count, width), jnp.bfloat16),
        DMA((24,)),
    ]
    total = jax.ShapeDtypeStruct((count, width), jnp.float32)
    if forward:
        products = jax.ShapeDtypeStruct((4 * count, quarter), jnp.float32)
        return remote_call(
            body, [total, products], [VMEM, ANY, ANY], [VMEM, ANY], scratch, collective_id, name
        )(rows, gate_up_w, down_w)
    return remote_call(
        body, total, [VMEM, ANY, ANY, ANY], VMEM, scratch, collective_id, name
    )(rows, gate_up_w, down_w, saved)


def turn(values, cosine, sine):
    width = values.shape[-1]
    lane = lax.broadcasted_iota(jnp.int32, values.shape, values.ndim - 1)
    swapped = jnp.where(
        lane % 64 < 32,
        pltpu.roll(values, width - 32, values.ndim - 1),
        pltpu.roll(values, 32, values.ndim - 1),
    )
    return values * cosine + swapped * sine


def key_value_window(key_value, cosine, sine, collective_id):
    def body(kv_ref, cos_ref, sin_ref, out, held, ssem, rsem, lsem):
        me = greet("seq", range(1, 5))
        for m in range(2):
            rows = kv_ref[pl.ds(m * TOK, TOK), :]
            held[m, :, 0:256] = turn(rows[:, 0:256], cos_ref[:, 0:256], sin_ref[:, 0:256]).astype(
                jnp.bfloat16
            )
            held[m, :, 256:512] = rows[:, 256:512].astype(jnp.bfloat16)
        copies = send_each(
            "seq", me, range(1, 5), lambda k, p: held,
            lambda k, p: out.at[:, pl.ds((4 - k) * TOK, TOK), :], ssem, rsem,
        )
        own = pltpu.make_async_copy(held, out.at[:, pl.ds(4 * TOK, TOK), :], lsem)
        own.start()
        for copy in copies:
            copy.wait()
        own.wait()

    return remote_call(
        body,
        jax.ShapeDtypeStruct((2, 5 * TOK, 512), jnp.bfloat16),
        [VMEM] * 3,
        VMEM,
        [pltpu.VMEM((2, TOK, 512), jnp.bfloat16)] + sems(4) + [DMA],
        collective_id,
        "key_value_window",
    )(key_value, cosine, sine)


def key_value_back(far, own, cosine, sine, collective_id):
    def body(far_ref, own_ref, cos_ref, sin_ref, out, held, ssem, rsem):
        me = greet("seq", range(12, 16))
        copies = send_each(
            "seq", me, range(12, 16),
            lambda k, p: far_ref.at[:, pl.ds((k - 12) * TOK, TOK), :],
            lambda k, p: held.at[k - 12], ssem, rsem,
        )
        for copy in copies:
            copy.wait_recv()
        for m in range(2):
            total = own_ref[m]
            for n in range(3, -1, -1):
                total = total + held[n, m].astype(jnp.float32)
            keys = turn(total[:, 0:256], cos_ref[:, 0:256], -sin_ref[:, 0:256])
            out[pl.ds(m * TOK, TOK), 0:256] = keys.astype(jnp.bfloat16)
            out[pl.ds(m * TOK, TOK), 256:512] = total[:, 256:512].astype(jnp.bfloat16)
        for copy in copies:
            copy.wait_send()

    return remote_call(
        body,
        jax.ShapeDtypeStruct((2 * TOK, 512), jnp.bfloat16),
        [VMEM] * 4,
        VMEM,
        [pltpu.VMEM((4, 2, TOK, 512), jnp.bfloat16)] + sems(4),
        collective_id,
        "key_value_back",
    )(far, own, cosine, sine)


def spread_heads(block):
    return jnp.concatenate([block[:, 64 * g : 64 * g + 64] for g in range(8)], axis=0)


def join_heads(block):
    return jnp.concatenate([block[64 * g : 64 * g + 64, :] for g in range(8)], axis=1)


def window_mask(start_ref, query_seg, key_seg, shift):
    start = start_ref[0]
    query = start + lax.broadcasted_iota(jnp.int32, (TOK, 5 * TOK), 0)
    key = start - 4 * TOK + lax.broadcasted_iota(jnp.int32, (TOK, 5 * TOK), 1)
    allowed = (
        (key <= query)
        & (key >= 0)
        & (query_seg == key_seg)
        & (((query + shift) >> 8) == ((key + shift) >> 8))
    )
    return jnp.concatenate([allowed.astype(jnp.float32)] * 8, axis=0) > 0.5


def nt(left, right):
    return lax.dot_general(
        left, right, (((1,), (1,)), ((), ())), preferred_element_type=jnp.float32
    )


def tn(left, right):
    return lax.dot_general(
        left, right, (((0,), (0,)), ((), ())), preferred_element_type=jnp.float32
    )


def probabilities(queries, keys, mask):
    scores = jnp.where(mask, nt(queries, keys) * 0.125, -1e30)
    top = jnp.max(scores, axis=-1, keepdims=True)
    raised = jnp.where(mask, jnp.exp(scores - top), 0.0)
    return raised / jnp.sum(raised, axis=-1, keepdims=True)


def attend(queries, window, cosine, sine, query_seg, key_seg, start, shifts):
    def body(start_ref, shift_ref, q_ref, kv_ref, cos_ref, sin_ref, qs_ref, ks_ref, q_out, a_out):
        for h in range(4):
            cols = slice(512 * h, 512 * h + 512)
            turned = turn(q_ref[:, cols], cos_ref[...], sin_ref[...]).astype(jnp.bfloat16)
            q_out[:, cols] = turned
            mask = window_mask(start_ref, qs_ref[0], ks_ref[0], shift_ref[h])
            probs = probabilities(spread_heads(turned), kv_ref[0, :, 64 * h : 64 * h + 64], mask)
            values = kv_ref[0, :, 256 + 64 * h : 256 + 64 * h + 64]
            mixed = jnp.dot(probs.astype(jnp.bfloat16), values, preferred_element_type=jnp.float32)
            a_out[:, cols] = join_heads(mixed).astype(jnp.bfloat16)

    wide = pl.BlockSpec((TOK, 2048), lambda m: (m, 0))
    return pl.pallas_call(
        body,
        out_shape=[jax.ShapeDtypeStruct((2 * TOK, 2048), jnp.bfloat16)] * 2,
        grid=(2,),
        in_specs=[
            SMEM,
            SMEM,
            wide,
            pl.BlockSpec((1, 5 * TOK, 512), lambda m: (m, 0, 0)),
            pl.BlockSpec((TOK, 512), lambda m: (0, 0)),
            pl.BlockSpec((TOK, 512), lambda m: (0, 0)),
            pl.BlockSpec((1, TOK, 1), lambda m: (m, 0, 0)),
            pl.BlockSpec((1, 1, 5 * TOK), lambda m: (m, 0, 0)),
        ],
        out_specs=[wide, wide],
        compiler_params=pltpu.CompilerParams(vmem_limit_bytes=VMEM_LIMIT),
        name="attend",
    )(start, shifts, queries, window, cosine, sine, query_seg, key_seg)


def attend_back(queries, window, upstream, cosine, sine, query_seg, key_seg, start, shifts):
    def body(
        start_ref, shift_ref, q_ref, kv_ref, g_ref, cos_ref, sin_ref, qs_ref, ks_ref,
        dq_out, far_out, own_out,
    ):
        for h in range(4):
            cols = slice(512 * h, 512 * h + 512)
            mask = window_mask(start_ref, qs_ref[0], ks_ref[0], shift_ref[h])
            spread = spread_heads(q_ref[:, cols])
            keys = kv_ref[0, :, 64 * h : 64 * h + 64]
            values = kv_ref[0, :, 256 + 64 * h : 256 + 64 * h + 64]
            probs = probabilities(spread, keys, mask)
            grads = spread_heads(g_ref[:, cols])
            d_probs = nt(grads, values)
            d_values = tn(probs.astype(jnp.bfloat16), grads)
            inner = jnp.sum(probs * d_probs, axis=-1, keepdims=True)
            d_scores = (0.125 * probs * (d_probs - inner)).astype(jnp.bfloat16)
            d_queries = join_heads(jnp.dot(d_scores, keys, preferred_element_type=jnp.float32))
            dq_out[:, cols] = turn(d_queries, cos_ref[...], -sin_ref[...]).astype(jnp.bfloat16)
            d_keys = tn(d_scores, spread)
            for at, part in ((64 * h, d_keys), (256 + 64 * h, d_values)):
                far_out[0, :, at : at + 64] = part[0 : 4 * TOK].astype(jnp.bfloat16)
                own_out[0, :, at : at + 64] = part[4 * TOK :]

    wide = pl.BlockSpec((TOK, 2048), lambda m: (m, 0))
    return pl.pallas_call(
        body,
        out_shape=[
            jax.ShapeDtypeStruct((2 * TOK, 2048), jnp.bfloat16),
            jax.ShapeDtypeStruct((2, 4 * TOK, 512), jnp.bfloat16),
            jax.ShapeDtypeStruct((2, TOK, 512), jnp.float32),
        ],
        grid=(2,),
        in_specs=[
            SMEM,
            SMEM,
            wide,
            pl.BlockSpec((1, 5 * TOK, 512), lambda m: (m, 0, 0)),
            wide,
            pl.BlockSpec((TOK, 512), lambda m: (0, 0)),
            pl.BlockSpec((TOK, 512), lambda m: (0, 0)),
            pl.BlockSpec((1, TOK, 1), lambda m: (m, 0, 0)),
            pl.BlockSpec((1, 1, 5 * TOK), lambda m: (m, 0, 0)),
        ],
        out_specs=[
            wide,
            pl.BlockSpec((1, 4 * TOK, 512), lambda m: (m, 0, 0)),
            pl.BlockSpec((1, TOK, 512), lambda m: (m, 0, 0)),
        ],
        compiler_params=pltpu.CompilerParams(vmem_limit_bytes=VMEM_LIMIT),
        name="attend_back",
    )(start, shifts, queries, window, upstream, cosine, sine, query_seg, key_seg)


def dot(left, right):
    return jnp.dot(left, right, preferred_element_type=jnp.float32)


def dot_exact(left, right):
    return jnp.dot(left, right, precision=HIGHEST)


def norm_scale(values):
    return lax.rsqrt(jnp.mean(values * values, axis=-1, keepdims=True) + NORM_EPS)


def norm_back(values, gain, upstream):
    scale_of = norm_scale(values)
    scaled = gain * upstream
    inward = scale_of * scaled - values * scale_of**3 * jnp.mean(
        scaled * values, axis=-1, keepdims=True
    )
    return (inward, jnp.sum(upstream * values * scale_of, axis=0))


def adam_update(weight_vals, first_old, second_old, gradient, rate):
    first_new = FIRST_DECAY * first_old + (1.0 - FIRST_DECAY) * gradient
    second_new = SECOND_DECAY * second_old + (1.0 - SECOND_DECAY) * gradient * gradient
    first_hat = first_new / (1.0 - FIRST_DECAY**STEP)
    second_hat = second_new / (1.0 - SECOND_DECAY**STEP)
    step_vals = first_hat / (jnp.sqrt(second_hat) + ADAM_EPS) + WEIGHT_DECAY * weight_vals
    return (first_new, second_new, weight_vals - rate * step_vals)


def factor_onehot(columns):
    factor_id = (
        (columns >= 2048).astype(jnp.int32)
        + (columns >= 2048 + 256).astype(jnp.int32)
        + (columns >= 2048 + 512).astype(jnp.int32)
    )
    return (factor_id[None, :] == jnp.arange(4)[:, None]).astype(jnp.float32)


def shampoo_parts(down_factor_gradient, up_factor_gradient, onehot):
    left_three = down_factor_gradient.reshape(4, up_factor_gradient.shape[0], -1)
    stats_left = jnp.einsum("krd,ksd->krs", left_three, left_three, precision=HIGHEST)
    stats_right = jnp.einsum(
        "rc,sc,kc->krs", up_factor_gradient, up_factor_gradient, onehot, precision=HIGHEST
    )
    return jnp.concatenate([stats_left, stats_right], 0)


def inverse_root(stats):
    unit_mat = jnp.eye(stats.shape[-1], dtype=stats.dtype)[None]
    norm_of = jnp.sqrt(jnp.sum(stats * stats, axis=(1, 2), keepdims=True))
    matrix = stats / norm_of
    root_mat = unit_mat * lax.rsqrt(jnp.sqrt(norm_of))
    for iteration in range(10):
        factor = (5.0 * unit_mat - matrix) * 0.25
        root_mat = jnp.einsum("kab,kbc->kac", root_mat, factor, precision=HIGHEST)
        square = jnp.einsum("kab,kbc->kac", factor, factor, precision=HIGHEST)
        fourth = jnp.einsum("kab,kbc->kac", square, square, precision=HIGHEST)
        matrix = jnp.einsum("kab,kbc->kac", fourth, matrix, precision=HIGHEST)
    return root_mat


def shampoo_apply(
    stats_new, width_left, width_right, down_factor_gradient, up_factor_gradient, onehot
):
    roots = inverse_root(stats_new)
    left_three = down_factor_gradient.reshape(4, up_factor_gradient.shape[0], -1)
    down_factor_step = (
        jnp.einsum("krs,ksd->krd", roots[:4], left_three, precision=HIGHEST)
        * lax.rsqrt(jnp.sqrt(width_left))[:, None, :]
    )
    up_factor_step = (
        jnp.einsum("krs,sc,kc->rc", roots[4:], up_factor_gradient, onehot, precision=HIGHEST)
        * lax.rsqrt(jnp.sqrt(width_right))[None, :]
    )
    return (down_factor_step.reshape(down_factor_gradient.shape), up_factor_step)


def per_device(
    input_token_index,
    target_token_index,
    loss_position_index,
    document_slot_index,
    row_used_length,
    head_group_offsets,
    embedding,
    embedding_first_moment,
    embedding_second_moment,
    frozen_output_table,
    frozen_query_key_value_weight,
    frozen_attention_output_weight,
    frozen_gate_up_weight,
    frozen_down_weight,
    norm_gain_vectors,
    norm_gain_first_moment,
    norm_gain_second_moment,
    adapter_down_factors,
    adapter_up_factors,
    rank_side_statistics,
    down_width_statistics,
    up_width_statistics,
):
    fsdp_here = lax.axis_index(FSDP)
    seq_here = lax.axis_index(SEQ)
    vocab_dev = embedding.shape[0]

    qkvo_own = jnp.concatenate([frozen_query_key_value_weight, frozen_attention_output_weight], 1)
    gate_up_own = frozen_gate_up_weight.reshape(16, 2, 8, 2, 2, 2, 2, 44).transpose(
        0, 5, 3, 1, 2, 4, 6, 7
    )
    gate_up_own = jnp.pad(gate_up_own, [(0, 0)] * 7 + [(0, 4)]).reshape(16, 2 * PAD_FF)
    down_own = jnp.pad(frozen_down_weight, ((0, 4), (0, 0)))
    small_own = jnp.pad(
        jnp.concatenate(
            [
                adapter_down_factors.reshape(-1),
                norm_gain_vectors.reshape(-1),
                adapter_up_factors.reshape(-1),
            ]
        ),
        (0, 1024 - 848),
    ).reshape(8, 128)
    ids_own = jnp.pad(input_token_index.reshape(16, TOK), ((0, 0), (0, 64)))
    qkvo, small, table, ids, gate_up_w, down_w = gather_weights(
        qkvo_own,
        small_own,
        embedding.astype(jnp.bfloat16),
        ids_own,
        gate_up_own,
        down_own,
    )
    gate_up_w = gate_up_w.reshape(2048, PAD_FF // 2)
    down_w = down_w.reshape(PAD_FF // 4, 2048)
    qkvo = qkvo.reshape(2048, 4608)
    w_qkv, w_out = qkvo[:, :2560], qkvo[:, 2560:]
    head_own, ids = lax.optimization_barrier((frozen_output_table, ids))
    head = lax.all_gather(head_own, SEQ, axis=1, tiled=True)
    small = small.reshape(128, 1024)
    down_full = small[:, :512].reshape(128, 32, 16).transpose(1, 0, 2).reshape(32, 2048)
    gain = small[:, 512:560].reshape(128, 3, 16).transpose(1, 0, 2).reshape(3, 2048)
    up_full = small[:, 560:848].reshape(128, 8, 36).transpose(1, 0, 2).reshape(8, 4608)
    a_low = down_full.astype(jnp.bfloat16)
    b_low = up_full.astype(jnp.bfloat16)
    a_in, a_out = a_low[:24], a_low[24:]
    factor_of = (jnp.arange(2560) >= 2048).astype(jnp.int32) + (jnp.arange(2560) >= 2304)
    b_in = jnp.where(
        (jnp.arange(24) // 8)[:, None] == factor_of[None, :],
        jnp.concatenate([b_low[:, :2560]] * 3, 0),
        jnp.zeros((), jnp.bfloat16),
    )
    b_out = b_low[:, 2560:]

    places = loss_position_index.reshape(2, 8, SEQ_N, 32)
    spots = jnp.arange(SEQ_N)[:, None] * TOK + places
    counted = spots < row_used_length[..., None, None]
    below = jnp.sum(
        (document_slot_index[..., None] < jnp.arange(1, 3)).astype(jnp.int32), axis=2
    )
    seg_at = jnp.sum(
        (spots[..., None] >= below[:, :, None, None, :]).astype(jnp.int32), axis=-1
    )
    member = counted[..., None] & (seg_at[..., None] == jnp.arange(3))
    counts = jnp.sum(member.astype(jnp.int32), axis=(2, 3))
    document_total = jnp.sum((counts > 0).astype(jnp.float32))
    own_places = lax.dynamic_index_in_dim(places, seq_here, 2, keepdims=False)
    own_counted = lax.dynamic_index_in_dim(counted, seq_here, 2, keepdims=False)
    own_seg = lax.dynamic_index_in_dim(seg_at, seq_here, 2, keepdims=False)
    per_doc = jnp.sum(
        jnp.where(own_seg[..., None] == jnp.arange(3), counts[:, :, None, :], 0), axis=-1
    )
    own_weight = jnp.where(own_counted, 1.0 / jnp.maximum(per_doc, 1).astype(jnp.float32), 0.0)
    weight_flat = own_weight.transpose(1, 0, 2).reshape(-1)
    row_places = lax.dynamic_index_in_dim(own_places, fsdp_here, 1, keepdims=False)
    chosen_at = (row_places + jnp.arange(2)[:, None] * TOK).reshape(64)
    pick = (chosen_at[:, None] == jnp.arange(128)[None, :]).astype(jnp.float32)

    ids = ids[:, :, :TOK].reshape(SEQ_N, 2, 8, TOK)
    row_ids = lax.dynamic_index_in_dim(ids, fsdp_here, 2, keepdims=False).reshape(SEQ_N, 128)
    x_start = rows_of_tokens(table.reshape(8 * vocab_dev, 128), row_ids, 2).astype(jnp.float32)

    half = 32
    freqs = ROPE_BASE ** (-2.0 * jnp.arange(half).astype(jnp.float32) / 64)
    angles = (seq_here * TOK + jnp.arange(TOK)).astype(jnp.float32)[:, None] * freqs[None, :]
    cosine = jnp.tile(jnp.cos(angles), (1, 16))
    sine = jnp.sin(angles)
    sine = jnp.tile(jnp.concatenate([-sine, sine], 1), (1, 8))
    own_docs = lax.dynamic_index_in_dim(document_slot_index, fsdp_here, 1, keepdims=False)
    padded = jnp.concatenate([jnp.full((2, 4 * TOK), -1, jnp.int32), own_docs], 1)
    key_seg = lax.dynamic_slice_in_dim(padded, seq_here * TOK, 5 * TOK, 1)[:, None, :]
    query_seg = key_seg[:, 0, 4 * TOK :][:, :, None]
    start = (seq_here * TOK).reshape(1)
    normed_one = (x_start * norm_scale(x_start) * gain[0]).astype(jnp.bfloat16)
    adapter_in = nt(normed_one, a_in).astype(jnp.bfloat16)
    packed = dot(normed_one, w_qkv) + ADAPTER_SCALE * dot(adapter_in, b_in)
    window = key_value_window(packed[:, 2048:], cosine, sine, 3)
    queries, attended = attend(
        packed, window, cosine, sine, query_seg, key_seg, start, head_group_offsets
    )
    adapter_mid = nt(attended, a_out).astype(jnp.bfloat16)
    x_mid = x_start + dot(attended, w_out) + ADAPTER_SCALE * dot(adapter_mid, b_out)

    normed_two = (x_mid * norm_scale(x_mid) * gain[1]).astype(jnp.bfloat16)
    hidden_sum, gate_up = feed_forward(normed_two, gate_up_w, down_w, None, 12, "feed_forward")
    x_end = x_mid + hidden_sum
    normed_end = (x_end * norm_scale(x_end) * gain[2]).astype(jnp.bfloat16)

    chosen = dot(pick.astype(jnp.bfloat16), normed_end).astype(jnp.bfloat16)
    local_target = target_token_index.transpose(1, 0, 2).reshape(512, 1) - fsdp_here * vocab_dev
    local_target = jnp.where(local_target < vocab_dev, local_target, -1)
    weight_column = weight_flat.reshape(512, 1)
    d_chosen, loss_tile = head_step(
        chosen, head, local_target, weight_column, weight_column / document_total, 4
    )
    loss_part = loss_tile[0, 0]

    upstream = lax.dot_general(pick, d_chosen, (((0,), (0,)), ((), ())), precision=HIGHEST)
    d_end, gain_end = norm_back(x_end, gain[2], upstream)
    d_normed = feed_forward(
        d_end.astype(jnp.bfloat16), gate_up_w, down_w, gate_up, 13, "feed_forward_back"
    )
    back_two, gain_mid = norm_back(x_mid, gain[1], d_normed)
    d_mid = d_end + back_two

    d_branch = d_mid.astype(jnp.bfloat16)
    d_adapter_mid = (ADAPTER_SCALE * nt(d_branch, b_out)).astype(jnp.bfloat16)
    d_attended = (nt(d_branch, w_out) + dot(d_adapter_mid, a_out)).astype(jnp.bfloat16)
    up_gradient_out = ADAPTER_SCALE * tn(adapter_mid, d_branch)
    down_gradient_out = tn(d_adapter_mid, attended)
    d_queries, d_far, d_own = attend_back(
        queries, window, d_attended, cosine, sine, query_seg, key_seg, start, head_group_offsets
    )
    d_key_value = key_value_back(d_far, d_own, cosine, sine, 7)
    d_packed = jnp.concatenate([d_queries, d_key_value], 1)
    d_adapter_in = (ADAPTER_SCALE * nt(d_packed, b_in)).astype(jnp.bfloat16)
    up_gradient_in = ADAPTER_SCALE * jnp.concatenate(
        [
            tn(adapter_in[:, 0:8], d_packed[:, :2048]),
            tn(adapter_in[:, 8:16], d_packed[:, 2048:2304]),
            tn(adapter_in[:, 16:24], d_packed[:, 2304:]),
        ],
        1,
    )
    down_gradient_in = tn(d_adapter_in, normed_one)
    back_one, gain_start = norm_back(
        x_start, gain[0], nt(d_packed, w_qkv) + dot(d_adapter_in, a_in)
    )
    d_start = (d_mid + back_one).astype(jnp.bfloat16)

    left = jnp.concatenate(
        [
            down_gradient_in,
            down_gradient_out,
            jnp.stack([gain_start, gain_mid, gain_end]),
            jnp.zeros((5, 2048), jnp.float32),
        ],
        0,
    )
    left = left.reshape(40, 16, 128).transpose(1, 0, 2)
    right = jnp.concatenate([up_gradient_in, up_gradient_out], 1).reshape(8, 16, 288)
    right = jnp.pad(right, ((0, 0), (0, 0), (0, 96))).transpose(1, 0, 2).reshape(16, 24, 128)
    all_ids = ids.transpose(2, 0, 1, 3).reshape(16, 1024) - fsdp_here * vocab_dev
    grad_embed, small_sum = token_gradients(
        d_start, jnp.concatenate([left, right], 1), all_ids, vocab_dev, 8
    )
    left_sum = small_sum[:40]
    right_sum = small_sum[40:].reshape(8, 384)[:, :288]
    group_onehot = factor_onehot(seq_here * 288 + jnp.arange(288))
    stats_part = shampoo_parts(left_sum[:32], right_sum, group_onehot)
    first = (fsdp_here == 0).astype(jnp.float32)
    squares = jnp.sum(grad_embed * grad_embed) + first * (
        jnp.sum(left_sum[:35] * left_sum[:35]) + jnp.sum(right_sum * right_sum)
    )
    totals = jnp.concatenate(
        [
            (first * stats_part).reshape(-1),
            squares.reshape(1),
            loss_part.reshape(1),
            jnp.zeros((510,), jnp.float32),
        ]
    ).reshape(8, 128)
    totals = sum_over("seq", totals, 10, "totals_seq", False)
    totals = sum_over("fsdp", totals, 11, "totals_fsdp", False)
    stats_all = totals[:4].reshape(8, 8, 8)
    document_loss_sum = totals[4, 1]
    global_gradient_norm = jnp.sqrt(totals[4, 0])
    clip_factor = CLIP_MAX / jnp.maximum(global_gradient_norm, CLIP_MAX)

    own_left = lax.dynamic_slice_in_dim(left_sum, fsdp_here * 16, 16, 1)
    down_factor_gradient = own_left[:32] * clip_factor
    grad_gain = own_left[32:35] * clip_factor
    up_factor_gradient = (
        lax.dynamic_slice_in_dim(right_sum, fsdp_here * 36, 36, 1) * clip_factor
    )
    grad_embed = grad_embed * clip_factor
    unused_first, updated_embedding_second_moment, updated_embedding_table = adam_update(
        embedding, embedding_first_moment, embedding_second_moment, grad_embed, RATE_EMBED
    )
    updated_gain_first_moment, updated_gain_second_moment, updated_norm_gains = adam_update(
        norm_gain_vectors, norm_gain_first_moment, norm_gain_second_moment, grad_gain, RATE_GAIN
    )
    updated_rank_statistics = (
        SECOND_DECAY * rank_side_statistics
        + (1.0 - SECOND_DECAY) * (clip_factor * clip_factor) * stats_all
    )
    updated_down_width_statistics = SECOND_DECAY * down_width_statistics + (
        1.0 - SECOND_DECAY
    ) * jnp.sum(down_factor_gradient.reshape(4, 8, -1) ** 2, axis=1)
    updated_up_width_statistics = SECOND_DECAY * up_width_statistics + (
        1.0 - SECOND_DECAY
    ) * jnp.sum(up_factor_gradient * up_factor_gradient, axis=0)
    onehot = factor_onehot((seq_here * 8 + fsdp_here) * 36 + jnp.arange(36))
    down_factor_step, up_factor_step = shampoo_apply(
        updated_rank_statistics,
        updated_down_width_statistics,
        updated_up_width_statistics,
        down_factor_gradient,
        up_factor_gradient,
        onehot,
    )
    updated_down_factors = adapter_down_factors - LEARN_RATE_DOWN * down_factor_step
    updated_up_factors = adapter_up_factors - LEARN_RATE_UP * up_factor_step
    return (
        document_loss_sum,
        document_total,
        global_gradient_norm,
        grad_embed,
        updated_embedding_second_moment,
        updated_embedding_table,
        updated_gain_first_moment,
        updated_gain_second_moment,
        updated_norm_gains,
        down_factor_gradient,
        up_factor_gradient,
        updated_rank_statistics,
        updated_down_width_statistics,
        updated_up_width_statistics,
        updated_down_factors,
        updated_up_factors,
    )


def solution(mesh):
    torus = Mesh(
        mesh.devices.reshape(2, 4, 2, 2, 2, 2), SEQ_FSDP
    )
    return jax.shard_map(
        per_device,
        mesh=torus,
        in_specs=(
            P(None, None, SEQ),
            P(None, None, SEQ),
            P(),
            P(),
            P(),
            P(),
            P(FSDP, SEQ),
            P(FSDP, SEQ),
            P(FSDP, SEQ),
            P(FSDP, SEQ),
            P(SEQ_FSDP, None),
            P(SEQ_FSDP, None),
            P(SEQ_FSDP, None),
            P(SEQ_FSDP, None),
            P(None, SEQ_FSDP),
            P(None, SEQ_FSDP),
            P(None, SEQ_FSDP),
            P(None, SEQ_FSDP),
            P(None, SEQ_FSDP),
            P(),
            P(None, SEQ_FSDP),
            P(SEQ_FSDP),
        ),
        out_specs=(
            P(),
            P(),
            P(),
            P(FSDP, SEQ),
            P(FSDP, SEQ),
            P(FSDP, SEQ),
            P(None, SEQ_FSDP),
            P(None, SEQ_FSDP),
            P(None, SEQ_FSDP),
            P(None, SEQ_FSDP),
            P(None, SEQ_FSDP),
            P(),
            P(None, SEQ_FSDP),
            P(SEQ_FSDP),
            P(None, SEQ_FSDP),
            P(None, SEQ_FSDP),
        ),
        check_vma=False,
    )
```

```python
import functools

import jax
import jax.numpy as jnp
from jax import lax
from jax.experimental import pallas as pl
from jax.experimental.pallas import tpu as pltpu
from jax.sharding import Mesh
from jax.sharding import PartitionSpec as P

STEP = 5
GROUP = 256
SEQ = ("seq_0", "seq_1", "seq_2")
FSDP = ("fsdp_0", "fsdp_1", "fsdp_2")
SEQ_FSDP = SEQ + FSDP
SEQ_N = 16
FSDP_N = 8
TOK = 64
PAD_FF = 6144
NORM_EPS = 1e-05
ADAPTER_SCALE = 2.0
ROPE_BASE = 10000.0
CLIP_MAX = 0.001
FIRST_DECAY = 0.5
SECOND_DECAY = 0.5
RATE_EMBED = 0.3
RATE_GAIN = 0.1
LEARN_RATE_DOWN = 0.1
LEARN_RATE_UP = 0.5
WEIGHT_DECAY = 0.01
ADAM_EPS = 1e-12
HIGHEST = lax.Precision.HIGHEST
MESH_ID = pl.DeviceIdType.MESH
ANY = pl.BlockSpec(memory_space=pl.ANY)
VMEM = pl.BlockSpec(memory_space=pltpu.VMEM)
SMEM = pl.BlockSpec(memory_space=pltpu.SMEM)
DMA = pltpu.SemaphoreType.DMA
VMEM_LIMIT = 56 * 1024 * 1024


def seq_me():
    return lax.axis_index("seq_0") * 8 + lax.axis_index("seq_1") * 2 + lax.axis_index("seq_2")


def z_me():
    return lax.axis_index("fsdp_0") * 2 + lax.axis_index("fsdp_1")


def z_at(i):
    return {"fsdp_0": i // 2, "fsdp_1": i % 2}


def fsdp_me():
    return z_me() * 2 + lax.axis_index("fsdp_2")


def seq_at(i):
    return {"seq_0": i // 8, "seq_1": (i // 2) % 4, "seq_2": i % 2}


def fsdp_at(i):
    return {**z_at(i // 2), "fsdp_2": i % 2}


def remote_call(body, out_shape, in_specs, out_specs, scratch, collective_id, name):
    return pl.pallas_call(
        body,
        out_shape=out_shape,
        in_specs=in_specs,
        out_specs=out_specs,
        scratch_shapes=scratch,
        compiler_params=pltpu.CompilerParams(
            collective_id=collective_id, has_side_effects=True, vmem_limit_bytes=VMEM_LIMIT
        ),
        name=name,
    )


ALL16 = range(1, SEQ_N)
ALL8 = range(1, FSDP_N)


ORDER = (
    "q2", "s", "q0", "d0", "t0", "q1", "q0", "q2", "d1", "d0", "s", "q2",
    "q1", "g0", "q1", "q0", "q2", "d1", "g1", "q0", "s", "q2", "q2", "g0",
    "t0", "t1", "g1", "q2", "t1", "q1", "g1", "d0", "q2", "g0", "s", "g1",
    "q0", "d0", "g0", "s", "d1", "d1", "s", "q1", "q2", "q1", "q1", "s",
    "q0", "t0", "d1", "g1", "d0", "q0", "g0", "t0", "q1", "g0", "q1", "d1",
    "d1", "t0", "g1", "g0", "q2", "q0", "g1", "d0", "q0", "s", "s", "d1",
    "t1", "d0", "q1", "t1", "q0", "g0", "s", "d0", "t1", "g1",
)
EVERY = slice(None)


class Post:
    def __init__(self, sem, count):
        self.sem, self.count, self.used, self.sent, self.late = sem, count, 0, [], []

    def fresh(self):
        self.used += 1
        assert self.used <= self.count, self.used
        return self.sem.at[self.used - 1]

    def start(self, src, dst, ssem, rsem, device):
        copy = pltpu.make_async_remote_copy(
            src_ref=src, dst_ref=dst, send_sem=ssem, recv_sem=rsem,
            device_id=device, device_id_type=MESH_ID,
        )
        copy.start()
        return copy

    def send(self, src, dst, device):
        copy = self.start(src, dst, self.fresh(), self.fresh(), device)
        self.sent.append(copy)
        return copy

    def finish(self):
        for copy in self.sent:
            copy.wait_send()
        for mark, view in self.late:
            pltpu.make_async_copy(view, view, mark).wait()


def greet_devices(devices):
    barrier = pltpu.get_barrier_semaphore()
    for device in devices:
        pl.semaphore_signal(barrier, inc=1, device_id=device, device_id_type=MESH_ID)
    pl.semaphore_wait(barrier, len(devices))


def fsdp_peers():
    me = fsdp_me()
    return [fsdp_at((me + k) % FSDP_N) for k in ALL8]


def seq_peers():
    me = seq_me()
    return [seq_at((me + k) % SEQ_N) for k in ALL16]


def relay(post, out, first, second, first_a, first_b):
    z, yl = z_me(), lax.axis_index("fsdp_2")
    partner, up, down = {"fsdp_2": 1 - yl}, z_at((z + 1) % 4), z_at((z + 3) % 4)
    before, after, far = (z + 3) % 4, (z + 1) % 4, (z + 2) % 4

    def at(zz, y, part=()):
        return out.at[(zz * 2 + y,) + part]

    def send(zz, y, part, device):
        view = at(zz, y, part)
        return post.send(view, view, device)

    to_partner = send(z, yl, (), partner)
    ring_up = send(z, yl, (), up)
    ring_down = send(z, yl, (), down)
    yield
    to_partner.wait_recv()
    other_up = send(z, 1 - yl, first, up)
    other_down = send(z, 1 - yl, first, down)
    yield
    ring_up.wait_recv()
    far_up = send(before, yl, first, up)
    across = [send(before, yl, second, partner)]
    yield
    ring_down.wait_recv()
    far_down = send(after, yl, second, down)
    across.append(send(after, yl, second, partner))
    yield
    other_up.wait_recv()
    last_up = send(before, 1 - yl, first_a, up)
    yield
    other_down.wait_recv()
    last_down = send(after, 1 - yl, first_b, down)
    yield
    far_up.wait_recv()
    far_down.wait_recv()
    across.append(send(far, yl, second, partner))
    yield
    last_up.wait_recv()
    last_down.wait_recv()
    for copy in across:
        copy.wait_recv()


def no_hand(view):
    return None


class Ways:
    def __init__(self, post):
        self.post = post
        self.yh, self.x, self.c = (lax.axis_index(a) for a in SEQ)
        self.z, self.yl = z_me(), lax.axis_index("fsdp_2")
        self.where = {"x": self.x, "y": 2 * self.yh + self.yl, "z": self.z}
        z, c = self.z, self.c
        self.column = [
            ((z + dz) % 4, (c + dc) % 2, dz, dc) for dz in range(4) for dc in range(2) if dz or dc
        ]

    def beside(self, axis, step):
        at = (self.where[axis] + step + 4) % 4
        if axis == "x":
            return {"seq_1": at}
        if axis == "z":
            return z_at(at)
        return {"seq_0": at // 2, "fsdp_2": at % 2}

    def all_devices(self):
        return (
            [self.beside("y", 1), self.beside("y", -1)]
            + [{**z_at(zz), "seq_2": cc} for zz, cc, dz, dc in self.column if dz]
            + seq_peers()
        )

    def arrived(self, ref, rsem):
        pltpu.make_async_copy(ref, ref, rsem).wait()

    def rings(self, block, order, sizes, halves, across):
        post = self.post
        for n, axis in enumerate(order):
            done = order[:n]
            at = self.where[axis]
            before, after, far = (at + 3) % 4, (at + 1) % 4, (at + 2) % 4
            send, from_before, from_after, far_first = (post.fresh() for _ in range(4))
            post.late.append((send, sizes[axis, n]))
            own = block(done, axis, at, None)
            post.start(own, own, send, from_before, self.beside(axis, 1))
            post.start(own, own, send, from_after, self.beside(axis, -1))
            yield
            got = block(done, axis, before, None)
            self.arrived(got, from_before)
            half = block(done, axis, before, 0)
            post.start(half, half, send, far_first, self.beside(axis, 1))
            across(got)
            yield
            got = block(done, axis, after, None)
            self.arrived(got, from_after)
            if halves:
                far_second = post.fresh()
                half = block(done, axis, after, 1)
                post.start(half, half, send, far_second, self.beside(axis, -1))
            across(got)
            yield
            self.arrived(block(done, axis, far, 0), far_first)
            if halves:
                self.arrived(block(done, axis, far, 1), far_second)
            across(block(done, axis, far, None))

    def place(self, done, axis, at):
        spot = {"yh": self.yh, "x": self.x, "z": self.z, "yl": self.yl}
        for a in done:
            if a == "y":
                spot["yh"] = spot["yl"] = EVERY
            else:
                spot[a] = EVERY
        if axis == "y":
            spot["yh"], spot["yl"] = at // 2, at % 2
        elif axis is not None:
            spot[axis] = at
        return spot

    def everything(self, ref, order, tails, halves=True):
        post, c = self.post, self.c

        def block(done, axis, at, half):
            spot = self.place(done, axis, at)
            tail = tails[0 if half is None else half + 1]
            return ref.at[(spot["yh"], spot["x"], c, spot["z"], spot["yl"]) + tail]

        across_s, across_r = post.fresh(), post.fresh()
        post.late.append((across_s, ref.at[(EVERY, EVERY, c, EVERY, EVERY) + tails[0]]))
        post.late.append((across_r, ref.at[(EVERY, EVERY, 1 - c, EVERY, EVERY) + tails[0]]))

        def across(view):
            post.start(view, view, across_s, across_r, {"seq_2": 1 - c})

        three = pl.ds(0, 3)
        sizes = {}
        for axis in "xyz":
            sizes[axis, 0] = ref.at[(0, 0, 0, three, 0) + tails[0]]
            sizes[axis, 1] = ref.at[(0, pl.ds(0, 2), 0, three, EVERY) + tails[0]]
            sizes[axis, 2] = ref.at[(EVERY, EVERY, 0, three, EVERY) + tails[0]]
        across(block([], None, None, None))
        yield from self.rings(block, order, sizes, halves, across)

    def gate_up(self, src, ref, order, start, width):
        post = self.post
        quarter = src.shape[1] // 4
        yh, x, c, z, yl = self.yh, self.x, self.c, self.z, self.yl
        tails = [
            (EVERY, pl.ds(start, width)),
            (EVERY, pl.ds(start, width // 2)),
            (EVERY, pl.ds(start + width // 2, width // 2)),
        ]

        def block(done, axis, at, half):
            spot = self.place(done, axis, at)
            tail = tails[0 if half is None else half + 1]
            return ref.at[(spot["yh"], spot["x"], EVERY, EVERY, spot["yl"]) + tail]

        marks = []
        for zz, cc, dz, dc in self.column:
            send, recv = post.fresh(), post.fresh()
            first = pl.multiple_of((2 * (zz % 2) + cc) * quarter + start, 128)
            here = ref.at[(yh, x, c, z, yl) + tails[0]]
            post.start(src.at[:, pl.ds(first, width)], here, send, recv, {**z_at(zz), "seq_2": cc})
            post.late.append((send, here))
            marks.append((ref.at[(yh, x, (c + dc) % 2, (z + 4 - dz) % 4, yl) + tails[0]], recv))
        yield
        for view, recv in marks:
            self.arrived(view, recv)
        three = pl.ds(0, 3)
        sizes = {}
        for axis in "xy":
            sizes[axis, 0] = ref.at[(0, three, EVERY, EVERY, 0) + tails[0]]
            sizes[axis, 1] = ref.at[(EVERY, three, EVERY, EVERY, EVERY) + tails[0]]
        yield from self.rings(block, order, sizes, True, no_hand)

    def down(self, ref, order, start, width):
        post = self.post
        yh, x, z, yl = self.yh, self.x, self.z, self.yl
        tails = [
            (EVERY, pl.ds(start, width)),
            (EVERY, pl.ds(start, width // 2)),
            (EVERY, pl.ds(start + width // 2, width // 2)),
        ]
        zh = z // 2

        def block(done, axis, at, half):
            spot = self.place(done, axis, at)
            tail = tails[0 if half is None else half + 1]
            return ref.at[(spot["yh"], spot["x"], EVERY, spot["yl"]) + tail]

        send, recv = post.fresh(), post.fresh()
        here = ref.at[(yh, x, zh, yl) + tails[0]]
        post.start(here, here, send, recv, z_at((z + 2) % 4))
        post.late.append((send, here))
        yield
        self.arrived(ref.at[(yh, x, 1 - zh, yl) + tails[0]], recv)
        three = pl.ds(0, 3)
        sizes = {}
        for axis in "xy":
            sizes[axis, 0] = ref.at[(0, three, EVERY, 0) + tails[0]]
            sizes[axis, 1] = ref.at[(EVERY, three, EVERY, EVERY) + tails[0]]
        yield from self.rings(block, order, sizes, True, no_hand)

    def table(self, ref, low, high):
        post, z, yl = self.post, self.z, self.yl
        middle = (low + high) // 32 * 16
        part = (pl.ds(low, high - low), pl.ds(low, middle - low), pl.ds(middle, high - middle))
        send_y, recv_y = post.fresh(), post.fresh()
        post.late.append((send_y, ref.at[0, part[0]]))
        own = ref.at[2 * z + yl, part[0]]
        post.start(own, own, send_y, recv_y, {"fsdp_2": 1 - yl})
        yield
        self.arrived(ref.at[2 * z + 1 - yl, part[0]], recv_y)

        def block(done, axis, at, half):
            return ref.at[pl.ds(2 * at, 2), part[0 if half is None else half + 1]]

        sizes = {("z", 0): ref.at[pl.ds(0, 6), part[0]]}
        yield from self.rings(block, ("z",), sizes, True, no_hand)

    def own_gate_up(self, src, ref):
        quarter = ref.shape[-1]
        first = pl.multiple_of((2 * (self.z % 2) + self.c) * quarter, 128)
        return src.at[:, pl.ds(first, quarter)], ref.at[self.yh, self.x, self.c, self.z, self.yl]


def local_copies(pairs, post):
    copies = [pltpu.make_async_copy(src, dst, post.fresh()) for src, dst in pairs]
    for copy in copies:
        copy.start()
    return copies


def gather_weights(qkvo, small, table, ids, gate_up, down):
    quarter = gate_up.shape[1] // 4
    out_shape = [
        jax.ShapeDtypeStruct((2, 4, 2, 4, 2, *qkvo.shape), qkvo.dtype),
        jax.ShapeDtypeStruct((2, 4, 2, 4, 2, *small.shape), small.dtype),
        jax.ShapeDtypeStruct((FSDP_N, *table.shape), table.dtype),
        jax.ShapeDtypeStruct((SEQ_N, *ids.shape), ids.dtype),
        jax.ShapeDtypeStruct((2, 4, 2, 4, 2, gate_up.shape[0], quarter), gate_up.dtype),
        jax.ShapeDtypeStruct((2, 4, 2, 2, *down.shape), down.dtype),
    ]
    sem_count = 320

    def body(*refs):
        ins, outs, sem = refs[:6], refs[6:12], refs[12]
        post = Post(sem, sem_count)
        ways = Ways(post)
        yh, x, c, z, yl = ways.yh, ways.x, ways.c, ways.z, ways.yl
        seq = seq_me()
        local = local_copies(
            [
                (ins[0], outs[0].at[yh, x, c, z, yl]),
                (ins[1], outs[1].at[yh, x, c, z, yl]),
                (ins[2], outs[2].at[z * 2 + yl]),
                (ins[3], outs[3].at[seq]),
                ways.own_gate_up(ins[4], outs[4]),
                (ins[5], outs[5].at[yh, x, z // 2, yl]),
            ],
            post,
        )
        greet_devices(ways.all_devices())
        for copy in local:
            copy.wait()

        send, recv = post.fresh(), post.fresh()
        for device in seq_peers():
            post.start(ins[3], outs[3].at[seq], send, recv, device)
        post.late.append((send, outs[3].at[pl.ds(0, 15)]))
        post.late.append((recv, outs[3].at[pl.ds(0, 15)]))

        third = qkvo.shape[1] // 3
        streams = {
            "s": ways.everything(outs[1], "xyz", [(EVERY, EVERY)] * 2, False),
        }
        rows = table.shape[0]
        cuts = (0, 1984, rows)
        for n in range(len(cuts) - 1):
            streams["t%d" % n] = ways.table(outs[2], cuts[n], cuts[n + 1])
        half, wide = quarter // 2, down.shape[1] // 2
        for n, order in enumerate(("xy", "yx")):
            streams["g%d" % n] = ways.gate_up(ins[4], outs[4], order, n * half, half)
            streams["d%d" % n] = ways.down(outs[5], order, n * wide, wide)
        for n, order in enumerate(('yxz', 'xyz', 'zyx')):
            streams["q%d" % n] = ways.everything(
                outs[0], order,
                [
                    (EVERY, pl.ds(n * third, third)),
                    (EVERY, pl.ds(n * third, third // 2)),
                    (EVERY, pl.ds(n * third + third // 2, third // 2)),
                ],
            )
        for name in ORDER:
            next(streams[name], None)
        for name in sorted(streams):
            assert next(streams[name], "end") == "end", name
        post.finish()

    return remote_call(
        body, out_shape, [ANY] * 6, [ANY] * 6, [DMA((sem_count,))], 1, "gather_weights"
    )(qkvo, small, table, ids, gate_up, down)


def attention_block(
    table, ids, qkvo, a_low, b_in, b_out, gain, cosine, sine, query_seg, key_seg, shifts, collective_id
):
    vocab, width = table.shape[1:]
    rows_n = 2 * TOK
    sem_count = 64

    def body(
        table_hbm, ids_ref, qkvo_hbm, a_ref, bi_ref, bo_ref, gain_ref, cos_ref, sin_ref, qs_ref, ks_ref,
        shift_ref,
        x_out, n_out, u_out, q_out, kv_out, a_out, v_out, mid_out, two_out,
        stage, wide, rows, block, low, packed, own_kv, w_qkv, w_out, sem,
    ):
        post = Post(sem, sem_count)
        me = seq_me()
        loads = [post.fresh() for _ in range(2)]

        def staged(n):
            return pltpu.make_async_copy(table_hbm.at[n], stage.at[n % 2], loads[n % 2])

        staged(0).start()
        weights = local_copies(
            [
                (qkvo_hbm.at[:, pl.ds(0, 2560)], w_qkv),
                (qkvo_hbm.at[:, pl.ds(2560, 2048)], w_out),
            ],
            post,
        )
        greet_devices(seq_peers())
        for n in range(FSDP_N):
            if n + 1 < FSDP_N:
                staged(n + 1).start()
            staged(n).wait()
            wide[pl.ds(n * vocab, vocab), :] = stage[n % 2].astype(jnp.float32)

        spot = pl.ds(pl.multiple_of(me * width, width), width)

        def fetch(s):
            def step(t, carry):
                rows[pl.ds(t, 1), :] = wide[pl.ds(ids_ref[s, t], 1), :]
                return carry

            lax.fori_loop(0, rows_n, step, 0, unroll=16)

        moved = []
        for k in list(ALL16) + [0]:
            peer = (me + k) % SEQ_N
            fetch(peer)
            block[k] = rows[...].astype(jnp.bfloat16)
            if k:
                moved.append(post.send(block.at[k], low.at[:, spot], seq_at(peer)))
        own = pltpu.make_async_copy(block.at[0], low.at[:, spot], post.fresh())
        own.start()
        for copy in moved:
            copy.wait_recv()
        own.wait()

        start = low[...].astype(jnp.float32)
        x_out[...] = start
        scale = lax.rsqrt(jnp.mean(start * start, axis=-1, keepdims=True) + NORM_EPS)
        n_out[...] = (start * scale * gain_ref[0:1, :]).astype(jnp.bfloat16)
        inner = nt(n_out[...], a_ref[0:24, :]).astype(jnp.bfloat16)
        u_out[...] = inner
        weights[0].wait()

        def project(at):
            packed[:, at] = jnp.dot(
                n_out[...], w_qkv[:, at], preferred_element_type=jnp.float32
            ) + ADAPTER_SCALE * jnp.dot(u_out[...], bi_ref[:, at], preferred_element_type=jnp.float32)

        project(pl.ds(2048, 512))
        for n in range(2):
            some = slice(n * TOK, n * TOK + TOK)
            own_kv[n, :, 0:256] = turn(
                packed[some, 2048:2304], cos_ref[:, 0:256], sin_ref[:, 0:256]
            ).astype(jnp.bfloat16)
            own_kv[n, :, 256:512] = packed[some, 2304:2560].astype(jnp.bfloat16)
        keys = [
            post.send(
                own_kv, kv_out.at[:, pl.ds((4 - k) * TOK, TOK), :], seq_at((me + k) % SEQ_N)
            )
            for k in range(1, 5)
        ]
        kv_out[:, 4 * TOK :, :] = own_kv[...]

        def project_some(n, carry):
            project(pl.ds(pl.multiple_of(n * 512, 512), 512))
            return carry

        lax.fori_loop(0, 4, project_some, 0)
        for copy in keys:
            copy.wait_recv()

        first = me * TOK

        def attend_one(n, carry):
            some = pl.ds(pl.multiple_of(n * TOK, TOK), TOK)
            for h in range(4):
                cols = slice(512 * h, 512 * h + 512)
                turned = turn(packed[some, cols], cos_ref[...], sin_ref[...]).astype(jnp.bfloat16)
                q_out[some, cols] = turned
                mask = window_mask(first, qs_ref[n], ks_ref[n], shift_ref[h])
                probs = probabilities(
                    spread_heads(turned), kv_out[n, :, 64 * h : 64 * h + 64], mask
                )
                values = kv_out[n, :, 256 + 64 * h : 256 + 64 * h + 64]
                mixed = jnp.dot(
                    probs.astype(jnp.bfloat16), values, preferred_element_type=jnp.float32
                )
                a_out[some, cols] = join_heads(mixed).astype(jnp.bfloat16)
            return carry

        lax.fori_loop(0, 2, attend_one, 0)
        middle = nt(a_out[...], a_ref[24:32, :]).astype(jnp.bfloat16)
        v_out[...] = middle
        weights[1].wait()

        def project_out(n, carry):
            at = pl.ds(pl.multiple_of(n * 512, 512), 512)
            mid_out[:, at] = (
                x_out[:, at]
                + jnp.dot(a_out[...], w_out[:, at], preferred_element_type=jnp.float32)
                + ADAPTER_SCALE
                * jnp.dot(v_out[...], bo_ref[:, at], preferred_element_type=jnp.float32)
            )
            return carry

        lax.fori_loop(0, 4, project_out, 0)
        middle_rows = mid_out[...]
        scale = lax.rsqrt(jnp.mean(middle_rows * middle_rows, axis=-1, keepdims=True) + NORM_EPS)
        two_out[...] = (middle_rows * scale * gain_ref[1:2, :]).astype(jnp.bfloat16)
        post.finish()

    def shape(*dims, dtype=jnp.bfloat16):
        return jax.ShapeDtypeStruct(dims, dtype)

    return remote_call(
        body,
        [
            shape(rows_n, 2048, dtype=jnp.float32),
            shape(rows_n, 2048),
            shape(rows_n, 24),
            shape(rows_n, 2048),
            shape(2, 5 * TOK, 512),
            shape(rows_n, 2048),
            shape(rows_n, 8),
            shape(rows_n, 2048, dtype=jnp.float32),
            shape(rows_n, 2048),
        ],
        [ANY, SMEM, ANY] + [VMEM] * 8 + [SMEM],
        [VMEM] * 9,
        [
            pltpu.VMEM((2, vocab, width), jnp.bfloat16),
            pltpu.VMEM((FSDP_N * vocab, width), jnp.float32),
            pltpu.VMEM((rows_n, width), jnp.float32),
            pltpu.VMEM((SEQ_N, rows_n, width), jnp.bfloat16),
            pltpu.VMEM((rows_n, 2048), jnp.bfloat16),
            pltpu.VMEM((rows_n, 2560), jnp.float32),
            pltpu.VMEM((2, TOK, 512), jnp.bfloat16),
            pltpu.VMEM((2048, 2560), jnp.bfloat16),
            pltpu.VMEM((2048, 2048), jnp.bfloat16),
            DMA((sem_count,)),
        ],
        collective_id,
        "attention_block",
    )(table, ids, qkvo, a_low, b_in, b_out, gain, cosine, sine, query_seg, key_seg, shifts)


def head_step(chosen, head, target, weight, scaled, collective_id):
    vocab, width = head.shape
    padded = -(-vocab // 512) * 512
    tiles = padded // 512

    def body(
        chosen_ref, head_hbm, target_ref, weight_ref, scaled_ref, out, loss, hd, held, raised, d_logits,
        prod, got, stat, stats, sem, lsem,
    ):
        post = Post(sem, 60)
        me = fsdp_me()
        load = pltpu.make_async_copy(head_hbm, hd.at[pl.ds(0, vocab)], lsem)
        load.start()
        held[me] = chosen_ref[...]
        greet_devices(fsdp_peers())
        for _ in relay(
            post, held, (pl.ds(0, 32),), (pl.ds(32, 32),), (pl.ds(0, 16),), (pl.ds(16, 16),)
        ):
            pass
        hd[vocab:, :] = jnp.zeros((padded - vocab, width), jnp.bfloat16)
        load.wait()
        rows = held[...].reshape(512, width)
        target_at = target_ref[...]

        def logits(n, carry):
            top, picked = carry
            at = pl.multiple_of(n * 512, 512)
            tile = nt(held[...].reshape(512, width), hd[pl.ds(at, 512), :])
            column = lax.broadcasted_iota(jnp.int32, (512, 512), 1) + at
            tile = jnp.where(column < vocab, tile, -1e30)
            raised[:, pl.ds(at, 512)] = tile
            top = jnp.maximum(top, jnp.max(tile, axis=1, keepdims=True))
            hit = jnp.where(column == target_at, tile, 0.0)
            return top, picked + jnp.sum(hit, axis=1, keepdims=True)

        top, picked = lax.fori_loop(
            0, tiles, logits, (jnp.full((512, 1), -1e30, jnp.float32), jnp.zeros((512, 1), jnp.float32))
        )

        def exponents(n, total):
            at = pl.ds(pl.multiple_of(n * 512, 512), 512)
            tile = jnp.exp(raised[:, at] - top)
            raised[:, at] = tile
            return total + jnp.sum(tile, axis=1, keepdims=True)

        total = lax.fori_loop(0, tiles, exponents, jnp.zeros((512, 1), jnp.float32))
        lane = lax.broadcasted_iota(jnp.int32, (512, 128), 1)
        both = jnp.where(lane == 0, top, jnp.where(lane == 1, total, 0.0))
        stat[...] = jnp.transpose(both)[0:8, :]
        copies = [
            post.send(stat, stats.at[k - 1], fsdp_at((me + k) % FSDP_N)) for k in ALL8
        ]
        for copy in copies:
            copy.wait_recv()
        top_all = stat[0:1, :]
        for n in range(7):
            top_all = jnp.maximum(top_all, stats[n, 0:1, :])
        sum_all = stat[1:2, :] * jnp.exp(stat[0:1, :] - top_all)
        for n in range(7):
            sum_all = sum_all + stats[n, 1:2, :] * jnp.exp(stats[n, 0:1, :] - top_all)
        log_row = top_all + jnp.log(sum_all)
        log_norm = jnp.transpose(jnp.broadcast_to(log_row, (128, 512)))[:, 0:1]
        weights = weight_ref[...]
        mine = lax.broadcasted_iota(jnp.int32, (512, 1), 0) // 64 == me
        value = jnp.sum(jnp.where(mine, log_norm * weights, 0.0) - weights * picked, axis=0, keepdims=True)
        loss[...] = jnp.broadcast_to(value, (8, 128))
        scale = scaled_ref[...]
        factor = scale * jnp.exp(top - log_norm)

        def slopes(n, carry):
            at = pl.multiple_of(n * 512, 512)
            column = lax.broadcasted_iota(jnp.int32, (512, 512), 1) + at
            hit = jnp.where(column == target_at, scale, 0.0)
            d_logits[:, pl.ds(at, 512)] = (factor * raised[:, pl.ds(at, 512)] - hit).astype(jnp.bfloat16)
            return carry

        lax.fori_loop(0, tiles, slopes, 0)
        half, inner = lax.axis_index("fsdp_0"), me % 4
        sums = []
        for n, part in enumerate((1 - half, half)):
            start = pl.multiple_of(part * 256, 256)

            def product(t, carry):
                at = pl.ds(pl.multiple_of(t * 512, 512), 512)
                tile = jnp.dot(
                    d_logits[pl.ds(start, 256), :], hd[:, at], preferred_element_type=jnp.float32
                )
                prod[pl.ds(part * 4, 4), :, at] = tile.astype(jnp.bfloat16).reshape(4, 64, 512)
                return carry

            lax.fori_loop(0, width // 512, product, 0)
            for j in range(n, 4):
                peer = part * 4 + (inner + j) % 4
                sums.append(post.send(prod.at[peer], got.at[4 * n + j - n], fsdp_at(peer)))
        out[...] = prod[me].astype(jnp.float32)
        for n, copy in enumerate(sums):
            copy.wait_recv()
            out[...] += got[n].astype(jnp.float32)
        post.finish()

    return remote_call(
        body,
        [
            jax.ShapeDtypeStruct((64, width), jnp.float32),
            jax.ShapeDtypeStruct((8, 128), jnp.float32),
        ],
        [VMEM, ANY, VMEM, VMEM, VMEM],
        [VMEM, VMEM],
        [
            pltpu.VMEM((padded, width), jnp.bfloat16),
            pltpu.VMEM((8, 64, width), jnp.bfloat16),
            pltpu.VMEM((512, padded), jnp.float32),
            pltpu.VMEM((512, padded), jnp.bfloat16),
            pltpu.VMEM((8, 64, width), jnp.bfloat16),
            pltpu.VMEM((7, 64, width), jnp.bfloat16),
            pltpu.VMEM((8, 512), jnp.float32),
            pltpu.VMEM((7, 8, 512), jnp.float32),
            DMA((60,)),
            DMA,
        ],
        collective_id,
        "head_step",
    )(chosen, head, target, weight, scaled)


def token_gradients(d_start, left, right, ids, loss, vocab, collective_id):
    width = 128
    low_n, tile = 1024, 1024

    def body(
        src, left_ref, right_ref, ids_ref, loss_ref, out, left_out, right_out, totals_out, held, left_parts,
        right_parts, left_mid, right_mid, left_more, right_more, total, spread, sums_a, parts_a, sums_b,
        parts_b, sem, lsem,
    ):
        post = Post(sem, 220)
        f, s = fsdp_me(), seq_me()
        z, yl = z_me(), lax.axis_index("fsdp_2")
        greet_devices(seq_peers() + fsdp_peers())

        def cols(p):
            return pl.ds(pl.multiple_of(p * width, width), width)

        def window(p):
            return pl.ds(pl.multiple_of((9 * p) // 4 * 128, 128), 384)

        moves, sums = [], []
        for k in ALL16:
            peer = (s + k) % SEQ_N
            sums.append(post.send(left_ref.at[:, cols(peer)], left_parts.at[k - 1], seq_at(peer)))
            sums.append(post.send(right_ref.at[:, window(peer)], right_parts.at[k - 1], seq_at(peer)))
            moves.append(post.send(src.at[:, cols(peer)], held.at[f, s], seq_at(peer)))
        own = pltpu.make_async_copy(src.at[:, cols(s)], held.at[f, s], lsem)
        own.start()
        total[...] = jnp.zeros_like(total)
        left_sum, right_sum = left_ref[:, cols(s)], right_ref[:, window(s)]
        for copy in sums:
            copy.wait_recv()
        for n in range(15):
            left_sum, right_sum = left_sum + left_parts[n], right_sum + right_parts[n]
        left_mid[...] = left_sum
        right_mid[...] = right_sum
        shares = []
        for k in ALL8:
            device = fsdp_at((f + k) % FSDP_N)
            shares.append(post.send(left_mid, left_more.at[k - 1], device))
            shares.append(post.send(right_mid, right_more.at[k - 1], device))
        for copy in moves:
            copy.wait_recv()
        own.wait()

        def add(block):
            def one(t, carry):
                ids_row = ids_ref[pl.ds(block * 2 + t, 1), :]
                high, low = ids_row >> 10, ids_row & 1023
                part = lax.broadcasted_iota(jnp.int32, (8, tile), 0)
                which = jnp.transpose((part == high).astype(jnp.float32))
                grad = held[block, pl.ds(t * 8, 8)].reshape(tile, width).astype(jnp.float32)
                for h in range(4):
                    spread[:, h * width : (h + 1) * width] = jnp.where(
                        which[:, h : h + 1] > 0.5, grad, 0.0
                    ).astype(jnp.bfloat16)

                def step(n, inner):
                    start = pl.multiple_of(n * 256, 256)
                    row = lax.broadcasted_iota(jnp.int32, (256, tile), 0) + start
                    hot = (row == low).astype(jnp.float32).astype(jnp.bfloat16)
                    total[pl.ds(start, 256), :] += jnp.dot(
                        hot, spread[...], preferred_element_type=jnp.float32
                    )
                    return inner

                lax.fori_loop(0, low_n // 256, step, 0)
                return carry

            lax.fori_loop(0, 2, one, 0)

        every = slice(None)
        steps = relay(
            post, held, (pl.ds(0, 8),), (pl.ds(8, 8),), (pl.ds(0, 4),), (pl.ds(4, 4),)
        )
        before, after, far = (z + 3) % 4, (z + 1) % 4, (z + 2) % 4
        next(steps)
        add(f)
        next(steps)
        next(steps)
        next(steps)
        add(z * 2 + 1 - yl)
        next(steps)
        next(steps)
        add(before * 2 + yl)
        next(steps)
        add(after * 2 + yl)
        add(far * 2 + yl)
        assert next(steps, "end") == "end"
        for zz in (before, after, far):
            add(zz * 2 + 1 - yl)
        squares = jnp.zeros((1, width), jnp.float32)
        for h in range(4):
            count = min(low_n, vocab - h * low_n)
            rows = total[0:count, h * width : (h + 1) * width]
            out[h * low_n : h * low_n + count, :] = rows
            squares = squares + jnp.sum(rows * rows, axis=0, keepdims=True)
        for copy in shares:
            copy.wait_recv()
        for n in range(7):
            left_sum, right_sum = left_sum + left_more[n], right_sum + right_more[n]
        left_out[...] = left_sum
        base = (9 * s) // 4 * 128
        column = lax.broadcasted_iota(jnp.int32, (8, 384), 1) + base
        right_own = jnp.where((column >= 288 * s) & (column < 288 * s + 288), right_sum, 0.0)
        right_out[...] = right_sum
        factor = (column >= 2048).astype(jnp.int32) + (column >= 2304) + (column >= 2560)
        blank = jnp.zeros((32, width), jnp.float32)

        def products(a, b):
            return lax.dot_general(
                a, b, (((1,), (1,)), ((), ())), preferred_element_type=jnp.float32, precision=HIGHEST
            )

        lane = lax.broadcasted_iota(jnp.int32, (8, width), 1)
        row = lax.broadcasted_iota(jnp.int32, (8, width), 0)
        factors = jnp.concatenate([left_sum[0:32], blank, blank, blank], axis=0)
        result = jnp.zeros((8, width), jnp.float32)
        for k in range(4):
            one = products(left_sum[8 * k : 8 * k + 8], factors)
            result = result + jnp.where(lane >> 3 == k, one, 0.0)
        for n in range(3):
            part = right_own[:, n * width : (n + 1) * width]
            which = factor[:, n * width : (n + 1) * width]
            spread_rows = [jnp.where(which == k, part, 0.0) for k in range(4)]
            result = result + products(
                part, jnp.concatenate([blank] + spread_rows + [blank, blank], axis=0)
            )
        small_squares = jnp.sum(
            jnp.sum(left_sum * left_sum, axis=0, keepdims=True), axis=1, keepdims=True
        ) + jnp.sum(jnp.sum(right_own * right_own, axis=0, keepdims=True), axis=1, keepdims=True)
        result = jnp.where((lane == 64) & (row == 0), small_squares, result)
        result = jnp.where(f == 0, result, 0.0)
        result = result + jnp.where(
            (lane == 64) & (row == 0), jnp.sum(squares, axis=1, keepdims=True), 0.0
        )
        result = result + jnp.where((lane == 65) & (row == 0), loss_ref[...], 0.0)
        sums_a[...] = result
        copies = [post.send(sums_a, parts_a.at[k - 1], seq_at((s + k) % SEQ_N)) for k in ALL16]
        for copy in copies:
            copy.wait_recv()
        for n in range(15):
            result = result + parts_a[n]
        sums_b[...] = result
        copies = [post.send(sums_b, parts_b.at[k - 1], fsdp_at((f + k) % FSDP_N)) for k in ALL8]
        for copy in copies:
            copy.wait_recv()
        for n in range(7):
            result = result + parts_b[n]
        totals_out[...] = result
        post.finish()

    return remote_call(
        body,
        [
            jax.ShapeDtypeStruct((vocab, width), jnp.float32),
            jax.ShapeDtypeStruct((40, width), jnp.float32),
            jax.ShapeDtypeStruct((8, 384), jnp.float32),
            jax.ShapeDtypeStruct((8, width), jnp.float32),
        ],
        [VMEM] * 5,
        [VMEM] * 4,
        [
            pltpu.VMEM((FSDP_N, SEQ_N, 128, width), jnp.bfloat16),
            pltpu.VMEM((15, 40, width), jnp.float32),
            pltpu.VMEM((15, 8, 384), jnp.float32),
            pltpu.VMEM((40, width), jnp.float32),
            pltpu.VMEM((8, 384), jnp.float32),
            pltpu.VMEM((7, 40, width), jnp.float32),
            pltpu.VMEM((7, 8, 384), jnp.float32),
            pltpu.VMEM((low_n, 4 * width), jnp.float32),
            pltpu.VMEM((tile, 4 * width), jnp.bfloat16),
            pltpu.VMEM((8, width), jnp.float32),
            pltpu.VMEM((15, 8, width), jnp.float32),
            pltpu.VMEM((8, width), jnp.float32),
            pltpu.VMEM((7, 8, width), jnp.float32),
            DMA((220,)),
            DMA,
        ],
        collective_id,
        "token_gradients",
    )(d_start, left, right, ids, loss)


def feed_forward(rows, gate_up_parts, down_parts, saved, collective_id, name):
    forward = saved is None
    count, width = rows.shape
    quarter = sum(part.shape[1] for part in gate_up_parts)
    units = quarter // 2
    parts_n = len(gate_up_parts)
    chunk = count // 2
    tile = 512

    def body(*refs):
        if forward:
            src, gu_hbm, dn_hbm = refs[0], refs[1 : 1 + parts_n], refs[1 + parts_n : 1 + 2 * parts_n]
            out, gu_out, held, gu, dn, saved_v, mid, part, give, got, sem = refs[1 + 2 * parts_n :]
        else:
            src, gu_hbm, dn_hbm = refs[0], refs[1 : 1 + parts_n], refs[1 + parts_n : 1 + 2 * parts_n]
            gu_in, out, held, gu, dn, saved_v, mid, part, give, got, sem = refs[1 + 2 * parts_n :]
        c = lax.axis_index("seq_2")
        sibling = {"seq_2": 1 - c}
        partner = {"fsdp_1": 1 - lax.axis_index("fsdp_1")}
        used = [0]

        def fresh():
            used[0] += 1
            return sem.at[used[0] - 1]

        load_gu, load_dn = [], []
        for copies, hbm, whole in ((load_gu, gu_hbm, gu), (load_dn, dn_hbm, dn)):
            at = 0
            for piece in hbm:
                view = whole.at[:, pl.ds(at, piece.shape[1])]
                copies.append(pltpu.make_async_copy(piece, view, fresh()))
                at += piece.shape[1]
        loads = [load_gu, load_dn]
        if not forward:
            load_dn.append(pltpu.make_async_copy(gu_in, saved_v, fresh()))
            loads = [load_dn, load_gu]
        for load in loads[0] + loads[1]:
            load.start()

        barrier = pltpu.get_barrier_semaphore()
        for device in (sibling, partner):
            pl.semaphore_signal(barrier, inc=1, device_id=device, device_id_type=MESH_ID)
        pl.semaphore_wait(barrier, 2)

        started = []

        def remote(src_ref, dst_ref, device):
            copy = pltpu.make_async_remote_copy(
                src_ref=src_ref, dst_ref=dst_ref, send_sem=fresh(), recv_sem=fresh(),
                device_id=device, device_id_type=MESH_ID,
            )
            copy.start()
            started.append(copy)
            return copy

        def lines(block, k=None):
            if k is None:
                return pl.ds(block * count, count)
            return pl.ds(block * count + k * chunk, chunk)

        along = [
            remote(src.at[pl.ds(k * chunk, chunk)], held.at[lines(2, k)], partner) for k in range(2)
        ]
        beside = remote(src, held.at[lines(1)], sibling)
        held[lines(0), :] = src[...]

        def first_product(pair):
            mine = pl.ds(pair * 2 * count, 2 * count)

            def step(n, carry):
                at = pl.multiple_of(n * tile, tile)
                low, high = pl.ds(at, tile), pl.ds(pl.multiple_of(at + units, tile), tile)
                block = held[mine, :]
                if forward:
                    gate = jnp.dot(block, gu[:, low], preferred_element_type=jnp.float32)
                    up = jnp.dot(block, gu[:, high], preferred_element_type=jnp.float32)
                    saved_v[mine, low] = gate
                    saved_v[mine, high] = up
                    mid[:, low] = (gate * jax.nn.sigmoid(gate) * up).astype(jnp.bfloat16)
                else:
                    d_hidden = nt(block, dn[low, :])
                    gate, up = saved_v[mine, low], saved_v[mine, high]
                    sigmoid_of = jax.nn.sigmoid(gate)
                    mid[:, low] = (
                        d_hidden * up * sigmoid_of * (1.0 + gate * (1.0 - sigmoid_of))
                    ).astype(jnp.bfloat16)
                    mid[:, high] = (d_hidden * gate * sigmoid_of).astype(jnp.bfloat16)
                return carry

            lax.fori_loop(0, units // tile, step, 0)

        def second_product(pair):
            def step(n, carry):
                at = pl.ds(pl.multiple_of(n * tile, tile), tile)
                if forward:
                    part[pair, :, at] = jnp.dot(
                        mid[...], dn[:, at], preferred_element_type=jnp.float32
                    )
                else:
                    part[pair, :, at] = nt(mid[...], gu[at, :])
                return carry

            lax.fori_loop(0, width // tile, step, 0)

        for load in loads[0]:
            load.wait()
        beside.wait_recv()
        first_product(0)
        along[0].wait_recv()
        passed = [remote(held.at[lines(2, 0)], held.at[lines(3, 0)], sibling)]
        for load in loads[1]:
            load.wait()
        second_product(0)
        along[1].wait_recv()
        passed.append(remote(held.at[lines(2, 1)], held.at[lines(3, 1)], sibling))
        give[0] = part[0, count:, :].astype(jnp.bfloat16)
        home = remote(give.at[0], got.at[0], sibling)
        if forward:
            stores = [
                pltpu.make_async_copy(
                    saved_v.at[pl.ds(0, 2 * count)], gu_out.at[pl.ds(0, 2 * count)], fresh()
                )
            ]
            stores[0].start()
        for copy in passed:
            copy.wait_recv()
        first_product(1)
        if forward:
            stores.append(
                pltpu.make_async_copy(
                    saved_v.at[pl.ds(2 * count, 2 * count)], gu_out.at[pl.ds(2 * count, 2 * count)], fresh()
                )
            )
            stores[1].start()
        second_product(1)
        give[1] = part[1, count:, :].astype(jnp.bfloat16)
        over = remote(give.at[1], got.at[1], sibling)
        over.wait_recv()
        back = []
        for k in range(2):
            some = pl.ds(k * chunk, chunk)
            give[2, some, :] = (part[1, some, :] + got[1, some, :].astype(jnp.float32)).astype(
                jnp.bfloat16
            )
            back.append(remote(give.at[2, some], got.at[2, some], partner))
        home.wait_recv()
        out[...] = part[0, 0:count, :] + got[0].astype(jnp.float32)
        for k in range(2):
            some = pl.ds(k * chunk, chunk)
            back[k].wait_recv()
            out[some, :] += got[2, some, :].astype(jnp.float32)
        for copy in started:
            copy.wait_send()
        if forward:
            for copy in stores:
                copy.wait()

    scratch = [
        pltpu.VMEM((4 * count, width), jnp.bfloat16),
        pltpu.VMEM((width, quarter), jnp.bfloat16),
        pltpu.VMEM((units, width), jnp.bfloat16),
        pltpu.VMEM((4 * count, quarter), jnp.float32),
        pltpu.VMEM((2 * count, units if forward else quarter), jnp.bfloat16),
        pltpu.VMEM((2, 2 * count, width), jnp.float32),
        pltpu.VMEM((3, count, width), jnp.bfloat16),
        pltpu.VMEM((3, count, width), jnp.bfloat16),
        DMA((24,)),
    ]
    total = jax.ShapeDtypeStruct((count, width), jnp.float32)
    if forward:
        products = jax.ShapeDtypeStruct((4 * count, quarter), jnp.float32)
        return remote_call(
            body, [total, products], [VMEM] + [ANY] * (2 * parts_n), [VMEM, ANY], scratch,
            collective_id, name,
        )(rows, *gate_up_parts, *down_parts)
    return remote_call(
        body, total, [VMEM] + [ANY] * (2 * parts_n + 1), VMEM, scratch, collective_id, name
    )(rows, *gate_up_parts, *down_parts, saved)


def turn(values, cosine, sine):
    width = values.shape[-1]
    lane = lax.broadcasted_iota(jnp.int32, values.shape, values.ndim - 1)
    swapped = jnp.where(
        lane % 64 < 32,
        pltpu.roll(values, width - 32, values.ndim - 1),
        pltpu.roll(values, 32, values.ndim - 1),
    )
    return values * cosine + swapped * sine


def key_value_back(far, own, cosine, sine, collective_id):
    def body(far_ref, own_ref, cos_ref, sin_ref, out, held, sem):
        me = seq_me()
        post = Post(sem, 8)
        barrier = pltpu.get_barrier_semaphore()
        for k in range(1, 5):
            pl.semaphore_signal(
                barrier, inc=1, device_id=seq_at((me + k) % SEQ_N), device_id_type=MESH_ID
            )
        pl.semaphore_wait(barrier, 4)
        copies = [
            post.send(
                far_ref.at[:, pl.ds((4 - k) * TOK, TOK), :], held.at[4 - k],
                seq_at((me + SEQ_N - k) % SEQ_N),
            )
            for k in range(1, 5)
        ]
        for copy in copies:
            copy.wait_recv()
        for m in range(2):
            total = own_ref[m]
            for n in range(3, -1, -1):
                total = total + held[n, m].astype(jnp.float32)
            keys = turn(total[:, 0:256], cos_ref[:, 0:256], -sin_ref[:, 0:256])
            out[pl.ds(m * TOK, TOK), 0:256] = keys.astype(jnp.bfloat16)
            out[pl.ds(m * TOK, TOK), 256:512] = total[:, 256:512].astype(jnp.bfloat16)
        post.finish()

    return remote_call(
        body,
        jax.ShapeDtypeStruct((2 * TOK, 512), jnp.bfloat16),
        [VMEM] * 4,
        VMEM,
        [pltpu.VMEM((4, 2, TOK, 512), jnp.bfloat16), DMA((8,))],
        collective_id,
        "key_value_back",
    )(far, own, cosine, sine)


def spread_heads(block):
    return jnp.concatenate([block[:, 64 * g : 64 * g + 64] for g in range(8)], axis=0)


def join_heads(block):
    return jnp.concatenate([block[64 * g : 64 * g + 64, :] for g in range(8)], axis=1)


def window_mask(start, query_seg, key_seg, shift):
    query = start + lax.broadcasted_iota(jnp.int32, (TOK, 5 * TOK), 0)
    key = start - 4 * TOK + lax.broadcasted_iota(jnp.int32, (TOK, 5 * TOK), 1)
    allowed = (
        (key <= query)
        & (key >= 0)
        & (query_seg == key_seg)
        & (((query + shift) >> 8) == ((key + shift) >> 8))
    )
    return jnp.concatenate([allowed.astype(jnp.float32)] * 8, axis=0) > 0.5


def nt(left, right):
    return lax.dot_general(
        left, right, (((1,), (1,)), ((), ())), preferred_element_type=jnp.float32
    )


def tn(left, right):
    return lax.dot_general(
        left, right, (((0,), (0,)), ((), ())), preferred_element_type=jnp.float32
    )


def probabilities(queries, keys, mask):
    scores = jnp.where(mask, nt(queries, keys) * 0.125, -1e30)
    top = jnp.max(scores, axis=-1, keepdims=True)
    raised = jnp.where(mask, jnp.exp(scores - top), 0.0)
    return raised / jnp.sum(raised, axis=-1, keepdims=True)


def attend_back(queries, window, upstream, cosine, sine, query_seg, key_seg, start, shifts):
    def body(
        start_ref, shift_ref, q_ref, kv_ref, g_ref, cos_ref, sin_ref, qs_ref, ks_ref,
        dq_out, far_out, own_out,
    ):
        for h in range(4):
            cols = slice(512 * h, 512 * h + 512)
            mask = window_mask(start_ref[0], qs_ref[0], ks_ref[0], shift_ref[h])
            spread = spread_heads(q_ref[:, cols])
            keys = kv_ref[0, :, 64 * h : 64 * h + 64]
            values = kv_ref[0, :, 256 + 64 * h : 256 + 64 * h + 64]
            probs = probabilities(spread, keys, mask)
            grads = spread_heads(g_ref[:, cols])
            d_probs = nt(grads, values)
            d_values = tn(probs.astype(jnp.bfloat16), grads)
            inner = jnp.sum(probs * d_probs, axis=-1, keepdims=True)
            d_scores = (0.125 * probs * (d_probs - inner)).astype(jnp.bfloat16)
            d_queries = join_heads(jnp.dot(d_scores, keys, preferred_element_type=jnp.float32))
            dq_out[:, cols] = turn(d_queries, cos_ref[...], -sin_ref[...]).astype(jnp.bfloat16)
            d_keys = tn(d_scores, spread)
            for at, part in ((64 * h, d_keys), (256 + 64 * h, d_values)):
                far_out[0, :, at : at + 64] = part[0 : 4 * TOK].astype(jnp.bfloat16)
                own_out[0, :, at : at + 64] = part[4 * TOK :]

    wide = pl.BlockSpec((TOK, 2048), lambda m: (m, 0))
    return pl.pallas_call(
        body,
        out_shape=[
            jax.ShapeDtypeStruct((2 * TOK, 2048), jnp.bfloat16),
            jax.ShapeDtypeStruct((2, 4 * TOK, 512), jnp.bfloat16),
            jax.ShapeDtypeStruct((2, TOK, 512), jnp.float32),
        ],
        grid=(2,),
        in_specs=[
            SMEM,
            SMEM,
            wide,
            pl.BlockSpec((1, 5 * TOK, 512), lambda m: (m, 0, 0)),
            wide,
            pl.BlockSpec((TOK, 512), lambda m: (0, 0)),
            pl.BlockSpec((TOK, 512), lambda m: (0, 0)),
            pl.BlockSpec((1, TOK, 1), lambda m: (m, 0, 0)),
            pl.BlockSpec((1, 1, 5 * TOK), lambda m: (m, 0, 0)),
        ],
        out_specs=[
            wide,
            pl.BlockSpec((1, 4 * TOK, 512), lambda m: (m, 0, 0)),
            pl.BlockSpec((1, TOK, 512), lambda m: (m, 0, 0)),
        ],
        compiler_params=pltpu.CompilerParams(vmem_limit_bytes=VMEM_LIMIT),
        name="attend_back",
    )(start, shifts, queries, window, upstream, cosine, sine, query_seg, key_seg)


def dot(left, right):
    return jnp.dot(left, right, preferred_element_type=jnp.float32)


def dot_exact(left, right):
    return jnp.dot(left, right, precision=HIGHEST)


def norm_scale(values):
    return lax.rsqrt(jnp.mean(values * values, axis=-1, keepdims=True) + NORM_EPS)


def norm_back(values, gain, upstream):
    scale_of = norm_scale(values)
    scaled = gain * upstream
    inward = scale_of * scaled - values * scale_of**3 * jnp.mean(
        scaled * values, axis=-1, keepdims=True
    )
    return (inward, jnp.sum(upstream * values * scale_of, axis=0))


def adam_update(weight_vals, first_old, second_old, gradient, rate):
    first_new = FIRST_DECAY * first_old + (1.0 - FIRST_DECAY) * gradient
    second_new = SECOND_DECAY * second_old + (1.0 - SECOND_DECAY) * gradient * gradient
    first_hat = first_new / (1.0 - FIRST_DECAY**STEP)
    second_hat = second_new / (1.0 - SECOND_DECAY**STEP)
    step_vals = first_hat / (jnp.sqrt(second_hat) + ADAM_EPS) + WEIGHT_DECAY * weight_vals
    return (first_new, second_new, weight_vals - rate * step_vals)


def factor_onehot(columns):
    factor_id = (
        (columns >= 2048).astype(jnp.int32)
        + (columns >= 2048 + 256).astype(jnp.int32)
        + (columns >= 2048 + 512).astype(jnp.int32)
    )
    return (factor_id[None, :] == jnp.arange(4)[:, None]).astype(jnp.float32)


def inverse_root(stats):
    unit_mat = jnp.eye(stats.shape[-1], dtype=stats.dtype)[None]
    norm_of = jnp.sqrt(jnp.sum(stats * stats, axis=(1, 2), keepdims=True))
    matrix = stats / norm_of
    root_mat = unit_mat * lax.rsqrt(jnp.sqrt(norm_of))
    for iteration in range(10):
        factor = (5.0 * unit_mat - matrix) * 0.25
        root_mat = jnp.einsum("kab,kbc->kac", root_mat, factor, precision=HIGHEST)
        square = jnp.einsum("kab,kbc->kac", factor, factor, precision=HIGHEST)
        fourth = jnp.einsum("kab,kbc->kac", square, square, precision=HIGHEST)
        matrix = jnp.einsum("kab,kbc->kac", fourth, matrix, precision=HIGHEST)
    return root_mat


def shampoo_apply(
    stats_new, width_left, width_right, down_factor_gradient, up_factor_gradient, onehot
):
    roots = inverse_root(stats_new)
    left_three = down_factor_gradient.reshape(4, up_factor_gradient.shape[0], -1)
    down_factor_step = (
        jnp.einsum("krs,ksd->krd", roots[:4], left_three, precision=HIGHEST)
        * lax.rsqrt(jnp.sqrt(width_left))[:, None, :]
    )
    up_factor_step = (
        jnp.einsum("krs,sc,kc->rc", roots[4:], up_factor_gradient, onehot, precision=HIGHEST)
        * lax.rsqrt(jnp.sqrt(width_right))[None, :]
    )
    return (down_factor_step.reshape(down_factor_gradient.shape), up_factor_step)


def per_device(
    input_token_index,
    target_token_index,
    loss_position_index,
    document_slot_index,
    row_used_length,
    head_group_offsets,
    embedding,
    embedding_first_moment,
    embedding_second_moment,
    frozen_output_table,
    frozen_query_key_value_weight,
    frozen_attention_output_weight,
    frozen_gate_up_weight,
    frozen_down_weight,
    norm_gain_vectors,
    norm_gain_first_moment,
    norm_gain_second_moment,
    adapter_down_factors,
    adapter_up_factors,
    rank_side_statistics,
    down_width_statistics,
    up_width_statistics,
):
    fsdp_here = lax.axis_index(FSDP)
    seq_here = lax.axis_index(SEQ)
    vocab_dev = embedding.shape[0]

    qkvo_own = jnp.concatenate([frozen_query_key_value_weight, frozen_attention_output_weight], 1)
    gate_up_own = frozen_gate_up_weight.reshape(16, 2, 8, 2, 2, 2, 2, 44).transpose(
        0, 5, 3, 1, 2, 4, 6, 7
    )
    gate_up_own = jnp.pad(gate_up_own, [(0, 0)] * 7 + [(0, 4)]).reshape(16, 2 * PAD_FF)
    down_own = jnp.pad(frozen_down_weight, ((0, 4), (0, 0)))
    small_own = jnp.pad(
        jnp.concatenate(
            [
                adapter_down_factors.reshape(-1),
                norm_gain_vectors.reshape(-1),
                adapter_up_factors.reshape(-1),
            ]
        ),
        (0, 1024 - 848),
    ).reshape(8, 128)
    ids_own = jnp.pad(input_token_index.reshape(16, TOK), ((0, 0), (0, 64)))
    qkvo, small, table, ids, gate_up_w, down_w = gather_weights(
        qkvo_own,
        small_own,
        embedding.astype(jnp.bfloat16),
        ids_own,
        gate_up_own,
        down_own,
    )
    qkvo = qkvo.reshape(2048, 4608)
    w_qkv, w_out = qkvo[:, :2560], qkvo[:, 2560:]
    head_own, ids = lax.optimization_barrier((frozen_output_table, ids))
    head = lax.all_gather(head_own, SEQ, axis=1, tiled=True)
    small = small.reshape(128, 1024)
    down_full = small[:, :512].reshape(128, 32, 16).transpose(1, 0, 2).reshape(32, 2048)
    gain = small[:, 512:560].reshape(128, 3, 16).transpose(1, 0, 2).reshape(3, 2048)
    up_full = small[:, 560:848].reshape(128, 8, 36).transpose(1, 0, 2).reshape(8, 4608)
    a_low = down_full.astype(jnp.bfloat16)
    b_low = up_full.astype(jnp.bfloat16)
    a_in, a_out = a_low[:24], a_low[24:]
    factor_of = (jnp.arange(2560) >= 2048).astype(jnp.int32) + (jnp.arange(2560) >= 2304)
    b_in = jnp.where(
        (jnp.arange(24) // 8)[:, None] == factor_of[None, :],
        jnp.concatenate([b_low[:, :2560]] * 3, 0),
        jnp.zeros((), jnp.bfloat16),
    )
    b_out = b_low[:, 2560:]

    places = loss_position_index.reshape(2, 8, SEQ_N, 32)
    spots = jnp.arange(SEQ_N)[:, None] * TOK + places
    counted = spots < row_used_length[..., None, None]
    below = jnp.sum(
        (document_slot_index[..., None] < jnp.arange(1, 3)).astype(jnp.int32), axis=2
    )
    seg_at = jnp.sum(
        (spots[..., None] >= below[:, :, None, None, :]).astype(jnp.int32), axis=-1
    )
    member = counted[..., None] & (seg_at[..., None] == jnp.arange(3))
    counts = jnp.sum(member.astype(jnp.int32), axis=(2, 3))
    document_total = jnp.sum((counts > 0).astype(jnp.float32))
    own_places = lax.dynamic_index_in_dim(places, seq_here, 2, keepdims=False)
    own_counted = lax.dynamic_index_in_dim(counted, seq_here, 2, keepdims=False)
    own_seg = lax.dynamic_index_in_dim(seg_at, seq_here, 2, keepdims=False)
    per_doc = jnp.sum(
        jnp.where(own_seg[..., None] == jnp.arange(3), counts[:, :, None, :], 0), axis=-1
    )
    own_weight = jnp.where(own_counted, 1.0 / jnp.maximum(per_doc, 1).astype(jnp.float32), 0.0)
    weight_flat = own_weight.transpose(1, 0, 2).reshape(-1)
    row_places = lax.dynamic_index_in_dim(own_places, fsdp_here, 1, keepdims=False)
    chosen_at = (row_places + jnp.arange(2)[:, None] * TOK).reshape(64)
    pick = (chosen_at[:, None] == jnp.arange(128)[None, :]).astype(jnp.float32)

    ids = ids[:, :, :TOK].reshape(SEQ_N, 2, 8, TOK)
    row_ids = lax.dynamic_index_in_dim(ids, fsdp_here, 2, keepdims=False).reshape(SEQ_N, 128)
    half = 32
    freqs = ROPE_BASE ** (-2.0 * jnp.arange(half).astype(jnp.float32) / 64)
    angles = (seq_here * TOK + jnp.arange(TOK)).astype(jnp.float32)[:, None] * freqs[None, :]
    cosine = jnp.tile(jnp.cos(angles), (1, 16))
    sine = jnp.sin(angles)
    sine = jnp.tile(jnp.concatenate([-sine, sine], 1), (1, 8))
    own_docs = lax.dynamic_index_in_dim(document_slot_index, fsdp_here, 1, keepdims=False)
    padded = jnp.concatenate([jnp.full((2, 4 * TOK), -1, jnp.int32), own_docs], 1)
    key_seg = lax.dynamic_slice_in_dim(padded, seq_here * TOK, 5 * TOK, 1)[:, None, :]
    query_seg = key_seg[:, 0, 4 * TOK :][:, :, None]
    start = (seq_here * TOK).reshape(1)
    (
        x_start, normed_one, adapter_in, queries, window, attended, adapter_mid, x_mid, normed_two,
    ) = attention_block(
        table, row_ids, qkvo, a_low, b_in, b_out, gain, cosine, sine, query_seg, key_seg,
        head_group_offsets, 2,
    )
    gate_up_w = [gate_up_w.reshape(2048, -1)]
    down_w = [down_w.reshape(PAD_FF // 4, -1)]

    hidden_sum, gate_up = feed_forward(normed_two, gate_up_w, down_w, None, 12, "feed_forward")
    x_end = x_mid + hidden_sum
    normed_end = (x_end * norm_scale(x_end) * gain[2]).astype(jnp.bfloat16)

    chosen = dot(pick.astype(jnp.bfloat16), normed_end).astype(jnp.bfloat16)
    local_target = target_token_index.transpose(1, 0, 2).reshape(512, 1) - fsdp_here * vocab_dev
    local_target = jnp.where(local_target < vocab_dev, local_target, -1)
    weight_column = weight_flat.reshape(512, 1)
    d_chosen, loss_tile = head_step(
        chosen, head, local_target, weight_column, weight_column / document_total, 4
    )

    upstream = lax.dot_general(pick, d_chosen, (((0,), (0,)), ((), ())), precision=HIGHEST)
    d_end, gain_end = norm_back(x_end, gain[2], upstream)
    d_normed = feed_forward(
        d_end.astype(jnp.bfloat16), gate_up_w, down_w, gate_up, 13, "feed_forward_back"
    )
    back_two, gain_mid = norm_back(x_mid, gain[1], d_normed)
    d_mid = d_end + back_two

    d_branch = d_mid.astype(jnp.bfloat16)
    d_adapter_mid = (ADAPTER_SCALE * nt(d_branch, b_out)).astype(jnp.bfloat16)
    d_attended = (nt(d_branch, w_out) + dot(d_adapter_mid, a_out)).astype(jnp.bfloat16)
    up_gradient_out = ADAPTER_SCALE * tn(adapter_mid, d_branch)
    down_gradient_out = tn(d_adapter_mid, attended)
    d_queries, d_far, d_own = attend_back(
        queries, window, d_attended, cosine, sine, query_seg, key_seg, start, head_group_offsets
    )
    d_key_value = key_value_back(d_far, d_own, cosine, sine, 7)
    d_packed = jnp.concatenate([d_queries, d_key_value], 1)
    d_adapter_in = (ADAPTER_SCALE * nt(d_packed, b_in)).astype(jnp.bfloat16)
    up_gradient_in = ADAPTER_SCALE * jnp.concatenate(
        [
            tn(adapter_in[:, 0:8], d_packed[:, :2048]),
            tn(adapter_in[:, 8:16], d_packed[:, 2048:2304]),
            tn(adapter_in[:, 16:24], d_packed[:, 2304:]),
        ],
        1,
    )
    down_gradient_in = tn(d_adapter_in, normed_one)
    back_one, gain_start = norm_back(
        x_start, gain[0], nt(d_packed, w_qkv) + dot(d_adapter_in, a_in)
    )
    d_start = (d_mid + back_one).astype(jnp.bfloat16)

    left = jnp.concatenate(
        [
            down_gradient_in,
            down_gradient_out,
            jnp.stack([gain_start, gain_mid, gain_end]),
            jnp.zeros((5, 2048), jnp.float32),
        ],
        0,
    )
    right = jnp.concatenate([up_gradient_in, up_gradient_out], 1)
    all_ids = ids.transpose(2, 0, 1, 3).reshape(16, 1024) - fsdp_here * vocab_dev
    grad_embed, left_sum, right_sum, totals = token_gradients(
        d_start, left, right, all_ids, loss_tile, vocab_dev, 8
    )
    stats_all = totals[:, :64].reshape(8, 8, 8).transpose(1, 0, 2)
    document_loss_sum = totals[0, 65]
    global_gradient_norm = jnp.sqrt(totals[0, 64])
    clip_factor = CLIP_MAX / jnp.maximum(global_gradient_norm, CLIP_MAX)

    own_left = lax.dynamic_slice_in_dim(left_sum, fsdp_here * 16, 16, 1)
    down_factor_gradient = own_left[:32] * clip_factor
    grad_gain = own_left[32:35] * clip_factor
    up_factor_gradient = (
        lax.dynamic_slice_in_dim(right_sum, 32 * ((9 * seq_here) % 4) + fsdp_here * 36, 36, 1) * clip_factor
    )
    grad_embed = grad_embed * clip_factor
    unused_first, updated_embedding_second_moment, updated_embedding_table = adam_update(
        embedding, embedding_first_moment, embedding_second_moment, grad_embed, RATE_EMBED
    )
    updated_gain_first_moment, updated_gain_second_moment, updated_norm_gains = adam_update(
        norm_gain_vectors, norm_gain_first_moment, norm_gain_second_moment, grad_gain, RATE_GAIN
    )
    updated_rank_statistics = (
        SECOND_DECAY * rank_side_statistics
        + (1.0 - SECOND_DECAY) * (clip_factor * clip_factor) * stats_all
    )
    updated_down_width_statistics = SECOND_DECAY * down_width_statistics + (
        1.0 - SECOND_DECAY
    ) * jnp.sum(down_factor_gradient.reshape(4, 8, -1) ** 2, axis=1)
    updated_up_width_statistics = SECOND_DECAY * up_width_statistics + (
        1.0 - SECOND_DECAY
    ) * jnp.sum(up_factor_gradient * up_factor_gradient, axis=0)
    onehot = factor_onehot((seq_here * 8 + fsdp_here) * 36 + jnp.arange(36))
    down_factor_step, up_factor_step = shampoo_apply(
        updated_rank_statistics,
        updated_down_width_statistics,
        updated_up_width_statistics,
        down_factor_gradient,
        up_factor_gradient,
        onehot,
    )
    updated_down_factors = adapter_down_factors - LEARN_RATE_DOWN * down_factor_step
    updated_up_factors = adapter_up_factors - LEARN_RATE_UP * up_factor_step
    return (
        document_loss_sum,
        document_total,
        global_gradient_norm,
        grad_embed,
        updated_embedding_second_moment,
        updated_embedding_table,
        updated_gain_first_moment,
        updated_gain_second_moment,
        updated_norm_gains,
        down_factor_gradient,
        up_factor_gradient,
        updated_rank_statistics,
        updated_down_width_statistics,
        updated_up_width_statistics,
        updated_down_factors,
        updated_up_factors,
    )


def solution(mesh):
    torus = Mesh(
        mesh.devices.reshape(2, 4, 2, 2, 2, 2), SEQ_FSDP
    )
    return jax.shard_map(
        per_device,
        mesh=torus,
        in_specs=(
            P(None, None, SEQ),
            P(None, None, SEQ),
            P(),
            P(),
            P(),
            P(),
            P(FSDP, SEQ),
            P(FSDP, SEQ),
            P(FSDP, SEQ),
            P(FSDP, SEQ),
            P(SEQ_FSDP, None),
            P(SEQ_FSDP, None),
            P(SEQ_FSDP, None),
            P(SEQ_FSDP, None),
            P(None, SEQ_FSDP),
            P(None, SEQ_FSDP),
            P(None, SEQ_FSDP),
            P(None, SEQ_FSDP),
            P(None, SEQ_FSDP),
            P(),
            P(None, SEQ_FSDP),
            P(SEQ_FSDP),
        ),
        out_specs=(
            P(),
            P(),
            P(),
            P(FSDP, SEQ),
            P(FSDP, SEQ),
            P(FSDP, SEQ),
            P(None, SEQ_FSDP),
            P(None, SEQ_FSDP),
            P(None, SEQ_FSDP),
            P(None, SEQ_FSDP),
            P(None, SEQ_FSDP),
            P(),
            P(None, SEQ_FSDP),
            P(SEQ_FSDP),
            P(None, SEQ_FSDP),
            P(None, SEQ_FSDP),
        ),
        check_vma=False,
    )
```

```python
import functools

import jax
import jax.numpy as jnp
from jax import lax
from jax.experimental import pallas as pl
from jax.experimental.pallas import tpu as pltpu
from jax.sharding import Mesh
from jax.sharding import PartitionSpec as P

STEP = 5
GROUP = 256
SEQ = ("seq_0", "seq_1", "seq_2")
FSDP = ("fsdp_0", "fsdp_1", "fsdp_2")
SEQ_FSDP = SEQ + FSDP
SEQ_N = 16
FSDP_N = 8
TOK = 64
PAD_FF = 6144
NORM_EPS = 1e-05
ADAPTER_SCALE = 2.0
ROPE_BASE = 10000.0
CLIP_MAX = 0.001
FIRST_DECAY = 0.5
SECOND_DECAY = 0.5
RATE_EMBED = 0.3
RATE_GAIN = 0.1
LEARN_RATE_DOWN = 0.1
LEARN_RATE_UP = 0.5
WEIGHT_DECAY = 0.01
ADAM_EPS = 1e-12
HIGHEST = lax.Precision.HIGHEST
MESH_ID = pl.DeviceIdType.MESH
ANY = pl.BlockSpec(memory_space=pl.ANY)
VMEM = pl.BlockSpec(memory_space=pltpu.VMEM)
SMEM = pl.BlockSpec(memory_space=pltpu.SMEM)
DMA = pltpu.SemaphoreType.DMA
VMEM_LIMIT = 56 * 1024 * 1024


def seq_me():
    return lax.axis_index("seq_0") * 8 + lax.axis_index("seq_1") * 2 + lax.axis_index("seq_2")


def z_me():
    return lax.axis_index("fsdp_0") * 2 + lax.axis_index("fsdp_1")


def z_at(i):
    return {"fsdp_0": i // 2, "fsdp_1": i % 2}


def fsdp_me():
    return z_me() * 2 + lax.axis_index("fsdp_2")


def seq_at(i):
    return {"seq_0": i // 8, "seq_1": (i // 2) % 4, "seq_2": i % 2}


def fsdp_at(i):
    return {**z_at(i // 2), "fsdp_2": i % 2}


def remote_call(body, out_shape, in_specs, out_specs, scratch, collective_id, name):
    return pl.pallas_call(
        body,
        out_shape=out_shape,
        in_specs=in_specs,
        out_specs=out_specs,
        scratch_shapes=scratch,
        compiler_params=pltpu.CompilerParams(
            collective_id=collective_id, has_side_effects=True, vmem_limit_bytes=VMEM_LIMIT
        ),
        name=name,
    )


ALL16 = range(1, SEQ_N)
ALL8 = range(1, FSDP_N)


ORDER = (
    "q2", "s", "q0", "d0", "t0", "q1", "q0", "q2", "d1", "d0", "s", "q2",
    "q1", "g0", "q1", "q0", "q2", "d1", "g1", "q0", "s", "q2", "q2", "g0",
    "t0", "t1", "g1", "q2", "t1", "q1", "g1", "d0", "q2", "g0", "s", "g1",
    "q0", "d0", "g0", "s", "d1", "d1", "s", "q1", "q2", "q1", "q1", "s",
    "q0", "t0", "d1", "g1", "d0", "q0", "g0", "t0", "q1", "g0", "q1", "d1",
    "d1", "t0", "g1", "g0", "q2", "q0", "g1", "d0", "q0", "s", "s", "d1",
    "t1", "d0", "q1", "t1", "q0", "g0", "s", "d0", "t1", "g1",
)
EVERY = slice(None)


class Post:
    def __init__(self, sem, count):
        self.sem, self.count, self.used, self.sent, self.late = sem, count, 0, [], []

    def fresh(self):
        self.used += 1
        assert self.used <= self.count, self.used
        return self.sem.at[self.used - 1]

    def start(self, src, dst, ssem, rsem, device):
        copy = pltpu.make_async_remote_copy(
            src_ref=src, dst_ref=dst, send_sem=ssem, recv_sem=rsem,
            device_id=device, device_id_type=MESH_ID,
        )
        copy.start()
        return copy

    def send(self, src, dst, device):
        copy = self.start(src, dst, self.fresh(), self.fresh(), device)
        self.sent.append(copy)
        return copy

    def finish(self):
        for copy in self.sent:
            copy.wait_send()
        for mark, view in self.late:
            pltpu.make_async_copy(view, view, mark).wait()


def greet_devices(devices):
    barrier = pltpu.get_barrier_semaphore()
    for device in devices:
        pl.semaphore_signal(barrier, inc=1, device_id=device, device_id_type=MESH_ID)
    pl.semaphore_wait(barrier, len(devices))


def fsdp_peers():
    me = fsdp_me()
    return [fsdp_at((me + k) % FSDP_N) for k in ALL8]


def seq_peers():
    me = seq_me()
    return [seq_at((me + k) % SEQ_N) for k in ALL16]


def relay(post, out, first, second, first_a, first_b):
    z, yl = z_me(), lax.axis_index("fsdp_2")
    partner, up, down = {"fsdp_2": 1 - yl}, z_at((z + 1) % 4), z_at((z + 3) % 4)
    before, after, far = (z + 3) % 4, (z + 1) % 4, (z + 2) % 4

    def at(zz, y, part=()):
        return out.at[(zz * 2 + y,) + part]

    def send(zz, y, part, device):
        view = at(zz, y, part)
        return post.send(view, view, device)

    to_partner = send(z, yl, (), partner)
    ring_up = send(z, yl, (), up)
    ring_down = send(z, yl, (), down)
    yield
    to_partner.wait_recv()
    other_up = send(z, 1 - yl, first, up)
    other_down = send(z, 1 - yl, first, down)
    yield
    ring_up.wait_recv()
    far_up = send(before, yl, first, up)
    across = [send(before, yl, second, partner)]
    yield
    ring_down.wait_recv()
    far_down = send(after, yl, second, down)
    across.append(send(after, yl, second, partner))
    yield
    other_up.wait_recv()
    last_up = send(before, 1 - yl, first_a, up)
    yield
    other_down.wait_recv()
    last_down = send(after, 1 - yl, first_b, down)
    yield
    far_up.wait_recv()
    far_down.wait_recv()
    across.append(send(far, yl, second, partner))
    yield
    last_up.wait_recv()
    last_down.wait_recv()
    for copy in across:
        copy.wait_recv()


def no_hand(view):
    return None


class Ways:
    def __init__(self, post):
        self.post = post
        self.yh, self.x, self.c = (lax.axis_index(a) for a in SEQ)
        self.z, self.yl = z_me(), lax.axis_index("fsdp_2")
        self.where = {"x": self.x, "y": 2 * self.yh + self.yl, "z": self.z}
        z, c = self.z, self.c
        self.column = [
            ((z + dz) % 4, (c + dc) % 2, dz, dc) for dz in range(4) for dc in range(2) if dz or dc
        ]

    def beside(self, axis, step):
        at = (self.where[axis] + step + 4) % 4
        if axis == "x":
            return {"seq_1": at}
        if axis == "z":
            return z_at(at)
        return {"seq_0": at // 2, "fsdp_2": at % 2}

    def all_devices(self):
        return (
            [self.beside("y", 1), self.beside("y", -1)]
            + [{**z_at(zz), "seq_2": cc} for zz, cc, dz, dc in self.column if dz]
            + seq_peers()
        )

    def arrived(self, ref, rsem):
        pltpu.make_async_copy(ref, ref, rsem).wait()

    def rings(self, block, order, sizes, halves, across):
        post = self.post
        for n, axis in enumerate(order):
            done = order[:n]
            at = self.where[axis]
            before, after, far = (at + 3) % 4, (at + 1) % 4, (at + 2) % 4
            send, from_before, from_after, far_first = (post.fresh() for _ in range(4))
            post.late.append((send, sizes[axis, n]))
            own = block(done, axis, at, None)
            post.start(own, own, send, from_before, self.beside(axis, 1))
            post.start(own, own, send, from_after, self.beside(axis, -1))
            yield
            got = block(done, axis, before, None)
            self.arrived(got, from_before)
            half = block(done, axis, before, 0)
            post.start(half, half, send, far_first, self.beside(axis, 1))
            across(got)
            yield
            got = block(done, axis, after, None)
            self.arrived(got, from_after)
            if halves:
                far_second = post.fresh()
                half = block(done, axis, after, 1)
                post.start(half, half, send, far_second, self.beside(axis, -1))
            across(got)
            yield
            self.arrived(block(done, axis, far, 0), far_first)
            if halves:
                self.arrived(block(done, axis, far, 1), far_second)
            across(block(done, axis, far, None))

    def place(self, done, axis, at):
        spot = {"yh": self.yh, "x": self.x, "z": self.z, "yl": self.yl}
        for a in done:
            if a == "y":
                spot["yh"] = spot["yl"] = EVERY
            else:
                spot[a] = EVERY
        if axis == "y":
            spot["yh"], spot["yl"] = at // 2, at % 2
        elif axis is not None:
            spot[axis] = at
        return spot

    def everything(self, ref, order, tails, halves=True):
        post, c = self.post, self.c

        def block(done, axis, at, half):
            spot = self.place(done, axis, at)
            tail = tails[0 if half is None else half + 1]
            return ref.at[(spot["yh"], spot["x"], c, spot["z"], spot["yl"]) + tail]

        across_s, across_r = post.fresh(), post.fresh()
        post.late.append((across_s, ref.at[(EVERY, EVERY, c, EVERY, EVERY) + tails[0]]))
        post.late.append((across_r, ref.at[(EVERY, EVERY, 1 - c, EVERY, EVERY) + tails[0]]))

        def across(view):
            post.start(view, view, across_s, across_r, {"seq_2": 1 - c})

        three = pl.ds(0, 3)
        sizes = {}
        for axis in "xyz":
            sizes[axis, 0] = ref.at[(0, 0, 0, three, 0) + tails[0]]
            sizes[axis, 1] = ref.at[(0, pl.ds(0, 2), 0, three, EVERY) + tails[0]]
            sizes[axis, 2] = ref.at[(EVERY, EVERY, 0, three, EVERY) + tails[0]]
        across(block([], None, None, None))
        yield from self.rings(block, order, sizes, halves, across)

    def gate_up(self, src, ref, order, start, width):
        post = self.post
        quarter = src.shape[1] // 4
        yh, x, c, z, yl = self.yh, self.x, self.c, self.z, self.yl
        tails = [
            (EVERY, pl.ds(start, width)),
            (EVERY, pl.ds(start, width // 2)),
            (EVERY, pl.ds(start + width // 2, width // 2)),
        ]

        def block(done, axis, at, half):
            spot = self.place(done, axis, at)
            tail = tails[0 if half is None else half + 1]
            return ref.at[(spot["yh"], spot["x"], EVERY, EVERY, spot["yl"]) + tail]

        marks = []
        for zz, cc, dz, dc in self.column:
            send, recv = post.fresh(), post.fresh()
            first = pl.multiple_of((2 * (zz % 2) + cc) * quarter + start, 128)
            here = ref.at[(yh, x, c, z, yl) + tails[0]]
            post.start(src.at[:, pl.ds(first, width)], here, send, recv, {**z_at(zz), "seq_2": cc})
            post.late.append((send, here))
            marks.append((ref.at[(yh, x, (c + dc) % 2, (z + 4 - dz) % 4, yl) + tails[0]], recv))
        yield
        for view, recv in marks:
            self.arrived(view, recv)
        three = pl.ds(0, 3)
        sizes = {}
        for axis in "xy":
            sizes[axis, 0] = ref.at[(0, three, EVERY, EVERY, 0) + tails[0]]
            sizes[axis, 1] = ref.at[(EVERY, three, EVERY, EVERY, EVERY) + tails[0]]
        yield from self.rings(block, order, sizes, True, no_hand)

    def down(self, ref, order, start, width):
        post = self.post
        yh, x, z, yl = self.yh, self.x, self.z, self.yl
        tails = [
            (EVERY, pl.ds(start, width)),
            (EVERY, pl.ds(start, width // 2)),
            (EVERY, pl.ds(start + width // 2, width // 2)),
        ]
        zh = z // 2

        def block(done, axis, at, half):
            spot = self.place(done, axis, at)
            tail = tails[0 if half is None else half + 1]
            return ref.at[(spot["yh"], spot["x"], EVERY, spot["yl"]) + tail]

        send, recv = post.fresh(), post.fresh()
        here = ref.at[(yh, x, zh, yl) + tails[0]]
        post.start(here, here, send, recv, z_at((z + 2) % 4))
        post.late.append((send, here))
        yield
        self.arrived(ref.at[(yh, x, 1 - zh, yl) + tails[0]], recv)
        three = pl.ds(0, 3)
        sizes = {}
        for axis in "xy":
            sizes[axis, 0] = ref.at[(0, three, EVERY, 0) + tails[0]]
            sizes[axis, 1] = ref.at[(EVERY, three, EVERY, EVERY) + tails[0]]
        yield from self.rings(block, order, sizes, True, no_hand)

    def table(self, ref, low, high):
        post, z, yl = self.post, self.z, self.yl
        middle = (low + high) // 32 * 16
        part = (pl.ds(low, high - low), pl.ds(low, middle - low), pl.ds(middle, high - middle))
        send_y, recv_y = post.fresh(), post.fresh()
        post.late.append((send_y, ref.at[0, part[0]]))
        own = ref.at[2 * z + yl, part[0]]
        post.start(own, own, send_y, recv_y, {"fsdp_2": 1 - yl})
        yield
        self.arrived(ref.at[2 * z + 1 - yl, part[0]], recv_y)

        def block(done, axis, at, half):
            return ref.at[pl.ds(2 * at, 2), part[0 if half is None else half + 1]]

        sizes = {("z", 0): ref.at[pl.ds(0, 6), part[0]]}
        yield from self.rings(block, ("z",), sizes, True, no_hand)

    def own_gate_up(self, src, ref):
        quarter = ref.shape[-1]
        first = pl.multiple_of((2 * (self.z % 2) + self.c) * quarter, 128)
        return src.at[:, pl.ds(first, quarter)], ref.at[self.yh, self.x, self.c, self.z, self.yl]


def local_copies(pairs, post):
    copies = [pltpu.make_async_copy(src, dst, post.fresh()) for src, dst in pairs]
    for copy in copies:
        copy.start()
    return copies


def gather_weights(qkvo, small, table, ids, gate_up, down):
    groups, units = 8, gate_up.shape[1] // 8
    spread = units // 44 * 48
    quarter = groups * spread // 4
    out_shape = [
        jax.ShapeDtypeStruct((2, 4, 2, 4, 2, *qkvo.shape), qkvo.dtype),
        jax.ShapeDtypeStruct((2, 4, 2, 4, 2, *small.shape), small.dtype),
        jax.ShapeDtypeStruct((FSDP_N, *table.shape), table.dtype),
        jax.ShapeDtypeStruct((SEQ_N, *ids.shape), ids.dtype),
        jax.ShapeDtypeStruct((2, 4, 2, 4, 2, gate_up.shape[0], quarter), gate_up.dtype),
        jax.ShapeDtypeStruct((2, 4, 2, 2, *down.shape), down.dtype),
    ]
    sem_count = 320

    def body(*refs):
        ins, outs, ordered, picks, sem = refs[:6], refs[6:12], refs[12], refs[13], refs[14]
        post = Post(sem, sem_count)
        ways = Ways(post)
        yh, x, c, z, yl = ways.yh, ways.x, ways.c, ways.z, ways.yl
        seq = seq_me()
        local = local_copies(
            [
                (ins[0], outs[0].at[yh, x, c, z, yl]),
                (ins[1], outs[1].at[yh, x, c, z, yl]),
                (ins[2], outs[2].at[z * 2 + yl]),
                (ins[3], outs[3].at[seq]),
                (ins[5], outs[5].at[yh, x, z // 2, yl]),
            ],
            post,
        )
        at = lax.broadcasted_iota(jnp.int32, (1, spread), 1)
        part, rest = at // (spread // 4), at % (spread // 4)
        unit = rest % 48
        here = rest // 48
        source = (
            (here // 4) * 16 + (part % 2) * 8 + ((here // 2) % 2) * 4 + (part // 2) * 2 + here % 2
        ) * 44 + unit
        source = jnp.where(unit < 44, source, -1)

        def pick(n, carry):
            start = pl.multiple_of(n * 128, 128)
            row = lax.broadcasted_iota(jnp.int32, (128, spread), 0) + start
            picks[pl.ds(start, 128), :] = (row == source).astype(jnp.float32).astype(jnp.bfloat16)
            return carry

        lax.fori_loop(0, units // 128, pick, 0)
        for n in range(groups):
            moved = jnp.dot(
                ins[4][:, n * units : (n + 1) * units], picks[...], preferred_element_type=jnp.float32
            ).astype(jnp.bfloat16)
            width = spread // 4
            for k in range(4):
                first = k * quarter + n * width
                ordered[:, first : first + width] = moved[:, k * width : (k + 1) * width]
        mine = ways.own_gate_up(ordered, outs[4])
        local += local_copies([mine], post)
        greet_devices(ways.all_devices())
        for copy in local:
            copy.wait()

        send, recv = post.fresh(), post.fresh()
        for device in seq_peers():
            post.start(ins[3], outs[3].at[seq], send, recv, device)
        post.late.append((send, outs[3].at[pl.ds(0, 15)]))
        post.late.append((recv, outs[3].at[pl.ds(0, 15)]))

        third = qkvo.shape[1] // 3
        streams = {
            "s": ways.everything(outs[1], "xyz", [(EVERY, EVERY)] * 2, False),
        }
        rows = table.shape[0]
        cuts = (0, 1984, rows)
        for n in range(len(cuts) - 1):
            streams["t%d" % n] = ways.table(outs[2], cuts[n], cuts[n + 1])
        half, wide = quarter // 2, down.shape[1] // 2
        for n, order in enumerate(("xy", "yx")):
            streams["g%d" % n] = ways.gate_up(ordered, outs[4], order, n * half, half)
            streams["d%d" % n] = ways.down(outs[5], order, n * wide, wide)
        for n, order in enumerate(('yxz', 'xyz', 'zyx')):
            streams["q%d" % n] = ways.everything(
                outs[0], order,
                [
                    (EVERY, pl.ds(n * third, third)),
                    (EVERY, pl.ds(n * third, third // 2)),
                    (EVERY, pl.ds(n * third + third // 2, third // 2)),
                ],
            )
        for name in ORDER:
            next(streams[name], None)
        for name in sorted(streams):
            assert next(streams[name], "end") == "end", name
        post.finish()

    return remote_call(
        body, out_shape, [ANY] * 4 + [VMEM, ANY], [ANY] * 6,
        [
            pltpu.VMEM((gate_up.shape[0], 4 * quarter), gate_up.dtype),
            pltpu.VMEM((units, spread), gate_up.dtype),
            DMA((sem_count,)),
        ],
        1, "gather_weights",
    )(qkvo, small, table, ids, gate_up, down)


def attention_block(
    table, ids, qkvo, a_low, b_in, b_out, gain, cosine, sine, query_seg, key_seg, shifts, collective_id
):
    vocab, width = table.shape[1:]
    rows_n = 2 * TOK
    sem_count = 64

    def body(
        table_hbm, ids_ref, qkvo_hbm, a_ref, bi_ref, bo_ref, gain_ref, cos_ref, sin_ref, qs_ref, ks_ref,
        shift_ref,
        x_out, n_out, u_out, q_out, kv_out, a_out, v_out, mid_out, two_out,
        stage, wide, rows, block, low, packed, own_kv, w_qkv, w_out, sem,
    ):
        post = Post(sem, sem_count)
        me = seq_me()
        loads = [post.fresh() for _ in range(2)]

        def staged(n):
            return pltpu.make_async_copy(table_hbm.at[n], stage.at[n % 2], loads[n % 2])

        staged(0).start()
        weights = local_copies(
            [
                (qkvo_hbm.at[:, pl.ds(0, 2560)], w_qkv),
                (qkvo_hbm.at[:, pl.ds(2560, 2048)], w_out),
            ],
            post,
        )
        greet_devices(seq_peers())
        for n in range(FSDP_N):
            if n + 1 < FSDP_N:
                staged(n + 1).start()
            staged(n).wait()
            wide[pl.ds(n * vocab, vocab), :] = stage[n % 2].astype(jnp.float32)

        spot = pl.ds(pl.multiple_of(me * width, width), width)

        def fetch(s):
            def step(t, carry):
                rows[pl.ds(t, 1), :] = wide[pl.ds(ids_ref[s, t], 1), :]
                return carry

            lax.fori_loop(0, rows_n, step, 0, unroll=16)

        moved = []
        for k in list(ALL16) + [0]:
            peer = (me + k) % SEQ_N
            fetch(peer)
            block[k] = rows[...].astype(jnp.bfloat16)
            if k:
                moved.append(post.send(block.at[k], low.at[:, spot], seq_at(peer)))
        own = pltpu.make_async_copy(block.at[0], low.at[:, spot], post.fresh())
        own.start()
        for copy in moved:
            copy.wait_recv()
        own.wait()

        start = low[...].astype(jnp.float32)
        x_out[...] = start
        scale = lax.rsqrt(jnp.mean(start * start, axis=-1, keepdims=True) + NORM_EPS)
        n_out[...] = (start * scale * gain_ref[0:1, :]).astype(jnp.bfloat16)
        inner = nt(n_out[...], a_ref[0:24, :]).astype(jnp.bfloat16)
        u_out[...] = inner
        weights[0].wait()

        def project(at):
            packed[:, at] = jnp.dot(
                n_out[...], w_qkv[:, at], preferred_element_type=jnp.float32
            ) + ADAPTER_SCALE * jnp.dot(u_out[...], bi_ref[:, at], preferred_element_type=jnp.float32)

        project(pl.ds(2048, 512))
        for n in range(2):
            some = slice(n * TOK, n * TOK + TOK)
            own_kv[n, :, 0:256] = turn(
                packed[some, 2048:2304], cos_ref[:, 0:256], sin_ref[:, 0:256]
            ).astype(jnp.bfloat16)
            own_kv[n, :, 256:512] = packed[some, 2304:2560].astype(jnp.bfloat16)
        keys = [
            post.send(
                own_kv, kv_out.at[:, pl.ds((4 - k) * TOK, TOK), :], seq_at((me + k) % SEQ_N)
            )
            for k in range(1, 5)
        ]
        kv_out[:, 4 * TOK :, :] = own_kv[...]

        def project_some(n, carry):
            project(pl.ds(pl.multiple_of(n * 512, 512), 512))
            return carry

        lax.fori_loop(0, 4, project_some, 0)
        for copy in keys:
            copy.wait_recv()

        first = me * TOK

        def attend_one(n, carry):
            some = pl.ds(pl.multiple_of(n * TOK, TOK), TOK)
            for h in range(4):
                cols = slice(512 * h, 512 * h + 512)
                turned = turn(packed[some, cols], cos_ref[...], sin_ref[...]).astype(jnp.bfloat16)
                q_out[some, cols] = turned
                mask = window_mask(first, qs_ref[n], ks_ref[n], shift_ref[h])
                probs = probabilities(
                    spread_heads(turned), kv_out[n, :, 64 * h : 64 * h + 64], mask
                )
                values = kv_out[n, :, 256 + 64 * h : 256 + 64 * h + 64]
                mixed = jnp.dot(
                    probs.astype(jnp.bfloat16), values, preferred_element_type=jnp.float32
                )
                a_out[some, cols] = join_heads(mixed).astype(jnp.bfloat16)
            return carry

        lax.fori_loop(0, 2, attend_one, 0)
        middle = nt(a_out[...], a_ref[24:32, :]).astype(jnp.bfloat16)
        v_out[...] = middle
        weights[1].wait()

        def project_out(n, carry):
            at = pl.ds(pl.multiple_of(n * 512, 512), 512)
            mid_out[:, at] = (
                x_out[:, at]
                + jnp.dot(a_out[...], w_out[:, at], preferred_element_type=jnp.float32)
                + ADAPTER_SCALE
                * jnp.dot(v_out[...], bo_ref[:, at], preferred_element_type=jnp.float32)
            )
            return carry

        lax.fori_loop(0, 4, project_out, 0)
        middle_rows = mid_out[...]
        scale = lax.rsqrt(jnp.mean(middle_rows * middle_rows, axis=-1, keepdims=True) + NORM_EPS)
        two_out[...] = (middle_rows * scale * gain_ref[1:2, :]).astype(jnp.bfloat16)
        post.finish()

    def shape(*dims, dtype=jnp.bfloat16):
        return jax.ShapeDtypeStruct(dims, dtype)

    return remote_call(
        body,
        [
            shape(rows_n, 2048, dtype=jnp.float32),
            shape(rows_n, 2048),
            shape(rows_n, 24),
            shape(rows_n, 2048),
            shape(2, 5 * TOK, 512),
            shape(rows_n, 2048),
            shape(rows_n, 8),
            shape(rows_n, 2048, dtype=jnp.float32),
            shape(rows_n, 2048),
        ],
        [ANY, SMEM, ANY] + [VMEM] * 8 + [SMEM],
        [VMEM] * 9,
        [
            pltpu.VMEM((2, vocab, width), jnp.bfloat16),
            pltpu.VMEM((FSDP_N * vocab, width), jnp.float32),
            pltpu.VMEM((rows_n, width), jnp.float32),
            pltpu.VMEM((SEQ_N, rows_n, width), jnp.bfloat16),
            pltpu.VMEM((rows_n, 2048), jnp.bfloat16),
            pltpu.VMEM((rows_n, 2560), jnp.float32),
            pltpu.VMEM((2, TOK, 512), jnp.bfloat16),
            pltpu.VMEM((2048, 2560), jnp.bfloat16),
            pltpu.VMEM((2048, 2048), jnp.bfloat16),
            DMA((sem_count,)),
        ],
        collective_id,
        "attention_block",
    )(table, ids, qkvo, a_low, b_in, b_out, gain, cosine, sine, query_seg, key_seg, shifts)


def head_step(chosen, head, target, weight, scaled, collective_id):
    vocab, width = head.shape
    padded = -(-vocab // 512) * 512
    tiles = padded // 512

    def body(
        chosen_ref, head_hbm, target_ref, weight_ref, scaled_ref, out, loss, hd, held, raised, d_logits,
        prod, got, stat, stats, sem, lsem,
    ):
        post = Post(sem, 60)
        me = fsdp_me()
        load = pltpu.make_async_copy(head_hbm, hd.at[pl.ds(0, vocab)], lsem)
        load.start()
        held[me] = chosen_ref[...]
        greet_devices(fsdp_peers())
        for _ in relay(
            post, held, (pl.ds(0, 32),), (pl.ds(32, 32),), (pl.ds(0, 16),), (pl.ds(16, 16),)
        ):
            pass
        hd[vocab:, :] = jnp.zeros((padded - vocab, width), jnp.bfloat16)
        load.wait()
        rows = held[...].reshape(512, width)
        target_at = target_ref[...]

        def logits(n, carry):
            top, picked = carry
            at = pl.multiple_of(n * 512, 512)
            tile = nt(held[...].reshape(512, width), hd[pl.ds(at, 512), :])
            column = lax.broadcasted_iota(jnp.int32, (512, 512), 1) + at
            tile = jnp.where(column < vocab, tile, -1e30)
            raised[:, pl.ds(at, 512)] = tile
            top = jnp.maximum(top, jnp.max(tile, axis=1, keepdims=True))
            hit = jnp.where(column == target_at, tile, 0.0)
            return top, picked + jnp.sum(hit, axis=1, keepdims=True)

        top, picked = lax.fori_loop(
            0, tiles, logits, (jnp.full((512, 1), -1e30, jnp.float32), jnp.zeros((512, 1), jnp.float32))
        )

        def exponents(n, total):
            at = pl.ds(pl.multiple_of(n * 512, 512), 512)
            tile = jnp.exp(raised[:, at] - top)
            raised[:, at] = tile
            return total + jnp.sum(tile, axis=1, keepdims=True)

        total = lax.fori_loop(0, tiles, exponents, jnp.zeros((512, 1), jnp.float32))
        lane = lax.broadcasted_iota(jnp.int32, (512, 128), 1)
        both = jnp.where(lane == 0, top, jnp.where(lane == 1, total, 0.0))
        stat[...] = jnp.transpose(both)[0:8, :]
        copies = [
            post.send(stat, stats.at[k - 1], fsdp_at((me + k) % FSDP_N)) for k in ALL8
        ]
        for copy in copies:
            copy.wait_recv()
        top_all = stat[0:1, :]
        for n in range(7):
            top_all = jnp.maximum(top_all, stats[n, 0:1, :])
        sum_all = stat[1:2, :] * jnp.exp(stat[0:1, :] - top_all)
        for n in range(7):
            sum_all = sum_all + stats[n, 1:2, :] * jnp.exp(stats[n, 0:1, :] - top_all)
        log_row = top_all + jnp.log(sum_all)
        log_norm = jnp.transpose(jnp.broadcast_to(log_row, (128, 512)))[:, 0:1]
        weights = weight_ref[...]
        mine = lax.broadcasted_iota(jnp.int32, (512, 1), 0) // 64 == me
        value = jnp.sum(jnp.where(mine, log_norm * weights, 0.0) - weights * picked, axis=0, keepdims=True)
        loss[...] = jnp.broadcast_to(value, (8, 128))
        scale = scaled_ref[...]
        factor = scale * jnp.exp(top - log_norm)

        def slopes(n, carry):
            at = pl.multiple_of(n * 512, 512)
            column = lax.broadcasted_iota(jnp.int32, (512, 512), 1) + at
            hit = jnp.where(column == target_at, scale, 0.0)
            d_logits[:, pl.ds(at, 512)] = (factor * raised[:, pl.ds(at, 512)] - hit).astype(jnp.bfloat16)
            return carry

        lax.fori_loop(0, tiles, slopes, 0)
        half, inner = lax.axis_index("fsdp_0"), me % 4
        sums = []
        for n, part in enumerate((1 - half, half)):
            start = pl.multiple_of(part * 256, 256)

            def product(t, carry):
                at = pl.ds(pl.multiple_of(t * 512, 512), 512)
                tile = jnp.dot(
                    d_logits[pl.ds(start, 256), :], hd[:, at], preferred_element_type=jnp.float32
                )
                prod[pl.ds(part * 4, 4), :, at] = tile.astype(jnp.bfloat16).reshape(4, 64, 512)
                return carry

            lax.fori_loop(0, width // 512, product, 0)
            for j in range(n, 4):
                peer = part * 4 + (inner + j) % 4
                sums.append(post.send(prod.at[peer], got.at[4 * n + j - n], fsdp_at(peer)))
        out[...] = prod[me].astype(jnp.float32)
        for n, copy in enumerate(sums):
            copy.wait_recv()
            out[...] += got[n].astype(jnp.float32)
        post.finish()

    return remote_call(
        body,
        [
            jax.ShapeDtypeStruct((64, width), jnp.float32),
            jax.ShapeDtypeStruct((8, 128), jnp.float32),
        ],
        [VMEM, ANY, VMEM, VMEM, VMEM],
        [VMEM, VMEM],
        [
            pltpu.VMEM((padded, width), jnp.bfloat16),
            pltpu.VMEM((8, 64, width), jnp.bfloat16),
            pltpu.VMEM((512, padded), jnp.float32),
            pltpu.VMEM((512, padded), jnp.bfloat16),
            pltpu.VMEM((8, 64, width), jnp.bfloat16),
            pltpu.VMEM((7, 64, width), jnp.bfloat16),
            pltpu.VMEM((8, 512), jnp.float32),
            pltpu.VMEM((7, 8, 512), jnp.float32),
            DMA((60,)),
            DMA,
        ],
        collective_id,
        "head_step",
    )(chosen, head, target, weight, scaled)


def token_gradients(d_start, left, right, ids, loss, vocab, collective_id):
    width = 128
    low_n, tile = 1024, 1024

    def body(
        src, left_ref, right_ref, ids_ref, loss_ref, out, left_out, right_out, totals_out, held, left_parts,
        right_parts, left_mid, right_mid, left_more, right_more, total, spread, sums_a, parts_a, sums_b,
        parts_b, sem, lsem,
    ):
        post = Post(sem, 220)
        f, s = fsdp_me(), seq_me()
        z, yl = z_me(), lax.axis_index("fsdp_2")
        greet_devices(seq_peers() + fsdp_peers())

        def cols(p):
            return pl.ds(pl.multiple_of(p * width, width), width)

        def window(p):
            return pl.ds(pl.multiple_of((9 * p) // 4 * 128, 128), 384)

        moves, sums = [], []
        for k in ALL16:
            peer = (s + k) % SEQ_N
            moves.append(post.send(src.at[:, cols(peer)], held.at[f, s], seq_at(peer)))
        own = pltpu.make_async_copy(src.at[:, cols(s)], held.at[f, s], lsem)
        own.start()
        for k in ALL16:
            peer = (s + k) % SEQ_N
            sums.append(post.send(left_ref.at[:, cols(peer)], left_parts.at[k - 1], seq_at(peer)))
            sums.append(post.send(right_ref.at[:, window(peer)], right_parts.at[k - 1], seq_at(peer)))
        total[...] = jnp.zeros_like(total)
        for copy in moves:
            copy.wait_recv()
        own.wait()

        def add(block):
            def one(t, carry):
                ids_row = ids_ref[pl.ds(block * 2 + t, 1), :]
                high, low = ids_row >> 10, ids_row & 1023
                part = lax.broadcasted_iota(jnp.int32, (8, tile), 0)
                which = jnp.transpose((part == high).astype(jnp.float32))
                grad = held[block, pl.ds(t * 8, 8)].reshape(tile, width).astype(jnp.float32)
                for h in range(4):
                    spread[:, h * width : (h + 1) * width] = jnp.where(
                        which[:, h : h + 1] > 0.5, grad, 0.0
                    ).astype(jnp.bfloat16)

                def step(n, inner):
                    start = pl.multiple_of(n * 256, 256)
                    row = lax.broadcasted_iota(jnp.int32, (256, tile), 0) + start
                    hot = (row == low).astype(jnp.float32).astype(jnp.bfloat16)
                    total[pl.ds(start, 256), :] += jnp.dot(
                        hot, spread[...], preferred_element_type=jnp.float32
                    )
                    return inner

                lax.fori_loop(0, low_n // 256, step, 0)
                return carry

            lax.fori_loop(0, 2, one, 0)

        every = slice(None)
        steps = relay(
            post, held, (pl.ds(0, 8),), (pl.ds(8, 8),), (pl.ds(0, 4),), (pl.ds(4, 4),)
        )
        before, after, far = (z + 3) % 4, (z + 1) % 4, (z + 2) % 4
        next(steps)
        add(f)
        next(steps)
        left_sum, right_sum = left_ref[:, cols(s)], right_ref[:, window(s)]
        for copy in sums:
            copy.wait_recv()
        for n in range(15):
            left_sum, right_sum = left_sum + left_parts[n], right_sum + right_parts[n]
        left_mid[...] = left_sum
        right_mid[...] = right_sum
        shares = []
        for k in ALL8:
            device = fsdp_at((f + k) % FSDP_N)
            shares.append(post.send(left_mid, left_more.at[k - 1], device))
            shares.append(post.send(right_mid, right_more.at[k - 1], device))
        next(steps)
        next(steps)
        add(z * 2 + 1 - yl)
        next(steps)
        next(steps)
        add(before * 2 + yl)
        next(steps)
        add(after * 2 + yl)
        add(far * 2 + yl)
        assert next(steps, "end") == "end"
        for zz in (before, after, far):
            add(zz * 2 + 1 - yl)
        squares = jnp.zeros((1, width), jnp.float32)
        for h in range(4):
            count = min(low_n, vocab - h * low_n)
            rows = total[0:count, h * width : (h + 1) * width]
            out[h * low_n : h * low_n + count, :] = rows
            squares = squares + jnp.sum(rows * rows, axis=0, keepdims=True)
        for copy in shares:
            copy.wait_recv()
        for n in range(7):
            left_sum, right_sum = left_sum + left_more[n], right_sum + right_more[n]
        left_out[...] = left_sum
        base = (9 * s) // 4 * 128
        column = lax.broadcasted_iota(jnp.int32, (8, 384), 1) + base
        right_own = jnp.where((column >= 288 * s) & (column < 288 * s + 288), right_sum, 0.0)
        right_out[...] = right_sum
        factor = (column >= 2048).astype(jnp.int32) + (column >= 2304) + (column >= 2560)
        blank = jnp.zeros((32, width), jnp.float32)

        def products(a, b):
            return lax.dot_general(
                a, b, (((1,), (1,)), ((), ())), preferred_element_type=jnp.float32, precision=HIGHEST
            )

        lane = lax.broadcasted_iota(jnp.int32, (8, width), 1)
        row = lax.broadcasted_iota(jnp.int32, (8, width), 0)
        factors = jnp.concatenate([left_sum[0:32], blank, blank, blank], axis=0)
        result = jnp.zeros((8, width), jnp.float32)
        for k in range(4):
            one = products(left_sum[8 * k : 8 * k + 8], factors)
            result = result + jnp.where(lane >> 3 == k, one, 0.0)
        for n in range(3):
            part = right_own[:, n * width : (n + 1) * width]
            which = factor[:, n * width : (n + 1) * width]
            spread_rows = [jnp.where(which == k, part, 0.0) for k in range(4)]
            result = result + products(
                part, jnp.concatenate([blank] + spread_rows + [blank, blank], axis=0)
            )
        small_squares = jnp.sum(
            jnp.sum(left_sum * left_sum, axis=0, keepdims=True), axis=1, keepdims=True
        ) + jnp.sum(jnp.sum(right_own * right_own, axis=0, keepdims=True), axis=1, keepdims=True)
        result = jnp.where((lane == 64) & (row == 0), small_squares, result)
        result = jnp.where(f == 0, result, 0.0)
        result = result + jnp.where(
            (lane == 64) & (row == 0), jnp.sum(squares, axis=1, keepdims=True), 0.0
        )
        result = result + jnp.where((lane == 65) & (row == 0), loss_ref[...], 0.0)
        sums_a[...] = result
        copies = [post.send(sums_a, parts_a.at[k - 1], seq_at((s + k) % SEQ_N)) for k in ALL16]
        for copy in copies:
            copy.wait_recv()
        for n in range(15):
            result = result + parts_a[n]
        sums_b[...] = result
        copies = [post.send(sums_b, parts_b.at[k - 1], fsdp_at((f + k) % FSDP_N)) for k in ALL8]
        for copy in copies:
            copy.wait_recv()
        for n in range(7):
            result = result + parts_b[n]
        totals_out[...] = result
        post.finish()

    return remote_call(
        body,
        [
            jax.ShapeDtypeStruct((vocab, width), jnp.float32),
            jax.ShapeDtypeStruct((40, width), jnp.float32),
            jax.ShapeDtypeStruct((8, 384), jnp.float32),
            jax.ShapeDtypeStruct((8, width), jnp.float32),
        ],
        [VMEM] * 5,
        [VMEM] * 4,
        [
            pltpu.VMEM((FSDP_N, SEQ_N, 128, width), jnp.bfloat16),
            pltpu.VMEM((15, 40, width), jnp.float32),
            pltpu.VMEM((15, 8, 384), jnp.float32),
            pltpu.VMEM((40, width), jnp.float32),
            pltpu.VMEM((8, 384), jnp.float32),
            pltpu.VMEM((7, 40, width), jnp.float32),
            pltpu.VMEM((7, 8, 384), jnp.float32),
            pltpu.VMEM((low_n, 4 * width), jnp.float32),
            pltpu.VMEM((tile, 4 * width), jnp.bfloat16),
            pltpu.VMEM((8, width), jnp.float32),
            pltpu.VMEM((15, 8, width), jnp.float32),
            pltpu.VMEM((8, width), jnp.float32),
            pltpu.VMEM((7, 8, width), jnp.float32),
            DMA((220,)),
            DMA,
        ],
        collective_id,
        "token_gradients",
    )(d_start, left, right, ids, loss)


def feed_forward(rows, gate_up_parts, down_parts, saved, collective_id, name):
    forward = saved is None
    count, width = rows.shape
    quarter = sum(part.shape[1] for part in gate_up_parts)
    units = quarter // 2
    parts_n = len(gate_up_parts)
    chunk = count // 2
    tile = 512

    def body(*refs):
        if forward:
            src, gu_hbm, dn_hbm = refs[0], refs[1 : 1 + parts_n], refs[1 + parts_n : 1 + 2 * parts_n]
            out, gu_out, held, gu, dn, saved_v, mid, part, give, got, sem = refs[1 + 2 * parts_n :]
        else:
            src, gu_hbm, dn_hbm = refs[0], refs[1 : 1 + parts_n], refs[1 + parts_n : 1 + 2 * parts_n]
            gu_in, out, held, gu, dn, saved_v, mid, part, give, got, sem = refs[1 + 2 * parts_n :]
        c = lax.axis_index("seq_2")
        sibling = {"seq_2": 1 - c}
        partner = {"fsdp_1": 1 - lax.axis_index("fsdp_1")}
        used = [0]

        def fresh():
            used[0] += 1
            return sem.at[used[0] - 1]

        load_gu, load_dn = [], []
        for copies, hbm, whole in ((load_gu, gu_hbm, gu), (load_dn, dn_hbm, dn)):
            at = 0
            for piece in hbm:
                view = whole.at[:, pl.ds(at, piece.shape[1])]
                copies.append(pltpu.make_async_copy(piece, view, fresh()))
                at += piece.shape[1]
        loads = [load_gu, load_dn]
        if not forward:
            load_dn.append(pltpu.make_async_copy(gu_in, saved_v, fresh()))
            loads = [load_dn, load_gu]
        for load in loads[0] + loads[1]:
            load.start()

        barrier = pltpu.get_barrier_semaphore()
        for device in (sibling, partner):
            pl.semaphore_signal(barrier, inc=1, device_id=device, device_id_type=MESH_ID)
        pl.semaphore_wait(barrier, 2)

        started = []

        def remote(src_ref, dst_ref, device):
            copy = pltpu.make_async_remote_copy(
                src_ref=src_ref, dst_ref=dst_ref, send_sem=fresh(), recv_sem=fresh(),
                device_id=device, device_id_type=MESH_ID,
            )
            copy.start()
            started.append(copy)
            return copy

        def lines(block, k=None):
            if k is None:
                return pl.ds(block * count, count)
            return pl.ds(block * count + k * chunk, chunk)

        along = [
            remote(src.at[pl.ds(k * chunk, chunk)], held.at[lines(2, k)], partner) for k in range(2)
        ]
        beside = remote(src, held.at[lines(1)], sibling)
        held[lines(0), :] = src[...]

        def first_product(pair):
            mine = pl.ds(pair * 2 * count, 2 * count)

            def step(n, carry):
                at = pl.multiple_of(n * tile, tile)
                low, high = pl.ds(at, tile), pl.ds(pl.multiple_of(at + units, tile), tile)
                block = held[mine, :]
                if forward:
                    gate = jnp.dot(block, gu[:, low], preferred_element_type=jnp.float32)
                    up = jnp.dot(block, gu[:, high], preferred_element_type=jnp.float32)
                    saved_v[mine, low] = gate
                    saved_v[mine, high] = up
                    mid[:, low] = (gate * jax.nn.sigmoid(gate) * up).astype(jnp.bfloat16)
                else:
                    d_hidden = nt(block, dn[low, :])
                    gate, up = saved_v[mine, low], saved_v[mine, high]
                    sigmoid_of = jax.nn.sigmoid(gate)
                    mid[:, low] = (
                        d_hidden * up * sigmoid_of * (1.0 + gate * (1.0 - sigmoid_of))
                    ).astype(jnp.bfloat16)
                    mid[:, high] = (d_hidden * gate * sigmoid_of).astype(jnp.bfloat16)
                return carry

            lax.fori_loop(0, units // tile, step, 0)

        def second_product(pair):
            def step(n, carry):
                at = pl.ds(pl.multiple_of(n * tile, tile), tile)
                if forward:
                    part[pair, :, at] = jnp.dot(
                        mid[...], dn[:, at], preferred_element_type=jnp.float32
                    )
                else:
                    part[pair, :, at] = nt(mid[...], gu[at, :])
                return carry

            lax.fori_loop(0, width // tile, step, 0)

        for load in loads[0]:
            load.wait()
        beside.wait_recv()
        first_product(0)
        along[0].wait_recv()
        passed = [remote(held.at[lines(2, 0)], held.at[lines(3, 0)], sibling)]
        for load in loads[1]:
            load.wait()
        second_product(0)
        along[1].wait_recv()
        passed.append(remote(held.at[lines(2, 1)], held.at[lines(3, 1)], sibling))
        give[0] = part[0, count:, :].astype(jnp.bfloat16)
        home = remote(give.at[0], got.at[0], sibling)
        if forward:
            stores = [
                pltpu.make_async_copy(
                    saved_v.at[pl.ds(0, 2 * count)], gu_out.at[pl.ds(0, 2 * count)], fresh()
                )
            ]
            stores[0].start()
        for copy in passed:
            copy.wait_recv()
        first_product(1)
        if forward:
            stores.append(
                pltpu.make_async_copy(
                    saved_v.at[pl.ds(2 * count, 2 * count)], gu_out.at[pl.ds(2 * count, 2 * count)], fresh()
                )
            )
            stores[1].start()
        second_product(1)
        give[1] = part[1, count:, :].astype(jnp.bfloat16)
        over = remote(give.at[1], got.at[1], sibling)
        over.wait_recv()
        back = []
        for k in range(2):
            some = pl.ds(k * chunk, chunk)
            give[2, some, :] = (part[1, some, :] + got[1, some, :].astype(jnp.float32)).astype(
                jnp.bfloat16
            )
            back.append(remote(give.at[2, some], got.at[2, some], partner))
        home.wait_recv()
        out[...] = part[0, 0:count, :] + got[0].astype(jnp.float32)
        for k in range(2):
            some = pl.ds(k * chunk, chunk)
            back[k].wait_recv()
            out[some, :] += got[2, some, :].astype(jnp.float32)
        for copy in started:
            copy.wait_send()
        if forward:
            for copy in stores:
                copy.wait()

    scratch = [
        pltpu.VMEM((4 * count, width), jnp.bfloat16),
        pltpu.VMEM((width, quarter), jnp.bfloat16),
        pltpu.VMEM((units, width), jnp.bfloat16),
        pltpu.VMEM((4 * count, quarter), jnp.float32),
        pltpu.VMEM((2 * count, units if forward else quarter), jnp.bfloat16),
        pltpu.VMEM((2, 2 * count, width), jnp.float32),
        pltpu.VMEM((3, count, width), jnp.bfloat16),
        pltpu.VMEM((3, count, width), jnp.bfloat16),
        DMA((24,)),
    ]
    total = jax.ShapeDtypeStruct((count, width), jnp.float32)
    if forward:
        products = jax.ShapeDtypeStruct((4 * count, quarter), jnp.float32)
        return remote_call(
            body, [total, products], [VMEM] + [ANY] * (2 * parts_n), [VMEM, ANY], scratch,
            collective_id, name,
        )(rows, *gate_up_parts, *down_parts)
    return remote_call(
        body, total, [VMEM] + [ANY] * (2 * parts_n + 1), VMEM, scratch, collective_id, name
    )(rows, *gate_up_parts, *down_parts, saved)


def turn(values, cosine, sine):
    width = values.shape[-1]
    lane = lax.broadcasted_iota(jnp.int32, values.shape, values.ndim - 1)
    swapped = jnp.where(
        lane % 64 < 32,
        pltpu.roll(values, width - 32, values.ndim - 1),
        pltpu.roll(values, 32, values.ndim - 1),
    )
    return values * cosine + swapped * sine


def key_value_back(far, own, cosine, sine, collective_id):
    def body(far_ref, own_ref, cos_ref, sin_ref, out, held, sem):
        me = seq_me()
        post = Post(sem, 8)
        barrier = pltpu.get_barrier_semaphore()
        for k in range(1, 5):
            pl.semaphore_signal(
                barrier, inc=1, device_id=seq_at((me + k) % SEQ_N), device_id_type=MESH_ID
            )
        pl.semaphore_wait(barrier, 4)
        copies = [
            post.send(
                far_ref.at[:, pl.ds((4 - k) * TOK, TOK), :], held.at[4 - k],
                seq_at((me + SEQ_N - k) % SEQ_N),
            )
            for k in range(1, 5)
        ]
        for copy in copies:
            copy.wait_recv()
        for m in range(2):
            total = own_ref[m]
            for n in range(3, -1, -1):
                total = total + held[n, m].astype(jnp.float32)
            keys = turn(total[:, 0:256], cos_ref[:, 0:256], -sin_ref[:, 0:256])
            out[pl.ds(m * TOK, TOK), 0:256] = keys.astype(jnp.bfloat16)
            out[pl.ds(m * TOK, TOK), 256:512] = total[:, 256:512].astype(jnp.bfloat16)
        post.finish()

    return remote_call(
        body,
        jax.ShapeDtypeStruct((2 * TOK, 512), jnp.bfloat16),
        [VMEM] * 4,
        VMEM,
        [pltpu.VMEM((4, 2, TOK, 512), jnp.bfloat16), DMA((8,))],
        collective_id,
        "key_value_back",
    )(far, own, cosine, sine)


def spread_heads(block):
    return jnp.concatenate([block[:, 64 * g : 64 * g + 64] for g in range(8)], axis=0)


def join_heads(block):
    return jnp.concatenate([block[64 * g : 64 * g + 64, :] for g in range(8)], axis=1)


def window_mask(start, query_seg, key_seg, shift):
    query = start + lax.broadcasted_iota(jnp.int32, (TOK, 5 * TOK), 0)
    key = start - 4 * TOK + lax.broadcasted_iota(jnp.int32, (TOK, 5 * TOK), 1)
    allowed = (
        (key <= query)
        & (key >= 0)
        & (query_seg == key_seg)
        & (((query + shift) >> 8) == ((key + shift) >> 8))
    )
    return jnp.concatenate([allowed.astype(jnp.float32)] * 8, axis=0) > 0.5


def nt(left, right):
    return lax.dot_general(
        left, right, (((1,), (1,)), ((), ())), preferred_element_type=jnp.float32
    )


def tn(left, right):
    return lax.dot_general(
        left, right, (((0,), (0,)), ((), ())), preferred_element_type=jnp.float32
    )


def probabilities(queries, keys, mask):
    scores = jnp.where(mask, nt(queries, keys) * 0.125, -1e30)
    top = jnp.max(scores, axis=-1, keepdims=True)
    raised = jnp.where(mask, jnp.exp(scores - top), 0.0)
    return raised / jnp.sum(raised, axis=-1, keepdims=True)


def attend_back(queries, window, upstream, cosine, sine, query_seg, key_seg, start, shifts):
    def body(
        start_ref, shift_ref, q_ref, kv_ref, g_ref, cos_ref, sin_ref, qs_ref, ks_ref,
        dq_out, far_out, own_out,
    ):
        for h in range(4):
            cols = slice(512 * h, 512 * h + 512)
            mask = window_mask(start_ref[0], qs_ref[0], ks_ref[0], shift_ref[h])
            spread = spread_heads(q_ref[:, cols])
            keys = kv_ref[0, :, 64 * h : 64 * h + 64]
            values = kv_ref[0, :, 256 + 64 * h : 256 + 64 * h + 64]
            probs = probabilities(spread, keys, mask)
            grads = spread_heads(g_ref[:, cols])
            d_probs = nt(grads, values)
            d_values = tn(probs.astype(jnp.bfloat16), grads)
            inner = jnp.sum(probs * d_probs, axis=-1, keepdims=True)
            d_scores = (0.125 * probs * (d_probs - inner)).astype(jnp.bfloat16)
            d_queries = join_heads(jnp.dot(d_scores, keys, preferred_element_type=jnp.float32))
            dq_out[:, cols] = turn(d_queries, cos_ref[...], -sin_ref[...]).astype(jnp.bfloat16)
            d_keys = tn(d_scores, spread)
            for at, part in ((64 * h, d_keys), (256 + 64 * h, d_values)):
                far_out[0, :, at : at + 64] = part[0 : 4 * TOK].astype(jnp.bfloat16)
                own_out[0, :, at : at + 64] = part[4 * TOK :]

    wide = pl.BlockSpec((TOK, 2048), lambda m: (m, 0))
    return pl.pallas_call(
        body,
        out_shape=[
            jax.ShapeDtypeStruct((2 * TOK, 2048), jnp.bfloat16),
            jax.ShapeDtypeStruct((2, 4 * TOK, 512), jnp.bfloat16),
            jax.ShapeDtypeStruct((2, TOK, 512), jnp.float32),
        ],
        grid=(2,),
        in_specs=[
            SMEM,
            SMEM,
            wide,
            pl.BlockSpec((1, 5 * TOK, 512), lambda m: (m, 0, 0)),
            wide,
            pl.BlockSpec((TOK, 512), lambda m: (0, 0)),
            pl.BlockSpec((TOK, 512), lambda m: (0, 0)),
            pl.BlockSpec((1, TOK, 1), lambda m: (m, 0, 0)),
            pl.BlockSpec((1, 1, 5 * TOK), lambda m: (m, 0, 0)),
        ],
        out_specs=[
            wide,
            pl.BlockSpec((1, 4 * TOK, 512), lambda m: (m, 0, 0)),
            pl.BlockSpec((1, TOK, 512), lambda m: (m, 0, 0)),
        ],
        compiler_params=pltpu.CompilerParams(vmem_limit_bytes=VMEM_LIMIT),
        name="attend_back",
    )(start, shifts, queries, window, upstream, cosine, sine, query_seg, key_seg)


def small_updates(
    totals, left, right, rank, a_old, b_old, width_a, width_b, gain, gain_first, gain_second, columns
):
    def body(
        t_ref, l_ref, r_ref, k_ref, a_ref, b_ref, wa_ref, wb_ref, g_ref, gf_ref, gs_ref, c_ref,
        scalars, ga_out, gb_out, gf_out, gs_out, g_out, k_out, wa_out, wb_out, a_out, b_out,
    ):
        totals_now = t_ref[...]
        norm = jnp.sqrt(totals_now[0:1, 64:65])
        clip = CLIP_MAX / jnp.maximum(norm, CLIP_MAX)
        lane = lax.broadcasted_iota(jnp.int32, (8, 128), 1)
        scalars[...] = jnp.where(lane == 0, norm, jnp.where(lane == 1, clip, 0.0))
        parts = [totals_now[:, 8 * k : 8 * k + 8] for k in range(8)]
        square = (clip * clip)[0:1, 0:1].reshape(1, 1, 1)
        stats = SECOND_DECAY * k_ref[...] + (1.0 - SECOND_DECAY) * square * jnp.stack(parts)
        k_out[...] = stats

        def times(x, y):
            total = x[:, :, 0:1] * y[:, 0:1, :]
            for n in range(1, 8):
                total = total + x[:, :, n : n + 1] * y[:, n : n + 1, :]
            return total

        size = jnp.sqrt(jnp.sum(jnp.sum(stats * stats, axis=2, keepdims=True), axis=1, keepdims=True))
        unit = (
            lax.broadcasted_iota(jnp.int32, (8, 8, 8), 1) == lax.broadcasted_iota(jnp.int32, (8, 8, 8), 2)
        ).astype(jnp.float32)

        def newton(n, carry):
            root, matrix = carry
            factor = (5.0 * unit - matrix) * 0.25
            square_of = times(factor, factor)
            return times(root, factor), times(times(square_of, square_of), matrix)

        roots, _ = lax.fori_loop(
            0, 10, newton, (unit * lax.rsqrt(jnp.sqrt(size)), stats / size)
        )

        gradient = l_ref[...] * clip
        down = gradient[0:32]
        ga_out[...] = down
        up = r_ref[...] * clip
        gb_out[...] = up

        first = FIRST_DECAY * gf_ref[...] + (1.0 - FIRST_DECAY) * gradient[32:35]
        second = SECOND_DECAY * gs_ref[...] + (1.0 - SECOND_DECAY) * gradient[32:35] * gradient[32:35]
        gf_out[...] = first
        gs_out[...] = second
        first_hat = first / (1.0 - FIRST_DECAY**STEP)
        second_hat = second / (1.0 - SECOND_DECAY**STEP)
        gains = g_ref[...]
        g_out[...] = gains - RATE_GAIN * (
            first_hat / (jnp.sqrt(second_hat) + ADAM_EPS) + WEIGHT_DECAY * gains
        )

        def apply(root, gradients):
            total = root[:, 0:1] * gradients[0:1, :]
            for n in range(1, 8):
                total = total + root[:, n : n + 1] * gradients[n : n + 1, :]
            return total

        for k in range(4):
            rows = slice(8 * k, 8 * k + 8)
            mine = down[rows]
            wide = SECOND_DECAY * wa_ref[k : k + 1, :] + (1.0 - SECOND_DECAY) * jnp.sum(
                mine * mine, axis=0, keepdims=True
            )
            wa_out[k : k + 1, :] = wide
            a_out[rows, :] = a_ref[rows, :] - LEARN_RATE_DOWN * (
                apply(roots[k], mine) * lax.rsqrt(jnp.sqrt(wide))
            )
        wide = SECOND_DECAY * wb_ref[...] + (1.0 - SECOND_DECAY) * jnp.sum(
            up * up, axis=0, keepdims=True
        )
        wb_out[...] = wide
        column = c_ref[...]
        factor = (column >= 2048).astype(jnp.int32) + (column >= 2304) + (column >= 2560)
        step = jnp.zeros(up.shape, jnp.float32)
        for k in range(4):
            step = step + jnp.where(factor == k, apply(roots[4 + k], up), 0.0)
        b_out[...] = b_ref[...] - LEARN_RATE_UP * (step * lax.rsqrt(jnp.sqrt(wide)))

    def like(array):
        return jax.ShapeDtypeStruct(array.shape, jnp.float32)

    return pl.pallas_call(
        body,
        out_shape=[
            jax.ShapeDtypeStruct((8, 128), jnp.float32), like(a_old), like(right), like(gain), like(gain),
            like(gain), like(rank), like(width_a), like(width_b), like(a_old), like(b_old),
        ],
        in_specs=[VMEM] * 12,
        out_specs=[VMEM] * 11,
        compiler_params=pltpu.CompilerParams(vmem_limit_bytes=VMEM_LIMIT),
        name="small_updates",
    )(
        totals, left, right, rank, a_old, b_old, width_a, width_b, gain, gain_first, gain_second, columns
    )


def dot(left, right):
    return jnp.dot(left, right, preferred_element_type=jnp.float32)


def dot_exact(left, right):
    return jnp.dot(left, right, precision=HIGHEST)


def norm_scale(values):
    return lax.rsqrt(jnp.mean(values * values, axis=-1, keepdims=True) + NORM_EPS)


def norm_back(values, gain, upstream):
    scale_of = norm_scale(values)
    scaled = gain * upstream
    inward = scale_of * scaled - values * scale_of**3 * jnp.mean(
        scaled * values, axis=-1, keepdims=True
    )
    return (inward, jnp.sum(upstream * values * scale_of, axis=0))


def adam_update(weight_vals, first_old, second_old, gradient, rate):
    first_new = FIRST_DECAY * first_old + (1.0 - FIRST_DECAY) * gradient
    second_new = SECOND_DECAY * second_old + (1.0 - SECOND_DECAY) * gradient * gradient
    first_hat = first_new / (1.0 - FIRST_DECAY**STEP)
    second_hat = second_new / (1.0 - SECOND_DECAY**STEP)
    step_vals = first_hat / (jnp.sqrt(second_hat) + ADAM_EPS) + WEIGHT_DECAY * weight_vals
    return (first_new, second_new, weight_vals - rate * step_vals)


def per_device(
    input_token_index,
    target_token_index,
    loss_position_index,
    document_slot_index,
    row_used_length,
    head_group_offsets,
    embedding,
    embedding_first_moment,
    embedding_second_moment,
    frozen_output_table,
    frozen_query_key_value_weight,
    frozen_attention_output_weight,
    frozen_gate_up_weight,
    frozen_down_weight,
    norm_gain_vectors,
    norm_gain_first_moment,
    norm_gain_second_moment,
    adapter_down_factors,
    adapter_up_factors,
    rank_side_statistics,
    down_width_statistics,
    up_width_statistics,
):
    fsdp_here = lax.axis_index(FSDP)
    seq_here = lax.axis_index(SEQ)
    vocab_dev = embedding.shape[0]

    qkvo_own = jnp.concatenate([frozen_query_key_value_weight, frozen_attention_output_weight], 1)
    down_own = jnp.pad(frozen_down_weight, ((0, 4), (0, 0)))
    small_own = jnp.pad(
        jnp.concatenate(
            [
                adapter_down_factors.reshape(-1),
                norm_gain_vectors.reshape(-1),
                adapter_up_factors.reshape(-1),
            ]
        ),
        (0, 1024 - 848),
    ).reshape(8, 128)
    ids_own = jnp.pad(input_token_index.reshape(16, TOK), ((0, 0), (0, 64)))
    qkvo, small, table, ids, gate_up_w, down_w = gather_weights(
        qkvo_own,
        small_own,
        embedding.astype(jnp.bfloat16),
        ids_own,
        frozen_gate_up_weight,
        down_own,
    )
    qkvo = qkvo.reshape(2048, 4608)
    w_qkv, w_out = qkvo[:, :2560], qkvo[:, 2560:]
    head_own, ids = lax.optimization_barrier((frozen_output_table, ids))
    head = lax.all_gather(head_own, SEQ, axis=1, tiled=True)
    small = small.reshape(128, 1024)
    down_full = small[:, :512].reshape(128, 32, 16).transpose(1, 0, 2).reshape(32, 2048)
    gain = small[:, 512:560].reshape(128, 3, 16).transpose(1, 0, 2).reshape(3, 2048)
    up_full = small[:, 560:848].reshape(128, 8, 36).transpose(1, 0, 2).reshape(8, 4608)
    a_low = down_full.astype(jnp.bfloat16)
    b_low = up_full.astype(jnp.bfloat16)
    a_in, a_out = a_low[:24], a_low[24:]
    factor_of = (jnp.arange(2560) >= 2048).astype(jnp.int32) + (jnp.arange(2560) >= 2304)
    b_in = jnp.where(
        (jnp.arange(24) // 8)[:, None] == factor_of[None, :],
        jnp.concatenate([b_low[:, :2560]] * 3, 0),
        jnp.zeros((), jnp.bfloat16),
    )
    b_out = b_low[:, 2560:]

    places = loss_position_index.reshape(2, 8, SEQ_N, 32)
    spots = jnp.arange(SEQ_N)[:, None] * TOK + places
    counted = spots < row_used_length[..., None, None]
    below = jnp.sum(
        (document_slot_index[..., None] < jnp.arange(1, 3)).astype(jnp.int32), axis=2
    )
    seg_at = jnp.sum(
        (spots[..., None] >= below[:, :, None, None, :]).astype(jnp.int32), axis=-1
    )
    member = counted[..., None] & (seg_at[..., None] == jnp.arange(3))
    counts = jnp.sum(member.astype(jnp.int32), axis=(2, 3))
    document_total = jnp.sum((counts > 0).astype(jnp.float32))
    own_places = lax.dynamic_index_in_dim(places, seq_here, 2, keepdims=False)
    own_counted = lax.dynamic_index_in_dim(counted, seq_here, 2, keepdims=False)
    own_seg = lax.dynamic_index_in_dim(seg_at, seq_here, 2, keepdims=False)
    per_doc = jnp.sum(
        jnp.where(own_seg[..., None] == jnp.arange(3), counts[:, :, None, :], 0), axis=-1
    )
    own_weight = jnp.where(own_counted, 1.0 / jnp.maximum(per_doc, 1).astype(jnp.float32), 0.0)
    weight_flat = own_weight.transpose(1, 0, 2).reshape(-1)
    row_places = lax.dynamic_index_in_dim(own_places, fsdp_here, 1, keepdims=False)
    chosen_at = (row_places + jnp.arange(2)[:, None] * TOK).reshape(64)
    pick = (chosen_at[:, None] == jnp.arange(128)[None, :]).astype(jnp.float32)

    ids = ids[:, :, :TOK].reshape(SEQ_N, 2, 8, TOK)
    row_ids = lax.dynamic_index_in_dim(ids, fsdp_here, 2, keepdims=False).reshape(SEQ_N, 128)
    half = 32
    freqs = ROPE_BASE ** (-2.0 * jnp.arange(half).astype(jnp.float32) / 64)
    angles = (seq_here * TOK + jnp.arange(TOK)).astype(jnp.float32)[:, None] * freqs[None, :]
    cosine = jnp.tile(jnp.cos(angles), (1, 16))
    sine = jnp.sin(angles)
    sine = jnp.tile(jnp.concatenate([-sine, sine], 1), (1, 8))
    own_docs = lax.dynamic_index_in_dim(document_slot_index, fsdp_here, 1, keepdims=False)
    padded = jnp.concatenate([jnp.full((2, 4 * TOK), -1, jnp.int32), own_docs], 1)
    key_seg = lax.dynamic_slice_in_dim(padded, seq_here * TOK, 5 * TOK, 1)[:, None, :]
    query_seg = key_seg[:, 0, 4 * TOK :][:, :, None]
    start = (seq_here * TOK).reshape(1)
    (
        x_start, normed_one, adapter_in, queries, window, attended, adapter_mid, x_mid, normed_two,
    ) = attention_block(
        table, row_ids, qkvo, a_low, b_in, b_out, gain, cosine, sine, query_seg, key_seg,
        head_group_offsets, 2,
    )
    gate_up_w = [gate_up_w.reshape(2048, -1)]
    down_w = [down_w.reshape(PAD_FF // 4, -1)]

    hidden_sum, gate_up = feed_forward(normed_two, gate_up_w, down_w, None, 12, "feed_forward")
    x_end = x_mid + hidden_sum
    normed_end = (x_end * norm_scale(x_end) * gain[2]).astype(jnp.bfloat16)

    chosen = dot(pick.astype(jnp.bfloat16), normed_end).astype(jnp.bfloat16)
    local_target = target_token_index.transpose(1, 0, 2).reshape(512, 1) - fsdp_here * vocab_dev
    local_target = jnp.where(local_target < vocab_dev, local_target, -1)
    weight_column = weight_flat.reshape(512, 1)
    d_chosen, loss_tile = head_step(
        chosen, head, local_target, weight_column, weight_column / document_total, 4
    )

    upstream = lax.dot_general(pick, d_chosen, (((0,), (0,)), ((), ())), precision=HIGHEST)
    d_end, gain_end = norm_back(x_end, gain[2], upstream)
    d_normed = feed_forward(
        d_end.astype(jnp.bfloat16), gate_up_w, down_w, gate_up, 13, "feed_forward_back"
    )
    back_two, gain_mid = norm_back(x_mid, gain[1], d_normed)
    d_mid = d_end + back_two

    d_branch = d_mid.astype(jnp.bfloat16)
    d_adapter_mid = (ADAPTER_SCALE * nt(d_branch, b_out)).astype(jnp.bfloat16)
    d_attended = (nt(d_branch, w_out) + dot(d_adapter_mid, a_out)).astype(jnp.bfloat16)
    up_gradient_out = ADAPTER_SCALE * tn(adapter_mid, d_branch)
    down_gradient_out = tn(d_adapter_mid, attended)
    d_queries, d_far, d_own = attend_back(
        queries, window, d_attended, cosine, sine, query_seg, key_seg, start, head_group_offsets
    )
    d_key_value = key_value_back(d_far, d_own, cosine, sine, 7)
    d_packed = jnp.concatenate([d_queries, d_key_value], 1)
    d_adapter_in = (ADAPTER_SCALE * nt(d_packed, b_in)).astype(jnp.bfloat16)
    up_gradient_in = ADAPTER_SCALE * jnp.concatenate(
        [
            tn(adapter_in[:, 0:8], d_packed[:, :2048]),
            tn(adapter_in[:, 8:16], d_packed[:, 2048:2304]),
            tn(adapter_in[:, 16:24], d_packed[:, 2304:]),
        ],
        1,
    )
    down_gradient_in = tn(d_adapter_in, normed_one)
    back_one, gain_start = norm_back(
        x_start, gain[0], nt(d_packed, w_qkv) + dot(d_adapter_in, a_in)
    )
    d_start = (d_mid + back_one).astype(jnp.bfloat16)

    left = jnp.concatenate(
        [
            down_gradient_in,
            down_gradient_out,
            jnp.stack([gain_start, gain_mid, gain_end]),
            jnp.zeros((5, 2048), jnp.float32),
        ],
        0,
    )
    right = jnp.concatenate([up_gradient_in, up_gradient_out], 1)
    all_ids = ids.transpose(2, 0, 1, 3).reshape(16, 1024) - fsdp_here * vocab_dev
    grad_embed, left_sum, right_sum, totals = token_gradients(
        d_start, left, right, all_ids, loss_tile, vocab_dev, 8
    )
    document_loss_sum = totals[0, 65]

    own_left = lax.dynamic_slice_in_dim(left_sum, fsdp_here * 16, 16, 1)
    own_right = lax.dynamic_slice_in_dim(
        right_sum, 32 * ((9 * seq_here) % 4) + fsdp_here * 36, 36, 1
    )
    columns = ((seq_here * 8 + fsdp_here) * 36 + jnp.arange(36)).reshape(1, 36)
    (
        scalars,
        down_factor_gradient,
        up_factor_gradient,
        updated_gain_first_moment,
        updated_gain_second_moment,
        updated_norm_gains,
        updated_rank_statistics,
        updated_down_width_statistics,
        updated_up_width_statistics,
        updated_down_factors,
        updated_up_factors,
    ) = small_updates(
        totals,
        own_left,
        own_right,
        rank_side_statistics,
        adapter_down_factors,
        adapter_up_factors,
        down_width_statistics,
        up_width_statistics.reshape(1, 36),
        norm_gain_vectors,
        norm_gain_first_moment,
        norm_gain_second_moment,
        columns,
    )
    updated_up_width_statistics = updated_up_width_statistics.reshape(36)
    global_gradient_norm = scalars[0, 0]
    grad_embed = grad_embed * scalars[0, 1]
    unused_first, updated_embedding_second_moment, updated_embedding_table = adam_update(
        embedding, embedding_first_moment, embedding_second_moment, grad_embed, RATE_EMBED
    )
    return (
        document_loss_sum,
        document_total,
        global_gradient_norm,
        grad_embed,
        updated_embedding_second_moment,
        updated_embedding_table,
        updated_gain_first_moment,
        updated_gain_second_moment,
        updated_norm_gains,
        down_factor_gradient,
        up_factor_gradient,
        updated_rank_statistics,
        updated_down_width_statistics,
        updated_up_width_statistics,
        updated_down_factors,
        updated_up_factors,
    )


def solution(mesh):
    torus = Mesh(
        mesh.devices.reshape(2, 4, 2, 2, 2, 2), SEQ_FSDP
    )
    return jax.shard_map(
        per_device,
        mesh=torus,
        in_specs=(
            P(None, None, SEQ),
            P(None, None, SEQ),
            P(),
            P(),
            P(),
            P(),
            P(FSDP, SEQ),
            P(FSDP, SEQ),
            P(FSDP, SEQ),
            P(FSDP, SEQ),
            P(SEQ_FSDP, None),
            P(SEQ_FSDP, None),
            P(SEQ_FSDP, None),
            P(SEQ_FSDP, None),
            P(None, SEQ_FSDP),
            P(None, SEQ_FSDP),
            P(None, SEQ_FSDP),
            P(None, SEQ_FSDP),
            P(None, SEQ_FSDP),
            P(),
            P(None, SEQ_FSDP),
            P(SEQ_FSDP),
        ),
        out_specs=(
            P(),
            P(),
            P(),
            P(FSDP, SEQ),
            P(FSDP, SEQ),
            P(FSDP, SEQ),
            P(None, SEQ_FSDP),
            P(None, SEQ_FSDP),
            P(None, SEQ_FSDP),
            P(None, SEQ_FSDP),
            P(None, SEQ_FSDP),
            P(),
            P(None, SEQ_FSDP),
            P(SEQ_FSDP),
            P(None, SEQ_FSDP),
            P(None, SEQ_FSDP),
        ),
        check_vma=False,
    )
```

```python
import functools

import jax
import jax.numpy as jnp
from jax import lax
from jax.experimental import pallas as pl
from jax.experimental.pallas import tpu as pltpu
from jax.sharding import Mesh
from jax.sharding import PartitionSpec as P

STEP = 5
GROUP = 256
SEQ = ("seq_0", "seq_1", "seq_2")
FSDP = ("fsdp_0", "fsdp_1", "fsdp_2")
SEQ_FSDP = SEQ + FSDP
SEQ_N = 16
FSDP_N = 8
TOK = 64
PAD_FF = 6144
NORM_EPS = 1e-05
ADAPTER_SCALE = 2.0
ROPE_BASE = 10000.0
CLIP_MAX = 0.001
FIRST_DECAY = 0.5
SECOND_DECAY = 0.5
RATE_EMBED = 0.3
RATE_GAIN = 0.1
LEARN_RATE_DOWN = 0.1
LEARN_RATE_UP = 0.5
WEIGHT_DECAY = 0.01
ADAM_EPS = 1e-12
HIGHEST = lax.Precision.HIGHEST
MESH_ID = pl.DeviceIdType.MESH
ANY = pl.BlockSpec(memory_space=pl.ANY)
VMEM = pl.BlockSpec(memory_space=pltpu.VMEM)
SMEM = pl.BlockSpec(memory_space=pltpu.SMEM)
DMA = pltpu.SemaphoreType.DMA
VMEM_LIMIT = 56 * 1024 * 1024


def seq_me():
    return lax.axis_index("seq_0") * 8 + lax.axis_index("seq_1") * 2 + lax.axis_index("seq_2")


def z_me():
    return lax.axis_index("fsdp_0") * 2 + lax.axis_index("fsdp_1")


def z_at(i):
    return {"fsdp_0": i // 2, "fsdp_1": i % 2}


def fsdp_me():
    return z_me() * 2 + lax.axis_index("fsdp_2")


def seq_at(i):
    return {"seq_0": i // 8, "seq_1": (i // 2) % 4, "seq_2": i % 2}


def fsdp_at(i):
    return {**z_at(i // 2), "fsdp_2": i % 2}


def remote_call(body, out_shape, in_specs, out_specs, scratch, collective_id, name):
    return pl.pallas_call(
        body,
        out_shape=out_shape,
        in_specs=in_specs,
        out_specs=out_specs,
        scratch_shapes=scratch,
        compiler_params=pltpu.CompilerParams(
            collective_id=collective_id, has_side_effects=True, vmem_limit_bytes=VMEM_LIMIT
        ),
        name=name,
    )


ALL16 = range(1, SEQ_N)
ALL8 = range(1, FSDP_N)


ORDER = (
    "q2", "s", "q0", "d0", "t0", "q1", "q0", "q2", "d1", "d0", "s", "q2",
    "q1", "g0", "q1", "q0", "q2", "d1", "g1", "q0", "s", "q2", "q2", "g0",
    "t0", "t1", "g1", "q2", "t1", "q1", "g1", "d0", "q2", "g0", "s", "g1",
    "q0", "d0", "g0", "s", "d1", "d1", "s", "q1", "q2", "q1", "q1", "s",
    "q0", "t0", "d1", "g1", "d0", "q0", "g0", "t0", "q1", "g0", "q1", "d1",
    "d1", "t0", "g1", "g0", "q2", "q0", "g1", "d0", "q0", "s", "s", "d1",
    "t1", "d0", "q1", "t1", "q0", "g0", "s", "d0", "t1", "g1",
)
EVERY = slice(None)


class Post:
    def __init__(self, sem, count):
        self.sem, self.count, self.used, self.sent, self.late = sem, count, 0, [], []

    def fresh(self):
        self.used += 1
        assert self.used <= self.count, self.used
        return self.sem.at[self.used - 1]

    def start(self, src, dst, ssem, rsem, device):
        copy = pltpu.make_async_remote_copy(
            src_ref=src, dst_ref=dst, send_sem=ssem, recv_sem=rsem,
            device_id=device, device_id_type=MESH_ID,
        )
        copy.start()
        return copy

    def send(self, src, dst, device):
        copy = self.start(src, dst, self.fresh(), self.fresh(), device)
        self.sent.append(copy)
        return copy

    def finish(self):
        for copy in self.sent:
            copy.wait_send()
        for mark, view in self.late:
            pltpu.make_async_copy(view, view, mark).wait()


def greet_devices(devices):
    barrier = pltpu.get_barrier_semaphore()
    for device in devices:
        pl.semaphore_signal(barrier, inc=1, device_id=device, device_id_type=MESH_ID)
    pl.semaphore_wait(barrier, len(devices))


def fsdp_peers():
    me = fsdp_me()
    return [fsdp_at((me + k) % FSDP_N) for k in ALL8]


def seq_peers():
    me = seq_me()
    return [seq_at((me + k) % SEQ_N) for k in ALL16]


def relay(post, out, first, second, first_a, first_b):
    z, yl = z_me(), lax.axis_index("fsdp_2")
    partner, up, down = {"fsdp_2": 1 - yl}, z_at((z + 1) % 4), z_at((z + 3) % 4)
    before, after, far = (z + 3) % 4, (z + 1) % 4, (z + 2) % 4

    def at(zz, y, part=()):
        return out.at[(zz * 2 + y,) + part]

    def send(zz, y, part, device):
        view = at(zz, y, part)
        return post.send(view, view, device)

    to_partner = send(z, yl, (), partner)
    ring_up = send(z, yl, (), up)
    ring_down = send(z, yl, (), down)
    yield
    to_partner.wait_recv()
    other_up = send(z, 1 - yl, first, up)
    other_down = send(z, 1 - yl, first, down)
    yield
    ring_up.wait_recv()
    far_up = send(before, yl, first, up)
    across = [send(before, yl, second, partner)]
    yield
    ring_down.wait_recv()
    far_down = send(after, yl, second, down)
    across.append(send(after, yl, second, partner))
    yield
    other_up.wait_recv()
    last_up = send(before, 1 - yl, first_a, up)
    yield
    other_down.wait_recv()
    last_down = send(after, 1 - yl, first_b, down)
    yield
    far_up.wait_recv()
    far_down.wait_recv()
    across.append(send(far, yl, second, partner))
    yield
    last_up.wait_recv()
    last_down.wait_recv()
    for copy in across:
        copy.wait_recv()


def no_hand(view):
    return None


class Ways:
    def __init__(self, post):
        self.post = post
        self.yh, self.x, self.c = (lax.axis_index(a) for a in SEQ)
        self.z, self.yl = z_me(), lax.axis_index("fsdp_2")
        self.where = {"x": self.x, "y": 2 * self.yh + self.yl, "z": self.z}
        z, c = self.z, self.c
        self.column = [
            ((z + dz) % 4, (c + dc) % 2, dz, dc) for dz in range(4) for dc in range(2) if dz or dc
        ]

    def beside(self, axis, step):
        at = (self.where[axis] + step + 4) % 4
        if axis == "x":
            return {"seq_1": at}
        if axis == "z":
            return z_at(at)
        return {"seq_0": at // 2, "fsdp_2": at % 2}

    def all_devices(self):
        return (
            [self.beside("y", 1), self.beside("y", -1)]
            + [{**z_at(zz), "seq_2": cc} for zz, cc, dz, dc in self.column if dz]
            + seq_peers()
        )

    def arrived(self, ref, rsem):
        pltpu.make_async_copy(ref, ref, rsem).wait()

    def rings(self, block, order, sizes, halves, across):
        post = self.post
        for n, axis in enumerate(order):
            done = order[:n]
            at = self.where[axis]
            before, after, far = (at + 3) % 4, (at + 1) % 4, (at + 2) % 4
            send, from_before, from_after, far_first = (post.fresh() for _ in range(4))
            post.late.append((send, sizes[axis, n]))
            own = block(done, axis, at, None)
            post.start(own, own, send, from_before, self.beside(axis, 1))
            post.start(own, own, send, from_after, self.beside(axis, -1))
            yield
            got = block(done, axis, before, None)
            self.arrived(got, from_before)
            half = block(done, axis, before, 0)
            post.start(half, half, send, far_first, self.beside(axis, 1))
            across(got)
            yield
            got = block(done, axis, after, None)
            self.arrived(got, from_after)
            if halves:
                far_second = post.fresh()
                half = block(done, axis, after, 1)
                post.start(half, half, send, far_second, self.beside(axis, -1))
            across(got)
            yield
            self.arrived(block(done, axis, far, 0), far_first)
            if halves:
                self.arrived(block(done, axis, far, 1), far_second)
            across(block(done, axis, far, None))

    def place(self, done, axis, at):
        spot = {"yh": self.yh, "x": self.x, "z": self.z, "yl": self.yl}
        for a in done:
            if a == "y":
                spot["yh"] = spot["yl"] = EVERY
            else:
                spot[a] = EVERY
        if axis == "y":
            spot["yh"], spot["yl"] = at // 2, at % 2
        elif axis is not None:
            spot[axis] = at
        return spot

    def everything(self, ref, order, tails, halves=True):
        post, c = self.post, self.c

        def block(done, axis, at, half):
            spot = self.place(done, axis, at)
            tail = tails[0 if half is None else half + 1]
            return ref.at[(spot["yh"], spot["x"], c, spot["z"], spot["yl"]) + tail]

        across_s, across_r = post.fresh(), post.fresh()
        post.late.append((across_s, ref.at[(EVERY, EVERY, c, EVERY, EVERY) + tails[0]]))
        post.late.append((across_r, ref.at[(EVERY, EVERY, 1 - c, EVERY, EVERY) + tails[0]]))

        def across(view):
            post.start(view, view, across_s, across_r, {"seq_2": 1 - c})

        three = pl.ds(0, 3)
        sizes = {}
        for axis in "xyz":
            sizes[axis, 0] = ref.at[(0, 0, 0, three, 0) + tails[0]]
            sizes[axis, 1] = ref.at[(0, pl.ds(0, 2), 0, three, EVERY) + tails[0]]
            sizes[axis, 2] = ref.at[(EVERY, EVERY, 0, three, EVERY) + tails[0]]
        across(block([], None, None, None))
        yield from self.rings(block, order, sizes, halves, across)

    def gate_up(self, src, ref, order, start, width):
        post = self.post
        quarter = src.shape[1] // 4
        yh, x, c, z, yl = self.yh, self.x, self.c, self.z, self.yl
        tails = [
            (EVERY, pl.ds(start, width)),
            (EVERY, pl.ds(start, width // 2)),
            (EVERY, pl.ds(start + width // 2, width // 2)),
        ]

        def block(done, axis, at, half):
            spot = self.place(done, axis, at)
            tail = tails[0 if half is None else half + 1]
            return ref.at[(spot["yh"], spot["x"], EVERY, EVERY, spot["yl"]) + tail]

        marks = []
        for zz, cc, dz, dc in self.column:
            send, recv = post.fresh(), post.fresh()
            first = pl.multiple_of((2 * (zz % 2) + cc) * quarter + start, 128)
            here = ref.at[(yh, x, c, z, yl) + tails[0]]
            post.start(src.at[:, pl.ds(first, width)], here, send, recv, {**z_at(zz), "seq_2": cc})
            post.late.append((send, here))
            marks.append((ref.at[(yh, x, (c + dc) % 2, (z + 4 - dz) % 4, yl) + tails[0]], recv))
        yield
        for view, recv in marks:
            self.arrived(view, recv)
        three = pl.ds(0, 3)
        sizes = {}
        for axis in "xy":
            sizes[axis, 0] = ref.at[(0, three, EVERY, EVERY, 0) + tails[0]]
            sizes[axis, 1] = ref.at[(EVERY, three, EVERY, EVERY, EVERY) + tails[0]]
        yield from self.rings(block, order, sizes, True, no_hand)

    def down(self, ref, order, start, width):
        post = self.post
        yh, x, z, yl = self.yh, self.x, self.z, self.yl
        tails = [
            (EVERY, pl.ds(start, width)),
            (EVERY, pl.ds(start, width // 2)),
            (EVERY, pl.ds(start + width // 2, width // 2)),
        ]
        zh = z // 2

        def block(done, axis, at, half):
            spot = self.place(done, axis, at)
            tail = tails[0 if half is None else half + 1]
            return ref.at[(spot["yh"], spot["x"], EVERY, spot["yl"]) + tail]

        send, recv = post.fresh(), post.fresh()
        here = ref.at[(yh, x, zh, yl) + tails[0]]
        post.start(here, here, send, recv, z_at((z + 2) % 4))
        post.late.append((send, here))
        yield
        self.arrived(ref.at[(yh, x, 1 - zh, yl) + tails[0]], recv)
        three = pl.ds(0, 3)
        sizes = {}
        for axis in "xy":
            sizes[axis, 0] = ref.at[(0, three, EVERY, 0) + tails[0]]
            sizes[axis, 1] = ref.at[(EVERY, three, EVERY, EVERY) + tails[0]]
        yield from self.rings(block, order, sizes, True, no_hand)

    def table(self, ref, low, high):
        post, z, yl = self.post, self.z, self.yl
        middle = (low + high) // 32 * 16
        part = (pl.ds(low, high - low), pl.ds(low, middle - low), pl.ds(middle, high - middle))
        send_y, recv_y = post.fresh(), post.fresh()
        post.late.append((send_y, ref.at[0, part[0]]))
        own = ref.at[2 * z + yl, part[0]]
        post.start(own, own, send_y, recv_y, {"fsdp_2": 1 - yl})
        yield
        self.arrived(ref.at[2 * z + 1 - yl, part[0]], recv_y)

        def block(done, axis, at, half):
            return ref.at[pl.ds(2 * at, 2), part[0 if half is None else half + 1]]

        sizes = {("z", 0): ref.at[pl.ds(0, 6), part[0]]}
        yield from self.rings(block, ("z",), sizes, True, no_hand)

    def own_gate_up(self, src, ref):
        quarter = ref.shape[-1]
        first = pl.multiple_of((2 * (self.z % 2) + self.c) * quarter, 128)
        return src.at[:, pl.ds(first, quarter)], ref.at[self.yh, self.x, self.c, self.z, self.yl]


def local_copies(pairs, post):
    copies = [pltpu.make_async_copy(src, dst, post.fresh()) for src, dst in pairs]
    for copy in copies:
        copy.start()
    return copies


def gather_weights(qkvo, small, table, ids, gate_up, down):
    groups, units = 8, gate_up.shape[1] // 8
    spread = units // 44 * 48
    quarter = groups * spread // 4
    out_shape = [
        jax.ShapeDtypeStruct((2, 4, 2, 4, 2, *qkvo.shape), qkvo.dtype),
        jax.ShapeDtypeStruct((2, 4, 2, 4, 2, *small.shape), small.dtype),
        jax.ShapeDtypeStruct((FSDP_N, *table.shape), table.dtype),
        jax.ShapeDtypeStruct((SEQ_N, *ids.shape), ids.dtype),
        jax.ShapeDtypeStruct((2, 4, 2, 4, 2, gate_up.shape[0], quarter), gate_up.dtype),
        jax.ShapeDtypeStruct((2, 4, 2, 2, *down.shape), down.dtype),
    ]
    sem_count = 320

    def body(*refs):
        ins, outs, ordered, picks, sem = refs[:6], refs[6:12], refs[12], refs[13], refs[14]
        post = Post(sem, sem_count)
        ways = Ways(post)
        yh, x, c, z, yl = ways.yh, ways.x, ways.c, ways.z, ways.yl
        seq = seq_me()
        local = local_copies(
            [
                (ins[0], outs[0].at[yh, x, c, z, yl]),
                (ins[1], outs[1].at[yh, x, c, z, yl]),
                (ins[2], outs[2].at[z * 2 + yl]),
                (ins[3], outs[3].at[seq]),
                (ins[5], outs[5].at[yh, x, z // 2, yl]),
            ],
            post,
        )
        at = lax.broadcasted_iota(jnp.int32, (1, spread), 1)
        part, rest = at // (spread // 4), at % (spread // 4)
        unit = rest % 48
        here = rest // 48
        source = (
            (here // 4) * 16 + (part % 2) * 8 + ((here // 2) % 2) * 4 + (part // 2) * 2 + here % 2
        ) * 44 + unit
        source = jnp.where(unit < 44, source, -1)

        def pick(n, carry):
            start = pl.multiple_of(n * 128, 128)
            row = lax.broadcasted_iota(jnp.int32, (128, spread), 0) + start
            picks[pl.ds(start, 128), :] = (row == source).astype(jnp.float32).astype(jnp.bfloat16)
            return carry

        lax.fori_loop(0, units // 128, pick, 0)
        for n in range(groups):
            moved = jnp.dot(
                ins[4][:, n * units : (n + 1) * units], picks[...], preferred_element_type=jnp.float32
            ).astype(jnp.bfloat16)
            width = spread // 4
            for k in range(4):
                first = k * quarter + n * width
                ordered[:, first : first + width] = moved[:, k * width : (k + 1) * width]
        mine = ways.own_gate_up(ordered, outs[4])
        local += local_copies([mine], post)
        greet_devices(ways.all_devices())
        for copy in local:
            copy.wait()

        send, recv = post.fresh(), post.fresh()
        for device in seq_peers():
            post.start(ins[3], outs[3].at[seq], send, recv, device)
        post.late.append((send, outs[3].at[pl.ds(0, 15)]))
        post.late.append((recv, outs[3].at[pl.ds(0, 15)]))

        third = qkvo.shape[1] // 3
        streams = {
            "s": ways.everything(outs[1], "xyz", [(EVERY, EVERY)] * 2, False),
        }
        rows = table.shape[0]
        cuts = (0, 1984, rows)
        for n in range(len(cuts) - 1):
            streams["t%d" % n] = ways.table(outs[2], cuts[n], cuts[n + 1])
        half, wide = quarter // 2, down.shape[1] // 2
        for n, order in enumerate(("xy", "yx")):
            streams["g%d" % n] = ways.gate_up(ordered, outs[4], order, n * half, half)
            streams["d%d" % n] = ways.down(outs[5], order, n * wide, wide)
        for n, order in enumerate(('yxz', 'xyz', 'zyx')):
            streams["q%d" % n] = ways.everything(
                outs[0], order,
                [
                    (EVERY, pl.ds(n * third, third)),
                    (EVERY, pl.ds(n * third, third // 2)),
                    (EVERY, pl.ds(n * third + third // 2, third // 2)),
                ],
            )
        for name in ORDER:
            next(streams[name], None)
        for name in sorted(streams):
            assert next(streams[name], "end") == "end", name
        post.finish()

    return remote_call(
        body, out_shape, [ANY] * 4 + [VMEM, ANY], [ANY] * 6,
        [
            pltpu.VMEM((gate_up.shape[0], 4 * quarter), gate_up.dtype),
            pltpu.VMEM((units, spread), gate_up.dtype),
            DMA((sem_count,)),
        ],
        1, "gather_weights",
    )(qkvo, small, table, ids, gate_up, down)


def attention_block(
    table, ids, qkvo, a_low, b_in, b_out, gain, cosine, sine, query_seg, key_seg, shifts, collective_id
):
    vocab, width = table.shape[1:]
    rows_n = 2 * TOK
    sem_count = 64

    def body(
        table_hbm, ids_ref, qkvo_hbm, a_ref, bi_ref, bo_ref, gain_ref, cos_ref, sin_ref, qs_ref, ks_ref,
        shift_ref,
        x_out, n_out, u_out, q_out, kv_out, a_out, v_out, mid_out, two_out,
        stage, wide, rows, block, low, packed, own_kv, w_qkv, w_out, sem,
    ):
        post = Post(sem, sem_count)
        me = seq_me()
        loads = [post.fresh() for _ in range(2)]

        def staged(n):
            return pltpu.make_async_copy(table_hbm.at[n], stage.at[n % 2], loads[n % 2])

        staged(0).start()
        weights = local_copies(
            [
                (qkvo_hbm.at[:, pl.ds(0, 2560)], w_qkv),
                (qkvo_hbm.at[:, pl.ds(2560, 2048)], w_out),
            ],
            post,
        )
        greet_devices(seq_peers())
        for n in range(FSDP_N):
            if n + 1 < FSDP_N:
                staged(n + 1).start()
            staged(n).wait()
            wide[pl.ds(n * vocab, vocab), :] = stage[n % 2].astype(jnp.float32)

        spot = pl.ds(pl.multiple_of(me * width, width), width)

        def fetch(s):
            def step(t, carry):
                rows[pl.ds(t, 1), :] = wide[pl.ds(ids_ref[s, t], 1), :]
                return carry

            lax.fori_loop(0, rows_n, step, 0, unroll=16)

        moved = []
        for k in list(ALL16) + [0]:
            peer = (me + k) % SEQ_N
            fetch(peer)
            block[k] = rows[...].astype(jnp.bfloat16)
            if k:
                moved.append(post.send(block.at[k], low.at[:, spot], seq_at(peer)))
        own = pltpu.make_async_copy(block.at[0], low.at[:, spot], post.fresh())
        own.start()
        for copy in moved:
            copy.wait_recv()
        own.wait()

        start = low[...].astype(jnp.float32)
        x_out[...] = start
        scale = lax.rsqrt(jnp.mean(start * start, axis=-1, keepdims=True) + NORM_EPS)
        n_out[...] = (start * scale * gain_ref[0:1, :]).astype(jnp.bfloat16)
        inner = nt(n_out[...], a_ref[0:24, :]).astype(jnp.bfloat16)
        u_out[...] = inner
        weights[0].wait()

        def project(at):
            packed[:, at] = jnp.dot(
                n_out[...], w_qkv[:, at], preferred_element_type=jnp.float32
            ) + ADAPTER_SCALE * jnp.dot(u_out[...], bi_ref[:, at], preferred_element_type=jnp.float32)

        project(pl.ds(2048, 512))
        for n in range(2):
            some = slice(n * TOK, n * TOK + TOK)
            own_kv[n, :, 0:256] = turn(
                packed[some, 2048:2304], cos_ref[:, 0:256], sin_ref[:, 0:256]
            ).astype(jnp.bfloat16)
            own_kv[n, :, 256:512] = packed[some, 2304:2560].astype(jnp.bfloat16)
        keys = [
            post.send(
                own_kv, kv_out.at[:, pl.ds((4 - k) * TOK, TOK), :], seq_at((me + k) % SEQ_N)
            )
            for k in range(1, 5)
        ]
        kv_out[:, 4 * TOK :, :] = own_kv[...]

        def project_some(n, carry):
            project(pl.ds(pl.multiple_of(n * 512, 512), 512))
            return carry

        lax.fori_loop(0, 4, project_some, 0)
        for copy in keys:
            copy.wait_recv()

        first = me * TOK

        def attend_one(n, carry):
            some = pl.ds(pl.multiple_of(n * TOK, TOK), TOK)
            for h in range(4):
                cols = slice(512 * h, 512 * h + 512)
                turned = turn(packed[some, cols], cos_ref[...], sin_ref[...]).astype(jnp.bfloat16)
                q_out[some, cols] = turned
                mask = window_mask(first, qs_ref[n], ks_ref[n], shift_ref[h])
                probs = probabilities(
                    spread_heads(turned), kv_out[n, :, 64 * h : 64 * h + 64], mask
                )
                values = kv_out[n, :, 256 + 64 * h : 256 + 64 * h + 64]
                mixed = jnp.dot(
                    probs.astype(jnp.bfloat16), values, preferred_element_type=jnp.float32
                )
                a_out[some, cols] = join_heads(mixed).astype(jnp.bfloat16)
            return carry

        lax.fori_loop(0, 2, attend_one, 0)
        middle = nt(a_out[...], a_ref[24:32, :]).astype(jnp.bfloat16)
        v_out[...] = middle
        weights[1].wait()

        def project_out(n, carry):
            at = pl.ds(pl.multiple_of(n * 512, 512), 512)
            mid_out[:, at] = (
                x_out[:, at]
                + jnp.dot(a_out[...], w_out[:, at], preferred_element_type=jnp.float32)
                + ADAPTER_SCALE
                * jnp.dot(v_out[...], bo_ref[:, at], preferred_element_type=jnp.float32)
            )
            return carry

        lax.fori_loop(0, 4, project_out, 0)
        middle_rows = mid_out[...]
        scale = lax.rsqrt(jnp.mean(middle_rows * middle_rows, axis=-1, keepdims=True) + NORM_EPS)
        two_out[...] = (middle_rows * scale * gain_ref[1:2, :]).astype(jnp.bfloat16)
        post.finish()

    def shape(*dims, dtype=jnp.bfloat16):
        return jax.ShapeDtypeStruct(dims, dtype)

    return remote_call(
        body,
        [
            shape(rows_n, 2048, dtype=jnp.float32),
            shape(rows_n, 2048),
            shape(rows_n, 24),
            shape(rows_n, 2048),
            shape(2, 5 * TOK, 512),
            shape(rows_n, 2048),
            shape(rows_n, 8),
            shape(rows_n, 2048, dtype=jnp.float32),
            shape(rows_n, 2048),
        ],
        [ANY, SMEM, ANY] + [VMEM] * 8 + [SMEM],
        [VMEM] * 9,
        [
            pltpu.VMEM((2, vocab, width), jnp.bfloat16),
            pltpu.VMEM((FSDP_N * vocab, width), jnp.float32),
            pltpu.VMEM((rows_n, width), jnp.float32),
            pltpu.VMEM((SEQ_N, rows_n, width), jnp.bfloat16),
            pltpu.VMEM((rows_n, 2048), jnp.bfloat16),
            pltpu.VMEM((rows_n, 2560), jnp.float32),
            pltpu.VMEM((2, TOK, 512), jnp.bfloat16),
            pltpu.VMEM((2048, 2560), jnp.bfloat16),
            pltpu.VMEM((2048, 2048), jnp.bfloat16),
            DMA((sem_count,)),
        ],
        collective_id,
        "attention_block",
    )(table, ids, qkvo, a_low, b_in, b_out, gain, cosine, sine, query_seg, key_seg, shifts)


def chosen_rows(chosen, collective_id):
    def body(src, out, sem):
        post = Post(sem, 24)
        out[fsdp_me()] = src[...]
        greet_devices(fsdp_peers())
        for _ in relay(
            post, out, (pl.ds(0, 32),), (pl.ds(32, 32),), (pl.ds(0, 16),), (pl.ds(16, 16),)
        ):
            pass
        post.finish()

    return remote_call(
        body,
        jax.ShapeDtypeStruct((FSDP_N, *chosen.shape), chosen.dtype),
        [VMEM], VMEM, [DMA((24,))], collective_id, "chosen_rows",
    )(chosen)


def head_step(rows, head, target, weight, scaled, collective_id):
    vocab, width = head.shape
    padded = -(-vocab // 512) * 512
    tiles = padded // 512

    def body(
        rows_ref, head_hbm, target_ref, weight_ref, scaled_ref, out, loss, hd, raised, d_logits, prod,
        got, stat, stats, sem, lsem,
    ):
        post = Post(sem, 60)
        me = fsdp_me()
        load = pltpu.make_async_copy(head_hbm, hd.at[pl.ds(0, vocab)], lsem)
        load.start()
        greet_devices(fsdp_peers())
        hd[vocab:, :] = jnp.zeros((padded - vocab, width), jnp.bfloat16)
        load.wait()
        target_at = target_ref[...]

        def logits(n, carry):
            top, picked = carry
            at = pl.multiple_of(n * 512, 512)
            tile = nt(rows_ref[...], hd[pl.ds(at, 512), :])
            column = lax.broadcasted_iota(jnp.int32, (512, 512), 1) + at
            tile = jnp.where(column < vocab, tile, -1e30)
            raised[:, pl.ds(at, 512)] = tile
            top = jnp.maximum(top, jnp.max(tile, axis=1, keepdims=True))
            hit = jnp.where(column == target_at, tile, 0.0)
            return top, picked + jnp.sum(hit, axis=1, keepdims=True)

        top, picked = lax.fori_loop(
            0, tiles, logits, (jnp.full((512, 1), -1e30, jnp.float32), jnp.zeros((512, 1), jnp.float32))
        )

        def exponents(n, total):
            at = pl.ds(pl.multiple_of(n * 512, 512), 512)
            tile = jnp.exp(raised[:, at] - top)
            raised[:, at] = tile
            return total + jnp.sum(tile, axis=1, keepdims=True)

        total = lax.fori_loop(0, tiles, exponents, jnp.zeros((512, 1), jnp.float32))
        lane = lax.broadcasted_iota(jnp.int32, (512, 128), 1)
        both = jnp.where(lane == 0, top, jnp.where(lane == 1, total, 0.0))
        stat[...] = jnp.transpose(both)[0:8, :]
        copies = [
            post.send(stat, stats.at[k - 1], fsdp_at((me + k) % FSDP_N)) for k in ALL8
        ]
        for copy in copies:
            copy.wait_recv()
        top_all = stat[0:1, :]
        for n in range(7):
            top_all = jnp.maximum(top_all, stats[n, 0:1, :])
        sum_all = stat[1:2, :] * jnp.exp(stat[0:1, :] - top_all)
        for n in range(7):
            sum_all = sum_all + stats[n, 1:2, :] * jnp.exp(stats[n, 0:1, :] - top_all)
        log_row = top_all + jnp.log(sum_all)
        log_norm = jnp.transpose(jnp.broadcast_to(log_row, (128, 512)))[:, 0:1]
        weights = weight_ref[...]
        mine = lax.broadcasted_iota(jnp.int32, (512, 1), 0) // 64 == me
        value = jnp.sum(jnp.where(mine, log_norm * weights, 0.0) - weights * picked, axis=0, keepdims=True)
        loss[...] = jnp.broadcast_to(value, (8, 128))
        scale = scaled_ref[...]
        factor = scale * jnp.exp(top - log_norm)

        def slopes(n, carry):
            at = pl.multiple_of(n * 512, 512)
            column = lax.broadcasted_iota(jnp.int32, (512, 512), 1) + at
            hit = jnp.where(column == target_at, scale, 0.0)
            d_logits[:, pl.ds(at, 512)] = (factor * raised[:, pl.ds(at, 512)] - hit).astype(jnp.bfloat16)
            return carry

        lax.fori_loop(0, tiles, slopes, 0)
        half, inner = lax.axis_index("fsdp_0"), me % 4
        sums = []
        for n, part in enumerate((1 - half, half)):
            start = pl.multiple_of(part * 256, 256)

            def product(t, carry):
                at = pl.ds(pl.multiple_of(t * 512, 512), 512)
                tile = jnp.dot(
                    d_logits[pl.ds(start, 256), :], hd[:, at], preferred_element_type=jnp.float32
                )
                prod[pl.ds(part * 4, 4), :, at] = tile.astype(jnp.bfloat16).reshape(4, 64, 512)
                return carry

            lax.fori_loop(0, width // 512, product, 0)
            for j in range(n, 4):
                peer = part * 4 + (inner + j) % 4
                sums.append(post.send(prod.at[peer], got.at[4 * n + j - n], fsdp_at(peer)))
        out[...] = prod[me].astype(jnp.float32)
        for n, copy in enumerate(sums):
            copy.wait_recv()
            out[...] += got[n].astype(jnp.float32)
        post.finish()

    return remote_call(
        body,
        [
            jax.ShapeDtypeStruct((64, width), jnp.float32),
            jax.ShapeDtypeStruct((8, 128), jnp.float32),
        ],
        [VMEM, ANY, VMEM, VMEM, VMEM],
        [VMEM, VMEM],
        [
            pltpu.VMEM((padded, width), jnp.bfloat16),
            pltpu.VMEM((512, padded), jnp.float32),
            pltpu.VMEM((512, padded), jnp.bfloat16),
            pltpu.VMEM((8, 64, width), jnp.bfloat16),
            pltpu.VMEM((7, 64, width), jnp.bfloat16),
            pltpu.VMEM((8, 512), jnp.float32),
            pltpu.VMEM((7, 8, 512), jnp.float32),
            DMA((60,)),
            DMA,
        ],
        collective_id,
        "head_step",
    )(rows, head, target, weight, scaled)


def token_gradients(d_start, left, right, ids, loss, vocab, collective_id):
    width = 128
    low_n, tile = 1024, 1024

    def body(
        src, left_ref, right_ref, ids_ref, loss_ref, out, left_out, right_out, totals_out, held, left_parts,
        right_parts, left_mid, right_mid, left_more, right_more, total, spread, sums_a, parts_a, sums_b,
        parts_b, sem, lsem,
    ):
        post = Post(sem, 220)
        f, s = fsdp_me(), seq_me()
        z, yl = z_me(), lax.axis_index("fsdp_2")
        greet_devices(seq_peers() + fsdp_peers())

        def cols(p):
            return pl.ds(pl.multiple_of(p * width, width), width)

        def window(p):
            return pl.ds(pl.multiple_of((9 * p) // 4 * 128, 128), 384)

        moves, sums = [], []
        for k in ALL16:
            peer = (s + k) % SEQ_N
            moves.append(post.send(src.at[:, cols(peer)], held.at[f, s], seq_at(peer)))
        own = pltpu.make_async_copy(src.at[:, cols(s)], held.at[f, s], lsem)
        own.start()
        for k in ALL16:
            peer = (s + k) % SEQ_N
            sums.append(post.send(left_ref.at[:, cols(peer)], left_parts.at[k - 1], seq_at(peer)))
            sums.append(post.send(right_ref.at[:, window(peer)], right_parts.at[k - 1], seq_at(peer)))
        total[...] = jnp.zeros_like(total)
        for copy in moves:
            copy.wait_recv()
        own.wait()

        def add(block, halves=(0, 2)):
            def one(t, carry):
                ids_row = ids_ref[pl.ds(block * 2 + t, 1), :]
                high, low = ids_row >> 10, ids_row & 1023
                part = lax.broadcasted_iota(jnp.int32, (8, tile), 0)
                which = jnp.transpose((part == high).astype(jnp.float32))
                grad = held[block, pl.ds(t * 8, 8)].reshape(tile, width).astype(jnp.float32)
                for h in range(4):
                    spread[:, h * width : (h + 1) * width] = jnp.where(
                        which[:, h : h + 1] > 0.5, grad, 0.0
                    ).astype(jnp.bfloat16)

                def step(n, inner):
                    start = pl.multiple_of(n * 256, 256)
                    row = lax.broadcasted_iota(jnp.int32, (256, tile), 0) + start
                    hot = (row == low).astype(jnp.float32).astype(jnp.bfloat16)
                    total[pl.ds(start, 256), :] += jnp.dot(
                        hot, spread[...], preferred_element_type=jnp.float32
                    )
                    return inner

                lax.fori_loop(0, low_n // 256, step, 0)
                return carry

            lax.fori_loop(*halves, one, 0)

        every = slice(None)
        steps = relay(
            post, held, (pl.ds(0, 8),), (pl.ds(8, 8),), (pl.ds(0, 4),), (pl.ds(4, 4),)
        )
        before, after, far = (z + 3) % 4, (z + 1) % 4, (z + 2) % 4
        next(steps)
        add(f)
        next(steps)
        left_sum, right_sum = left_ref[:, cols(s)], right_ref[:, window(s)]
        for copy in sums:
            copy.wait_recv()
        for n in range(15):
            left_sum, right_sum = left_sum + left_parts[n], right_sum + right_parts[n]
        left_mid[...] = left_sum
        right_mid[...] = right_sum
        shares = []
        for k in ALL8:
            device = fsdp_at((f + k) % FSDP_N)
            shares.append(post.send(left_mid, left_more.at[k - 1], device))
            shares.append(post.send(right_mid, right_more.at[k - 1], device))
        next(steps)
        next(steps)
        add(z * 2 + 1 - yl)
        next(steps)
        next(steps)
        add(before * 2 + yl)
        add(after * 2 + yl)
        next(steps)
        for zz in (before, after):
            add(zz * 2 + 1 - yl, (0, 1))
        add(far * 2 + yl)
        assert next(steps, "end") == "end"
        for zz in (before, after):
            add(zz * 2 + 1 - yl, (1, 2))
        add(far * 2 + 1 - yl)
        squares = jnp.zeros((1, width), jnp.float32)
        for h in range(4):
            count = min(low_n, vocab - h * low_n)
            rows = total[0:count, h * width : (h + 1) * width]
            out[h * low_n : h * low_n + count, :] = rows
            squares = squares + jnp.sum(rows * rows, axis=0, keepdims=True)
        for copy in shares:
            copy.wait_recv()
        for n in range(7):
            left_sum, right_sum = left_sum + left_more[n], right_sum + right_more[n]
        left_out[...] = left_sum
        base = (9 * s) // 4 * 128
        column = lax.broadcasted_iota(jnp.int32, (8, 384), 1) + base
        right_own = jnp.where((column >= 288 * s) & (column < 288 * s + 288), right_sum, 0.0)
        right_out[...] = right_sum
        factor = (column >= 2048).astype(jnp.int32) + (column >= 2304) + (column >= 2560)
        blank = jnp.zeros((32, width), jnp.float32)

        def products(a, b):
            return lax.dot_general(
                a, b, (((1,), (1,)), ((), ())), preferred_element_type=jnp.float32, precision=HIGHEST
            )

        lane = lax.broadcasted_iota(jnp.int32, (8, width), 1)
        row = lax.broadcasted_iota(jnp.int32, (8, width), 0)
        factors = jnp.concatenate([left_sum[0:32], blank, blank, blank], axis=0)
        result = jnp.zeros((8, width), jnp.float32)
        for k in range(4):
            one = products(left_sum[8 * k : 8 * k + 8], factors)
            result = result + jnp.where(lane >> 3 == k, one, 0.0)
        for n in range(3):
            part = right_own[:, n * width : (n + 1) * width]
            which = factor[:, n * width : (n + 1) * width]
            spread_rows = [jnp.where(which == k, part, 0.0) for k in range(4)]
            result = result + products(
                part, jnp.concatenate([blank] + spread_rows + [blank, blank], axis=0)
            )
        small_squares = jnp.sum(
            jnp.sum(left_sum * left_sum, axis=0, keepdims=True), axis=1, keepdims=True
        ) + jnp.sum(jnp.sum(right_own * right_own, axis=0, keepdims=True), axis=1, keepdims=True)
        result = jnp.where((lane == 64) & (row == 0), small_squares, result)
        result = jnp.where(f == 0, result, 0.0)
        result = result + jnp.where(
            (lane == 64) & (row == 0), jnp.sum(squares, axis=1, keepdims=True), 0.0
        )
        result = result + jnp.where((lane == 65) & (row == 0), loss_ref[...], 0.0)
        sums_a[...] = result
        copies = [post.send(sums_a, parts_a.at[k - 1], seq_at((s + k) % SEQ_N)) for k in ALL16]
        for copy in copies:
            copy.wait_recv()
        for n in range(15):
            result = result + parts_a[n]
        sums_b[...] = result
        copies = [post.send(sums_b, parts_b.at[k - 1], fsdp_at((f + k) % FSDP_N)) for k in ALL8]
        for copy in copies:
            copy.wait_recv()
        for n in range(7):
            result = result + parts_b[n]
        totals_out[...] = result
        post.finish()

    return remote_call(
        body,
        [
            jax.ShapeDtypeStruct((vocab, width), jnp.float32),
            jax.ShapeDtypeStruct((40, width), jnp.float32),
            jax.ShapeDtypeStruct((8, 384), jnp.float32),
            jax.ShapeDtypeStruct((8, width), jnp.float32),
        ],
        [VMEM] * 5,
        [VMEM] * 4,
        [
            pltpu.VMEM((FSDP_N, SEQ_N, 128, width), jnp.bfloat16),
            pltpu.VMEM((15, 40, width), jnp.float32),
            pltpu.VMEM((15, 8, 384), jnp.float32),
            pltpu.VMEM((40, width), jnp.float32),
            pltpu.VMEM((8, 384), jnp.float32),
            pltpu.VMEM((7, 40, width), jnp.float32),
            pltpu.VMEM((7, 8, 384), jnp.float32),
            pltpu.VMEM((low_n, 4 * width), jnp.float32),
            pltpu.VMEM((tile, 4 * width), jnp.bfloat16),
            pltpu.VMEM((8, width), jnp.float32),
            pltpu.VMEM((15, 8, width), jnp.float32),
            pltpu.VMEM((8, width), jnp.float32),
            pltpu.VMEM((7, 8, width), jnp.float32),
            DMA((220,)),
            DMA,
        ],
        collective_id,
        "token_gradients",
    )(d_start, left, right, ids, loss)


def feed_forward(rows, gate_up_parts, down_parts, saved, collective_id, name):
    forward = saved is None
    count, width = rows.shape
    quarter = sum(part.shape[1] for part in gate_up_parts)
    units = quarter // 2
    parts_n = len(gate_up_parts)
    chunk = count // 2
    tile = 512

    def body(*refs):
        if forward:
            src, gu_hbm, dn_hbm = refs[0], refs[1 : 1 + parts_n], refs[1 + parts_n : 1 + 2 * parts_n]
            out, gu_out, held, gu, dn, saved_v, mid, part, give, got, sem = refs[1 + 2 * parts_n :]
        else:
            src, gu_hbm, dn_hbm = refs[0], refs[1 : 1 + parts_n], refs[1 + parts_n : 1 + 2 * parts_n]
            gu_in, out, held, gu, dn, saved_v, mid, part, give, got, sem = refs[1 + 2 * parts_n :]
        c = lax.axis_index("seq_2")
        sibling = {"seq_2": 1 - c}
        partner = {"fsdp_1": 1 - lax.axis_index("fsdp_1")}
        used = [0]

        def fresh():
            used[0] += 1
            return sem.at[used[0] - 1]

        load_gu, load_dn = [], []
        for copies, hbm, whole in ((load_gu, gu_hbm, gu), (load_dn, dn_hbm, dn)):
            at = 0
            for piece in hbm:
                view = whole.at[:, pl.ds(at, piece.shape[1])]
                copies.append(pltpu.make_async_copy(piece, view, fresh()))
                at += piece.shape[1]
        loads = [load_gu, load_dn]
        if not forward:
            load_dn.append(pltpu.make_async_copy(gu_in, saved_v, fresh()))
            loads = [load_dn, load_gu]
        for load in loads[0] + loads[1]:
            load.start()

        barrier = pltpu.get_barrier_semaphore()
        for device in (sibling, partner):
            pl.semaphore_signal(barrier, inc=1, device_id=device, device_id_type=MESH_ID)
        pl.semaphore_wait(barrier, 2)

        started = []

        def remote(src_ref, dst_ref, device):
            copy = pltpu.make_async_remote_copy(
                src_ref=src_ref, dst_ref=dst_ref, send_sem=fresh(), recv_sem=fresh(),
                device_id=device, device_id_type=MESH_ID,
            )
            copy.start()
            started.append(copy)
            return copy

        def lines(block, k=None):
            if k is None:
                return pl.ds(block * count, count)
            return pl.ds(2 * count + (2 * k + block - 2) * chunk, chunk)

        along = [
            remote(src.at[pl.ds(k * chunk, chunk)], held.at[lines(2, k)], partner) for k in range(2)
        ]
        beside = remote(src, held.at[lines(1)], sibling)
        held[lines(0), :] = src[...]

        def first_product(first, size):
            mine, low_rows = pl.ds(first, size), pl.ds(0, size)

            def step(n, carry):
                at = pl.multiple_of(n * tile, tile)
                low, high = pl.ds(at, tile), pl.ds(pl.multiple_of(at + units, tile), tile)
                block = held[mine, :]
                if forward:
                    gate = jnp.dot(block, gu[:, low], preferred_element_type=jnp.float32)
                    up = jnp.dot(block, gu[:, high], preferred_element_type=jnp.float32)
                    saved_v[mine, low] = gate
                    saved_v[mine, high] = up
                    mid[low_rows, low] = (gate * jax.nn.sigmoid(gate) * up).astype(jnp.bfloat16)
                else:
                    d_hidden = nt(block, dn[low, :])
                    gate, up = saved_v[mine, low], saved_v[mine, high]
                    sigmoid_of = jax.nn.sigmoid(gate)
                    mid[low_rows, low] = (
                        d_hidden * up * sigmoid_of * (1.0 + gate * (1.0 - sigmoid_of))
                    ).astype(jnp.bfloat16)
                    mid[low_rows, high] = (d_hidden * gate * sigmoid_of).astype(jnp.bfloat16)
                return carry

            lax.fori_loop(0, units // tile, step, 0)

        def second_product(first, size):
            mine, low_rows = pl.ds(first, size), pl.ds(0, size)

            def step(n, carry):
                at = pl.ds(pl.multiple_of(n * tile, tile), tile)
                if forward:
                    part[mine, at] = jnp.dot(
                        mid[low_rows, :], dn[:, at], preferred_element_type=jnp.float32
                    )
                else:
                    part[mine, at] = nt(mid[low_rows, :], gu[at, :])
                return carry

            lax.fori_loop(0, width // tile, step, 0)

        for load in loads[0]:
            load.wait()
        beside.wait_recv()
        first_product(0, 2 * count)
        along[0].wait_recv()
        passed = [remote(held.at[lines(2, 0)], held.at[lines(3, 0)], sibling)]
        for load in loads[1]:
            load.wait()
        second_product(0, 2 * count)
        give[0] = part[lines(1), :].astype(jnp.bfloat16)
        home = remote(give.at[0], got.at[0], sibling)
        stores = []

        def store(first, size):
            if forward:
                copy = pltpu.make_async_copy(
                    saved_v.at[pl.ds(first, size)], gu_out.at[pl.ds(first, size)], fresh()
                )
                copy.start()
                stores.append(copy)

        store(0, 2 * count)
        over, back = [], []

        def hand_over(k):
            some = pl.ds(k * chunk, chunk)
            give[1, some, :] = part[lines(3, k), :].astype(jnp.bfloat16)
            over.append(remote(give.at[1, some], got.at[1, some], sibling))

        def send_back(k):
            some = pl.ds(k * chunk, chunk)
            over[k].wait_recv()
            give[2, some, :] = (part[lines(2, k), :] + got[1, some, :].astype(jnp.float32)).astype(
                jnp.bfloat16
            )
            back.append(remote(give.at[2, some], got.at[2, some], partner))

        first, second = 2 * count, 2 * count + 2 * chunk
        passed[0].wait_recv()
        first_product(first, 2 * chunk)
        along[1].wait_recv()
        passed.append(remote(held.at[lines(2, 1)], held.at[lines(3, 1)], sibling))
        second_product(first, 2 * chunk)
        hand_over(0)
        passed[1].wait_recv()
        first_product(second, 2 * chunk)
        send_back(0)
        store(first, 4 * chunk)
        second_product(second, 2 * chunk)
        hand_over(1)
        send_back(1)
        home.wait_recv()
        out[...] = part[lines(0), :] + got[0].astype(jnp.float32)
        for k in range(2):
            some = pl.ds(k * chunk, chunk)
            back[k].wait_recv()
            out[some, :] += got[2, some, :].astype(jnp.float32)
        for copy in started:
            copy.wait_send()
        if forward:
            for copy in stores:
                copy.wait()

    scratch = [
        pltpu.VMEM((4 * count, width), jnp.bfloat16),
        pltpu.VMEM((width, quarter), jnp.bfloat16),
        pltpu.VMEM((units, width), jnp.bfloat16),
        pltpu.VMEM((4 * count, quarter), jnp.float32),
        pltpu.VMEM((2 * count, units if forward else quarter), jnp.bfloat16),
        pltpu.VMEM((4 * count, width), jnp.float32),
        pltpu.VMEM((3, count, width), jnp.bfloat16),
        pltpu.VMEM((3, count, width), jnp.bfloat16),
        DMA((32,)),
    ]
    total = jax.ShapeDtypeStruct((count, width), jnp.float32)
    if forward:
        products = jax.ShapeDtypeStruct((4 * count, quarter), jnp.float32)
        return remote_call(
            body, [total, products], [VMEM] + [ANY] * (2 * parts_n), [VMEM, ANY], scratch,
            collective_id, name,
        )(rows, *gate_up_parts, *down_parts)
    return remote_call(
        body, total, [VMEM] + [ANY] * (2 * parts_n + 1), VMEM, scratch, collective_id, name
    )(rows, *gate_up_parts, *down_parts, saved)


def turn(values, cosine, sine):
    width = values.shape[-1]
    lane = lax.broadcasted_iota(jnp.int32, values.shape, values.ndim - 1)
    swapped = jnp.where(
        lane % 64 < 32,
        pltpu.roll(values, width - 32, values.ndim - 1),
        pltpu.roll(values, 32, values.ndim - 1),
    )
    return values * cosine + swapped * sine


def key_value_back(far, own, cosine, sine, collective_id):
    def body(far_ref, own_ref, cos_ref, sin_ref, out, held, sem):
        me = seq_me()
        post = Post(sem, 8)
        barrier = pltpu.get_barrier_semaphore()
        for k in range(1, 5):
            pl.semaphore_signal(
                barrier, inc=1, device_id=seq_at((me + k) % SEQ_N), device_id_type=MESH_ID
            )
        pl.semaphore_wait(barrier, 4)
        copies = [
            post.send(
                far_ref.at[:, pl.ds((4 - k) * TOK, TOK), :], held.at[4 - k],
                seq_at((me + SEQ_N - k) % SEQ_N),
            )
            for k in range(1, 5)
        ]
        for copy in copies:
            copy.wait_recv()
        for m in range(2):
            total = own_ref[m]
            for n in range(3, -1, -1):
                total = total + held[n, m].astype(jnp.float32)
            keys = turn(total[:, 0:256], cos_ref[:, 0:256], -sin_ref[:, 0:256])
            out[pl.ds(m * TOK, TOK), 0:256] = keys.astype(jnp.bfloat16)
            out[pl.ds(m * TOK, TOK), 256:512] = total[:, 256:512].astype(jnp.bfloat16)
        post.finish()

    return remote_call(
        body,
        jax.ShapeDtypeStruct((2 * TOK, 512), jnp.bfloat16),
        [VMEM] * 4,
        VMEM,
        [pltpu.VMEM((4, 2, TOK, 512), jnp.bfloat16), DMA((8,))],
        collective_id,
        "key_value_back",
    )(far, own, cosine, sine)


def spread_heads(block):
    return jnp.concatenate([block[:, 64 * g : 64 * g + 64] for g in range(8)], axis=0)


def join_heads(block):
    return jnp.concatenate([block[64 * g : 64 * g + 64, :] for g in range(8)], axis=1)


def window_mask(start, query_seg, key_seg, shift):
    query = start + lax.broadcasted_iota(jnp.int32, (TOK, 5 * TOK), 0)
    key = start - 4 * TOK + lax.broadcasted_iota(jnp.int32, (TOK, 5 * TOK), 1)
    allowed = (
        (key <= query)
        & (key >= 0)
        & (query_seg == key_seg)
        & (((query + shift) >> 8) == ((key + shift) >> 8))
    )
    return jnp.concatenate([allowed.astype(jnp.float32)] * 8, axis=0) > 0.5


def nt(left, right):
    return lax.dot_general(
        left, right, (((1,), (1,)), ((), ())), preferred_element_type=jnp.float32
    )


def tn(left, right):
    return lax.dot_general(
        left, right, (((0,), (0,)), ((), ())), preferred_element_type=jnp.float32
    )


def probabilities(queries, keys, mask):
    scores = jnp.where(mask, nt(queries, keys) * 0.125, -1e30)
    top = jnp.max(scores, axis=-1, keepdims=True)
    raised = jnp.where(mask, jnp.exp(scores - top), 0.0)
    return raised / jnp.sum(raised, axis=-1, keepdims=True)


def attend_back(queries, window, upstream, cosine, sine, query_seg, key_seg, start, shifts):
    def body(
        start_ref, shift_ref, q_ref, kv_ref, g_ref, cos_ref, sin_ref, qs_ref, ks_ref,
        dq_out, far_out, own_out,
    ):
        for h in range(4):
            cols = slice(512 * h, 512 * h + 512)
            mask = window_mask(start_ref[0], qs_ref[0], ks_ref[0], shift_ref[h])
            spread = spread_heads(q_ref[:, cols])
            keys = kv_ref[0, :, 64 * h : 64 * h + 64]
            values = kv_ref[0, :, 256 + 64 * h : 256 + 64 * h + 64]
            probs = probabilities(spread, keys, mask)
            grads = spread_heads(g_ref[:, cols])
            d_probs = nt(grads, values)
            d_values = tn(probs.astype(jnp.bfloat16), grads)
            inner = jnp.sum(probs * d_probs, axis=-1, keepdims=True)
            d_scores = (0.125 * probs * (d_probs - inner)).astype(jnp.bfloat16)
            d_queries = join_heads(jnp.dot(d_scores, keys, preferred_element_type=jnp.float32))
            dq_out[:, cols] = turn(d_queries, cos_ref[...], -sin_ref[...]).astype(jnp.bfloat16)
            d_keys = tn(d_scores, spread)
            for at, part in ((64 * h, d_keys), (256 + 64 * h, d_values)):
                far_out[0, :, at : at + 64] = part[0 : 4 * TOK].astype(jnp.bfloat16)
                own_out[0, :, at : at + 64] = part[4 * TOK :]

    wide = pl.BlockSpec((TOK, 2048), lambda m: (m, 0))
    return pl.pallas_call(
        body,
        out_shape=[
            jax.ShapeDtypeStruct((2 * TOK, 2048), jnp.bfloat16),
            jax.ShapeDtypeStruct((2, 4 * TOK, 512), jnp.bfloat16),
            jax.ShapeDtypeStruct((2, TOK, 512), jnp.float32),
        ],
        grid=(2,),
        in_specs=[
            SMEM,
            SMEM,
            wide,
            pl.BlockSpec((1, 5 * TOK, 512), lambda m: (m, 0, 0)),
            wide,
            pl.BlockSpec((TOK, 512), lambda m: (0, 0)),
            pl.BlockSpec((TOK, 512), lambda m: (0, 0)),
            pl.BlockSpec((1, TOK, 1), lambda m: (m, 0, 0)),
            pl.BlockSpec((1, 1, 5 * TOK), lambda m: (m, 0, 0)),
        ],
        out_specs=[
            wide,
            pl.BlockSpec((1, 4 * TOK, 512), lambda m: (m, 0, 0)),
            pl.BlockSpec((1, TOK, 512), lambda m: (m, 0, 0)),
        ],
        compiler_params=pltpu.CompilerParams(vmem_limit_bytes=VMEM_LIMIT),
        name="attend_back",
    )(start, shifts, queries, window, upstream, cosine, sine, query_seg, key_seg)


def small_updates(
    totals, left, right, rank, a_old, b_old, width_a, width_b, gain, gain_first, gain_second, columns
):
    def body(
        t_ref, l_ref, r_ref, k_ref, a_ref, b_ref, wa_ref, wb_ref, g_ref, gf_ref, gs_ref, c_ref,
        scalars, ga_out, gb_out, gf_out, gs_out, g_out, k_out, wa_out, wb_out, a_out, b_out,
    ):
        totals_now = t_ref[...]
        norm = jnp.sqrt(totals_now[0:1, 64:65])
        clip = CLIP_MAX / jnp.maximum(norm, CLIP_MAX)
        lane = lax.broadcasted_iota(jnp.int32, (8, 128), 1)
        scalars[...] = jnp.where(lane == 0, norm, jnp.where(lane == 1, clip, 0.0))
        parts = [totals_now[:, 8 * k : 8 * k + 8] for k in range(8)]
        square = (clip * clip)[0:1, 0:1].reshape(1, 1, 1)
        stats = SECOND_DECAY * k_ref[...] + (1.0 - SECOND_DECAY) * square * jnp.stack(parts)
        k_out[...] = stats

        def times(x, y):
            total = x[:, :, 0:1] * y[:, 0:1, :]
            for n in range(1, 8):
                total = total + x[:, :, n : n + 1] * y[:, n : n + 1, :]
            return total

        size = jnp.sqrt(jnp.sum(jnp.sum(stats * stats, axis=2, keepdims=True), axis=1, keepdims=True))
        unit = (
            lax.broadcasted_iota(jnp.int32, (8, 8, 8), 1) == lax.broadcasted_iota(jnp.int32, (8, 8, 8), 2)
        ).astype(jnp.float32)

        def newton(n, carry):
            root, matrix = carry
            factor = (5.0 * unit - matrix) * 0.25
            square_of = times(factor, factor)
            return times(root, factor), times(times(square_of, square_of), matrix)

        roots, _ = lax.fori_loop(
            0, 10, newton, (unit * lax.rsqrt(jnp.sqrt(size)), stats / size)
        )

        gradient = l_ref[...] * clip
        down = gradient[0:32]
        ga_out[...] = down
        up = r_ref[...] * clip
        gb_out[...] = up

        first = FIRST_DECAY * gf_ref[...] + (1.0 - FIRST_DECAY) * gradient[32:35]
        second = SECOND_DECAY * gs_ref[...] + (1.0 - SECOND_DECAY) * gradient[32:35] * gradient[32:35]
        gf_out[...] = first
        gs_out[...] = second
        first_hat = first / (1.0 - FIRST_DECAY**STEP)
        second_hat = second / (1.0 - SECOND_DECAY**STEP)
        gains = g_ref[...]
        g_out[...] = gains - RATE_GAIN * (
            first_hat / (jnp.sqrt(second_hat) + ADAM_EPS) + WEIGHT_DECAY * gains
        )

        def apply(root, gradients):
            total = root[:, 0:1] * gradients[0:1, :]
            for n in range(1, 8):
                total = total + root[:, n : n + 1] * gradients[n : n + 1, :]
            return total

        for k in range(4):
            rows = slice(8 * k, 8 * k + 8)
            mine = down[rows]
            wide = SECOND_DECAY * wa_ref[k : k + 1, :] + (1.0 - SECOND_DECAY) * jnp.sum(
                mine * mine, axis=0, keepdims=True
            )
            wa_out[k : k + 1, :] = wide
            a_out[rows, :] = a_ref[rows, :] - LEARN_RATE_DOWN * (
                apply(roots[k], mine) * lax.rsqrt(jnp.sqrt(wide))
            )
        wide = SECOND_DECAY * wb_ref[...] + (1.0 - SECOND_DECAY) * jnp.sum(
            up * up, axis=0, keepdims=True
        )
        wb_out[...] = wide
        column = c_ref[...]
        factor = (column >= 2048).astype(jnp.int32) + (column >= 2304) + (column >= 2560)
        step = jnp.zeros(up.shape, jnp.float32)
        for k in range(4):
            step = step + jnp.where(factor == k, apply(roots[4 + k], up), 0.0)
        b_out[...] = b_ref[...] - LEARN_RATE_UP * (step * lax.rsqrt(jnp.sqrt(wide)))

    def like(array):
        return jax.ShapeDtypeStruct(array.shape, jnp.float32)

    return pl.pallas_call(
        body,
        out_shape=[
            jax.ShapeDtypeStruct((8, 128), jnp.float32), like(a_old), like(right), like(gain), like(gain),
            like(gain), like(rank), like(width_a), like(width_b), like(a_old), like(b_old),
        ],
        in_specs=[VMEM] * 12,
        out_specs=[VMEM] * 11,
        compiler_params=pltpu.CompilerParams(vmem_limit_bytes=VMEM_LIMIT),
        name="small_updates",
    )(
        totals, left, right, rank, a_old, b_old, width_a, width_b, gain, gain_first, gain_second, columns
    )


def dot(left, right):
    return jnp.dot(left, right, preferred_element_type=jnp.float32)


def dot_exact(left, right):
    return jnp.dot(left, right, precision=HIGHEST)


def norm_scale(values):
    return lax.rsqrt(jnp.mean(values * values, axis=-1, keepdims=True) + NORM_EPS)


def norm_back(values, gain, upstream):
    scale_of = norm_scale(values)
    scaled = gain * upstream
    inward = scale_of * scaled - values * scale_of**3 * jnp.mean(
        scaled * values, axis=-1, keepdims=True
    )
    return (inward, jnp.sum(upstream * values * scale_of, axis=0))


def adam_update(weight_vals, first_old, second_old, gradient, rate):
    first_new = FIRST_DECAY * first_old + (1.0 - FIRST_DECAY) * gradient
    second_new = SECOND_DECAY * second_old + (1.0 - SECOND_DECAY) * gradient * gradient
    first_hat = first_new / (1.0 - FIRST_DECAY**STEP)
    second_hat = second_new / (1.0 - SECOND_DECAY**STEP)
    step_vals = first_hat / (jnp.sqrt(second_hat) + ADAM_EPS) + WEIGHT_DECAY * weight_vals
    return (first_new, second_new, weight_vals - rate * step_vals)


def per_device(
    input_token_index,
    target_token_index,
    loss_position_index,
    document_slot_index,
    row_used_length,
    head_group_offsets,
    embedding,
    embedding_first_moment,
    embedding_second_moment,
    frozen_output_table,
    frozen_query_key_value_weight,
    frozen_attention_output_weight,
    frozen_gate_up_weight,
    frozen_down_weight,
    norm_gain_vectors,
    norm_gain_first_moment,
    norm_gain_second_moment,
    adapter_down_factors,
    adapter_up_factors,
    rank_side_statistics,
    down_width_statistics,
    up_width_statistics,
):
    fsdp_here = lax.axis_index(FSDP)
    seq_here = lax.axis_index(SEQ)
    vocab_dev = embedding.shape[0]

    qkvo_own = jnp.concatenate([frozen_query_key_value_weight, frozen_attention_output_weight], 1)
    down_own = jnp.pad(frozen_down_weight, ((0, 4), (0, 0)))
    small_own = jnp.pad(
        jnp.concatenate(
            [
                adapter_down_factors.reshape(-1),
                norm_gain_vectors.reshape(-1),
                adapter_up_factors.reshape(-1),
            ]
        ),
        (0, 1024 - 848),
    ).reshape(8, 128)
    ids_own = jnp.pad(input_token_index.reshape(16, TOK), ((0, 0), (0, 64)))
    qkvo, small, table, ids, gate_up_w, down_w = gather_weights(
        qkvo_own,
        small_own,
        embedding.astype(jnp.bfloat16),
        ids_own,
        frozen_gate_up_weight,
        down_own,
    )
    qkvo = qkvo.reshape(2048, 4608)
    w_qkv, w_out = qkvo[:, :2560], qkvo[:, 2560:]
    head_own, ids = lax.optimization_barrier((frozen_output_table, ids))
    head = lax.all_gather(head_own, SEQ, axis=1, tiled=True)
    small = small.reshape(128, 1024)
    down_full = small[:, :512].reshape(128, 32, 16).transpose(1, 0, 2).reshape(32, 2048)
    gain = small[:, 512:560].reshape(128, 3, 16).transpose(1, 0, 2).reshape(3, 2048)
    up_full = small[:, 560:848].reshape(128, 8, 36).transpose(1, 0, 2).reshape(8, 4608)
    a_low = down_full.astype(jnp.bfloat16)
    b_low = up_full.astype(jnp.bfloat16)
    a_low, b_low, gain = lax.optimization_barrier((a_low, b_low, gain))
    a_in, a_out = a_low[:24], a_low[24:]
    factor_of = (jnp.arange(2560) >= 2048).astype(jnp.int32) + (jnp.arange(2560) >= 2304)
    b_in = jnp.where(
        (jnp.arange(24) // 8)[:, None] == factor_of[None, :],
        jnp.concatenate([b_low[:, :2560]] * 3, 0),
        jnp.zeros((), jnp.bfloat16),
    )
    b_out = b_low[:, 2560:]

    places = loss_position_index.reshape(2, 8, SEQ_N, 32)
    spots = jnp.arange(SEQ_N)[:, None] * TOK + places
    counted = spots < row_used_length[..., None, None]
    below = jnp.sum(
        (document_slot_index[..., None] < jnp.arange(1, 3)).astype(jnp.int32), axis=2
    )
    seg_at = jnp.sum(
        (spots[..., None] >= below[:, :, None, None, :]).astype(jnp.int32), axis=-1
    )
    member = counted[..., None] & (seg_at[..., None] == jnp.arange(3))
    counts = jnp.sum(member.astype(jnp.int32), axis=(2, 3))
    document_total = jnp.sum((counts > 0).astype(jnp.float32))
    own_places = lax.dynamic_index_in_dim(places, seq_here, 2, keepdims=False)
    own_counted = lax.dynamic_index_in_dim(counted, seq_here, 2, keepdims=False)
    own_seg = lax.dynamic_index_in_dim(seg_at, seq_here, 2, keepdims=False)
    per_doc = jnp.sum(
        jnp.where(own_seg[..., None] == jnp.arange(3), counts[:, :, None, :], 0), axis=-1
    )
    own_weight = jnp.where(own_counted, 1.0 / jnp.maximum(per_doc, 1).astype(jnp.float32), 0.0)
    weight_flat = own_weight.transpose(1, 0, 2).reshape(-1)
    row_places = lax.dynamic_index_in_dim(own_places, fsdp_here, 1, keepdims=False)
    chosen_at = (row_places + jnp.arange(2)[:, None] * TOK).reshape(64)
    pick = (chosen_at[:, None] == jnp.arange(128)[None, :]).astype(jnp.float32)

    ids = ids[:, :, :TOK].reshape(SEQ_N, 2, 8, TOK)
    row_ids = lax.dynamic_index_in_dim(ids, fsdp_here, 2, keepdims=False).reshape(SEQ_N, 128)
    half = 32
    freqs = ROPE_BASE ** (-2.0 * jnp.arange(half).astype(jnp.float32) / 64)
    angles = (seq_here * TOK + jnp.arange(TOK)).astype(jnp.float32)[:, None] * freqs[None, :]
    cosine = jnp.tile(jnp.cos(angles), (1, 16))
    sine = jnp.sin(angles)
    sine = jnp.tile(jnp.concatenate([-sine, sine], 1), (1, 8))
    own_docs = lax.dynamic_index_in_dim(document_slot_index, fsdp_here, 1, keepdims=False)
    padded = jnp.concatenate([jnp.full((2, 4 * TOK), -1, jnp.int32), own_docs], 1)
    key_seg = lax.dynamic_slice_in_dim(padded, seq_here * TOK, 5 * TOK, 1)[:, None, :]
    query_seg = key_seg[:, 0, 4 * TOK :][:, :, None]
    start = (seq_here * TOK).reshape(1)
    (
        x_start, normed_one, adapter_in, queries, window, attended, adapter_mid, x_mid, normed_two,
    ) = attention_block(
        table, row_ids, qkvo, a_low, b_in, b_out, gain, cosine, sine, query_seg, key_seg,
        head_group_offsets, 2,
    )
    gate_up_w = [gate_up_w.reshape(2048, -1)]
    down_w = [down_w.reshape(PAD_FF // 4, -1)]

    hidden_sum, gate_up = feed_forward(normed_two, gate_up_w, down_w, None, 12, "feed_forward")
    x_end = x_mid + hidden_sum
    normed_end = (x_end * norm_scale(x_end) * gain[2]).astype(jnp.bfloat16)

    chosen = dot(pick.astype(jnp.bfloat16), normed_end).astype(jnp.bfloat16)
    local_target = target_token_index.transpose(1, 0, 2).reshape(512, 1) - fsdp_here * vocab_dev
    local_target = jnp.where(local_target < vocab_dev, local_target, -1)
    weight_column = weight_flat.reshape(512, 1)
    rows = chosen_rows(chosen, 5).reshape(512, 2048)
    head, rows = lax.optimization_barrier((head, rows))
    d_chosen, loss_tile = head_step(
        rows, head, local_target, weight_column, weight_column / document_total, 4
    )

    upstream = lax.dot_general(pick, d_chosen, (((0,), (0,)), ((), ())), precision=HIGHEST)
    d_end, gain_end = norm_back(x_end, gain[2], upstream)
    d_normed = feed_forward(
        d_end.astype(jnp.bfloat16), gate_up_w, down_w, gate_up, 13, "feed_forward_back"
    )
    back_two, gain_mid = norm_back(x_mid, gain[1], d_normed)
    d_mid = d_end + back_two

    d_branch = d_mid.astype(jnp.bfloat16)
    d_adapter_mid = (ADAPTER_SCALE * nt(d_branch, b_out)).astype(jnp.bfloat16)
    d_attended = (nt(d_branch, w_out) + dot(d_adapter_mid, a_out)).astype(jnp.bfloat16)
    up_gradient_out = ADAPTER_SCALE * tn(adapter_mid, d_branch)
    down_gradient_out = tn(d_adapter_mid, attended)
    d_queries, d_far, d_own = attend_back(
        queries, window, d_attended, cosine, sine, query_seg, key_seg, start, head_group_offsets
    )
    d_key_value = key_value_back(d_far, d_own, cosine, sine, 7)
    d_packed = jnp.concatenate([d_queries, d_key_value], 1)
    d_adapter_in = (ADAPTER_SCALE * nt(d_packed, b_in)).astype(jnp.bfloat16)
    up_gradient_in = ADAPTER_SCALE * jnp.concatenate(
        [
            tn(adapter_in[:, 0:8], d_packed[:, :2048]),
            tn(adapter_in[:, 8:16], d_packed[:, 2048:2304]),
            tn(adapter_in[:, 16:24], d_packed[:, 2304:]),
        ],
        1,
    )
    down_gradient_in = tn(d_adapter_in, normed_one)
    back_one, gain_start = norm_back(
        x_start, gain[0], nt(d_packed, w_qkv) + dot(d_adapter_in, a_in)
    )
    d_start = (d_mid + back_one).astype(jnp.bfloat16)

    left = jnp.concatenate(
        [
            down_gradient_in,
            down_gradient_out,
            jnp.stack([gain_start, gain_mid, gain_end]),
            jnp.zeros((5, 2048), jnp.float32),
        ],
        0,
    )
    right = jnp.concatenate([up_gradient_in, up_gradient_out], 1)
    all_ids = ids.transpose(2, 0, 1, 3).reshape(16, 1024) - fsdp_here * vocab_dev
    grad_embed, left_sum, right_sum, totals = token_gradients(
        d_start, left, right, all_ids, loss_tile, vocab_dev, 8
    )
    document_loss_sum = totals[0, 65]

    own_left = lax.dynamic_slice_in_dim(left_sum, fsdp_here * 16, 16, 1)
    own_right = lax.dynamic_slice_in_dim(
        right_sum, 32 * ((9 * seq_here) % 4) + fsdp_here * 36, 36, 1
    )
    columns = ((seq_here * 8 + fsdp_here) * 36 + jnp.arange(36)).reshape(1, 36)
    (
        scalars,
        down_factor_gradient,
        up_factor_gradient,
        updated_gain_first_moment,
        updated_gain_second_moment,
        updated_norm_gains,
        updated_rank_statistics,
        updated_down_width_statistics,
        updated_up_width_statistics,
        updated_down_factors,
        updated_up_factors,
    ) = small_updates(
        totals,
        own_left,
        own_right,
        rank_side_statistics,
        adapter_down_factors,
        adapter_up_factors,
        down_width_statistics,
        up_width_statistics.reshape(1, 36),
        norm_gain_vectors,
        norm_gain_first_moment,
        norm_gain_second_moment,
        columns,
    )
    updated_up_width_statistics = updated_up_width_statistics.reshape(36)
    global_gradient_norm = scalars[0, 0]
    grad_embed = grad_embed * scalars[0, 1]
    unused_first, updated_embedding_second_moment, updated_embedding_table = adam_update(
        embedding, embedding_first_moment, embedding_second_moment, grad_embed, RATE_EMBED
    )
    return (
        document_loss_sum,
        document_total,
        global_gradient_norm,
        grad_embed,
        updated_embedding_second_moment,
        updated_embedding_table,
        updated_gain_first_moment,
        updated_gain_second_moment,
        updated_norm_gains,
        down_factor_gradient,
        up_factor_gradient,
        updated_rank_statistics,
        updated_down_width_statistics,
        updated_up_width_statistics,
        updated_down_factors,
        updated_up_factors,
    )


def solution(mesh):
    torus = Mesh(
        mesh.devices.reshape(2, 4, 2, 2, 2, 2), SEQ_FSDP
    )
    return jax.shard_map(
        per_device,
        mesh=torus,
        in_specs=(
            P(None, None, SEQ),
            P(None, None, SEQ),
            P(),
            P(),
            P(),
            P(),
            P(FSDP, SEQ),
            P(FSDP, SEQ),
            P(FSDP, SEQ),
            P(FSDP, SEQ),
            P(SEQ_FSDP, None),
            P(SEQ_FSDP, None),
            P(SEQ_FSDP, None),
            P(SEQ_FSDP, None),
            P(None, SEQ_FSDP),
            P(None, SEQ_FSDP),
            P(None, SEQ_FSDP),
            P(None, SEQ_FSDP),
            P(None, SEQ_FSDP),
            P(),
            P(None, SEQ_FSDP),
            P(SEQ_FSDP),
        ),
        out_specs=(
            P(),
            P(),
            P(),
            P(FSDP, SEQ),
            P(FSDP, SEQ),
            P(FSDP, SEQ),
            P(None, SEQ_FSDP),
            P(None, SEQ_FSDP),
            P(None, SEQ_FSDP),
            P(None, SEQ_FSDP),
            P(None, SEQ_FSDP),
            P(),
            P(None, SEQ_FSDP),
            P(SEQ_FSDP),
            P(None, SEQ_FSDP),
            P(None, SEQ_FSDP),
        ),
        check_vma=False,
    )
```

```python
import functools

import jax
import jax.numpy as jnp
from jax import lax
from jax.experimental import pallas as pl
from jax.experimental.pallas import tpu as pltpu
from jax.sharding import Mesh
from jax.sharding import PartitionSpec as P

STEP = 5
GROUP = 256
SEQ = ("seq_0", "seq_1", "seq_2")
FSDP = ("fsdp_0", "fsdp_1", "fsdp_2")
SEQ_FSDP = SEQ + FSDP
SEQ_N = 16
FSDP_N = 8
TOK = 64
PAD_FF = 6144
NORM_EPS = 1e-05
ADAPTER_SCALE = 2.0
ROPE_BASE = 10000.0
CLIP_MAX = 0.001
FIRST_DECAY = 0.5
SECOND_DECAY = 0.5
RATE_EMBED = 0.3
RATE_GAIN = 0.1
LEARN_RATE_DOWN = 0.1
LEARN_RATE_UP = 0.5
WEIGHT_DECAY = 0.01
ADAM_EPS = 1e-12
HIGHEST = lax.Precision.HIGHEST
MESH_ID = pl.DeviceIdType.MESH
ANY = pl.BlockSpec(memory_space=pl.ANY)
VMEM = pl.BlockSpec(memory_space=pltpu.VMEM)
SMEM = pl.BlockSpec(memory_space=pltpu.SMEM)
DMA = pltpu.SemaphoreType.DMA
VMEM_LIMIT = 56 * 1024 * 1024


def seq_me():
    return lax.axis_index("seq_0") * 8 + lax.axis_index("seq_1") * 2 + lax.axis_index("seq_2")


def z_me():
    return lax.axis_index("fsdp_0") * 2 + lax.axis_index("fsdp_1")


def z_at(i):
    return {"fsdp_0": i // 2, "fsdp_1": i % 2}


def fsdp_me():
    return z_me() * 2 + lax.axis_index("fsdp_2")


def seq_at(i):
    return {"seq_0": i // 8, "seq_1": (i // 2) % 4, "seq_2": i % 2}


def fsdp_at(i):
    return {**z_at(i // 2), "fsdp_2": i % 2}


def remote_call(body, out_shape, in_specs, out_specs, scratch, collective_id, name):
    return pl.pallas_call(
        body,
        out_shape=out_shape,
        in_specs=in_specs,
        out_specs=out_specs,
        scratch_shapes=scratch,
        compiler_params=pltpu.CompilerParams(
            collective_id=collective_id, has_side_effects=True, vmem_limit_bytes=VMEM_LIMIT
        ),
        name=name,
    )


ALL16 = range(1, SEQ_N)
ALL8 = range(1, FSDP_N)


ORDER = (
    "q2", "s", "q0", "d0", "t0", "q1", "q0", "q2", "d1", "d0", "s", "q2",
    "q1", "g0", "q1", "q0", "q2", "d1", "g1", "q0", "s", "q2", "q2", "g0",
    "t0", "t1", "g1", "q2", "t1", "q1", "g1", "d0", "q2", "g0", "s", "g1",
    "q0", "d0", "g0", "s", "d1", "d1", "s", "q1", "q2", "q1", "q1", "s",
    "q0", "t0", "d1", "g1", "d0", "q0", "g0", "t0", "q1", "g0", "q1", "d1",
    "d1", "t0", "g1", "g0", "q2", "q0", "g1", "d0", "q0", "s", "s", "d1",
    "t1", "d0", "q1", "t1", "q0", "g0", "s", "d0", "t1", "g1",
)
EVERY = slice(None)


class Post:
    def __init__(self, sem, count):
        self.sem, self.count, self.used, self.sent, self.late = sem, count, 0, [], []

    def fresh(self):
        self.used += 1
        assert self.used <= self.count, self.used
        return self.sem.at[self.used - 1]

    def start(self, src, dst, ssem, rsem, device):
        copy = pltpu.make_async_remote_copy(
            src_ref=src, dst_ref=dst, send_sem=ssem, recv_sem=rsem,
            device_id=device, device_id_type=MESH_ID,
        )
        copy.start()
        return copy

    def send(self, src, dst, device):
        copy = self.start(src, dst, self.fresh(), self.fresh(), device)
        self.sent.append(copy)
        return copy

    def finish(self):
        for copy in self.sent:
            copy.wait_send()
        for mark, view in self.late:
            pltpu.make_async_copy(view, view, mark).wait()


def greet_devices(devices):
    barrier = pltpu.get_barrier_semaphore()
    for device in devices:
        pl.semaphore_signal(barrier, inc=1, device_id=device, device_id_type=MESH_ID)
    pl.semaphore_wait(barrier, len(devices))


def fsdp_peers():
    me = fsdp_me()
    return [fsdp_at((me + k) % FSDP_N) for k in ALL8]


def seq_peers():
    me = seq_me()
    return [seq_at((me + k) % SEQ_N) for k in ALL16]


def relay(post, out, first, second, first_a, first_b):
    z, yl = z_me(), lax.axis_index("fsdp_2")
    partner, up, down = {"fsdp_2": 1 - yl}, z_at((z + 1) % 4), z_at((z + 3) % 4)
    before, after, far = (z + 3) % 4, (z + 1) % 4, (z + 2) % 4

    def at(zz, y, part=()):
        return out.at[(zz * 2 + y,) + part]

    def send(zz, y, part, device):
        view = at(zz, y, part)
        return post.send(view, view, device)

    to_partner = send(z, yl, (), partner)
    ring_up = send(z, yl, (), up)
    ring_down = send(z, yl, (), down)
    yield
    to_partner.wait_recv()
    other_up = send(z, 1 - yl, first, up)
    other_down = send(z, 1 - yl, first, down)
    yield
    ring_up.wait_recv()
    far_up = send(before, yl, first, up)
    across = [send(before, yl, second, partner)]
    yield
    ring_down.wait_recv()
    far_down = send(after, yl, second, down)
    across.append(send(after, yl, second, partner))
    yield
    other_up.wait_recv()
    last_up = send(before, 1 - yl, first_a, up)
    yield
    other_down.wait_recv()
    last_down = send(after, 1 - yl, first_b, down)
    yield
    far_up.wait_recv()
    far_down.wait_recv()
    across.append(send(far, yl, second, partner))
    yield
    last_up.wait_recv()
    last_down.wait_recv()
    for copy in across:
        copy.wait_recv()


def no_hand(view):
    return None


class Ways:
    def __init__(self, post):
        self.post = post
        self.yh, self.x, self.c = (lax.axis_index(a) for a in SEQ)
        self.z, self.yl = z_me(), lax.axis_index("fsdp_2")
        self.where = {"x": self.x, "y": 2 * self.yh + self.yl, "z": self.z}
        z, c = self.z, self.c
        self.column = [
            ((z + dz) % 4, (c + dc) % 2, dz, dc) for dz in range(4) for dc in range(2) if dz or dc
        ]

    def beside(self, axis, step):
        at = (self.where[axis] + step + 4) % 4
        if axis == "x":
            return {"seq_1": at}
        if axis == "z":
            return z_at(at)
        return {"seq_0": at // 2, "fsdp_2": at % 2}

    def all_devices(self):
        return (
            [self.beside("y", 1), self.beside("y", -1)]
            + [{**z_at(zz), "seq_2": cc} for zz, cc, dz, dc in self.column if dz]
            + seq_peers()
        )

    def arrived(self, ref, rsem):
        pltpu.make_async_copy(ref, ref, rsem).wait()

    def rings(self, block, order, sizes, halves, across):
        post = self.post
        for n, axis in enumerate(order):
            done = order[:n]
            at = self.where[axis]
            before, after, far = (at + 3) % 4, (at + 1) % 4, (at + 2) % 4
            send, from_before, from_after, far_first = (post.fresh() for _ in range(4))
            post.late.append((send, sizes[axis, n]))
            own = block(done, axis, at, None)
            post.start(own, own, send, from_before, self.beside(axis, 1))
            post.start(own, own, send, from_after, self.beside(axis, -1))
            yield
            got = block(done, axis, before, None)
            self.arrived(got, from_before)
            half = block(done, axis, before, 0)
            post.start(half, half, send, far_first, self.beside(axis, 1))
            across(got)
            yield
            got = block(done, axis, after, None)
            self.arrived(got, from_after)
            if halves:
                far_second = post.fresh()
                half = block(done, axis, after, 1)
                post.start(half, half, send, far_second, self.beside(axis, -1))
            across(got)
            yield
            self.arrived(block(done, axis, far, 0), far_first)
            if halves:
                self.arrived(block(done, axis, far, 1), far_second)
            across(block(done, axis, far, None))

    def place(self, done, axis, at):
        spot = {"yh": self.yh, "x": self.x, "z": self.z, "yl": self.yl}
        for a in done:
            if a == "y":
                spot["yh"] = spot["yl"] = EVERY
            else:
                spot[a] = EVERY
        if axis == "y":
            spot["yh"], spot["yl"] = at // 2, at % 2
        elif axis is not None:
            spot[axis] = at
        return spot

    def everything(self, ref, order, tails, halves=True):
        post, c = self.post, self.c

        def block(done, axis, at, half):
            spot = self.place(done, axis, at)
            tail = tails[0 if half is None else half + 1]
            return ref.at[(spot["yh"], spot["x"], c, spot["z"], spot["yl"]) + tail]

        across_s, across_r = post.fresh(), post.fresh()
        post.late.append((across_s, ref.at[(EVERY, EVERY, c, EVERY, EVERY) + tails[0]]))
        post.late.append((across_r, ref.at[(EVERY, EVERY, 1 - c, EVERY, EVERY) + tails[0]]))

        def across(view):
            post.start(view, view, across_s, across_r, {"seq_2": 1 - c})

        three = pl.ds(0, 3)
        sizes = {}
        for axis in "xyz":
            sizes[axis, 0] = ref.at[(0, 0, 0, three, 0) + tails[0]]
            sizes[axis, 1] = ref.at[(0, pl.ds(0, 2), 0, three, EVERY) + tails[0]]
            sizes[axis, 2] = ref.at[(EVERY, EVERY, 0, three, EVERY) + tails[0]]
        across(block([], None, None, None))
        yield from self.rings(block, order, sizes, halves, across)

    def gate_up(self, src, ref, order, start, width):
        post = self.post
        quarter = src.shape[1] // 4
        yh, x, c, z, yl = self.yh, self.x, self.c, self.z, self.yl
        tails = [
            (EVERY, pl.ds(start, width)),
            (EVERY, pl.ds(start, width // 2)),
            (EVERY, pl.ds(start + width // 2, width // 2)),
        ]

        def block(done, axis, at, half):
            spot = self.place(done, axis, at)
            tail = tails[0 if half is None else half + 1]
            return ref.at[(spot["yh"], spot["x"], EVERY, EVERY, spot["yl"]) + tail]

        marks = []
        for zz, cc, dz, dc in self.column:
            send, recv = post.fresh(), post.fresh()
            first = pl.multiple_of((2 * (zz % 2) + cc) * quarter + start, 128)
            here = ref.at[(yh, x, c, z, yl) + tails[0]]
            post.start(src.at[:, pl.ds(first, width)], here, send, recv, {**z_at(zz), "seq_2": cc})
            post.late.append((send, here))
            marks.append((ref.at[(yh, x, (c + dc) % 2, (z + 4 - dz) % 4, yl) + tails[0]], recv))
        yield
        for view, recv in marks:
            self.arrived(view, recv)
        three = pl.ds(0, 3)
        sizes = {}
        for axis in "xy":
            sizes[axis, 0] = ref.at[(0, three, EVERY, EVERY, 0) + tails[0]]
            sizes[axis, 1] = ref.at[(EVERY, three, EVERY, EVERY, EVERY) + tails[0]]
        yield from self.rings(block, order, sizes, True, no_hand)

    def down(self, ref, order, start, width):
        post = self.post
        yh, x, z, yl = self.yh, self.x, self.z, self.yl
        tails = [
            (EVERY, pl.ds(start, width)),
            (EVERY, pl.ds(start, width // 2)),
            (EVERY, pl.ds(start + width // 2, width // 2)),
        ]
        zh = z // 2

        def block(done, axis, at, half):
            spot = self.place(done, axis, at)
            tail = tails[0 if half is None else half + 1]
            return ref.at[(spot["yh"], spot["x"], EVERY, spot["yl"]) + tail]

        send, recv = post.fresh(), post.fresh()
        here = ref.at[(yh, x, zh, yl) + tails[0]]
        post.start(here, here, send, recv, z_at((z + 2) % 4))
        post.late.append((send, here))
        yield
        self.arrived(ref.at[(yh, x, 1 - zh, yl) + tails[0]], recv)
        three = pl.ds(0, 3)
        sizes = {}
        for axis in "xy":
            sizes[axis, 0] = ref.at[(0, three, EVERY, 0) + tails[0]]
            sizes[axis, 1] = ref.at[(EVERY, three, EVERY, EVERY) + tails[0]]
        yield from self.rings(block, order, sizes, True, no_hand)

    def table(self, ref, low, high):
        post, z, yl = self.post, self.z, self.yl
        middle = (low + high) // 32 * 16
        part = (pl.ds(low, high - low), pl.ds(low, middle - low), pl.ds(middle, high - middle))
        send_y, recv_y = post.fresh(), post.fresh()
        post.late.append((send_y, ref.at[0, part[0]]))
        own = ref.at[2 * z + yl, part[0]]
        post.start(own, own, send_y, recv_y, {"fsdp_2": 1 - yl})
        yield
        self.arrived(ref.at[2 * z + 1 - yl, part[0]], recv_y)

        def block(done, axis, at, half):
            return ref.at[pl.ds(2 * at, 2), part[0 if half is None else half + 1]]

        sizes = {("z", 0): ref.at[pl.ds(0, 6), part[0]]}
        yield from self.rings(block, ("z",), sizes, True, no_hand)

    def own_gate_up(self, src, ref):
        quarter = ref.shape[-1]
        first = pl.multiple_of((2 * (self.z % 2) + self.c) * quarter, 128)
        return src.at[:, pl.ds(first, quarter)], ref.at[self.yh, self.x, self.c, self.z, self.yl]


def local_copies(pairs, post):
    copies = [pltpu.make_async_copy(src, dst, post.fresh()) for src, dst in pairs]
    for copy in copies:
        copy.start()
    return copies


def gather_weights(qkvo, small, table, ids, gate_up, down):
    groups, units = 8, gate_up.shape[1] // 8
    spread = units // 44 * 48
    quarter = groups * spread // 4
    out_shape = [
        jax.ShapeDtypeStruct((2, 4, 2, 4, 2, *qkvo.shape), qkvo.dtype),
        jax.ShapeDtypeStruct((2, 4, 2, 4, 2, *small.shape), small.dtype),
        jax.ShapeDtypeStruct((FSDP_N, *table.shape), table.dtype),
        jax.ShapeDtypeStruct((SEQ_N, *ids.shape), ids.dtype),
        jax.ShapeDtypeStruct((2, 4, 2, 4, 2, gate_up.shape[0], quarter), gate_up.dtype),
        jax.ShapeDtypeStruct((2, 4, 2, 2, *down.shape), down.dtype),
    ]
    sem_count = 320

    def body(*refs):
        ins, outs, ordered, picks, sem = refs[:6], refs[6:12], refs[12], refs[13], refs[14]
        post = Post(sem, sem_count)
        ways = Ways(post)
        yh, x, c, z, yl = ways.yh, ways.x, ways.c, ways.z, ways.yl
        seq = seq_me()
        local = local_copies(
            [
                (ins[0], outs[0].at[yh, x, c, z, yl]),
                (ins[1], outs[1].at[yh, x, c, z, yl]),
                (ins[2], outs[2].at[z * 2 + yl]),
                (ins[3], outs[3].at[seq]),
                (ins[5], outs[5].at[yh, x, z // 2, yl]),
            ],
            post,
        )
        at = lax.broadcasted_iota(jnp.int32, (1, spread), 1)
        part, rest = at // (spread // 4), at % (spread // 4)
        unit = rest % 48
        here = rest // 48
        source = (
            (here // 4) * 16 + (part % 2) * 8 + ((here // 2) % 2) * 4 + (part // 2) * 2 + here % 2
        ) * 44 + unit
        source = jnp.where(unit < 44, source, -1)

        def pick(n, carry):
            start = pl.multiple_of(n * 128, 128)
            row = lax.broadcasted_iota(jnp.int32, (128, spread), 0) + start
            picks[pl.ds(start, 128), :] = (row == source).astype(jnp.float32).astype(jnp.bfloat16)
            return carry

        lax.fori_loop(0, units // 128, pick, 0)
        for n in range(groups):
            moved = jnp.dot(
                ins[4][:, n * units : (n + 1) * units], picks[...], preferred_element_type=jnp.float32
            ).astype(jnp.bfloat16)
            width = spread // 4
            for k in range(4):
                first = k * quarter + n * width
                ordered[:, first : first + width] = moved[:, k * width : (k + 1) * width]
        mine = ways.own_gate_up(ordered, outs[4])
        local += local_copies([mine], post)
        greet_devices(ways.all_devices())
        for copy in local:
            copy.wait()

        send, recv = post.fresh(), post.fresh()
        for device in seq_peers():
            post.start(ins[3], outs[3].at[seq], send, recv, device)
        post.late.append((send, outs[3].at[pl.ds(0, 15)]))
        post.late.append((recv, outs[3].at[pl.ds(0, 15)]))

        third = qkvo.shape[1] // 3
        streams = {
            "s": ways.everything(outs[1], "xyz", [(EVERY, EVERY)] * 2, False),
        }
        rows = table.shape[0]
        cuts = (0, 1984, rows)
        for n in range(len(cuts) - 1):
            streams["t%d" % n] = ways.table(outs[2], cuts[n], cuts[n + 1])
        half, wide = quarter // 2, down.shape[1] // 2
        for n, order in enumerate(("xy", "yx")):
            streams["g%d" % n] = ways.gate_up(ordered, outs[4], order, n * half, half)
            streams["d%d" % n] = ways.down(outs[5], order, n * wide, wide)
        for n, order in enumerate(('yxz', 'xyz', 'zyx')):
            streams["q%d" % n] = ways.everything(
                outs[0], order,
                [
                    (EVERY, pl.ds(n * third, third)),
                    (EVERY, pl.ds(n * third, third // 2)),
                    (EVERY, pl.ds(n * third + third // 2, third // 2)),
                ],
            )
        for name in ORDER:
            next(streams[name], None)
        for name in sorted(streams):
            assert next(streams[name], "end") == "end", name
        post.finish()

    return remote_call(
        body, out_shape, [ANY] * 4 + [VMEM, ANY], [ANY] * 6,
        [
            pltpu.VMEM((gate_up.shape[0], 4 * quarter), gate_up.dtype),
            pltpu.VMEM((units, spread), gate_up.dtype),
            DMA((sem_count,)),
        ],
        1, "gather_weights",
    )(qkvo, small, table, ids, gate_up, down)


def attention_block(
    table, ids, qkvo, a_low, b_in, b_out, gain, cosine, sine, query_seg, key_seg, shifts, collective_id
):
    vocab, width = table.shape[1:]
    rows_n = 2 * TOK
    sem_count = 64

    def body(
        table_hbm, ids_ref, qkvo_hbm, a_ref, bi_ref, bo_ref, gain_ref, cos_ref, sin_ref, qs_ref, ks_ref,
        shift_ref,
        x_out, n_out, u_out, q_out, kv_out, a_out, v_out, mid_out, two_out,
        stage, wide, rows, block, low, packed, own_kv, w_qkv, w_out, sem,
    ):
        post = Post(sem, sem_count)
        me = seq_me()
        loads = [post.fresh() for _ in range(2)]

        def staged(n):
            return pltpu.make_async_copy(table_hbm.at[n], stage.at[n % 2], loads[n % 2])

        staged(0).start()
        weights = local_copies(
            [
                (qkvo_hbm.at[:, pl.ds(0, 2560)], w_qkv),
                (qkvo_hbm.at[:, pl.ds(2560, 2048)], w_out),
            ],
            post,
        )
        greet_devices(seq_peers())
        for n in range(FSDP_N):
            if n + 1 < FSDP_N:
                staged(n + 1).start()
            staged(n).wait()
            wide[pl.ds(n * vocab, vocab), :] = stage[n % 2].astype(jnp.float32)

        spot = pl.ds(pl.multiple_of(me * width, width), width)

        def fetch(s):
            def step(t, carry):
                rows[pl.ds(t, 1), :] = wide[pl.ds(ids_ref[s, t], 1), :]
                return carry

            lax.fori_loop(0, rows_n, step, 0, unroll=16)

        moved = []
        for k in list(ALL16) + [0]:
            peer = (me + k) % SEQ_N
            fetch(peer)
            block[k] = rows[...].astype(jnp.bfloat16)
            if k:
                moved.append(post.send(block.at[k], low.at[:, spot], seq_at(peer)))
        own = pltpu.make_async_copy(block.at[0], low.at[:, spot], post.fresh())
        own.start()
        for copy in moved:
            copy.wait_recv()
        own.wait()

        start = low[...].astype(jnp.float32)
        x_out[...] = start
        scale = lax.rsqrt(jnp.mean(start * start, axis=-1, keepdims=True) + NORM_EPS)
        n_out[...] = (start * scale * gain_ref[0:1, :]).astype(jnp.bfloat16)
        inner = nt(n_out[...], a_ref[0:24, :]).astype(jnp.bfloat16)
        u_out[...] = inner
        weights[0].wait()

        def project(at):
            packed[:, at] = jnp.dot(
                n_out[...], w_qkv[:, at], preferred_element_type=jnp.float32
            ) + ADAPTER_SCALE * jnp.dot(u_out[...], bi_ref[:, at], preferred_element_type=jnp.float32)

        project(pl.ds(2048, 512))
        for n in range(2):
            some = slice(n * TOK, n * TOK + TOK)
            own_kv[n, :, 0:256] = turn(
                packed[some, 2048:2304], cos_ref[:, 0:256], sin_ref[:, 0:256]
            ).astype(jnp.bfloat16)
            own_kv[n, :, 256:512] = packed[some, 2304:2560].astype(jnp.bfloat16)
        keys = [
            post.send(
                own_kv, kv_out.at[:, pl.ds((4 - k) * TOK, TOK), :], seq_at((me + k) % SEQ_N)
            )
            for k in range(1, 5)
        ]
        kv_out[:, 4 * TOK :, :] = own_kv[...]

        def project_some(n, carry):
            project(pl.ds(pl.multiple_of(n * 512, 512), 512))
            return carry

        lax.fori_loop(0, 4, project_some, 0)
        for copy in keys:
            copy.wait_recv()

        first = me * TOK

        def attend_one(n, carry):
            some = pl.ds(pl.multiple_of(n * TOK, TOK), TOK)
            for h in range(4):
                cols = slice(512 * h, 512 * h + 512)
                turned = turn(packed[some, cols], cos_ref[...], sin_ref[...]).astype(jnp.bfloat16)
                q_out[some, cols] = turned
                mask = window_mask(first, qs_ref[n], ks_ref[n], shift_ref[h])
                probs = probabilities(
                    spread_heads(turned), kv_out[n, :, 64 * h : 64 * h + 64], mask
                )
                values = kv_out[n, :, 256 + 64 * h : 256 + 64 * h + 64]
                mixed = jnp.dot(
                    probs.astype(jnp.bfloat16), values, preferred_element_type=jnp.float32
                )
                a_out[some, cols] = join_heads(mixed).astype(jnp.bfloat16)
            return carry

        lax.fori_loop(0, 2, attend_one, 0)
        middle = nt(a_out[...], a_ref[24:32, :]).astype(jnp.bfloat16)
        v_out[...] = middle
        weights[1].wait()

        def project_out(n, carry):
            at = pl.ds(pl.multiple_of(n * 512, 512), 512)
            mid_out[:, at] = (
                x_out[:, at]
                + jnp.dot(a_out[...], w_out[:, at], preferred_element_type=jnp.float32)
                + ADAPTER_SCALE
                * jnp.dot(v_out[...], bo_ref[:, at], preferred_element_type=jnp.float32)
            )
            return carry

        lax.fori_loop(0, 4, project_out, 0)
        middle_rows = mid_out[...]
        scale = lax.rsqrt(jnp.mean(middle_rows * middle_rows, axis=-1, keepdims=True) + NORM_EPS)
        two_out[...] = (middle_rows * scale * gain_ref[1:2, :]).astype(jnp.bfloat16)
        post.finish()

    def shape(*dims, dtype=jnp.bfloat16):
        return jax.ShapeDtypeStruct(dims, dtype)

    return remote_call(
        body,
        [
            shape(rows_n, 2048, dtype=jnp.float32),
            shape(rows_n, 2048),
            shape(rows_n, 24),
            shape(rows_n, 2048),
            shape(2, 5 * TOK, 512),
            shape(rows_n, 2048),
            shape(rows_n, 8),
            shape(rows_n, 2048, dtype=jnp.float32),
            shape(rows_n, 2048),
        ],
        [ANY, SMEM, ANY] + [VMEM] * 8 + [SMEM],
        [VMEM] * 9,
        [
            pltpu.VMEM((2, vocab, width), jnp.bfloat16),
            pltpu.VMEM((FSDP_N * vocab, width), jnp.float32),
            pltpu.VMEM((rows_n, width), jnp.float32),
            pltpu.VMEM((SEQ_N, rows_n, width), jnp.bfloat16),
            pltpu.VMEM((rows_n, 2048), jnp.bfloat16),
            pltpu.VMEM((rows_n, 2560), jnp.float32),
            pltpu.VMEM((2, TOK, 512), jnp.bfloat16),
            pltpu.VMEM((2048, 2560), jnp.bfloat16),
            pltpu.VMEM((2048, 2048), jnp.bfloat16),
            DMA((sem_count,)),
        ],
        collective_id,
        "attention_block",
    )(table, ids, qkvo, a_low, b_in, b_out, gain, cosine, sine, query_seg, key_seg, shifts)


def chosen_rows(chosen, collective_id):
    def body(src, out, sem):
        post = Post(sem, 24)
        out[fsdp_me()] = src[...]
        greet_devices(fsdp_peers())
        for _ in relay(
            post, out, (pl.ds(0, 32),), (pl.ds(32, 32),), (pl.ds(0, 16),), (pl.ds(16, 16),)
        ):
            pass
        post.finish()

    return remote_call(
        body,
        jax.ShapeDtypeStruct((FSDP_N, *chosen.shape), chosen.dtype),
        [VMEM], VMEM, [DMA((24,))], collective_id, "chosen_rows",
    )(chosen)


def head_step(rows, head, target, weight, scaled, collective_id):
    vocab, width = head.shape
    padded = -(-vocab // 512) * 512
    tiles = padded // 512

    def body(
        rows_ref, head_hbm, target_ref, weight_ref, scaled_ref, out, loss, hd, raised, d_logits, prod,
        got, stat, stats, sem, lsem,
    ):
        post = Post(sem, 60)
        me = fsdp_me()
        last = (tiles - 1) * 512

        def load(n):
            at = pl.ds(pl.multiple_of(n * 512, 512), 512)
            return pltpu.make_async_copy(head_hbm.at[at], hd.at[at], lsem.at[n])

        rest = pl.ds(last, vocab - last)
        load_last = pltpu.make_async_copy(head_hbm.at[rest], hd.at[rest], lsem.at[tiles - 1])
        for n in range(tiles - 1):
            load(n).start()
        load_last.start()
        greet_devices(fsdp_peers())
        hd[vocab:, :] = jnp.zeros((padded - vocab, width), jnp.bfloat16)
        target_at = target_ref[...]

        def logits(n, carry):
            top, picked = carry
            at = pl.multiple_of(n * 512, 512)
            tile = nt(rows_ref[...], hd[pl.ds(at, 512), :])
            column = lax.broadcasted_iota(jnp.int32, (512, 512), 1) + at
            tile = jnp.where(column < vocab, tile, -1e30)
            raised[:, pl.ds(at, 512)] = tile
            top = jnp.maximum(top, jnp.max(tile, axis=1, keepdims=True))
            hit = jnp.where(column == target_at, tile, 0.0)
            return top, picked + jnp.sum(hit, axis=1, keepdims=True)

        def loaded(n, carry):
            load(n).wait()
            return logits(n, carry)

        top, picked = lax.fori_loop(
            0, tiles - 1, loaded,
            (jnp.full((512, 1), -1e30, jnp.float32), jnp.zeros((512, 1), jnp.float32)),
        )
        load_last.wait()
        top, picked = logits(tiles - 1, (top, picked))

        def exponents(n, total):
            at = pl.ds(pl.multiple_of(n * 512, 512), 512)
            tile = jnp.exp(raised[:, at] - top)
            raised[:, at] = tile
            return total + jnp.sum(tile, axis=1, keepdims=True)

        total = lax.fori_loop(0, tiles, exponents, jnp.zeros((512, 1), jnp.float32))
        lane = lax.broadcasted_iota(jnp.int32, (512, 128), 1)
        both = jnp.where(lane == 0, top, jnp.where(lane == 1, total, 0.0))
        stat[...] = jnp.transpose(both)[0:8, :]
        copies = [
            post.send(stat, stats.at[k - 1], fsdp_at((me + k) % FSDP_N)) for k in ALL8
        ]
        for copy in copies:
            copy.wait_recv()
        top_all = stat[0:1, :]
        for n in range(7):
            top_all = jnp.maximum(top_all, stats[n, 0:1, :])
        sum_all = stat[1:2, :] * jnp.exp(stat[0:1, :] - top_all)
        for n in range(7):
            sum_all = sum_all + stats[n, 1:2, :] * jnp.exp(stats[n, 0:1, :] - top_all)
        log_row = top_all + jnp.log(sum_all)
        log_norm = jnp.transpose(jnp.broadcast_to(log_row, (128, 512)))[:, 0:1]
        weights = weight_ref[...]
        mine = lax.broadcasted_iota(jnp.int32, (512, 1), 0) // 64 == me
        value = jnp.sum(jnp.where(mine, log_norm * weights, 0.0) - weights * picked, axis=0, keepdims=True)
        loss[...] = jnp.broadcast_to(value, (8, 128))
        scale = scaled_ref[...]
        factor = scale * jnp.exp(top - log_norm)

        def slopes(n, carry):
            at = pl.multiple_of(n * 512, 512)
            column = lax.broadcasted_iota(jnp.int32, (512, 512), 1) + at
            hit = jnp.where(column == target_at, scale, 0.0)
            d_logits[:, pl.ds(at, 512)] = (factor * raised[:, pl.ds(at, 512)] - hit).astype(jnp.bfloat16)
            return carry

        lax.fori_loop(0, tiles, slopes, 0)
        half, inner = lax.axis_index("fsdp_0"), me % 4
        sums = []
        for n, part in enumerate((1 - half, half)):
            start = pl.multiple_of(part * 256, 256)

            def product(t, carry):
                at = pl.ds(pl.multiple_of(t * 512, 512), 512)
                tile = jnp.dot(
                    d_logits[pl.ds(start, 256), :], hd[:, at], preferred_element_type=jnp.float32
                )
                prod[pl.ds(part * 4, 4), :, at] = tile.astype(jnp.bfloat16).reshape(4, 64, 512)
                return carry

            lax.fori_loop(0, width // 512, product, 0)
            for j in range(n, 4):
                peer = part * 4 + (inner + j) % 4
                sums.append(post.send(prod.at[peer], got.at[4 * n + j - n], fsdp_at(peer)))
        out[...] = prod[me].astype(jnp.float32)
        for n, copy in enumerate(sums):
            copy.wait_recv()
            out[...] += got[n].astype(jnp.float32)
        post.finish()

    return remote_call(
        body,
        [
            jax.ShapeDtypeStruct((64, width), jnp.float32),
            jax.ShapeDtypeStruct((8, 128), jnp.float32),
        ],
        [VMEM, ANY, VMEM, VMEM, VMEM],
        [VMEM, VMEM],
        [
            pltpu.VMEM((padded, width), jnp.bfloat16),
            pltpu.VMEM((512, padded), jnp.float32),
            pltpu.VMEM((512, padded), jnp.bfloat16),
            pltpu.VMEM((8, 64, width), jnp.bfloat16),
            pltpu.VMEM((7, 64, width), jnp.bfloat16),
            pltpu.VMEM((8, 512), jnp.float32),
            pltpu.VMEM((7, 8, 512), jnp.float32),
            DMA((60,)),
            DMA((tiles,)),
        ],
        collective_id,
        "head_step",
    )(rows, head, target, weight, scaled)


def token_gradients(d_start, left, right, ids, loss, vocab, collective_id):
    width = 128
    low_n, tile = 1024, 1024

    def body(
        src, left_ref, right_ref, ids_ref, loss_ref, out, left_out, right_out, totals_out, held, left_parts,
        right_parts, left_mid, right_mid, left_more, right_more, total, spread, sums_a, parts_a, sums_b,
        parts_b, sem, lsem,
    ):
        post = Post(sem, 220)
        f, s = fsdp_me(), seq_me()
        z, yl = z_me(), lax.axis_index("fsdp_2")
        greet_devices(seq_peers() + fsdp_peers())

        def cols(p):
            return pl.ds(pl.multiple_of(p * width, width), width)

        def window(p):
            return pl.ds(pl.multiple_of((9 * p) // 4 * 128, 128), 384)

        moves, sums = [], []
        for k in ALL16:
            peer = (s + k) % SEQ_N
            moves.append(post.send(src.at[:, cols(peer)], held.at[f, s], seq_at(peer)))
        own = pltpu.make_async_copy(src.at[:, cols(s)], held.at[f, s], lsem)
        own.start()
        for k in ALL16:
            peer = (s + k) % SEQ_N
            sums.append(post.send(left_ref.at[:, cols(peer)], left_parts.at[k - 1], seq_at(peer)))
            sums.append(post.send(right_ref.at[:, window(peer)], right_parts.at[k - 1], seq_at(peer)))
        total[...] = jnp.zeros_like(total)
        for copy in moves:
            copy.wait_recv()
        own.wait()

        def add(block, halves=(0, 2)):
            def one(t, carry):
                ids_row = ids_ref[pl.ds(block * 2 + t, 1), :]
                high, low = ids_row >> 10, ids_row & 1023
                part = lax.broadcasted_iota(jnp.int32, (8, tile), 0)
                which = jnp.transpose((part == high).astype(jnp.float32))
                grad = held[block, pl.ds(t * 8, 8)].reshape(tile, width).astype(jnp.float32)
                for h in range(4):
                    spread[:, h * width : (h + 1) * width] = jnp.where(
                        which[:, h : h + 1] > 0.5, grad, 0.0
                    ).astype(jnp.bfloat16)

                def step(n, inner):
                    start = pl.multiple_of(n * 256, 256)
                    row = lax.broadcasted_iota(jnp.int32, (256, tile), 0) + start
                    hot = (row == low).astype(jnp.float32).astype(jnp.bfloat16)
                    total[pl.ds(start, 256), :] += jnp.dot(
                        hot, spread[...], preferred_element_type=jnp.float32
                    )
                    return inner

                lax.fori_loop(0, low_n // 256, step, 0)
                return carry

            lax.fori_loop(*halves, one, 0)

        every = slice(None)
        steps = relay(
            post, held, (pl.ds(0, 8),), (pl.ds(8, 8),), (pl.ds(0, 4),), (pl.ds(4, 4),)
        )
        before, after, far = (z + 3) % 4, (z + 1) % 4, (z + 2) % 4
        next(steps)
        add(f)
        next(steps)
        left_sum, right_sum = left_ref[:, cols(s)], right_ref[:, window(s)]
        for copy in sums:
            copy.wait_recv()
        for n in range(15):
            left_sum, right_sum = left_sum + left_parts[n], right_sum + right_parts[n]
        left_mid[...] = left_sum
        right_mid[...] = right_sum
        shares = []
        for k in ALL8:
            device = fsdp_at((f + k) % FSDP_N)
            shares.append(post.send(left_mid, left_more.at[k - 1], device))
            shares.append(post.send(right_mid, right_more.at[k - 1], device))
        next(steps)
        next(steps)
        add(z * 2 + 1 - yl)
        next(steps)
        next(steps)
        add(before * 2 + yl)
        add(after * 2 + yl)
        next(steps)
        for zz in (before, after):
            add(zz * 2 + 1 - yl, (0, 1))
        add(far * 2 + yl)
        assert next(steps, "end") == "end"
        for zz in (before, after):
            add(zz * 2 + 1 - yl, (1, 2))
        add(far * 2 + 1 - yl)
        squares = jnp.zeros((1, width), jnp.float32)
        for h in range(4):
            count = min(low_n, vocab - h * low_n)
            rows = total[0:count, h * width : (h + 1) * width]
            out[h * low_n : h * low_n + count, :] = rows
            squares = squares + jnp.sum(rows * rows, axis=0, keepdims=True)
        for copy in shares:
            copy.wait_recv()
        for n in range(7):
            left_sum, right_sum = left_sum + left_more[n], right_sum + right_more[n]
        left_out[...] = left_sum
        base = (9 * s) // 4 * 128
        column = lax.broadcasted_iota(jnp.int32, (8, 384), 1) + base
        right_own = jnp.where((column >= 288 * s) & (column < 288 * s + 288), right_sum, 0.0)
        right_out[...] = right_sum
        factor = (column >= 2048).astype(jnp.int32) + (column >= 2304) + (column >= 2560)
        blank = jnp.zeros((32, width), jnp.float32)

        def products(a, b):
            return lax.dot_general(
                a, b, (((1,), (1,)), ((), ())), preferred_element_type=jnp.float32, precision=HIGHEST
            )

        lane = lax.broadcasted_iota(jnp.int32, (8, width), 1)
        row = lax.broadcasted_iota(jnp.int32, (8, width), 0)
        factors = jnp.concatenate([left_sum[0:32], blank, blank, blank], axis=0)
        result = jnp.zeros((8, width), jnp.float32)
        for k in range(4):
            one = products(left_sum[8 * k : 8 * k + 8], factors)
            result = result + jnp.where(lane >> 3 == k, one, 0.0)
        for n in range(3):
            part = right_own[:, n * width : (n + 1) * width]
            which = factor[:, n * width : (n + 1) * width]
            spread_rows = [jnp.where(which == k, part, 0.0) for k in range(4)]
            result = result + products(
                part, jnp.concatenate([blank] + spread_rows + [blank, blank], axis=0)
            )
        small_squares = jnp.sum(
            jnp.sum(left_sum * left_sum, axis=0, keepdims=True), axis=1, keepdims=True
        ) + jnp.sum(jnp.sum(right_own * right_own, axis=0, keepdims=True), axis=1, keepdims=True)
        result = jnp.where((lane == 64) & (row == 0), small_squares, result)
        result = jnp.where(f == 0, result, 0.0)
        result = result + jnp.where(
            (lane == 64) & (row == 0), jnp.sum(squares, axis=1, keepdims=True), 0.0
        )
        result = result + jnp.where((lane == 65) & (row == 0), loss_ref[...], 0.0)
        sums_a[...] = result
        copies = [post.send(sums_a, parts_a.at[k - 1], seq_at((s + k) % SEQ_N)) for k in ALL16]
        for copy in copies:
            copy.wait_recv()
        for n in range(15):
            result = result + parts_a[n]
        sums_b[...] = result
        copies = [post.send(sums_b, parts_b.at[k - 1], fsdp_at((f + k) % FSDP_N)) for k in ALL8]
        for copy in copies:
            copy.wait_recv()
        for n in range(7):
            result = result + parts_b[n]
        totals_out[...] = result
        post.finish()

    return remote_call(
        body,
        [
            jax.ShapeDtypeStruct((vocab, width), jnp.float32),
            jax.ShapeDtypeStruct((40, width), jnp.float32),
            jax.ShapeDtypeStruct((8, 384), jnp.float32),
            jax.ShapeDtypeStruct((8, width), jnp.float32),
        ],
        [VMEM] * 5,
        [VMEM] * 4,
        [
            pltpu.VMEM((FSDP_N, SEQ_N, 128, width), jnp.bfloat16),
            pltpu.VMEM((15, 40, width), jnp.float32),
            pltpu.VMEM((15, 8, 384), jnp.float32),
            pltpu.VMEM((40, width), jnp.float32),
            pltpu.VMEM((8, 384), jnp.float32),
            pltpu.VMEM((7, 40, width), jnp.float32),
            pltpu.VMEM((7, 8, 384), jnp.float32),
            pltpu.VMEM((low_n, 4 * width), jnp.float32),
            pltpu.VMEM((tile, 4 * width), jnp.bfloat16),
            pltpu.VMEM((8, width), jnp.float32),
            pltpu.VMEM((15, 8, width), jnp.float32),
            pltpu.VMEM((8, width), jnp.float32),
            pltpu.VMEM((7, 8, width), jnp.float32),
            DMA((220,)),
            DMA,
        ],
        collective_id,
        "token_gradients",
    )(d_start, left, right, ids, loss)


def feed_forward(rows, gate_up_parts, down_parts, saved, collective_id, name):
    forward = saved is None
    count, width = rows.shape
    quarter = sum(part.shape[1] for part in gate_up_parts)
    units = quarter // 2
    parts_n = len(gate_up_parts)
    chunk = count // 2
    tile = 512

    def body(*refs):
        if forward:
            src, gu_hbm, dn_hbm = refs[0], refs[1 : 1 + parts_n], refs[1 + parts_n : 1 + 2 * parts_n]
            out, gu_out, held, gu, dn, saved_v, mid, part, give, got, sem = refs[1 + 2 * parts_n :]
        else:
            src, gu_hbm, dn_hbm = refs[0], refs[1 : 1 + parts_n], refs[1 + parts_n : 1 + 2 * parts_n]
            gu_in, out, held, gu, dn, saved_v, mid, part, give, got, sem = refs[1 + 2 * parts_n :]
        c = lax.axis_index("seq_2")
        sibling = {"seq_2": 1 - c}
        partner = {"fsdp_1": 1 - lax.axis_index("fsdp_1")}
        used = [0]

        def fresh():
            used[0] += 1
            return sem.at[used[0] - 1]

        load_gu, load_dn = [], []
        for copies, hbm, whole in ((load_gu, gu_hbm, gu), (load_dn, dn_hbm, dn)):
            at = 0
            for piece in hbm:
                view = whole.at[:, pl.ds(at, piece.shape[1])]
                copies.append(pltpu.make_async_copy(piece, view, fresh()))
                at += piece.shape[1]
        loads = [load_gu, load_dn]
        if not forward:
            load_dn.append(pltpu.make_async_copy(gu_in, saved_v, fresh()))
            loads = [load_dn, load_gu]
        for load in loads[0] + loads[1]:
            load.start()

        barrier = pltpu.get_barrier_semaphore()
        for device in (sibling, partner):
            pl.semaphore_signal(barrier, inc=1, device_id=device, device_id_type=MESH_ID)
        pl.semaphore_wait(barrier, 2)

        started = []

        def remote(src_ref, dst_ref, device):
            copy = pltpu.make_async_remote_copy(
                src_ref=src_ref, dst_ref=dst_ref, send_sem=fresh(), recv_sem=fresh(),
                device_id=device, device_id_type=MESH_ID,
            )
            copy.start()
            started.append(copy)
            return copy

        def lines(block, k=None):
            if k is None:
                return pl.ds(block * count, count)
            return pl.ds(2 * count + (2 * k + block - 2) * chunk, chunk)

        along = [
            remote(src.at[pl.ds(k * chunk, chunk)], held.at[lines(2, k)], partner) for k in range(2)
        ]
        beside = remote(src, held.at[lines(1)], sibling)
        held[lines(0), :] = src[...]

        def first_product(first, size):
            mine, low_rows = pl.ds(first, size), pl.ds(0, size)

            def step(n, carry):
                at = pl.multiple_of(n * tile, tile)
                low, high = pl.ds(at, tile), pl.ds(pl.multiple_of(at + units, tile), tile)
                block = held[mine, :]
                if forward:
                    gate = jnp.dot(block, gu[:, low], preferred_element_type=jnp.float32)
                    up = jnp.dot(block, gu[:, high], preferred_element_type=jnp.float32)
                    saved_v[mine, low] = gate
                    saved_v[mine, high] = up
                    mid[low_rows, low] = (gate * jax.nn.sigmoid(gate) * up).astype(jnp.bfloat16)
                else:
                    d_hidden = nt(block, dn[low, :])
                    gate, up = saved_v[mine, low], saved_v[mine, high]
                    sigmoid_of = jax.nn.sigmoid(gate)
                    mid[low_rows, low] = (
                        d_hidden * up * sigmoid_of * (1.0 + gate * (1.0 - sigmoid_of))
                    ).astype(jnp.bfloat16)
                    mid[low_rows, high] = (d_hidden * gate * sigmoid_of).astype(jnp.bfloat16)
                return carry

            lax.fori_loop(0, units // tile, step, 0)

        def second_product(first, size):
            mine, low_rows = pl.ds(first, size), pl.ds(0, size)

            def step(n, carry):
                at = pl.ds(pl.multiple_of(n * tile, tile), tile)
                if forward:
                    part[mine, at] = jnp.dot(
                        mid[low_rows, :], dn[:, at], preferred_element_type=jnp.float32
                    )
                else:
                    part[mine, at] = nt(mid[low_rows, :], gu[at, :])
                return carry

            lax.fori_loop(0, width // tile, step, 0)

        for load in loads[0]:
            load.wait()
        beside.wait_recv()
        first_product(0, 2 * count)
        along[0].wait_recv()
        passed = [remote(held.at[lines(2, 0)], held.at[lines(3, 0)], sibling)]
        for load in loads[1]:
            load.wait()
        second_product(0, 2 * count)
        give[0] = part[lines(1), :].astype(jnp.bfloat16)
        home = remote(give.at[0], got.at[0], sibling)
        stores = []

        def store(first, size):
            if forward:
                copy = pltpu.make_async_copy(
                    saved_v.at[pl.ds(first, size)], gu_out.at[pl.ds(first, size)], fresh()
                )
                copy.start()
                stores.append(copy)

        store(0, 2 * count)
        over, back = [], []

        def hand_over(k):
            some = pl.ds(k * chunk, chunk)
            give[1, some, :] = part[lines(3, k), :].astype(jnp.bfloat16)
            over.append(remote(give.at[1, some], got.at[1, some], sibling))

        def send_back(k):
            some = pl.ds(k * chunk, chunk)
            over[k].wait_recv()
            give[2, some, :] = (part[lines(2, k), :] + got[1, some, :].astype(jnp.float32)).astype(
                jnp.bfloat16
            )
            back.append(remote(give.at[2, some], got.at[2, some], partner))

        first, second = 2 * count, 2 * count + 2 * chunk
        passed[0].wait_recv()
        first_product(first, 2 * chunk)
        along[1].wait_recv()
        passed.append(remote(held.at[lines(2, 1)], held.at[lines(3, 1)], sibling))
        second_product(first, 2 * chunk)
        hand_over(0)
        passed[1].wait_recv()
        first_product(second, 2 * chunk)
        send_back(0)
        store(first, 4 * chunk)
        second_product(second, 2 * chunk)
        hand_over(1)
        send_back(1)
        home.wait_recv()
        out[...] = part[lines(0), :] + got[0].astype(jnp.float32)
        for k in range(2):
            some = pl.ds(k * chunk, chunk)
            back[k].wait_recv()
            out[some, :] += got[2, some, :].astype(jnp.float32)
        for copy in started:
            copy.wait_send()
        if forward:
            for copy in stores:
                copy.wait()

    scratch = [
        pltpu.VMEM((4 * count, width), jnp.bfloat16),
        pltpu.VMEM((width, quarter), jnp.bfloat16),
        pltpu.VMEM((units, width), jnp.bfloat16),
        pltpu.VMEM((4 * count, quarter), jnp.float32),
        pltpu.VMEM((2 * count, units if forward else quarter), jnp.bfloat16),
        pltpu.VMEM((4 * count, width), jnp.float32),
        pltpu.VMEM((3, count, width), jnp.bfloat16),
        pltpu.VMEM((3, count, width), jnp.bfloat16),
        DMA((32,)),
    ]
    total = jax.ShapeDtypeStruct((count, width), jnp.float32)
    if forward:
        products = jax.ShapeDtypeStruct((4 * count, quarter), jnp.float32)
        return remote_call(
            body, [total, products], [VMEM] + [ANY] * (2 * parts_n), [VMEM, ANY], scratch,
            collective_id, name,
        )(rows, *gate_up_parts, *down_parts)
    return remote_call(
        body, total, [VMEM] + [ANY] * (2 * parts_n + 1), VMEM, scratch, collective_id, name
    )(rows, *gate_up_parts, *down_parts, saved)


def turn(values, cosine, sine):
    width = values.shape[-1]
    lane = lax.broadcasted_iota(jnp.int32, values.shape, values.ndim - 1)
    swapped = jnp.where(
        lane % 64 < 32,
        pltpu.roll(values, width - 32, values.ndim - 1),
        pltpu.roll(values, 32, values.ndim - 1),
    )
    return values * cosine + swapped * sine


def key_value_back(far, own, cosine, sine, collective_id):
    def body(far_ref, own_ref, cos_ref, sin_ref, out, held, sem):
        me = seq_me()
        post = Post(sem, 8)
        barrier = pltpu.get_barrier_semaphore()
        for k in range(1, 5):
            pl.semaphore_signal(
                barrier, inc=1, device_id=seq_at((me + k) % SEQ_N), device_id_type=MESH_ID
            )
        pl.semaphore_wait(barrier, 4)
        copies = [
            post.send(
                far_ref.at[:, pl.ds((4 - k) * TOK, TOK), :], held.at[4 - k],
                seq_at((me + SEQ_N - k) % SEQ_N),
            )
            for k in range(1, 5)
        ]
        for copy in copies:
            copy.wait_recv()
        for m in range(2):
            total = own_ref[m]
            for n in range(3, -1, -1):
                total = total + held[n, m].astype(jnp.float32)
            keys = turn(total[:, 0:256], cos_ref[:, 0:256], -sin_ref[:, 0:256])
            out[pl.ds(m * TOK, TOK), 0:256] = keys.astype(jnp.bfloat16)
            out[pl.ds(m * TOK, TOK), 256:512] = total[:, 256:512].astype(jnp.bfloat16)
        post.finish()

    return remote_call(
        body,
        jax.ShapeDtypeStruct((2 * TOK, 512), jnp.bfloat16),
        [VMEM] * 4,
        VMEM,
        [pltpu.VMEM((4, 2, TOK, 512), jnp.bfloat16), DMA((8,))],
        collective_id,
        "key_value_back",
    )(far, own, cosine, sine)


def spread_heads(block):
    return jnp.concatenate([block[:, 64 * g : 64 * g + 64] for g in range(8)], axis=0)


def join_heads(block):
    return jnp.concatenate([block[64 * g : 64 * g + 64, :] for g in range(8)], axis=1)


def window_mask(start, query_seg, key_seg, shift):
    query = start + lax.broadcasted_iota(jnp.int32, (TOK, 5 * TOK), 0)
    key = start - 4 * TOK + lax.broadcasted_iota(jnp.int32, (TOK, 5 * TOK), 1)
    allowed = (
        (key <= query)
        & (key >= 0)
        & (query_seg == key_seg)
        & (((query + shift) >> 8) == ((key + shift) >> 8))
    )
    return jnp.concatenate([allowed.astype(jnp.float32)] * 8, axis=0) > 0.5


def nt(left, right):
    return lax.dot_general(
        left, right, (((1,), (1,)), ((), ())), preferred_element_type=jnp.float32
    )


def tn(left, right):
    return lax.dot_general(
        left, right, (((0,), (0,)), ((), ())), preferred_element_type=jnp.float32
    )


def probabilities(queries, keys, mask):
    scores = jnp.where(mask, nt(queries, keys) * 0.125, -1e30)
    top = jnp.max(scores, axis=-1, keepdims=True)
    raised = jnp.where(mask, jnp.exp(scores - top), 0.0)
    return raised / jnp.sum(raised, axis=-1, keepdims=True)


def attend_back(queries, window, upstream, cosine, sine, query_seg, key_seg, start, shifts):
    def body(
        start_ref, shift_ref, q_ref, kv_ref, g_ref, cos_ref, sin_ref, qs_ref, ks_ref,
        dq_out, far_out, own_out,
    ):
        for h in range(4):
            cols = slice(512 * h, 512 * h + 512)
            mask = window_mask(start_ref[0], qs_ref[0], ks_ref[0], shift_ref[h])
            spread = spread_heads(q_ref[:, cols])
            keys = kv_ref[0, :, 64 * h : 64 * h + 64]
            values = kv_ref[0, :, 256 + 64 * h : 256 + 64 * h + 64]
            probs = probabilities(spread, keys, mask)
            grads = spread_heads(g_ref[:, cols])
            d_probs = nt(grads, values)
            d_values = tn(probs.astype(jnp.bfloat16), grads)
            inner = jnp.sum(probs * d_probs, axis=-1, keepdims=True)
            d_scores = (0.125 * probs * (d_probs - inner)).astype(jnp.bfloat16)
            d_queries = join_heads(jnp.dot(d_scores, keys, preferred_element_type=jnp.float32))
            dq_out[:, cols] = turn(d_queries, cos_ref[...], -sin_ref[...]).astype(jnp.bfloat16)
            d_keys = tn(d_scores, spread)
            for at, part in ((64 * h, d_keys), (256 + 64 * h, d_values)):
                far_out[0, :, at : at + 64] = part[0 : 4 * TOK].astype(jnp.bfloat16)
                own_out[0, :, at : at + 64] = part[4 * TOK :]

    wide = pl.BlockSpec((TOK, 2048), lambda m: (m, 0))
    return pl.pallas_call(
        body,
        out_shape=[
            jax.ShapeDtypeStruct((2 * TOK, 2048), jnp.bfloat16),
            jax.ShapeDtypeStruct((2, 4 * TOK, 512), jnp.bfloat16),
            jax.ShapeDtypeStruct((2, TOK, 512), jnp.float32),
        ],
        grid=(2,),
        in_specs=[
            SMEM,
            SMEM,
            wide,
            pl.BlockSpec((1, 5 * TOK, 512), lambda m: (m, 0, 0)),
            wide,
            pl.BlockSpec((TOK, 512), lambda m: (0, 0)),
            pl.BlockSpec((TOK, 512), lambda m: (0, 0)),
            pl.BlockSpec((1, TOK, 1), lambda m: (m, 0, 0)),
            pl.BlockSpec((1, 1, 5 * TOK), lambda m: (m, 0, 0)),
        ],
        out_specs=[
            wide,
            pl.BlockSpec((1, 4 * TOK, 512), lambda m: (m, 0, 0)),
            pl.BlockSpec((1, TOK, 512), lambda m: (m, 0, 0)),
        ],
        compiler_params=pltpu.CompilerParams(vmem_limit_bytes=VMEM_LIMIT),
        name="attend_back",
    )(start, shifts, queries, window, upstream, cosine, sine, query_seg, key_seg)


def small_updates(
    totals, left, right, rank, a_old, b_old, width_a, width_b, gain, gain_first, gain_second, columns
):
    def body(
        t_ref, l_ref, r_ref, k_ref, a_ref, b_ref, wa_ref, wb_ref, g_ref, gf_ref, gs_ref, c_ref,
        scalars, ga_out, gb_out, gf_out, gs_out, g_out, k_out, wa_out, wb_out, a_out, b_out,
    ):
        totals_now = t_ref[...]
        norm = jnp.sqrt(totals_now[0:1, 64:65])
        clip = CLIP_MAX / jnp.maximum(norm, CLIP_MAX)
        lane = lax.broadcasted_iota(jnp.int32, (8, 128), 1)
        scalars[...] = jnp.where(lane == 0, norm, jnp.where(lane == 1, clip, 0.0))
        parts = [totals_now[:, 8 * k : 8 * k + 8] for k in range(8)]
        square = (clip * clip)[0:1, 0:1].reshape(1, 1, 1)
        stats = SECOND_DECAY * k_ref[...] + (1.0 - SECOND_DECAY) * square * jnp.stack(parts)
        k_out[...] = stats

        def times(x, y):
            total = x[:, :, 0:1] * y[:, 0:1, :]
            for n in range(1, 8):
                total = total + x[:, :, n : n + 1] * y[:, n : n + 1, :]
            return total

        size = jnp.sqrt(jnp.sum(jnp.sum(stats * stats, axis=2, keepdims=True), axis=1, keepdims=True))
        unit = (
            lax.broadcasted_iota(jnp.int32, (8, 8, 8), 1) == lax.broadcasted_iota(jnp.int32, (8, 8, 8), 2)
        ).astype(jnp.float32)

        def newton(n, carry):
            root, matrix = carry
            factor = (5.0 * unit - matrix) * 0.25
            square_of = times(factor, factor)
            return times(root, factor), times(times(square_of, square_of), matrix)

        roots, _ = lax.fori_loop(
            0, 10, newton, (unit * lax.rsqrt(jnp.sqrt(size)), stats / size)
        )

        gradient = l_ref[...] * clip
        down = gradient[0:32]
        ga_out[...] = down
        up = r_ref[...] * clip
        gb_out[...] = up

        first = FIRST_DECAY * gf_ref[...] + (1.0 - FIRST_DECAY) * gradient[32:35]
        second = SECOND_DECAY * gs_ref[...] + (1.0 - SECOND_DECAY) * gradient[32:35] * gradient[32:35]
        gf_out[...] = first
        gs_out[...] = second
        first_hat = first / (1.0 - FIRST_DECAY**STEP)
        second_hat = second / (1.0 - SECOND_DECAY**STEP)
        gains = g_ref[...]
        g_out[...] = gains - RATE_GAIN * (
            first_hat / (jnp.sqrt(second_hat) + ADAM_EPS) + WEIGHT_DECAY * gains
        )

        def apply(root, gradients):
            total = root[:, 0:1] * gradients[0:1, :]
            for n in range(1, 8):
                total = total + root[:, n : n + 1] * gradients[n : n + 1, :]
            return total

        for k in range(4):
            rows = slice(8 * k, 8 * k + 8)
            mine = down[rows]
            wide = SECOND_DECAY * wa_ref[k : k + 1, :] + (1.0 - SECOND_DECAY) * jnp.sum(
                mine * mine, axis=0, keepdims=True
            )
            wa_out[k : k + 1, :] = wide
            a_out[rows, :] = a_ref[rows, :] - LEARN_RATE_DOWN * (
                apply(roots[k], mine) * lax.rsqrt(jnp.sqrt(wide))
            )
        wide = SECOND_DECAY * wb_ref[...] + (1.0 - SECOND_DECAY) * jnp.sum(
            up * up, axis=0, keepdims=True
        )
        wb_out[...] = wide
        column = c_ref[...]
        factor = (column >= 2048).astype(jnp.int32) + (column >= 2304) + (column >= 2560)
        step = jnp.zeros(up.shape, jnp.float32)
        for k in range(4):
            step = step + jnp.where(factor == k, apply(roots[4 + k], up), 0.0)
        b_out[...] = b_ref[...] - LEARN_RATE_UP * (step * lax.rsqrt(jnp.sqrt(wide)))

    def like(array):
        return jax.ShapeDtypeStruct(array.shape, jnp.float32)

    return pl.pallas_call(
        body,
        out_shape=[
            jax.ShapeDtypeStruct((8, 128), jnp.float32), like(a_old), like(right), like(gain), like(gain),
            like(gain), like(rank), like(width_a), like(width_b), like(a_old), like(b_old),
        ],
        in_specs=[VMEM] * 12,
        out_specs=[VMEM] * 11,
        compiler_params=pltpu.CompilerParams(vmem_limit_bytes=VMEM_LIMIT),
        name="small_updates",
    )(
        totals, left, right, rank, a_old, b_old, width_a, width_b, gain, gain_first, gain_second, columns
    )


def dot(left, right):
    return jnp.dot(left, right, preferred_element_type=jnp.float32)


def dot_exact(left, right):
    return jnp.dot(left, right, precision=HIGHEST)


def norm_scale(values):
    return lax.rsqrt(jnp.mean(values * values, axis=-1, keepdims=True) + NORM_EPS)


def norm_back(values, gain, upstream):
    scale_of = norm_scale(values)
    scaled = gain * upstream
    inward = scale_of * scaled - values * scale_of**3 * jnp.mean(
        scaled * values, axis=-1, keepdims=True
    )
    return (inward, jnp.sum(upstream * values * scale_of, axis=0))


def adam_update(weight_vals, first_old, second_old, gradient, rate):
    first_new = FIRST_DECAY * first_old + (1.0 - FIRST_DECAY) * gradient
    second_new = SECOND_DECAY * second_old + (1.0 - SECOND_DECAY) * gradient * gradient
    first_hat = first_new / (1.0 - FIRST_DECAY**STEP)
    second_hat = second_new / (1.0 - SECOND_DECAY**STEP)
    step_vals = first_hat / (jnp.sqrt(second_hat) + ADAM_EPS) + WEIGHT_DECAY * weight_vals
    return (first_new, second_new, weight_vals - rate * step_vals)


def per_device(
    input_token_index,
    target_token_index,
    loss_position_index,
    document_slot_index,
    row_used_length,
    head_group_offsets,
    embedding,
    embedding_first_moment,
    embedding_second_moment,
    frozen_output_table,
    frozen_query_key_value_weight,
    frozen_attention_output_weight,
    frozen_gate_up_weight,
    frozen_down_weight,
    norm_gain_vectors,
    norm_gain_first_moment,
    norm_gain_second_moment,
    adapter_down_factors,
    adapter_up_factors,
    rank_side_statistics,
    down_width_statistics,
    up_width_statistics,
):
    fsdp_here = lax.axis_index(FSDP)
    seq_here = lax.axis_index(SEQ)
    vocab_dev = embedding.shape[0]

    qkvo_own = jnp.concatenate([frozen_query_key_value_weight, frozen_attention_output_weight], 1)
    down_own = jnp.pad(frozen_down_weight, ((0, 4), (0, 0)))
    small_own = jnp.pad(
        jnp.concatenate(
            [
                adapter_down_factors.reshape(-1),
                norm_gain_vectors.reshape(-1),
                adapter_up_factors.reshape(-1),
            ]
        ),
        (0, 1024 - 848),
    ).reshape(8, 128)
    ids_own = jnp.pad(input_token_index.reshape(16, TOK), ((0, 0), (0, 64)))
    qkvo, small, table, ids, gate_up_w, down_w = gather_weights(
        qkvo_own,
        small_own,
        embedding.astype(jnp.bfloat16),
        ids_own,
        frozen_gate_up_weight,
        down_own,
    )
    qkvo = qkvo.reshape(2048, 4608)
    w_qkv, w_out = qkvo[:, :2560], qkvo[:, 2560:]
    head_own, ids = lax.optimization_barrier((frozen_output_table, ids))
    head = lax.all_gather(head_own, SEQ, axis=1, tiled=True)
    small = small.reshape(128, 1024)
    down_full = small[:, :512].reshape(128, 32, 16).transpose(1, 0, 2).reshape(32, 2048)
    gain = small[:, 512:560].reshape(128, 3, 16).transpose(1, 0, 2).reshape(3, 2048)
    up_full = small[:, 560:848].reshape(128, 8, 36).transpose(1, 0, 2).reshape(8, 4608)
    a_low = down_full.astype(jnp.bfloat16)
    b_low = up_full.astype(jnp.bfloat16)
    a_low, b_low, gain = lax.optimization_barrier((a_low, b_low, gain))
    a_in, a_out = a_low[:24], a_low[24:]
    factor_of = (jnp.arange(2560) >= 2048).astype(jnp.int32) + (jnp.arange(2560) >= 2304)
    b_in = jnp.where(
        (jnp.arange(24) // 8)[:, None] == factor_of[None, :],
        jnp.concatenate([b_low[:, :2560]] * 3, 0),
        jnp.zeros((), jnp.bfloat16),
    )
    b_out = b_low[:, 2560:]

    places = loss_position_index.reshape(2, 8, SEQ_N, 32)
    spots = jnp.arange(SEQ_N)[:, None] * TOK + places
    counted = spots < row_used_length[..., None, None]
    below = jnp.sum(
        (document_slot_index[..., None] < jnp.arange(1, 3)).astype(jnp.int32), axis=2
    )
    seg_at = jnp.sum(
        (spots[..., None] >= below[:, :, None, None, :]).astype(jnp.int32), axis=-1
    )
    member = counted[..., None] & (seg_at[..., None] == jnp.arange(3))
    counts = jnp.sum(member.astype(jnp.int32), axis=(2, 3))
    document_total = jnp.sum((counts > 0).astype(jnp.float32))
    own_places = lax.dynamic_index_in_dim(places, seq_here, 2, keepdims=False)
    own_counted = lax.dynamic_index_in_dim(counted, seq_here, 2, keepdims=False)
    own_seg = lax.dynamic_index_in_dim(seg_at, seq_here, 2, keepdims=False)
    per_doc = jnp.sum(
        jnp.where(own_seg[..., None] == jnp.arange(3), counts[:, :, None, :], 0), axis=-1
    )
    own_weight = jnp.where(own_counted, 1.0 / jnp.maximum(per_doc, 1).astype(jnp.float32), 0.0)
    weight_flat = own_weight.transpose(1, 0, 2).reshape(-1)
    row_places = lax.dynamic_index_in_dim(own_places, fsdp_here, 1, keepdims=False)
    chosen_at = (row_places + jnp.arange(2)[:, None] * TOK).reshape(64)
    pick = (chosen_at[:, None] == jnp.arange(128)[None, :]).astype(jnp.float32)

    ids = ids[:, :, :TOK].reshape(SEQ_N, 2, 8, TOK)
    row_ids = lax.dynamic_index_in_dim(ids, fsdp_here, 2, keepdims=False).reshape(SEQ_N, 128)
    half = 32
    freqs = ROPE_BASE ** (-2.0 * jnp.arange(half).astype(jnp.float32) / 64)
    angles = (seq_here * TOK + jnp.arange(TOK)).astype(jnp.float32)[:, None] * freqs[None, :]
    cosine = jnp.tile(jnp.cos(angles), (1, 16))
    sine = jnp.sin(angles)
    sine = jnp.tile(jnp.concatenate([-sine, sine], 1), (1, 8))
    own_docs = lax.dynamic_index_in_dim(document_slot_index, fsdp_here, 1, keepdims=False)
    padded = jnp.concatenate([jnp.full((2, 4 * TOK), -1, jnp.int32), own_docs], 1)
    key_seg = lax.dynamic_slice_in_dim(padded, seq_here * TOK, 5 * TOK, 1)[:, None, :]
    query_seg = key_seg[:, 0, 4 * TOK :][:, :, None]
    start = (seq_here * TOK).reshape(1)
    (
        x_start, normed_one, adapter_in, queries, window, attended, adapter_mid, x_mid, normed_two,
    ) = attention_block(
        table, row_ids, qkvo, a_low, b_in, b_out, gain, cosine, sine, query_seg, key_seg,
        head_group_offsets, 2,
    )
    gate_up_w = [gate_up_w.reshape(2048, -1)]
    down_w = [down_w.reshape(PAD_FF // 4, -1)]

    hidden_sum, gate_up = feed_forward(normed_two, gate_up_w, down_w, None, 12, "feed_forward")
    x_end = x_mid + hidden_sum
    normed_end = (x_end * norm_scale(x_end) * gain[2]).astype(jnp.bfloat16)

    chosen = dot(pick.astype(jnp.bfloat16), normed_end).astype(jnp.bfloat16)
    local_target = target_token_index.transpose(1, 0, 2).reshape(512, 1) - fsdp_here * vocab_dev
    local_target = jnp.where(local_target < vocab_dev, local_target, -1)
    weight_column = weight_flat.reshape(512, 1)
    rows = chosen_rows(chosen, 5).reshape(512, 2048)
    head, rows = lax.optimization_barrier((head, rows))
    d_chosen, loss_tile = head_step(
        rows, head, local_target, weight_column, weight_column / document_total, 4
    )

    upstream = lax.dot_general(pick, d_chosen, (((0,), (0,)), ((), ())), precision=HIGHEST)
    d_end, gain_end = norm_back(x_end, gain[2], upstream)
    d_normed = feed_forward(
        d_end.astype(jnp.bfloat16), gate_up_w, down_w, gate_up, 13, "feed_forward_back"
    )
    back_two, gain_mid = norm_back(x_mid, gain[1], d_normed)
    d_mid = d_end + back_two

    d_branch = d_mid.astype(jnp.bfloat16)
    d_adapter_mid = (ADAPTER_SCALE * nt(d_branch, b_out)).astype(jnp.bfloat16)
    d_attended = (nt(d_branch, w_out) + dot(d_adapter_mid, a_out)).astype(jnp.bfloat16)
    up_gradient_out = ADAPTER_SCALE * tn(adapter_mid, d_branch)
    down_gradient_out = tn(d_adapter_mid, attended)
    d_queries, d_far, d_own = attend_back(
        queries, window, d_attended, cosine, sine, query_seg, key_seg, start, head_group_offsets
    )
    d_key_value = key_value_back(d_far, d_own, cosine, sine, 7)
    d_packed = jnp.concatenate([d_queries, d_key_value], 1)
    d_adapter_in = (ADAPTER_SCALE * nt(d_packed, b_in)).astype(jnp.bfloat16)
    up_gradient_in = ADAPTER_SCALE * jnp.concatenate(
        [
            tn(adapter_in[:, 0:8], d_packed[:, :2048]),
            tn(adapter_in[:, 8:16], d_packed[:, 2048:2304]),
            tn(adapter_in[:, 16:24], d_packed[:, 2304:]),
        ],
        1,
    )
    down_gradient_in = tn(d_adapter_in, normed_one)
    back_one, gain_start = norm_back(
        x_start, gain[0], nt(d_packed, w_qkv) + dot(d_adapter_in, a_in)
    )
    d_start = (d_mid + back_one).astype(jnp.bfloat16)

    left = jnp.concatenate(
        [
            down_gradient_in,
            down_gradient_out,
            jnp.stack([gain_start, gain_mid, gain_end]),
            jnp.zeros((5, 2048), jnp.float32),
        ],
        0,
    )
    right = jnp.concatenate([up_gradient_in, up_gradient_out], 1)
    all_ids = ids.transpose(2, 0, 1, 3).reshape(16, 1024) - fsdp_here * vocab_dev
    grad_embed, left_sum, right_sum, totals = token_gradients(
        d_start, left, right, all_ids, loss_tile, vocab_dev, 8
    )
    document_loss_sum = totals[0, 65]

    own_left = lax.dynamic_slice_in_dim(left_sum, fsdp_here * 16, 16, 1)
    own_right = lax.dynamic_slice_in_dim(
        right_sum, 32 * ((9 * seq_here) % 4) + fsdp_here * 36, 36, 1
    )
    columns = ((seq_here * 8 + fsdp_here) * 36 + jnp.arange(36)).reshape(1, 36)
    (
        scalars,
        down_factor_gradient,
        up_factor_gradient,
        updated_gain_first_moment,
        updated_gain_second_moment,
        updated_norm_gains,
        updated_rank_statistics,
        updated_down_width_statistics,
        updated_up_width_statistics,
        updated_down_factors,
        updated_up_factors,
    ) = small_updates(
        totals,
        own_left,
        own_right,
        rank_side_statistics,
        adapter_down_factors,
        adapter_up_factors,
        down_width_statistics,
        up_width_statistics.reshape(1, 36),
        norm_gain_vectors,
        norm_gain_first_moment,
        norm_gain_second_moment,
        columns,
    )
    updated_up_width_statistics = updated_up_width_statistics.reshape(36)
    global_gradient_norm = scalars[0, 0]
    grad_embed = grad_embed * scalars[0, 1]
    unused_first, updated_embedding_second_moment, updated_embedding_table = adam_update(
        embedding, embedding_first_moment, embedding_second_moment, grad_embed, RATE_EMBED
    )
    return (
        document_loss_sum,
        document_total,
        global_gradient_norm,
        grad_embed,
        updated_embedding_second_moment,
        updated_embedding_table,
        updated_gain_first_moment,
        updated_gain_second_moment,
        updated_norm_gains,
        down_factor_gradient,
        up_factor_gradient,
        updated_rank_statistics,
        updated_down_width_statistics,
        updated_up_width_statistics,
        updated_down_factors,
        updated_up_factors,
    )


def solution(mesh):
    torus = Mesh(
        mesh.devices.reshape(2, 4, 2, 2, 2, 2), SEQ_FSDP
    )
    return jax.shard_map(
        per_device,
        mesh=torus,
        in_specs=(
            P(None, None, SEQ),
            P(None, None, SEQ),
            P(),
            P(),
            P(),
            P(),
            P(FSDP, SEQ),
            P(FSDP, SEQ),
            P(FSDP, SEQ),
            P(FSDP, SEQ),
            P(SEQ_FSDP, None),
            P(SEQ_FSDP, None),
            P(SEQ_FSDP, None),
            P(SEQ_FSDP, None),
            P(None, SEQ_FSDP),
            P(None, SEQ_FSDP),
            P(None, SEQ_FSDP),
            P(None, SEQ_FSDP),
            P(None, SEQ_FSDP),
            P(),
            P(None, SEQ_FSDP),
            P(SEQ_FSDP),
        ),
        out_specs=(
            P(),
            P(),
            P(),
            P(FSDP, SEQ),
            P(FSDP, SEQ),
            P(FSDP, SEQ),
            P(None, SEQ_FSDP),
            P(None, SEQ_FSDP),
            P(None, SEQ_FSDP),
            P(None, SEQ_FSDP),
            P(None, SEQ_FSDP),
            P(),
            P(None, SEQ_FSDP),
            P(SEQ_FSDP),
            P(None, SEQ_FSDP),
            P(None, SEQ_FSDP),
        ),
        check_vma=False,
    )
```
